32 devices in a mesh: dp: 16 (over z, x, core), mp: 2 (over y).
Axes of the slice: x: 2, y: 2, z: 4, core: 2. Of those that a mesh axis runs over, the one named last changes fastest.
Arguments:
- tokens: bfloat16 [8192, 1024], P('dp'), may hold values from -6 to 6
- seq_lengths: int32 [64], P('dp'), may hold values from 0 to 512, as said below
- ln_gain: float32 [4, 1024], replicated, may hold values from 0.1 to 1.9
- ln_bias: float32 [4, 1024], replicated, may hold values from -3 to 3
- w_qkv: bfloat16 [3, 1024, 1024], P(None, 'dp', 'mp'), may hold values from -0.25 to 0.25
- w_out: bfloat16 [1024, 1024], P('mp', 'dp'), may hold values from -0.5 to 0.5
- w_up: bfloat16 [1024, 4096], P('dp', 'mp'), may hold values from -0.1875 to 0.1875
- w_down: bfloat16 [4096, 1024], P('mp', 'dp'), may hold values from -0.09375 to 0.09375
- cotangent: bfloat16 [8192, 1024], P(('dp', 'mp')), may hold values from -6 to 6
Outputs:
- output: bfloat16 [8192, 1024], P(('dp', 'mp'))
- grad_tokens: float32 [8192, 1024], P(('dp', 'mp'))
- grad_qkv: float32 [3, 1024, 1024], P(None, 'dp', 'mp')
- grad_out: float32 [1024, 1024], P('mp', 'dp')
- grad_up: float32 [1024, 4096], P('dp', 'mp')
- grad_down: float32 [4096, 1024], P('mp', 'dp')
- grad_gain: float32 [4, 1024], P(None, 'dp')
- grad_bias: float32 [4, 1024], P(None, 'dp')
The draws below stay inside these ranges and needn't reach their ends.
Inputs may be any that keep to these rules, and one draw needn't show every extreme that they name: `seq_lengths`: within every group of 512 tokens (blocks of 128), the first block starts a sequence; a sequence that starts at block b and covers n blocks has a length from n * 128 - 128 // 2 + 1 to n * 128, the rest of its last block being padding. In every draw some group holds a single sequence of exactly 512 tokens.
All inputs are finite; a program needn't handle non-finite values.
Results may differ from the reference program's by a relative error of at most 0.023.
Values may be sent and summed in bfloat16 or wider, within the bound.
No kernel may reach another device: no remote copies, remote signals or barrier semaphores. Data moves between devices by JAX's collectives and lax.ppermute only.
A program may use at most 128 MiB of HBM per device.

```python
import jax
import jax.numpy as jnp
from jax import lax

D = 1024
HEADS = 16
HD = 64
FF = 4096
TOK_DEV = 512
BLOCK = 128
TOKENS = 8192
N_MP = 2


def draw_seq_lengths(key, part):
    key = jax.random.fold_in(key, 11)
    group_count = TOKENS // TOK_DEV
    block_count = TOK_DEV // BLOCK
    key_flags, key_full, key_trim = jax.random.split(key, 3)
    block_ids = jnp.arange(block_count, dtype=jnp.int32)
    group_ids = jnp.arange(group_count, dtype=jnp.int32)
    flags = jax.random.randint(key_flags, (group_count, block_count), 0, 3) == 0
    flags = flags | (block_ids[None, :] == 0)
    full_group = jax.random.randint(key_full, (), 0, group_count)
    flags = jnp.where(group_ids[:, None] == full_group, block_ids[None, :] == 0, flags)
    later = flags[:, None, :] & (block_ids[None, None, :] > block_ids[None, :, None])
    following = jnp.min(jnp.where(later, block_ids[None, None, :], block_count), axis=2)
    span = following - block_ids[None, :]
    trimmed = jax.random.randint(key_trim, (group_count, block_count), 0, BLOCK // 2)
    trimmed = jnp.where(group_ids[:, None] == full_group, 0, trimmed)
    lengths = jnp.where(flags, span * BLOCK - trimmed, 0)
    return lengths.reshape(-1).astype(jnp.int32)


def spiked(drawn, key, source, target, shards_of, factor):
    owner, partner = [(jnp.arange(drawn.shape[axis_at]) // (drawn.shape[axis_at] // shards_of)).reshape([-1 if axis == axis_at else 1 for axis in range(drawn.ndim)]) for axis_at in (source, target)]
    chosen = jax.random.permutation(key, shards_of)[partner]
    strong = (owner == chosen) | (owner == (partner + shards_of // 2) % shards_of)
    return jnp.where(strong, factor * drawn, drawn)


def level_of(rng, dims, pieces, low, largest):
    loudness = 1.0
    for dim, parts in pieces:
        steps = jax.random.uniform(jax.random.fold_in(jax.random.fold_in(rng, 6), dim), (parts,), jnp.float32, low / len(pieces), largest / len(pieces))
        loudness = loudness * jnp.repeat(jnp.exp(steps), dims[dim] // parts).reshape((-1,) + (1,) * (len(dims) - 1 - dim))
    return loudness


def bell_draw(own_key, dims, spread, reach, cuts=(), kind=jnp.bfloat16):
    factor_of = level_of(own_key, dims, cuts, -0.22, 0.18) if cuts else 1.0
    result = jax.random.normal(own_key, dims, jnp.float32) * spread * factor_of
    return jnp.minimum(jnp.maximum(result, -reach), reach).astype(kind)


def bell_draw_with(own_key, dims, scale, bound, shards, heavy, held_as=jnp.bfloat16):
    drawn = scale * jax.random.normal(own_key, dims, jnp.float32)
    if shards:
        drawn = drawn * level_of(own_key, dims, shards, -0.22, 0.18)
    return jnp.clip(spiked(drawn, jax.random.fold_in(own_key, 3), *heavy), -bound, bound).astype(held_as)


def setup_inputs(seed: int = 0) -> dict:
    keys = jax.random.split(jax.random.key(seed), 10)
    tokens = bell_draw(keys[0], (TOKENS, D), 1.0, 6.0, ((0, 16),))
    seq_lengths = draw_seq_lengths(jax.random.fold_in(keys[9], 71), 0)
    ln_gain = jnp.clip(1.0 + 0.18 * jax.random.normal(keys[2], (4, D), jnp.float32), 0.1, 1.9)
    ln_bias = bell_draw(keys[3], (4, D), 0.5, 3.0, (), jnp.float32)
    w_qkv = bell_draw(keys[4], (3, D, D), (D // 2) ** -0.5, 0.25, ((1, 16), (2, 2)))
    w_out = bell_draw(keys[5], (D, D), (D // 8) ** -0.5, 0.5, ((0, 2), (1, 16)))
    w_up = bell_draw(keys[6], (D, FF), D ** -0.5, 0.1875, ((0, 16), (1, 2)))
    w_down = bell_draw(keys[7], (FF, D), FF ** -0.5, 0.09375, ((0, 2), (1, 16)))
    cotangent = bell_draw_with(keys[8], (TOKENS, D), 1.0, 6.0, ((0, 32),), (0, 1, 32, 2.75))
    return dict(tokens=tokens, seq_lengths=seq_lengths, ln_gain=ln_gain, ln_bias=ln_bias, w_qkv=w_qkv, w_out=w_out, w_up=w_up, w_down=w_down, cotangent=cotangent)


NORM_EPS = 1e-05
ROPE_BASE = 10000.0
MASK_FILL = -1e+30
HIGHEST = lax.Precision.HIGHEST

@jax.custom_vjp
def low(v):
    return lax.optimization_barrier(v.astype(jnp.bfloat16)).astype(jnp.float32)

@jax.custom_vjp
def low_back(v):
    return v

def low_keep(v):
    return (low(v), None)

def low_pass(kept, grad):
    return (grad,)

def back_keep(v):
    return (v, None)

def back_low(kept, grad):
    return (low(grad),)
low.defvjp(low_keep, low_pass)
low_back.defvjp(back_keep, back_low)

def layer_norm(values, norm_gain, norm_bias):
    average = lax.optimization_barrier(jnp.mean(values, axis=-1, keepdims=True))
    centred = values - average
    variance = lax.optimization_barrier(jnp.mean(centred * centred, axis=-1, keepdims=True))
    return centred * lax.rsqrt(variance + NORM_EPS) * norm_gain + norm_bias

def seq_layout(lengths, block_size):
    block_count = lengths.shape[0]
    block_ids = jnp.arange(block_count, dtype=jnp.int32)
    starts = lengths > 0
    earlier = starts[None, :] & (block_ids[None, :] <= block_ids[:, None])
    owners = lax.optimization_barrier(jnp.max(jnp.where(earlier, block_ids[None, :], 0), axis=1)).astype(jnp.int32)
    owner_len = lax.optimization_barrier(jnp.sum(jnp.where(block_ids[None, :] == owners[:, None], lengths[None, :], 0), axis=1))
    places = jnp.arange(block_count * block_size, dtype=jnp.int32)
    tok_owner = jnp.repeat(owners, block_size)
    position = places - tok_owner * block_size
    is_valid = position < jnp.repeat(owner_len, block_size)
    allowed = (tok_owner[:, None] == tok_owner[None, :]) & (places[None, :] <= places[:, None]) & is_valid[None, :]
    return (position, allowed)

def rotary_tables(position, width):
    frequency = ROPE_BASE ** (-jnp.arange(width // 2, dtype=jnp.float32) * 2.0 / width)
    angles = position.astype(jnp.float32)[:, None] * frequency[None, :]
    return (jnp.cos(angles), jnp.sin(angles))

def rotate(values, cos_table, sin_table):
    half_width = values.shape[-1] // 2
    front_half = values[..., :half_width]
    back_half = values[..., half_width:]
    cos_part = cos_table[:, None, :]
    sin_part = sin_table[:, None, :]
    return jnp.concatenate([front_half * cos_part - back_half * sin_part, back_half * cos_part + front_half * sin_part], axis=-1)

def rounded_partials(left, right, width):
    total = None
    for group in range(N_MP):
        term = low(jnp.dot(left[:, group * width:(group + 1) * width], right[group * width:(group + 1) * width], precision=HIGHEST))
        total = term if total is None else total + term
    return total

def group_layer(inputs, lengths, ln_gain, ln_bias, w_qkv, w_out, w_up, w_down):
    tok_count = inputs.shape[0]
    head_cols = D // N_MP
    unit_cols = FF // N_MP
    position, allowed = seq_layout(lengths, BLOCK)
    cos_table, sin_table = rotary_tables(position, HD)
    normed_in = low(layer_norm(inputs, ln_gain[0], ln_bias[0]))
    projected = jnp.concatenate([jnp.einsum('td,cde->cte', low_back(normed_in), w_qkv[:, :, group * head_cols:(group + 1) * head_cols], precision=HIGHEST) for group in range(N_MP)], axis=2)
    queries = low(rotate(low_back(projected[0]).reshape(tok_count, HEADS, HD), cos_table, sin_table))
    keys_rot = low(rotate(low_back(projected[1]).reshape(tok_count, HEADS, HD), cos_table, sin_table))
    values_h = low(low_back(projected[2]).reshape(tok_count, HEADS, HD))
    raw_scores = low_back(jnp.einsum('qhd,khd->hqk', queries, keys_rot, precision=HIGHEST)) * HD ** (-0.5)
    scores = jnp.where(allowed[None, :, :], raw_scores, MASK_FILL)
    top_score = lax.optimization_barrier(jnp.max(scores, axis=-1, keepdims=True))
    expo = jnp.exp(scores - top_score)
    probs = expo / lax.optimization_barrier(jnp.sum(expo, axis=-1, keepdims=True))
    attended = jnp.einsum('hqk,khd->qhd', low(probs), values_h, precision=HIGHEST)
    mixed = low(low_back(attended.reshape(tok_count, HEADS * HD)))
    attn_sum = low_back(rounded_partials(mixed, w_out, head_cols))
    hidden_state = inputs + layer_norm(attn_sum, ln_gain[1], ln_bias[1])
    normed_mid = low(layer_norm(hidden_state, ln_gain[2], ln_bias[2]))
    pre_act = low_back(jnp.concatenate([jnp.dot(low_back(normed_mid), w_up[:, group * unit_cols:(group + 1) * unit_cols], precision=HIGHEST) for group in range(N_MP)], axis=1))
    activated = low(jax.nn.gelu(pre_act, approximate=True))
    mlp_sum = low_back(rounded_partials(activated, w_down, unit_cols))
    return hidden_state + layer_norm(mlp_sum, ln_gain[3], ln_bias[3])

def reference(tokens, seq_lengths, ln_gain, ln_bias, w_qkv, w_out, w_up, w_down, cotangent):
    group_count = TOKENS // TOK_DEV
    lengths = seq_lengths.reshape(group_count, TOK_DEV // BLOCK)

    def forward(inputs, norm_gain, norm_bias, qkv_weight, out_weight, up_weight, down_weight):
        grouped = inputs.reshape(group_count, TOK_DEV, D)

        def one_group(item):
            return group_layer(item[0], item[1], norm_gain, norm_bias, qkv_weight, out_weight, up_weight, down_weight)
        results = lax.map(jax.checkpoint(one_group), (grouped, lengths))
        return results.reshape(TOKENS, D)
    output, pull = jax.vjp(forward, tokens.astype(jnp.float32), ln_gain.astype(jnp.float32), ln_bias.astype(jnp.float32), w_qkv.astype(jnp.float32), w_out.astype(jnp.float32), w_up.astype(jnp.float32), w_down.astype(jnp.float32))
    grads = pull(cotangent.astype(jnp.float32))
    return (output.astype(jnp.bfloat16), grads[0], grads[3], grads[4], grads[5], grads[6], grads[1], grads[2])
```

```python
import functools

import jax
import jax.numpy as jnp
from jax import lax
from jax.experimental import pallas as pl
from jax.experimental.pallas import tpu as pltpu
from jax.sharding import PartitionSpec as P

HD = 64
BLOCK = 128
PAIR = 2 * HD
NORM_EPS = 1e-05
ROPE_BASE = 10000.0
MASK_FILL = -1e30
F32 = jnp.float32
BF16 = jnp.bfloat16
VMEM_LIMIT = 24 * 1024 * 1024
NN = (((1,), (0,)), ((), ()))
NT = (((1,), (1,)), ((), ()))
TN = (((0,), (0,)), ((), ()))


def mm(left, right, dims):
    return lax.dot_general(left, right, dims, preferred_element_type=F32)


def sds(shape, dtype):
    return jax.ShapeDtypeStruct(shape, dtype)


def whole():
    return pl.BlockSpec(memory_space=pltpu.VMEM)


def smem():
    return pl.BlockSpec(memory_space=pltpu.SMEM)


def anywhere():
    return pl.BlockSpec(memory_space=pl.ANY)


def params(**extra):
    return pltpu.CompilerParams(vmem_limit_bytes=VMEM_LIMIT, **extra)


def cost(flops, nbytes, transcendentals=0):
    return pl.CostEstimate(
        flops=int(flops), bytes_accessed=int(nbytes), transcendentals=int(transcendentals)
    )


def norm_stats(values):
    centred = values - jnp.mean(values, axis=-1, keepdims=True)
    rstd = lax.rsqrt(jnp.mean(centred * centred, axis=-1, keepdims=True) + NORM_EPS)
    return centred * rstd, rstd


def norm_back(normed, rstd, scaled_grad):
    first = jnp.mean(scaled_grad, axis=-1, keepdims=True)
    second = jnp.mean(scaled_grad * normed, axis=-1, keepdims=True)
    return (scaled_grad - first - normed * second) * rstd


def fold_rows(values):
    return jnp.sum(values.reshape(-1, 8, values.shape[-1]), axis=0)


def norm_in_kernel(x_ref, gain_ref, bias_ref, out_ref):
    normed, _ = norm_stats(x_ref[...].astype(F32))
    out_ref[...] = (normed * gain_ref[0:1, :] + bias_ref[0:1, :]).astype(BF16)


def norm_in(x, gain, bias, rows=64):
    count, width = x.shape
    return pl.pallas_call(
        norm_in_kernel,
        grid=(count // rows,),
        in_specs=[pl.BlockSpec((rows, width), lambda i: (i, 0)), whole(), whole()],
        out_specs=pl.BlockSpec((rows, width), lambda i: (i, 0)),
        out_shape=sds(x.shape, BF16),
        compiler_params=params(),
        cost_estimate=cost(8 * x.size, 4 * x.size),
        name="norm_in",
    )(x, gain, bias)


def partner(values):
    lane = lax.broadcasted_iota(jnp.int32, values.shape, 1)
    ahead = pltpu.roll(values, PAIR - HD // 2, 1)
    behind = pltpu.roll(values, HD // 2, 1)
    return jnp.where(lax.rem(lane, HD) < HD // 2, ahead, behind)


def qkv_kernel(a_ref, wm_ref, wo_ref, cos_ref, sin_ref, qm_ref, qo_ref):
    cols = wm_ref.shape[1] // 3
    cos, sin = cos_ref[...], sin_ref[...]
    for w_ref, out_ref in ((wm_ref, qm_ref), (wo_ref, qo_ref)):
        proj = mm(a_ref[...], w_ref[...], NN)
        for start in range(0, 3 * cols, PAIR):
            part = proj[:, start : start + PAIR]
            if start < 2 * cols:
                part = part * cos + partner(part) * sin
            if start < cols:
                part = part.astype(BF16).astype(F32) * HD ** (-0.5)
            out_ref[:, start : start + PAIR] = part.astype(BF16)


def qkv_project(a1, wm, wo, cos, sin, rows=128):
    count, width = a1.shape
    cols = wm.shape[1] // 4 * 3
    row = lambda i: (i, 0)
    fixed = lambda i: (0, 0)
    return pl.pallas_call(
        qkv_kernel,
        grid=(count // rows,),
        in_specs=[
            pl.BlockSpec((rows, width), row),
            pl.BlockSpec((width, cols), fixed),
            pl.BlockSpec((width, cols), fixed),
            pl.BlockSpec((rows, PAIR), row),
            pl.BlockSpec((rows, PAIR), row),
        ],
        out_specs=[pl.BlockSpec((rows, cols), row)] * 2,
        out_shape=[sds((count, cols), BF16)] * 2,
        compiler_params=params(),
        cost_estimate=cost(4 * count * width * cols, 4 * width * cols + 2 * a1.size),
        name="qkv_project",
    )(a1, wm, wo, cos, sin)


def span_of(len_ref, block):
    start, size = jnp.int32(0), jnp.int32(0)
    for b in range(block + 1):
        here = len_ref[b]
        start = jnp.where(here > 0, b * BLOCK, start)
        size = jnp.where(here > 0, here, size)
    return start, start + size


def pair_lane(rows, first):
    lane = lax.broadcasted_iota(jnp.int32, (rows, PAIR), 1)
    return (lane < HD) == first


def attend_kernel(row0, len_ref, qm_ref, qo_ref, wm_ref, wo_ref, p_ref, om_ref, oo_ref, part_ref):
    rows = part_ref.shape[0]
    ext = p_ref.shape[2]
    cols = om_ref.shape[1]
    key = lax.broadcasted_iota(jnp.int32, (BLOCK, ext), 1)
    query = lax.broadcasted_iota(jnp.int32, (BLOCK, ext), 0)
    masks = []
    for b in range(rows // BLOCK):
        lo, hi = span_of(len_ref, row0 // BLOCK + b)
        seen = (key >= lo) & (key < hi) & (key <= query + (row0 + b * BLOCK))
        masks.append(jnp.where(seen, 0.0, MASK_FILL))
    mask = jnp.concatenate(masks, axis=0)
    head = 0
    for q_ref, o_ref in ((qm_ref, om_ref), (qo_ref, oo_ref)):
        for start in range(0, cols, PAIR):
            q = q_ref[row0 : row0 + rows, start : start + PAIR]
            k = q_ref[0:ext, cols + start : cols + start + PAIR]
            v = q_ref[0:ext, 2 * cols + start : 2 * cols + start + PAIR]
            outs = []
            for first in (True, False):
                mine = pair_lane(rows, first)
                s = mm(jnp.where(mine, q, jnp.zeros_like(q)), k, NT) + mask
                e = jnp.exp(s - jnp.max(s, axis=-1, keepdims=True))
                p = (e * (1.0 / jnp.sum(e, axis=-1, keepdims=True))).astype(BF16)
                p_ref[head] = p
                head += 1
                outs.append(mm(p, v, NN))
            o_ref[:, start : start + PAIR] = jnp.where(
                pair_lane(rows, True), outs[0], outs[1]
            ).astype(BF16)
    part = mm(om_ref[...], wm_ref[...], NT) + mm(oo_ref[...], wo_ref[...], NT)
    part_ref[...] = part.astype(BF16)


def attend(row0, rows, lengths, qkv_m, qkv_o, wm, wo):
    ext = row0 + rows
    cols = qkv_m.shape[1] // 3
    heads = 2 * cols // HD
    width = wm.shape[0]
    out_block = pl.BlockSpec((width, cols), lambda i: (0, 3))
    return pl.pallas_call(
        functools.partial(attend_kernel, row0),
        grid=(1,),
        in_specs=[smem(), whole(), whole(), out_block, out_block],
        out_specs=[whole()] * 4,
        out_shape=[
            sds((heads, rows, ext), BF16),
            sds((rows, cols), BF16),
            sds((rows, cols), BF16),
            sds((rows, width), BF16),
        ],
        compiler_params=params(),
        cost_estimate=cost(
            8 * heads * rows * ext * HD + 4 * rows * width * cols,
            2 * heads * rows * ext + 4 * width * cols,
            heads * rows * ext,
        ),
        name="attend",
    )(lengths, qkv_m, qkv_o, wm, wo)


def hidden_of(x_ref, ya_ref, yb_ref, gain_ref, bias_ref, at):
    y = ya_ref[at, :].astype(F32) + yb_ref[at, :].astype(F32)
    n1, r1 = norm_stats(y)
    return x_ref[at, :].astype(F32) + n1 * gain_ref[1:2, :] + bias_ref[1:2, :], n1, r1


STEP = 32


def up_kernel(x_ref, ya_ref, yb_ref, gain_ref, bias_ref, wm_ref, wo_ref, a3_ref, g_ref, gp_ref, a3_sc):
    rows = x_ref.shape[0]

    @pl.when(pl.program_id(0) == 0)
    def _():
        @pl.loop(0, rows // STEP)
        def _(i):
            at = pl.ds(pl.multiple_of(i * STEP, STEP), STEP)
            h, _, _ = hidden_of(x_ref, ya_ref, yb_ref, gain_ref, bias_ref, at)
            n2, _ = norm_stats(h)
            a3_sc[at, :] = (n2 * gain_ref[2:3, :] + bias_ref[2:3, :]).astype(BF16)

        a3_ref[...] = a3_sc[...]

    for half, w_ref in enumerate((wm_ref, wo_ref)):
        u = mm(a3_sc[...], w_ref[...], NN)
        k0 = 0.7978845608028654
        k1 = 0.044715
        sq = u * u
        th = jnp.tanh(k0 * (u + k1 * u * sq))
        plus = 0.5 * (1.0 + th)
        g_ref[half] = (u * plus).astype(BF16)
        slope = plus + 0.5 * u * (1.0 - th * th) * (k0 + 3.0 * k0 * k1 * sq)
        gp_ref[half] = slope.astype(BF16)


def up_project(chunk, rows, x, ya, yb, gain, bias, wm, wo, blocks=4):
    width = x.shape[1]
    half = wm.shape[1]
    blk = half // blocks
    col = pl.BlockSpec((width, blk), lambda i: (0, i))
    out = pl.BlockSpec((2, rows, blk), lambda i: (0, 0, i))
    return pl.pallas_call(
        up_kernel,
        grid=(blocks,),
        in_specs=[
            pl.BlockSpec((rows, width), lambda i: (chunk, 0)),
            pl.BlockSpec((rows, width), lambda i: (0, 0)),
            pl.BlockSpec((rows, width), lambda i: (0, 0)),
            whole(),
            whole(),
            col,
            col,
        ],
        out_specs=[pl.BlockSpec((rows, width), lambda i: (0, 0)), out, out],
        out_shape=[
            sds((rows, width), BF16),
            sds((2, rows, half), BF16),
            sds((2, rows, half), BF16),
        ],
        scratch_shapes=[pltpu.VMEM((rows, width), BF16)],
        compiler_params=params(),
        cost_estimate=cost(4 * rows * width * half, 4 * width * half, rows * half * 2),
        name="up_project",
    )(x, ya, yb, gain, bias, wm, wo)


def down_kernel(g_ref, wm_ref, wo_ref, z_ref):
    z = mm(g_ref[0], wm_ref[...], NT) + mm(g_ref[1], wo_ref[...], NT)
    z_ref[...] = z.astype(BF16)


def down_project(g, wm, wo, blocks=4):
    _, rows, half = g.shape
    width = wm.shape[0]
    blk = width // blocks
    row = pl.BlockSpec((blk, half), lambda i: (i, 0))
    return pl.pallas_call(
        down_kernel,
        grid=(blocks,),
        in_specs=[pl.BlockSpec((2, rows, half), lambda i: (0, 0, 0)), row, row],
        out_specs=pl.BlockSpec((rows, blk), lambda i: (0, i)),
        out_shape=sds((rows, width), BF16),
        compiler_params=params(),
        cost_estimate=cost(4 * rows * width * half, 4 * width * half),
        name="down_project",
    )(g, wm, wo)


def mlp_back_kernel(
    x_ref, ya_ref, yb_ref, za_ref, zb_ref, cot_ref, gain_ref, bias_ref, gp_ref,
    dm_ref, do_ref, um_ref, uo_ref, out_ref, dz_ref, du_ref, part_ref, gb_ref, dz_sc, acc,
):
    rows = x_ref.shape[0]
    step = pl.program_id(0)

    @pl.when(step == 0)
    def _():
        gb_ref[...] = jnp.zeros_like(gb_ref)

        @pl.loop(0, rows // STEP)
        def _(i):
            at = pl.ds(pl.multiple_of(i * STEP, STEP), STEP)
            h, _, _ = hidden_of(x_ref, ya_ref, yb_ref, gain_ref, bias_ref, at)
            z = za_ref[at, :].astype(F32) + zb_ref[at, :].astype(F32)
            n3, r3 = norm_stats(z)
            cot = cot_ref[at, :].astype(F32)
            gain = gain_ref[3:4, :]
            out_ref[at, :] = (h + (n3 * gain + bias_ref[3:4, :])).astype(BF16)
            dz_sc[at, :] = norm_back(n3, r3, cot * gain).astype(BF16)
            gb_ref[0] += fold_rows(cot * n3)
            gb_ref[1] += fold_rows(cot)

        dz_ref[...] = dz_sc[...]
        acc[...] = jnp.zeros_like(acc)

    for half, (w3, w2) in enumerate(((dm_ref, um_ref), (do_ref, uo_ref))):
        du = (mm(dz_sc[...], w3[...], NN) * gp_ref[half].astype(F32)).astype(BF16)
        du_ref[half] = du
        acc[...] += mm(du, w2[...], NT)

    @pl.when(step == pl.num_programs(0) - 1)
    def _():
        part_ref[...] = acc[...].astype(BF16)


def mlp_back(chunk, rows, x, ya, yb, za, zb, cot, gain, bias, gp, dm, do, um, uo, blocks=4):
    width = x.shape[1]
    half = dm.shape[1]
    blk = half // blocks
    col = pl.BlockSpec((width, blk), lambda i: (0, i))
    mid = pl.BlockSpec((2, rows, blk), lambda i: (0, 0, i))
    own = pl.BlockSpec((rows, width), lambda i: (0, 0))
    nth = pl.BlockSpec((rows, width), lambda i: (chunk, 0))
    return pl.pallas_call(
        mlp_back_kernel,
        grid=(blocks,),
        in_specs=[nth, own, own, own, own, nth, whole(), whole(), mid, col, col, col, col],
        out_specs=[own, own, mid, own, pl.BlockSpec((2, 8, width), lambda i: (0, 0, 0))],
        out_shape=[
            sds((rows, width), BF16),
            sds((rows, width), BF16),
            sds((2, rows, half), BF16),
            sds((rows, width), BF16),
            sds((2, 8, width), F32),
        ],
        scratch_shapes=[pltpu.VMEM((rows, width), BF16), pltpu.VMEM((rows, width), F32)],
        compiler_params=params(),
        cost_estimate=cost(8 * rows * width * half, 8 * width * half),
        name="mlp_back",
    )(x, ya, yb, za, zb, cot, gain, bias, gp, dm, do, um, uo)


def weight_grad_kernel(n_chunks, *refs):
    lefts, rights, out_ref = refs[:n_chunks], refs[n_chunks : 2 * n_chunks], refs[-1]
    total = None
    for left, right in zip(lefts, rights):
        term = mm(left[...], right[0], TN)
        total = term if total is None else total + term
    out_ref[...] = total.astype(BF16)


def weight_grad(lefts, rights, half, blocks=4, deps=()):
    rows, width = lefts[0].shape
    cols = rights[0].shape[2]
    blk = width // blocks
    count = len(lefts)
    return pl.pallas_call(
        functools.partial(weight_grad_kernel, count),
        grid=(blocks,),
        in_specs=[pl.BlockSpec((rows, blk), lambda i: (0, i))] * count
        + [pl.BlockSpec((1, rows, cols), lambda i: (half, 0, 0))] * count
        + [anywhere()] * len(deps),
        out_specs=pl.BlockSpec((blk, cols), lambda i: (i, 0)),
        out_shape=sds((width, cols), BF16),
        compiler_params=params(),
        cost_estimate=cost(2 * count * rows * width * cols, 2 * width * cols),
        name="weight_grad",
    )(*lefts, *rights, *deps)


def mid_back_kernel(
    x_ref, ya_ref, yb_ref, ea_ref, eb_ref, cot_ref, gain_ref, bias_ref, wm_ref, wo_ref, *refs
):
    dh_ref, dy_ref, dom_ref, doo_ref, gb_ref = refs[-5:]
    rows = x_ref.shape[0]
    gb_ref[...] = jnp.zeros_like(gb_ref)

    @pl.loop(0, rows // STEP)
    def _(i):
        at = pl.ds(pl.multiple_of(i * STEP, STEP), STEP)
        h, n1, r1 = hidden_of(x_ref, ya_ref, yb_ref, gain_ref, bias_ref, at)
        n2, r2 = norm_stats(h)
        e = ea_ref[at, :].astype(F32) + eb_ref[at, :].astype(F32)
        dh = cot_ref[at, :].astype(F32) + norm_back(n2, r2, e * gain_ref[2:3, :])
        dh_ref[at, :] = dh
        dy_ref[at, :] = norm_back(n1, r1, dh * gain_ref[1:2, :]).astype(BF16)
        gb_ref[0] += fold_rows(e * n2)
        gb_ref[1] += fold_rows(e)
        gb_ref[2] += fold_rows(dh * n1)
        gb_ref[3] += fold_rows(dh)

    dom_ref[...] = mm(dy_ref[...], wm_ref[...], NN).astype(BF16)
    doo_ref[...] = mm(dy_ref[...], wo_ref[...], NN).astype(BF16)


def mid_back(chunk, rows, x, ya, yb, ea, eb, cot, gain, bias, wm, wo, deps=()):
    width = x.shape[1]
    cols = wm.shape[1] // 4
    own = pl.BlockSpec((rows, width), lambda i: (0, 0))
    nth = pl.BlockSpec((rows, width), lambda i: (chunk, 0))
    out_block = pl.BlockSpec((width, cols), lambda i: (0, 3))
    return pl.pallas_call(
        mid_back_kernel,
        grid=(1,),
        in_specs=[nth, own, own, own, own, nth, whole(), whole(), out_block, out_block]
        + [anywhere()] * len(deps),
        out_specs=[whole()] * 5,
        out_shape=[
            sds((rows, width), F32),
            sds((rows, width), BF16),
            sds((rows, cols), BF16),
            sds((rows, cols), BF16),
            sds((4, 8, width), F32),
        ],
        compiler_params=params(),
        cost_estimate=cost(4 * rows * width * cols, 20 * rows * width + 4 * width * cols),
        name="mid_back",
    )(x, ya, yb, ea, eb, cot, gain, bias, wm, wo, *deps)


def attend_back_kernel(head0, q_ref, p0_ref, p1_ref, o0, o1, d0, d1, cos_ref, sin_ref, *refs):
    g_ref = refs[-1]
    rows, cols = o0.shape
    cos, sin = cos_ref[...], sin_ref[...]
    head = head0
    for start in range(0, cols, PAIR):
        at = slice(start, start + PAIR)
        q = q_ref[:, at]
        k = q_ref[:, cols + start : cols + start + PAIR]
        v = q_ref[:, 2 * cols + start : 2 * cols + start + PAIR]
        do = (d0[:, at], d1[:, at])
        prod = [a.astype(F32) * b[:, at].astype(F32) for a, b in zip(do, (o0, o1))]
        dq, dk, dv = [], [], []
        for first in (True, False):
            mine = pair_lane(rows, first)
            dqs = []
            for c, p_ref in enumerate((p0_ref, p1_ref)):
                ext = p_ref.shape[2]
                p = p_ref[head]
                dp = mm(jnp.where(mine, do[c], jnp.zeros_like(do[c])), v[:ext], NT)
                dot = jnp.sum(jnp.where(mine, prod[c], 0.0), axis=-1, keepdims=True)
                ds = (p.astype(F32) * (dp - dot)).astype(BF16)
                dqs.append(mm(ds, k[:ext], NN))
                dkc = mm(ds, q[c * rows : (c + 1) * rows], TN)
                dvc = mm(p, do[c], TN)
                if c == 0:
                    dk0, dv0 = dkc, dvc
            dk.append(jnp.concatenate([dk0 + dkc[:rows], dkc[rows:]], axis=0))
            dv.append(jnp.concatenate([dv0 + dvc[:rows], dvc[rows:]], axis=0))
            dq.append(jnp.concatenate(dqs, axis=0))
            head += 1
        low = pair_lane(2 * rows, True)
        gq = jnp.where(low, dq[0], dq[1]) * HD ** (-0.5)
        gk = jnp.where(low, dk[0], dk[1])
        g_ref[:, at] = (gq * cos - partner(gq) * sin).astype(BF16)
        g_ref[:, cols + start : cols + start + PAIR] = (gk * cos - partner(gk) * sin).astype(BF16)
        g_ref[:, 2 * cols + start : 2 * cols + start + PAIR] = jnp.where(
            low, dv[0], dv[1]
        ).astype(BF16)


def attend_back(side, qkv, probs, outs, grads, cos, sin, deps=()):
    count, three = qkv.shape
    heads, rows, _ = probs[0].shape
    return pl.pallas_call(
        functools.partial(attend_back_kernel, side * heads // 2),
        in_specs=[whole()] * 9 + [anywhere()] * len(deps),
        out_specs=whole(),
        out_shape=sds((count, three), BF16),
        compiler_params=params(),
        cost_estimate=cost(8 * heads * count * count * HD, heads * count * count),
        name="attend_back",
    )(qkv, *probs, *outs, *grads, cos, sin, *deps)


def in_back_kernel(gm_ref, go_ref, wm_ref, wo_ref, x_ref, *refs):
    part_ref, gb_ref = refs[-2:]
    part = mm(gm_ref[...], wm_ref[...], NT) + mm(go_ref[...], wo_ref[...], NT)
    part = part.astype(BF16)
    part_ref[...] = part
    e = part.astype(F32)
    n0, _ = norm_stats(x_ref[...].astype(F32))

    @pl.when(pl.program_id(0) == 0)
    def _():
        gb_ref[...] = jnp.zeros_like(gb_ref)

    gb_ref[0] += fold_rows(e * n0)
    gb_ref[1] += fold_rows(e)


def in_back(g_m, g_o, wm, wo, x, rows=128, deps=()):
    count, three = g_m.shape
    width = wm.shape[0]
    w_block = pl.BlockSpec((width, three), lambda i: (0, 0))
    g_block = pl.BlockSpec((rows, three), lambda i: (i, 0))
    row = pl.BlockSpec((rows, width), lambda i: (i, 0))
    return pl.pallas_call(
        in_back_kernel,
        grid=(count // rows,),
        in_specs=[g_block, g_block, w_block, w_block, row] + [anywhere()] * len(deps),
        out_specs=[row, pl.BlockSpec((2, 8, width), lambda i: (0, 0, 0))],
        out_shape=[sds((count, width), BF16), sds((2, 8, width), F32)],
        compiler_params=params(),
        cost_estimate=cost(4 * count * width * three, 4 * width * three),
        name="in_back",
    )(g_m, g_o, wm, wo, x, *deps)


def up_out_grad_kernel(a0, a1, u0, u1, y0, y1, o0, o1, *refs):
    out_ref = refs[-1]
    cols = u0.shape[2]
    out_ref[:, :cols] = (mm(a0[...], u0[0], TN) + mm(a1[...], u1[0], TN)).astype(BF16)
    out_ref[:, cols:] = (mm(y0[...], o0[...], TN) + mm(y1[...], o1[...], TN)).astype(BF16)


def up_out_grad(a3s, dus, half, dys, outs, blocks=4, deps=()):
    rows, width = a3s[0].shape
    cols, extra = dus[0].shape[2], outs[0].shape[1]
    blk = width // blocks
    left = pl.BlockSpec((rows, blk), lambda i: (0, i))
    return pl.pallas_call(
        up_out_grad_kernel,
        grid=(blocks,),
        in_specs=[left] * 2
        + [pl.BlockSpec((1, rows, cols), lambda i: (half, 0, 0))] * 2
        + [left] * 2
        + [pl.BlockSpec((rows, extra), lambda i: (0, 0))] * 2
        + [anywhere()] * len(deps),
        out_specs=pl.BlockSpec((blk, cols + extra), lambda i: (i, 0)),
        out_shape=sds((width, cols + extra), BF16),
        compiler_params=params(),
        cost_estimate=cost(4 * rows * width * (cols + extra), 2 * width * (cols + extra)),
        name="up_out_grad",
    )(*a3s, *dus, *dys, *outs, *deps)


def qkv_grad_kernel(a_ref, q_ref, extra_ref, *refs):
    out_ref = refs[-1]
    three = q_ref.shape[1]
    out_ref[:, :three] = mm(a_ref[...], q_ref[...], TN).astype(BF16)
    out_ref[:, three:] = extra_ref[...]


def qkv_grad(a1, g_qkv, extra, blocks=4, deps=()):
    count, width = a1.shape
    three = g_qkv.shape[1]
    lanes = extra.shape[1]
    blk = width // blocks
    return pl.pallas_call(
        qkv_grad_kernel,
        grid=(blocks,),
        in_specs=[
            pl.BlockSpec((count, blk), lambda i: (0, i)),
            pl.BlockSpec((count, three), lambda i: (0, 0)),
            pl.BlockSpec((blk, lanes), lambda i: (i, 0)),
        ]
        + [anywhere()] * len(deps),
        out_specs=pl.BlockSpec((blk, three + lanes), lambda i: (i, 0)),
        out_shape=sds((width, three + lanes), BF16),
        compiler_params=params(),
        cost_estimate=cost(2 * count * width * three, 4 * width * three),
        name="qkv_grad",
    )(a1, g_qkv, extra, *deps)


def tokens_back_kernel(x_ref, a_ref, b_ref, dh_ref, gain_ref, out_ref):
    e = a_ref[...].astype(F32) + b_ref[...].astype(F32)
    n0, r0 = norm_stats(x_ref[...].astype(F32))
    out_ref[...] = dh_ref[...] + norm_back(n0, r0, e * gain_ref[0:1, :])


def tokens_back(x, a, b, dh, gain, rows=64):
    count, width = x.shape
    row = pl.BlockSpec((rows, width), lambda i: (i, 0))
    return pl.pallas_call(
        tokens_back_kernel,
        grid=(count // rows,),
        in_specs=[row, row, row, row, whole()],
        out_specs=row,
        out_shape=sds(x.shape, F32),
        compiler_params=params(),
        cost_estimate=cost(16 * x.size, 14 * x.size),
        name="tokens_back",
    )(x, a, b, dh, gain)


def assemble_kernel(off_ref, *refs):
    ins, outs, sem = refs[:-3], refs[-3:-1], refs[-1]
    unit = min(ref.shape[0] for ref in ins)
    copies = []
    per = len(ins) // 2
    for side in range(2):
        for i in range(per):
            src = ins[side * per + i]
            dst = outs[side].at[pl.ds(pl.multiple_of(off_ref[i], unit), src.shape[0])]
            copies.append(pltpu.make_async_copy(src, dst, sem.at[side * per + i]))
    for copy in copies:
        copy.start()
    for copy in copies:
        copy.wait()


def assemble(offsets, mine, other, total_rows):
    width = mine[0].shape[1]
    count = len(mine)
    return pl.pallas_call(
        assemble_kernel,
        in_specs=[smem()] + [anywhere()] * (2 * count),
        out_specs=[whole()] * 2,
        out_shape=[sds((total_rows, width), BF16)] * 2,
        scratch_shapes=[pltpu.SemaphoreType.DMA((2 * count,))],
        compiler_params=params(),
        cost_estimate=cost(0, 8 * total_rows * width),
        name="assemble",
    )(offsets, *mine, *other)


def ring_sum_kernel(spot_ref, gu_ref, su_ref, gd_ref, sd_ref, up_ref, down_ref, *refs):
    up_out, down_out = refs[-2:]
    half = up_ref.shape[0]
    up = gu_ref[...].astype(F32) + su_ref[...].astype(F32)
    down = gd_ref[...].astype(F32) + sd_ref[...].astype(F32)
    if half == gu_ref.shape[0]:
        up_out[...] = (up + up_ref[...].astype(F32)).astype(BF16)
        down_out[...] = (down + down_ref[...].astype(F32)).astype(BF16)
    else:
        up_out[:half] = (up[:half] + up_ref[...].astype(F32)).astype(BF16)
        up_out[half:] = up[half:].astype(BF16)
        down_out[:half] = down[:half].astype(BF16)
        down_out[half:] = (down[half:] + down_ref[...].astype(F32)).astype(BF16)


def ring_sum(spots, grad, got, up, down, rows, deps=()):
    width = grad.shape[1]
    first = pl.BlockSpec((rows, width), lambda i, s: (s[0], 0))
    second = pl.BlockSpec((rows, width), lambda i, s: (s[1], 0))
    came = pl.BlockSpec(up.shape, lambda i, s: (0, 0))
    out = pl.BlockSpec((rows, width), lambda i, s: (0, 0))
    return pl.pallas_call(
        ring_sum_kernel,
        grid_spec=pltpu.PrefetchScalarGridSpec(
            num_scalar_prefetch=1,
            grid=(1,),
            in_specs=[first, first, second, second, came, came] + [anywhere()] * len(deps),
            out_specs=[out, out],
        ),
        out_shape=[sds((rows, width), BF16)] * 2,
        compiler_params=params(),
        cost_estimate=cost(0, 16 * rows * width),
        name="ring_sum",
    )(spots, grad, got, grad, got, up, down, *deps)


def ring_start_kernel(spot_ref, gu_ref, su_ref, gd_ref, sd_ref, *refs):
    up_out, down_out = refs[-2:]
    up_out[...] = (gu_ref[...].astype(F32) + su_ref[...].astype(F32)).astype(BF16)
    down_out[...] = (gd_ref[...].astype(F32) + sd_ref[...].astype(F32)).astype(BF16)


def ring_start(spots, grad, got, half, deps=()):
    width = grad.shape[1]
    first = pl.BlockSpec((half, width), lambda i, s: (2 * s[0], 0))
    second = pl.BlockSpec((half, width), lambda i, s: (2 * s[0] + 1, 0))
    out = pl.BlockSpec((half, width), lambda i, s: (0, 0))
    return pl.pallas_call(
        ring_start_kernel,
        grid_spec=pltpu.PrefetchScalarGridSpec(
            num_scalar_prefetch=1,
            grid=(1,),
            in_specs=[first, first, second, second] + [anywhere()] * len(deps),
            out_specs=[out, out],
        ),
        out_shape=[sds((half, width), BF16)] * 2,
        compiler_params=params(),
        cost_estimate=cost(0, 12 * half * width),
        name="ring_start",
    )(spots, grad, got, grad, got, *deps)


def ring_end_kernel(spot_ref, g_ref, s_ref, up_ref, down_ref, *refs):
    keep_out, give_out, total = refs[-3:]
    rows = keep_out.shape[0]
    core = spot_ref[1]
    total[...] = (
        g_ref[...].astype(F32)
        + s_ref[...].astype(F32)
        + up_ref[...].astype(F32)
        + down_ref[...].astype(F32)
    )
    keep_out[...] = total[pl.ds(pl.multiple_of(core * rows, rows), rows), :]
    give_out[...] = total[pl.ds(pl.multiple_of((1 - core) * rows, rows), rows), :].astype(BF16)


def ring_end(spots, grad, got, up, down, deps=()):
    rows, width = up.shape
    own = pl.BlockSpec((rows, width), lambda i, s: (s[0], 0))
    came = pl.BlockSpec((rows, width), lambda i, s: (0, 0))
    out = pl.BlockSpec((rows // 2, width), lambda i, s: (0, 0))
    return pl.pallas_call(
        ring_end_kernel,
        grid_spec=pltpu.PrefetchScalarGridSpec(
            num_scalar_prefetch=1,
            grid=(1,),
            in_specs=[own, own, came, came] + [anywhere()] * len(deps),
            out_specs=[out, out],
            scratch_shapes=[pltpu.VMEM((rows, width), F32)],
        ),
        out_shape=[sds((rows // 2, width), F32), sds((rows // 2, width), BF16)],
        compiler_params=params(),
        cost_estimate=cost(0, 16 * rows * width),
        name="ring_end",
    )(spots, grad, got, up, down, *deps)


def gain_pack_kernel(core_ref, gb0_ref, g12a, g12b, g3a, g3b, mine_ref, other_ref):
    width = mine_ref.shape[0]
    lanes = mine_ref.shape[1]
    share = 0.5
    core = core_ref[0]
    sides = []
    for kind in range(2):
        rows = [
            gb0_ref[kind],
            share * (g12a[2 + kind] + g12b[2 + kind]),
            share * (g12a[kind] + g12b[kind]),
            share * (g3a[kind] + g3b[kind]),
        ]
        rows = [jnp.sum(r, axis=0, keepdims=True) for r in rows]
        sides.append(jnp.concatenate(rows + [jnp.zeros((lanes - 4, width), F32)], axis=0).T)
    mine_ref[...] = jnp.where(core == 0, sides[0], sides[1]).astype(BF16)
    other_ref[...] = jnp.where(core == 0, sides[1], sides[0]).astype(BF16)


def gain_pack(core, gb0, g12, g3):
    width = gb0.shape[-1]
    return pl.pallas_call(
        gain_pack_kernel,
        in_specs=[smem()] + [whole()] * 5,
        out_specs=[whole()] * 2,
        out_shape=[sds((width, 128), BF16)] * 2,
        compiler_params=params(),
        cost_estimate=cost(0, 200 * width),
        name="gain_pack",
    )(core, gb0, *g12, *g3)


class Ring:
    def __init__(self, n_dp):
        self.size = n_dp // 2
        self.z = self.size // 2
        self.up = self.shift(1)
        self.down = self.shift(-1)
        self.cores = [(i, i ^ 1) for i in range(n_dp)]

    def chip(self, place):
        place %= self.size
        return 2 * place if place < self.z else 2 * (self.size - 1 - place) + 1

    def shift(self, by):
        return [
            (2 * self.chip(p) + c, 2 * self.chip(p + by) + c)
            for p in range(self.size)
            for c in range(2)
        ]

    def here(self):
        chip = lax.axis_index("dp") // 2
        z, x = chip // 2, chip % 2
        return jnp.where(x == 0, z, self.size - 1 - z)

    def chip_at(self, place):
        place = lax.rem(place + self.size, self.size)
        return jnp.where(place < self.z, 2 * place, 2 * (self.size - 1 - place) + 1)


def swap_cores(ring, value):
    return lax.ppermute(value, "dp", ring.cores)


def pack(ring, core, halves):
    keep = lax.dynamic_index_in_dim(halves, core, 0, keepdims=False)
    give = lax.dynamic_index_in_dim(halves, 1 - core, 0, keepdims=False)
    got = swap_cores(ring, give)
    return jnp.where(
        core == 0, jnp.concatenate([keep, got], 0), jnp.concatenate([got, keep], 0)
    )


def gather_ring(ring, here, piece):
    rows = piece.shape[0]
    half = rows // 2
    mine, other, offsets = [], [], []

    def keep(value, step, shift):
        mine.append(value)
        other.append(swap_cores(ring, value))
        offsets.append(ring.chip_at(here + step) * rows + shift)

    keep(piece, 0, 0)
    up = down = piece
    for step in range(1, ring.size // 2):
        up = lax.ppermute(up, "dp", ring.up)
        down = lax.ppermute(down, "dp", ring.down)
        keep(up, -step, 0)
        keep(down, step, 0)
    up = lax.ppermute(up[:half], "dp", ring.up)
    down = lax.ppermute(down[half:], "dp", ring.down)
    keep(up, ring.size // 2, 0)
    keep(down, ring.size // 2, half)
    places = jnp.stack(offsets).astype(jnp.int32)
    return assemble(places, mine, other, rows * ring.size)


class Reduce:
    def __init__(self, ring, here, core, grad_other):
        self.ring, self.here, self.core = ring, here, core
        self.got = swap_cores(ring, grad_other)
        self.step_now = ring.size // 2
        self.up = self.down = None

    def start(self, grad, deps=()):
        self.grad = grad
        self.rows = grad.shape[0] // self.ring.size
        self.send(ring_start(self.spots(self.step_now), grad, self.got, self.rows // 2, deps))
        return self

    def spots(self, step):
        ring = self.ring
        spots = [ring.chip_at(self.here + step), ring.chip_at(self.here - step)]
        return jnp.stack(spots).astype(jnp.int32)

    def send(self, sums):
        self.up = lax.ppermute(sums[0], "dp", self.ring.up)
        self.down = lax.ppermute(sums[1], "dp", self.ring.down)
        self.step_now -= 1

    def step(self, deps=()):
        spots = self.spots(self.step_now)
        self.send(ring_sum(spots, self.grad, self.got, self.up, self.down, self.rows, deps))
        return self

    def end(self, deps=()):
        spots = jnp.stack([self.ring.chip_at(self.here), self.core]).astype(jnp.int32)
        keep, give = ring_end(spots, self.grad, self.got, self.up, self.down, deps)
        came = swap_cores(self.ring, give).astype(F32)
        return jnp.where(self.core == 0, jnp.stack([keep, came]), jnp.stack([came, keep]))


def rotary_pair(lengths, count):
    blocks = jnp.arange(count // BLOCK, dtype=jnp.int32)
    earlier = (lengths > 0)[None, :] & (blocks[None, :] <= blocks[:, None])
    owners = jnp.max(jnp.where(earlier, blocks[None, :], 0), axis=1)
    position = jnp.arange(count, dtype=jnp.int32) - jnp.repeat(owners, BLOCK) * BLOCK
    frequency = ROPE_BASE ** (-jnp.arange(HD // 2, dtype=F32) * 2.0 / HD)
    angles = position.astype(F32)[:, None] * frequency[None, :]
    cos, sin = jnp.cos(angles), jnp.sin(angles)
    return jnp.concatenate([cos] * 4, 1), jnp.concatenate([-sin, sin, -sin, sin], 1)


def per_device(n_dp, tokens, seq_lengths, ln_gain, ln_bias, w_qkv, w_out, w_up, w_down, cotangent):
    ring = Ring(n_dp)
    here = ring.here()
    core = lax.rem(lax.axis_index("dp"), 2)
    side = lax.axis_index("mp")
    count, width = tokens.shape
    rows = count // 2
    w_rows = w_up.shape[0]
    cols = w_out.shape[0] // 2
    units = w_up.shape[1] // 2
    pair = [(0, 1), (1, 0)]

    def swap_sides(value):
        return lax.ppermute(value, "mp", pair)

    attn_w = jnp.concatenate([w_qkv, w_out.T[None]], 0).reshape(4, w_rows, 2, cols)
    attn_w = jnp.transpose(attn_w, (2, 1, 0, 3)).reshape(2, w_rows, 4 * cols)
    up_w = jnp.transpose(w_up.reshape(w_rows, 2, units), (1, 0, 2))
    down_w = jnp.transpose(w_down.reshape(2, units, w_rows), (0, 2, 1))

    attn_m, attn_o = gather_ring(ring, here, pack(ring, core, attn_w))
    cot_got = swap_sides(cotangent)
    cot = jnp.where(
        side == 0,
        jnp.concatenate([cotangent, cot_got], 0),
        jnp.concatenate([cot_got, cotangent], 0),
    )
    a1 = norm_in(tokens, ln_gain, ln_bias)
    cos, sin = rotary_pair(seq_lengths, count)
    up_m, up_o = gather_ring(ring, here, pack(ring, core, up_w))
    down_m, down_o = gather_ring(ring, here, pack(ring, core, down_w))

    qkv_m, qkv_o = qkv_project(a1, attn_m, attn_o, cos, sin)
    probs, outs, ys, mids, zs, backs, mid_backs = [], [], [], [], [], [], []
    for c in range(2):
        p, om, oo, part = attend(c * rows, rows, seq_lengths, qkv_m, qkv_o, attn_m, attn_o)
        probs.append(p)
        outs.append((om, oo))
        ys.append((part, swap_sides(part)))
    for c in range(2):
        mids.append(up_project(c, rows, tokens, *ys[c], ln_gain, ln_bias, up_m, up_o))
    for c in range(2):
        part = down_project(mids[c][1], down_m, down_o)
        zs.append((part, swap_sides(part)))
    for c in range(2):
        out, dz, du, part, gb = mlp_back(
            c, rows, tokens, *ys[c], *zs[c], cot, ln_gain, ln_bias, mids[c][2],
            down_m, down_o, up_m, up_o,
        )
        backs.append((out, dz, du, gb, (part, swap_sides(part))))
    dzs, dus = [b[1] for b in backs], [b[2] for b in backs]
    a3s, gs = [m[0] for m in mids], [m[1] for m in mids]

    def mid(c, deps=()):
        return mid_back(
            c, rows, tokens, *ys[c], *backs[c][4], cot, ln_gain, ln_bias, attn_m, attn_o, deps
        )

    def heads_back(side, qkv, deps=()):
        return attend_back(
            side,
            qkv,
            probs,
            [o[side] for o in outs],
            [m[2 + side] for m in mid_backs],
            cos,
            sin,
            deps,
        )

    def up_out(side, deps=()):
        return up_out_grad(
            a3s, dus, side, [m[1] for m in mid_backs], [o[side] for o in outs], deps=deps
        )

    down_ring = Reduce(ring, here, core, weight_grad(dzs, gs, 1))
    down_mine = weight_grad(dzs, gs, 0)
    mid_backs.append(mid(0, [down_mine]))
    down_ring.start(down_mine, [mid_backs[0][0]])
    mid_backs.append(mid(1))
    up_other = up_out(1)
    up_ring = Reduce(ring, here, core, up_other)
    down_ring.step([up_other])
    up_mine = up_out(0, [down_ring.up])
    up_ring.start(up_mine)
    g_o = heads_back(1, qkv_o, [up_ring.up])
    down_ring.step([g_o])
    up_ring.step([g_o])
    g_m = heads_back(0, qkv_m, [down_ring.up, up_ring.up])
    part, gb0 = in_back(g_m, g_o, attn_m, attn_o, tokens)
    extra_m, extra_o = gain_pack(
        core.reshape(1).astype(jnp.int32),
        gb0,
        [m[4] for m in mid_backs],
        [b[3] for b in backs],
    )
    halves = part.reshape(2, rows, width)
    part_keep = lax.dynamic_index_in_dim(halves, side, 0, keepdims=False)
    part_got = swap_sides(lax.dynamic_index_in_dim(halves, 1 - side, 0, keepdims=False))
    attn_other = qkv_grad(a1, g_o, extra_o)
    attn_ring = Reduce(ring, here, core, attn_other)
    down_ring.step([attn_other])
    up_ring.step([attn_other])
    attn_mine = qkv_grad(a1, g_m, extra_m, deps=[down_ring.up, up_ring.up])
    attn_ring.start(attn_mine)
    grad_down = down_ring.end()
    up_ring.step([attn_ring.up])
    attn_ring.step()
    grad_up = up_ring.end()
    attn_ring.step()
    attn_ring.step()
    grad_attn = attn_ring.end()

    dh_own = jnp.where(side == 0, mid_backs[0][0], mid_backs[1][0])
    x_own = lax.dynamic_slice_in_dim(tokens, side * rows, rows, 0)
    grad_tokens = tokens_back(x_own, part_keep, part_got, dh_own, ln_gain)
    output = jnp.where(side == 0, backs[0][0], backs[1][0])

    gains = grad_attn[:, :, 3 * cols : 3 * cols + 4]
    gains = gains + swap_sides(gains)
    gains = jnp.transpose(gains, (0, 2, 1))
    grad_qkv = grad_attn[:, :, : 3 * cols].reshape(2, w_rows, 3, cols)
    grad_qkv = jnp.transpose(grad_qkv, (2, 1, 0, 3)).reshape(3, w_rows, 2 * cols)
    grad_out = jnp.transpose(grad_up[:, :, units:], (0, 2, 1)).reshape(2 * cols, w_rows)
    grad_up = jnp.transpose(grad_up[:, :, :units], (1, 0, 2)).reshape(w_rows, 2 * units)
    grad_down = jnp.transpose(grad_down, (0, 2, 1)).reshape(2 * units, w_rows)
    return output, grad_tokens, grad_qkv, grad_out, grad_up, grad_down, gains[0], gains[1]


def layer_norm(values, norm_gain, norm_bias):
    average = jnp.mean(values, axis=-1, keepdims=True)
    centred = values - average
    variance = jnp.mean(centred * centred, axis=-1, keepdims=True)
    return centred * lax.rsqrt(variance + NORM_EPS) * norm_gain + norm_bias


def norm_pull(values, norm_gain, norm_bias, grad_result):
    result, puller = jax.vjp(layer_norm, values, norm_gain, norm_bias)
    return puller(grad_result)


def seq_layout(lengths, block_size):
    block_count = lengths.shape[0]
    block_ids = jnp.arange(block_count, dtype=jnp.int32)
    starts = lengths > 0
    earlier = starts[None, :] & (block_ids[None, :] <= block_ids[:, None])
    owners = jnp.max(jnp.where(earlier, block_ids[None, :], 0), axis=1)
    owner_len = jnp.sum(
        jnp.where(block_ids[None, :] == owners[:, None], lengths[None, :], 0), axis=1
    )
    places = jnp.arange(block_count * block_size, dtype=jnp.int32)
    tok_owner = jnp.repeat(owners, block_size)
    position = places - tok_owner * block_size
    is_valid = position < jnp.repeat(owner_len, block_size)
    allowed = (
        (tok_owner[:, None] == tok_owner[None, :])
        & (places[None, :] <= places[:, None])
        & is_valid[None, :]
    )
    return (position, allowed)


def rotary_tables(position, width):
    frequency = ROPE_BASE ** (-jnp.arange(width // 2, dtype=jnp.float32) * 2.0 / width)
    angles = position.astype(jnp.float32)[:, None] * frequency[None, :]
    return (jnp.cos(angles), jnp.sin(angles))


def rotate(values, cos_table, sin_table):
    half_width = values.shape[-1] // 2
    front_half = values[..., :half_width]
    back_half = values[..., half_width:]
    cos_part = cos_table[:, None, :]
    sin_part = sin_table[:, None, :]
    return jnp.concatenate(
        [
            front_half * cos_part - back_half * sin_part,
            back_half * cos_part + front_half * sin_part,
        ],
        axis=-1,
    )


def attention_scores(queries, keys_rot, allowed, scale):
    raw_scores = (
        jnp.einsum("hqd,hkd->hqk", queries, keys_rot, preferred_element_type=jnp.float32) * scale
    )
    return jnp.where(allowed[None, :, :], raw_scores, MASK_FILL)


def plain_device(tokens, seq_lengths, ln_gain, ln_bias, w_qkv, w_out, w_up, w_down, cotangent):
    full_qkv, full_out, full_up, full_down = (
        lax.all_gather(w_qkv, "dp", axis=1, tiled=True),
        lax.all_gather(w_out, "dp", axis=1, tiled=True),
        lax.all_gather(w_up, "dp", axis=0, tiled=True),
        lax.all_gather(w_down, "dp", axis=1, tiled=True),
    )
    tok_count = tokens.shape[0]
    shard_rows = cotangent.shape[0]
    row_start = lax.axis_index("mp") * shard_rows
    heads_here = full_out.shape[0] // HD
    scale = HD ** (-0.5)
    position, allowed = seq_layout(seq_lengths, BLOCK)
    cos_table, sin_table = rotary_tables(position, HD)

    def to_heads(values):
        return jnp.transpose(values.reshape(tok_count, heads_here, HD), (1, 0, 2))

    def from_heads(values):
        return jnp.transpose(values, (1, 0, 2)).reshape(tok_count, heads_here * HD)

    def rotated(values):
        return rotate(values.reshape(tok_count, heads_here, HD), cos_table, sin_table)

    inputs = tokens.astype(jnp.float32)
    normed_in = layer_norm(inputs, ln_gain[0], ln_bias[0]).astype(jnp.bfloat16)
    projected = jnp.einsum("td,cde->cte", normed_in, full_qkv, preferred_element_type=jnp.float32)
    queries = jnp.transpose(rotated(projected[0]), (1, 0, 2)).astype(jnp.bfloat16)
    keys_rot = jnp.transpose(rotated(projected[1]), (1, 0, 2)).astype(jnp.bfloat16)
    values_h = to_heads(projected[2]).astype(jnp.bfloat16)
    scores = attention_scores(queries, keys_rot, allowed, scale)
    top_score = jnp.max(scores, axis=-1, keepdims=True)
    expo = jnp.exp(scores - top_score)
    row_total = jnp.sum(expo, axis=-1, keepdims=True)
    probs = expo / row_total
    log_total = top_score + jnp.log(row_total)
    attended = jnp.einsum(
        "hqk,hkd->hqd", probs.astype(jnp.bfloat16), values_h, preferred_element_type=jnp.float32
    )
    mixed_heads = from_heads(attended).astype(jnp.bfloat16)
    attn_part = jnp.dot(mixed_heads, full_out, preferred_element_type=jnp.float32)
    attn_sum = lax.psum_scatter(
        attn_part.astype(jnp.bfloat16), "mp", scatter_dimension=0, tiled=True
    ).astype(jnp.float32)
    resid_in = lax.dynamic_slice_in_dim(inputs, row_start, shard_rows, 0)
    hidden_state = resid_in + layer_norm(attn_sum, ln_gain[1], ln_bias[1])
    normed_mid = layer_norm(hidden_state, ln_gain[2], ln_bias[2]).astype(jnp.bfloat16)
    mlp_input = lax.all_gather(normed_mid, "mp", axis=0, tiled=True)
    pre_act = jnp.dot(mlp_input, full_up, preferred_element_type=jnp.float32)
    act_low = jax.nn.gelu(pre_act, approximate=True).astype(jnp.bfloat16)
    mlp_part = jnp.dot(act_low, full_down, preferred_element_type=jnp.float32)
    mlp_sum = lax.psum_scatter(
        mlp_part.astype(jnp.bfloat16), "mp", scatter_dimension=0, tiled=True
    ).astype(jnp.float32)
    output = (hidden_state + layer_norm(mlp_sum, ln_gain[3], ln_bias[3])).astype(jnp.bfloat16)
    grad_result = cotangent.astype(jnp.float32)
    grad_mlp_sum, grad_gain3, grad_bias3 = norm_pull(mlp_sum, ln_gain[3], ln_bias[3], grad_result)
    grad_mlp_rows = lax.all_gather(grad_mlp_sum.astype(jnp.bfloat16), "mp", axis=0, tiled=True)
    grad_down = jnp.einsum("tf,te->fe", act_low, grad_mlp_rows, preferred_element_type=jnp.float32)
    grad_act = jnp.einsum("te,fe->tf", grad_mlp_rows, full_down, preferred_element_type=jnp.float32)
    gelu_puller = jax.vjp(lambda values: jax.nn.gelu(values, approximate=True), pre_act)[1]
    grad_pre = gelu_puller(grad_act)[0].astype(jnp.bfloat16)
    grad_up = jnp.einsum("td,tf->df", mlp_input, grad_pre, preferred_element_type=jnp.float32)
    grad_mid_part = jnp.einsum("tf,df->td", grad_pre, full_up, preferred_element_type=jnp.float32)
    grad_mid = lax.psum_scatter(
        grad_mid_part.astype(jnp.bfloat16), "mp", scatter_dimension=0, tiled=True
    ).astype(jnp.float32)
    grad_hidden_norm, grad_gain2, grad_bias2 = norm_pull(
        hidden_state, ln_gain[2], ln_bias[2], grad_mid
    )
    grad_hidden = grad_result + grad_hidden_norm
    grad_attn_sum, grad_gain1, grad_bias1 = norm_pull(attn_sum, ln_gain[1], ln_bias[1], grad_hidden)
    grad_attn_rows = lax.all_gather(grad_attn_sum.astype(jnp.bfloat16), "mp", axis=0, tiled=True)
    grad_outproj = jnp.einsum(
        "tc,te->ce", mixed_heads, grad_attn_rows, preferred_element_type=jnp.float32
    )
    grad_mixed = jnp.einsum(
        "te,ce->tc", grad_attn_rows, full_out, preferred_element_type=jnp.float32
    ).astype(jnp.bfloat16)
    grad_heads = to_heads(grad_mixed)
    again_scores = attention_scores(queries, keys_rot, allowed, scale)
    again_probs = jnp.exp(again_scores - log_total)
    grad_probs = jnp.einsum(
        "hqd,hkd->hqk", grad_heads, values_h, preferred_element_type=jnp.float32
    )
    grad_values = jnp.einsum(
        "hqk,hqd->hkd",
        again_probs.astype(jnp.bfloat16),
        grad_heads,
        preferred_element_type=jnp.float32,
    )
    row_dot = jnp.sum(again_probs * grad_probs, axis=-1, keepdims=True)
    grad_scores = (again_probs * (grad_probs - row_dot) * scale).astype(jnp.bfloat16)
    grad_q_rot = jnp.einsum(
        "hqk,hkd->hqd", grad_scores, keys_rot, preferred_element_type=jnp.float32
    )
    grad_k_rot = jnp.einsum(
        "hqk,hqd->hkd", grad_scores, queries, preferred_element_type=jnp.float32
    )
    zero_heads = jnp.zeros((tok_count, heads_here, HD), jnp.float32)
    unrotate = jax.vjp(lambda values: rotate(values, cos_table, sin_table), zero_heads)[1]
    grad_query = unrotate(jnp.transpose(grad_q_rot, (1, 0, 2)))[0].reshape(
        tok_count, heads_here * HD
    )
    grad_key = unrotate(jnp.transpose(grad_k_rot, (1, 0, 2)))[0].reshape(tok_count, heads_here * HD)
    grad_value = from_heads(grad_values)
    grad_proj = jnp.stack(
        [
            grad_query.astype(jnp.bfloat16),
            grad_key.astype(jnp.bfloat16),
            grad_value.astype(jnp.bfloat16),
        ]
    )
    grad_qkv = jnp.einsum("td,cte->cde", normed_in, grad_proj, preferred_element_type=jnp.float32)
    grad_in_part = jnp.einsum(
        "cte,cde->td", grad_proj, full_qkv, preferred_element_type=jnp.float32
    )
    grad_in = lax.psum_scatter(
        grad_in_part.astype(jnp.bfloat16), "mp", scatter_dimension=0, tiled=True
    ).astype(jnp.float32)
    grad_norm_in, grad_gain0, grad_bias0 = norm_pull(resid_in, ln_gain[0], ln_bias[0], grad_in)
    grad_tokens = grad_hidden + grad_norm_in
    gain_grads = jnp.stack([grad_gain0, grad_gain1, grad_gain2, grad_gain3])
    bias_grads = jnp.stack([grad_bias0, grad_bias1, grad_bias2, grad_bias3])
    gain_grads, bias_grads = (
        lax.psum(gain_grads.astype(jnp.bfloat16), "mp").astype(jnp.float32),
        lax.psum(bias_grads.astype(jnp.bfloat16), "mp").astype(jnp.float32),
    )
    grad_qkv, grad_outproj, grad_up, grad_down, gain_grads, bias_grads = (
        lax.psum_scatter(
            grad_qkv.astype(jnp.bfloat16), "dp", scatter_dimension=1, tiled=True
        ).astype(jnp.float32),
        lax.psum_scatter(
            grad_outproj.astype(jnp.bfloat16), "dp", scatter_dimension=1, tiled=True
        ).astype(jnp.float32),
        lax.psum_scatter(
            grad_up.astype(jnp.bfloat16), "dp", scatter_dimension=0, tiled=True
        ).astype(jnp.float32),
        lax.psum_scatter(
            grad_down.astype(jnp.bfloat16), "dp", scatter_dimension=1, tiled=True
        ).astype(jnp.float32),
        lax.psum_scatter(
            gain_grads.astype(jnp.bfloat16), "dp", scatter_dimension=1, tiled=True
        ).astype(jnp.float32),
        lax.psum_scatter(
            bias_grads.astype(jnp.bfloat16), "dp", scatter_dimension=1, tiled=True
        ).astype(jnp.float32),
    )
    return (output, grad_tokens, grad_qkv, grad_outproj, grad_up, grad_down, gain_grads, bias_grads)


def solution(mesh):
    placed = (
        P("dp", None),
        P("dp"),
        P(),
        P(),
        P(None, "dp", "mp"),
        P("mp", "dp"),
        P("dp", "mp"),
        P("mp", "dp"),
        P(("dp", "mp"), None),
    )
    if mesh.shape["mp"] == 2:
        body = functools.partial(per_device, mesh.shape["dp"])
    else:
        body = plain_device
    return jax.shard_map(
        body,
        mesh=mesh,
        in_specs=placed,
        out_specs=(
            P(("dp", "mp"), None),
            P(("dp", "mp"), None),
            P(None, "dp", "mp"),
            P("mp", "dp"),
            P("dp", "mp"),
            P("mp", "dp"),
            P(None, "dp"),
            P(None, "dp"),
        ),
        check_vma=False,
    )
```

```python
import functools

import jax
import jax.numpy as jnp
from jax import lax
from jax.experimental import pallas as pl
from jax.experimental.pallas import tpu as pltpu
from jax.sharding import PartitionSpec as P

HD = 64
BLOCK = 128
LANES = 128
NORM_EPS = 1e-05
ROPE_BASE = 10000.0
MASK_FILL = -1e30
F32 = jnp.float32
BF16 = jnp.bfloat16
VMEM_LIMIT = 6 * 1024 * 1024
STEP = 64
NN = (((1,), (0,)), ((), ()))
NT = (((1,), (1,)), ((), ()))
TN = (((0,), (0,)), ((), ()))


def mm(left, right, dims):
    return lax.dot_general(left, right, dims, preferred_element_type=F32)


def sds(shape, dtype):
    return jax.ShapeDtypeStruct(shape, dtype)


def whole():
    return pl.BlockSpec(memory_space=pltpu.VMEM)


def smem():
    return pl.BlockSpec(memory_space=pltpu.SMEM)


def anywhere():
    return pl.BlockSpec(memory_space=pl.ANY)


TIMES = {
    "prepare": 3.3, "cotangent_rows": 1.5, "qkv_project": 2.0, "attend0": 2.5, "attend1": 4.4,
    "up_project": 4.3, "down_project": 1.3, "mlp_back": 5.4, "weight_grad": 1.3, "mid_back": 3.3,
    "attend_back": 5.0, "in_back": 3.6, "gain_pack": 0.4, "tokens_back": 3.9, "stage": 0.5,
    "assemble": 1.2, "ring_sum": 1.3, "ring_end": 2.0, "rotary": 2.0, "split": 0.4, "gain_end": 0.5,
}
TIME_SHARE = 1.0


def cost_of(name):
    return pl.CostEstimate(
        flops=0, bytes_accessed=int(TIMES[name] * TIME_SHARE * 3.69e6), transcendentals=0
    )


def kernel_call(body, name, out_shape, args, smems=1, flops=0, nbytes=0, scratch=(), **extra):
    many = isinstance(out_shape, (list, tuple))
    return pl.pallas_call(
        body,
        in_specs=[smem()] * smems + [whole()] * (len(args) - smems),
        out_specs=[whole()] * len(out_shape) if many else whole(),
        out_shape=out_shape,
        scratch_shapes=list(scratch),
        compiler_params=pltpu.CompilerParams(vmem_limit_bytes=VMEM_LIMIT),
        cost_estimate=cost_of(name),
        name=name,
        **extra,
    )(*args)


def after(value, *others):
    return lax.optimization_barrier((value,) + others)[0]


def chip_of(place, size):
    if isinstance(place, int):
        return 2 * place if place < size // 2 else 2 * (size - 1 - place) + 1
    return jnp.where(place < size // 2, 2 * place, 2 * (size - 1 - place) + 1)


def chip_near(ids_ref, step, size):
    chip = ids_ref[0] // 2
    here = jnp.where(chip % 2 == 0, chip // 2, size - 1 - chip // 2)
    return chip_of((here + step + size) % size, size)


def split_cores(values, core):
    half = values.shape[1] // 2
    lane = lax.broadcasted_iota(jnp.int32, (values.shape[0], LANES), 1)
    low = lane < LANES // 2
    own, other = [], []
    for start in range(0, 2 * half, 2 * LANES):
        a = values[:, start : start + LANES]
        b = values[:, start + LANES : start + 2 * LANES]
        first = jnp.where(low, a, pltpu.roll(b, LANES // 2, 1))
        second = jnp.where(low, pltpu.roll(a, LANES // 2, 1), b)
        own.append(jnp.where(core == 0, first, second))
        other.append(jnp.where(core == 0, second, first))
    return jnp.concatenate(own + other, axis=1)


def join_cores(values, core):
    half = values.shape[1] // 2
    lane = lax.broadcasted_iota(jnp.int32, (values.shape[0], LANES), 1)
    low = lane < LANES // 2
    out = []
    for start in range(0, half, LANES):
        own = values[:, start : start + LANES]
        other = values[:, half + start : half + start + LANES]
        first = jnp.where(core == 0, own, other)
        second = jnp.where(core == 0, other, own)
        out.append(jnp.where(low, first, pltpu.roll(second, LANES // 2, 1)))
        out.append(jnp.where(low, pltpu.roll(first, LANES // 2, 1), second))
    return jnp.concatenate(out, axis=1)


def norm_stats(values):
    centred = values - jnp.mean(values, axis=-1, keepdims=True)
    rstd = lax.rsqrt(jnp.mean(centred * centred, axis=-1, keepdims=True) + NORM_EPS)
    return centred * rstd, rstd


def norm_back(normed, rstd, scaled_grad):
    first = jnp.mean(scaled_grad, axis=-1, keepdims=True)
    second = jnp.mean(scaled_grad * normed, axis=-1, keepdims=True)
    return (scaled_grad - first - normed * second) * rstd


def fold_rows(values):
    return jnp.sum(values.reshape(-1, 8, values.shape[-1]), axis=0)


def row_steps(rows, body):
    @pl.loop(0, rows // STEP)
    def _(i):
        body(pl.ds(pl.multiple_of(i * STEP, STEP), STEP))


def prepare_kernel(ids_ref, x_ref, gain_ref, bias_ref, xp_ref, a1_ref, gp_ref, bp_ref):
    core = ids_ref[0] % 2
    gp_ref[...] = split_cores(gain_ref[...], core)
    bp_ref[...] = split_cores(bias_ref[...], core)

    def body(at):
        x = split_cores(x_ref[at, :].astype(F32), core)
        xp_ref[at, :] = x.astype(BF16)
        normed, _ = norm_stats(x)
        a1_ref[at, :] = (normed * gp_ref[0:1, :] + bp_ref[0:1, :]).astype(BF16)

    row_steps(x_ref.shape[0], body)


def prepare(ids, x, gain, bias):
    return kernel_call(
        prepare_kernel,
        "prepare",
        [sds(x.shape, BF16), sds(x.shape, BF16), sds(gain.shape, F32), sds(bias.shape, F32)],
        (ids, x, gain, bias),
        nbytes=6 * x.size,
    )


def cotangent_kernel(ids_ref, own_ref, got_ref, out_ref):
    core, side = ids_ref[0] % 2, ids_ref[1]
    rows = own_ref.shape[0]
    for ref, base in ((own_ref, side * rows), (got_ref, (1 - side) * rows)):

        @pl.loop(0, rows // STEP)
        def _(i, ref=ref, base=base):
            at = pl.ds(pl.multiple_of(i * STEP, STEP), STEP)
            to = pl.ds(pl.multiple_of(base + i * STEP, STEP), STEP)
            out_ref[to, :] = split_cores(ref[at, :].astype(F32), core).astype(BF16)


def cotangent_rows(ids, own, got):
    rows, width = own.shape
    return kernel_call(
        cotangent_kernel, "cotangent_rows", sds((2 * rows, width), BF16), (ids, own, got),
        nbytes=8 * own.size,
    )


def partner(values):
    lane = lax.broadcasted_iota(jnp.int32, values.shape, 1)
    ahead = pltpu.roll(values, LANES - HD // 2, 1)
    behind = pltpu.roll(values, HD // 2, 1)
    return jnp.where(lax.rem(lane, HD) < HD // 2, ahead, behind)


def qkv_kernel(a_ref, wo_ref, wg_ref, cos_ref, sin_ref, out_ref):
    half = wo_ref.shape[0]
    cols = wo_ref.shape[1] // 4
    rows = 2 * BLOCK

    @pl.loop(0, a_ref.shape[0] // rows)
    def _(i):
        at = pl.ds(pl.multiple_of(i * rows, rows), rows)
        cos, sin = cos_ref[at, :], sin_ref[at, :]
        for which in range(3):
            to = slice(which * cols, (which + 1) * cols)
            proj = mm(a_ref[at, :half], wo_ref[:, to], NN) + mm(a_ref[at, half:], wg_ref[:, to], NN)
            for start in range(0, cols, LANES):
                part = proj[:, start : start + LANES]
                if which < 2:
                    part = part * cos + partner(part) * sin
                if which == 0:
                    part = part.astype(BF16).astype(F32) * HD ** (-0.5)
                out_ref[at, which * cols + start : which * cols + start + LANES] = part.astype(BF16)


def qkv_project(a1, wo, wg, cos, sin):
    count, width = a1.shape
    three = wo.shape[1] // 4 * 3
    return kernel_call(
        qkv_kernel, "qkv_project", sds((count, three), BF16), (a1, wo, wg, cos, sin), smems=0,
        flops=2 * count * width * three, nbytes=2 * width * three,
    )


def span_of(len_ref, block):
    start, size = jnp.int32(0), jnp.int32(0)
    for b in range(block + 1):
        here = len_ref[b]
        start = jnp.where(here > 0, b * BLOCK, start)
        size = jnp.where(here > 0, here, size)
    return start, start + size


def rotary_kernel(len_ref, cos_ref, sin_ref):
    lane = lax.broadcasted_iota(jnp.int32, (BLOCK, LANES), 1)
    row = lax.broadcasted_iota(jnp.int32, (BLOCK, LANES), 0)
    index = (lane % (HD // 2)).astype(F32)
    frequency = jnp.exp(index * (-2.0 / HD * 9.210340371976184))
    back = lane % HD >= HD // 2
    for b in range(cos_ref.shape[0] // BLOCK):
        start, _ = span_of(len_ref, b)
        angle = (row + (b * BLOCK - start)).astype(F32) * frequency
        sin = jnp.sin(angle)
        cos_ref[b * BLOCK : (b + 1) * BLOCK, :] = jnp.cos(angle)
        sin_ref[b * BLOCK : (b + 1) * BLOCK, :] = jnp.where(back, sin, -sin)


def rotary_pair(lengths, count):
    out = sds((count, LANES), F32)
    return kernel_call(rotary_kernel, "rotary", [out, out], (lengths,))


def head_lanes(rows, first):
    lane = lax.broadcasted_iota(jnp.int32, (rows, LANES), 1)
    return (lane < HD) == first


def attend_kernel(row0, len_ref, q_ref, wo_ref, wg_ref, p_ref, o_ref, part_ref):
    rows, cols = o_ref.shape
    ext = p_ref.shape[2]
    half = wo_ref.shape[0]
    key = lax.broadcasted_iota(jnp.int32, (BLOCK, ext), 1)
    query = lax.broadcasted_iota(jnp.int32, (BLOCK, ext), 0)
    masks = []
    for b in range(rows // BLOCK):
        lo, hi = span_of(len_ref, row0 // BLOCK + b)
        seen = (key >= lo) & (key < hi) & (key <= query + (row0 + b * BLOCK))
        masks.append(jnp.where(seen, 0.0, MASK_FILL))
    mask = jnp.concatenate(masks, axis=0)
    head = 0
    for start in range(0, cols, LANES):
        q = q_ref[row0 : row0 + rows, start : start + LANES]
        k = q_ref[0:ext, cols + start : cols + start + LANES]
        v = q_ref[0:ext, 2 * cols + start : 2 * cols + start + LANES]
        outs = []
        for first in (True, False):
            mine = head_lanes(rows, first)
            s = mm(jnp.where(mine, q, jnp.zeros_like(q)), k, NT) + mask
            e = jnp.exp(s - jnp.max(s, axis=-1, keepdims=True))
            p = (e * (1.0 / jnp.sum(e, axis=-1, keepdims=True))).astype(BF16)
            p_ref[head] = p
            head += 1
            outs.append(mm(p, v, NN))
        o_ref[:, start : start + LANES] = jnp.where(
            head_lanes(rows, True), outs[0], outs[1]
        ).astype(BF16)
    part_ref[:, :half] = mm(o_ref[...], wo_ref[:, 3 * cols :], NT).astype(BF16)
    part_ref[:, half:] = mm(o_ref[...], wg_ref[:, 3 * cols :], NT).astype(BF16)


def attend(row0, rows, lengths, qkv, wo, wg):
    ext = row0 + rows
    cols = qkv.shape[1] // 3
    heads = cols // HD
    width = 2 * wo.shape[0]
    return kernel_call(
        functools.partial(attend_kernel, row0),
        "attend0" if row0 == 0 else "attend1",
        [sds((heads, rows, ext), BF16), sds((rows, cols), BF16), sds((rows, width), BF16)],
        (lengths, qkv, wo, wg),
        flops=4 * heads * rows * ext * HD + 2 * rows * width * cols,
    )


def hidden_of(x, ya, yb, gain_ref, bias_ref):
    n1, r1 = norm_stats(ya.astype(F32) + yb.astype(F32))
    return x.astype(F32) + n1 * gain_ref[1:2, :] + bias_ref[1:2, :], n1, r1


def chunk_rows(chunk, rows, at):
    return pl.ds(pl.multiple_of(chunk * rows + at.start, STEP), STEP)


UNITS = 512


def up_kernel(chunk, x_ref, ya_ref, yb_ref, gain_ref, bias_ref, wo_ref, wg_ref, a3_ref, g_ref, gp_ref):
    rows = ya_ref.shape[0]
    half = wo_ref.shape[0]

    def body(at):
        x = x_ref[chunk_rows(chunk, rows, at), :]
        h, _, _ = hidden_of(x, ya_ref[at, :], yb_ref[at, :], gain_ref, bias_ref)
        n2, _ = norm_stats(h)
        a3_ref[at, :] = (n2 * gain_ref[2:3, :] + bias_ref[2:3, :]).astype(BF16)

    row_steps(rows, body)

    @pl.loop(0, wo_ref.shape[1] // UNITS)
    def _(i):
        to = pl.ds(pl.multiple_of(i * UNITS, UNITS), UNITS)
        u = mm(a3_ref[:, :half], wo_ref[:, to], NN) + mm(a3_ref[:, half:], wg_ref[:, to], NN)
        k0 = 0.7978845608028654
        k1 = 0.044715
        sq = u * u
        th = jnp.tanh(u * (k0 + (k0 * k1) * sq))
        plus = 0.5 + 0.5 * th
        g_ref[:, to] = (u * plus).astype(BF16)
        slope = plus + (u * (k0 + (3.0 * k0 * k1) * sq)) * (0.5 - (0.5 * th) * th)
        gp_ref[:, to] = slope.astype(BF16)


def up_project(chunk, x, ya, yb, gain, bias, wo, wg):
    rows, width = ya.shape
    units = wo.shape[1]
    return kernel_call(
        functools.partial(up_kernel, chunk),
        "up_project",
        [sds((rows, width), BF16), sds((rows, units), BF16), sds((rows, units), BF16)],
        (x, ya, yb, gain, bias, wo, wg),
        smems=0,
        flops=2 * rows * width * units,
    )


def down_kernel(g_ref, wo_ref, wg_ref, z_ref):
    half = wo_ref.shape[0]
    z_ref[:, :half] = mm(g_ref[...], wo_ref[...], NT).astype(BF16)
    z_ref[:, half:] = mm(g_ref[...], wg_ref[...], NT).astype(BF16)


def down_project(g, wo, wg):
    rows, units = g.shape
    width = 2 * wo.shape[0]
    return kernel_call(
        down_kernel, "down_project", sds((rows, width), BF16), (g, wo, wg), smems=0,
        flops=2 * rows * width * units,
    )


def mlp_back_kernel(
    chunk, ids_ref, x_ref, ya_ref, yb_ref, za_ref, zb_ref, cot_ref, gain_ref, bias_ref, gp_ref,
    w3o, w3g, w2o, w2g, *refs
):
    out_ref, dz_ref, du_ref, part_ref, gb_ref = refs[-5:]
    rows = ya_ref.shape[0]
    half = w3o.shape[0]
    core, side = ids_ref[0] % 2, ids_ref[1]
    gb_ref[...] = jnp.zeros_like(gb_ref)

    def body(at):
        far = chunk_rows(chunk, rows, at)
        h, _, _ = hidden_of(x_ref[far, :], ya_ref[at, :], yb_ref[at, :], gain_ref, bias_ref)
        n3, r3 = norm_stats(za_ref[at, :].astype(F32) + zb_ref[at, :].astype(F32))
        cot = cot_ref[far, :].astype(F32)
        gain = gain_ref[3:4, :]
        out = join_cores(h + (n3 * gain + bias_ref[3:4, :]), core)
        if chunk > 0:
            out = jnp.where(side == chunk, out, refs[0][at, :].astype(F32))
        out_ref[at, :] = out.astype(BF16)
        dz_ref[at, :] = norm_back(n3, r3, cot * gain).astype(BF16)
        gb_ref[0] += fold_rows(cot * n3)
        gb_ref[1] += fold_rows(cot)

    row_steps(rows, body)

    @pl.loop(0, w3o.shape[1] // UNITS)
    def _(i):
        to = pl.ds(pl.multiple_of(i * UNITS, UNITS), UNITS)
        dg = mm(dz_ref[:, :half], w3o[:, to], NN) + mm(dz_ref[:, half:], w3g[:, to], NN)
        du_ref[:, to] = (dg * gp_ref[:, to].astype(F32)).astype(BF16)

    part_ref[:, :half] = mm(du_ref[...], w2o[...], NT).astype(BF16)
    part_ref[:, half:] = mm(du_ref[...], w2g[...], NT).astype(BF16)


def mlp_back(chunk, ids, x, ya, yb, za, zb, cot, gain, bias, gp, w3, w2, before=()):
    rows, width = ya.shape
    units = w3[0].shape[1]
    return kernel_call(
        functools.partial(mlp_back_kernel, chunk),
        "mlp_back",
        [
            sds((rows, width), BF16),
            sds((rows, width), BF16),
            sds((rows, units), BF16),
            sds((rows, width), BF16),
            sds((2, 8, width), F32),
        ],
        (ids, x, ya, yb, za, zb, cot, gain, bias, gp, *w3, *w2, *before),
        flops=4 * rows * width * units,
    )


def weight_grad_kernel(which, sizes, *refs):
    out_ref, left_sc = refs[-2:]
    half, count = left_sc.shape
    start = 0
    for lefts, rights, cols in sizes:
        rows = 0
        for ref in refs[lefts[0] : lefts[1]]:
            part = ref[:, which * half : (which + 1) * half]
            left_sc[:, rows : rows + part.shape[0]] = part.T
            rows += part.shape[0]
        for c in range(0, cols, UNITS):
            total, rows = None, 0
            for ref in refs[rights[0] : rights[1]]:
                n = ref.shape[0]
                term = mm(left_sc[:, rows : rows + n], ref[:, c : c + UNITS], NN)
                total = term if total is None else total + term
                rows += n
            out_ref[:, start + c : start + c + UNITS] = total.astype(BF16)
        start += cols
    if out_ref.shape[1] > start:
        out_ref[:, start:] = refs[-3][which * half : (which + 1) * half, :]


def weight_grad(which, products, extra=None):
    args, sizes, total = [], [], 0
    for lefts, rights in products:
        cols = rights[0].shape[1]
        n = len(args)
        sizes.append(((n, n + len(lefts)), (n + len(lefts), n + len(lefts) + len(rights)), cols))
        args += list(lefts) + list(rights)
        total += cols
    width = args[0].shape[1]
    count = sum(a.shape[0] for a in products[0][0])
    if extra is not None:
        args.append(extra)
        total += extra.shape[1]
    return kernel_call(
        functools.partial(weight_grad_kernel, which, sizes),
        "weight_grad",
        sds((width // 2, total), BF16),
        tuple(args),
        smems=0,
        flops=count * width * total,
        scratch=[pltpu.VMEM((width // 2, count), BF16)],
    )


def mid_back_kernel(
    chunk, x_ref, ya_ref, yb_ref, ea_ref, eb_ref, cot_ref, gain_ref, bias_ref, wo_ref, wg_ref,
    dh_ref, dy_ref, do_ref, gb_ref,
):
    rows, cols = do_ref.shape
    half = wo_ref.shape[0]
    gb_ref[...] = jnp.zeros_like(gb_ref)

    def body(at):
        far = chunk_rows(chunk, rows, at)
        h, n1, r1 = hidden_of(x_ref[far, :], ya_ref[at, :], yb_ref[at, :], gain_ref, bias_ref)
        n2, r2 = norm_stats(h)
        e = ea_ref[at, :].astype(F32) + eb_ref[at, :].astype(F32)
        dh = cot_ref[far, :].astype(F32) + norm_back(n2, r2, e * gain_ref[2:3, :])
        dh_ref[at, :] = dh
        dy_ref[at, :] = norm_back(n1, r1, dh * gain_ref[1:2, :]).astype(BF16)
        gb_ref[0] += fold_rows(e * n2)
        gb_ref[1] += fold_rows(e)
        gb_ref[2] += fold_rows(dh * n1)
        gb_ref[3] += fold_rows(dh)

    row_steps(rows, body)
    do = mm(dy_ref[:, :half], wo_ref[:, 3 * cols :], NN)
    do_ref[...] = (do + mm(dy_ref[:, half:], wg_ref[:, 3 * cols :], NN)).astype(BF16)


def mid_back(chunk, x, ya, yb, ea, eb, cot, gain, bias, wo, wg):
    rows, width = ya.shape
    cols = wo.shape[1] // 4
    return kernel_call(
        functools.partial(mid_back_kernel, chunk),
        "mid_back",
        [
            sds((rows, width), F32),
            sds((rows, width), BF16),
            sds((rows, cols), BF16),
            sds((4, 8, width), F32),
        ],
        (x, ya, yb, ea, eb, cot, gain, bias, wo, wg),
        smems=0,
        flops=2 * rows * width * cols,
    )


def attend_back_kernel(q_ref, p0_ref, p1_ref, o0, o1, d0, d1, cos_ref, sin_ref, g_ref):
    rows, cols = o0.shape
    cos, sin = cos_ref[...], sin_ref[...]
    head = 0
    for start in range(0, cols, LANES):
        at = slice(start, start + LANES)
        q = q_ref[:, at]
        k = q_ref[:, cols + start : cols + start + LANES]
        v = q_ref[:, 2 * cols + start : 2 * cols + start + LANES]
        do = (d0[:, at], d1[:, at])
        prod = [a.astype(F32) * b[:, at].astype(F32) for a, b in zip(do, (o0, o1))]
        dq, dk, dv = [], [], []
        for first in (True, False):
            mine = head_lanes(rows, first)
            dqs = []
            for c, p_ref in enumerate((p0_ref, p1_ref)):
                ext = p_ref.shape[2]
                p = p_ref[head]
                dp = mm(jnp.where(mine, do[c], jnp.zeros_like(do[c])), v[:ext], NT)
                dot = jnp.sum(jnp.where(mine, prod[c], 0.0), axis=-1, keepdims=True)
                ds = (p.astype(F32) * (dp - dot)).astype(BF16)
                dqs.append(mm(ds, k[:ext], NN))
                dkc = mm(ds, q[c * rows : (c + 1) * rows], TN)
                dvc = mm(p, do[c], TN)
                if c == 0:
                    dk0, dv0 = dkc, dvc
            dk.append(jnp.concatenate([dk0 + dkc[:rows], dkc[rows:]], axis=0))
            dv.append(jnp.concatenate([dv0 + dvc[:rows], dvc[rows:]], axis=0))
            dq.append(jnp.concatenate(dqs, axis=0))
            head += 1
        low = head_lanes(2 * rows, True)
        gq = jnp.where(low, dq[0], dq[1]) * HD ** (-0.5)
        gk = jnp.where(low, dk[0], dk[1])
        gv = jnp.where(low, dv[0], dv[1])
        g_ref[:, at] = (gq * cos - partner(gq) * sin).astype(BF16)
        g_ref[:, cols + start : cols + start + LANES] = (gk * cos - partner(gk) * sin).astype(BF16)
        g_ref[:, 2 * cols + start : 2 * cols + start + LANES] = gv.astype(BF16)


def attend_back(qkv, probs, outs, grads, cos, sin):
    count, three = qkv.shape
    heads = probs[0].shape[0]
    return kernel_call(
        attend_back_kernel,
        "attend_back",
        sds((count, three), BF16),
        (qkv, *probs, *outs, *grads, cos, sin),
        smems=0,
        flops=10 * heads * count * count * HD,
    )


def in_back_kernel(ids_ref, g_ref, wo_ref, wg_ref, x_ref, keep_ref, give_ref, gb_ref):
    three = g_ref.shape[1]
    half = wo_ref.shape[0]
    rows = keep_ref.shape[0]
    gb_ref[...] = jnp.zeros_like(gb_ref)
    for turn, out_ref in enumerate((give_ref, keep_ref)):
        base = (1 - ids_ref[1] if turn == 0 else ids_ref[1]) * rows
        g = g_ref[pl.ds(pl.multiple_of(base, rows), rows), :]
        out_ref[:, :half] = mm(g, wo_ref[:, :three], NT).astype(BF16)
        out_ref[:, half:] = mm(g, wg_ref[:, :three], NT).astype(BF16)

        @pl.loop(0, rows // STEP)
        def _(i, base=base, out_ref=out_ref):
            e = out_ref[pl.ds(pl.multiple_of(i * STEP, STEP), STEP), :].astype(F32)
            far = pl.ds(pl.multiple_of(base + i * STEP, STEP), STEP)
            n0, _ = norm_stats(x_ref[far, :].astype(F32))
            gb_ref[0] += fold_rows(e * n0)
            gb_ref[1] += fold_rows(e)


def in_back(ids, g, wo, wg, x):
    count, three = g.shape
    width = x.shape[1]
    part = sds((count // 2, width), BF16)
    return kernel_call(
        in_back_kernel, "in_back", [part, part, sds((2, 8, width), F32)], (ids, g, wo, wg, x),
    )


def gain_pack_kernel(gb0_ref, g12a, g12b, g3a, g3b, out_ref):
    share = 0.5
    rows = []
    for kind in range(2):
        rows += [
            gb0_ref[kind],
            share * (g12a[2 + kind] + g12b[2 + kind]),
            share * (g12a[kind] + g12b[kind]),
            share * (g3a[kind] + g3b[kind]),
        ]
    rows = [jnp.sum(r, axis=0, keepdims=True) for r in rows]
    rows.append(jnp.zeros((LANES - len(rows), out_ref.shape[0]), F32))
    out_ref[...] = jnp.concatenate(rows, axis=0).T.astype(BF16)


def gain_pack(gb0, g12, g3):
    width = gb0.shape[-1]
    return kernel_call(
        gain_pack_kernel, "gain_pack", sds((width, LANES), BF16), (gb0, *g12, *g3), smems=0,
        nbytes=500 * width,
    )


def tokens_back_kernel(ids_ref, x_ref, keep_ref, got_ref, dh0_ref, dh1_ref, gain_ref, out_ref):
    core, side = ids_ref[0] % 2, ids_ref[1]
    rows = got_ref.shape[0]

    def body(at):
        far = pl.ds(pl.multiple_of(side * rows + at.start, STEP), STEP)
        e = keep_ref[at, :].astype(F32) + got_ref[at, :].astype(F32)
        n0, r0 = norm_stats(x_ref[far, :].astype(F32))
        dh = jnp.where(side == 0, dh0_ref[at, :], dh1_ref[at, :])
        out_ref[at, :] = join_cores(dh + norm_back(n0, r0, e * gain_ref[0:1, :]), core)

    row_steps(rows, body)


def tokens_back(ids, x, keep, got, dhs, gain):
    return kernel_call(
        tokens_back_kernel, "tokens_back", sds(got.shape, F32), (ids, x, keep, got, *dhs, gain),
    )


def gain_end_kernel(a_ref, b_ref, gain_ref, bias_ref):
    total = (a_ref[...] + b_ref[...]).T
    gain_ref[...] = total[0:4, :]
    bias_ref[...] = total[4:8, :]


def gain_end(a, b):
    out = sds((4, a.shape[0]), F32)
    return kernel_call(gain_end_kernel, "gain_end", [out, out], (a, b), smems=0)


def split_kernel(up_ref, down_ref, up_out, down_out):
    half = up_out.shape[0]
    up_out[...] = up_ref[:half, :]
    down_out[...] = down_ref[half:, :]


def split(up, down):
    out = sds((up.shape[0] // 2, up.shape[1]), BF16)
    return kernel_call(split_kernel, "split", [out, out], (up, down), smems=0)


def stage_kernel(*refs):
    ins, out_ref, sem = refs[:-2], refs[-2], refs[-1]
    copies, start = [], 0
    for ref in ins:
        parts = [ref.at[i] for i in range(ref.shape[0])] if len(ref.shape) == 3 else [ref]
        for part in parts:
            cols = part.shape[1]
            dst = out_ref.at[:, pl.ds(start, cols)]
            copies.append(pltpu.make_async_copy(part, dst, sem.at[len(copies)]))
            start += cols
    for copy in copies:
        copy.start()
    for copy in copies:
        copy.wait()


def stage(*arrays):
    rows = arrays[0].shape[-2]
    cols = sum(a.size // rows for a in arrays)
    return pl.pallas_call(
        stage_kernel,
        in_specs=[anywhere()] * len(arrays),
        out_specs=whole(),
        out_shape=sds((rows, cols), BF16),
        scratch_shapes=[pltpu.SemaphoreType.DMA((4 * len(arrays),))],
        compiler_params=pltpu.CompilerParams(vmem_limit_bytes=VMEM_LIMIT),
        cost_estimate=cost_of("stage"),
        name="stage",
    )(*arrays)


def assemble_kernel(places, size, ids_ref, *refs):
    ins, out, sem = refs[:-2], refs[-2], refs[-1]
    rows, unit = ins[0].shape[0], ins[-1].shape[0]
    copies = []
    for i, (src, (step, shift)) in enumerate(zip(ins, places)):
        at = pl.multiple_of(chip_near(ids_ref, step, size) * rows + shift, unit)
        copies.append(pltpu.make_async_copy(src, out.at[pl.ds(at, src.shape[0])], sem.at[i]))
    for copy in copies:
        copy.start()
    for copy in copies:
        copy.wait()


def assemble(ids, places, pieces, size):
    rows, width = pieces[0].shape
    return pl.pallas_call(
        functools.partial(assemble_kernel, places, size),
        in_specs=[smem()] + [anywhere()] * len(pieces),
        out_specs=whole(),
        out_shape=sds((rows * size, width), BF16),
        scratch_shapes=[pltpu.SemaphoreType.DMA((len(pieces),))],
        compiler_params=pltpu.CompilerParams(vmem_limit_bytes=VMEM_LIMIT),
        cost_estimate=cost_of("assemble"),
        name="assemble",
    )(ids, *pieces)


def ring_sum_kernel(parts, rows, kind, step, size, ids_ref, *refs):
    pairs = [(refs[2 * i], refs[2 * i + 1]) for i in range(parts)]
    came, outs = refs[2 * parts : -2], refs[-2:]
    half = rows // 2
    for way in range(2):
        out_ref = outs[way]
        chip = chip_near(ids_ref, step if way == 0 else -step, size)
        start = 0
        for mine, got in pairs:
            cols = mine.shape[1]
            to = slice(start, start + cols)
            if kind == 0:
                at = pl.ds(pl.multiple_of(chip * rows + way * half, half), half)
                out_ref[:, to] = (mine[at, :].astype(F32) + got[at, :].astype(F32)).astype(BF16)
            else:
                at = pl.ds(pl.multiple_of(chip * rows, rows), rows)
                term = mine[at, :].astype(F32) + got[at, :].astype(F32)
                in_ref = came[way]
                if kind == 2:
                    out_ref[:, to] = (term + in_ref[:, to].astype(F32)).astype(BF16)
                else:
                    hit = slice(0, half) if way == 0 else slice(half, rows)
                    rest = slice(half, rows) if way == 0 else slice(0, half)
                    out_ref[hit, to] = (term[hit] + in_ref[:, to].astype(F32)).astype(BF16)
                    out_ref[rest, to] = term[rest].astype(BF16)
            start += cols


def ring_sum(kind, rows, step, size, ids, pairs, came=()):
    flat = [a for pair in pairs for a in pair]
    cols = sum(mine.shape[1] for mine, _ in pairs)
    out = sds((rows // 2 if kind == 0 else rows, cols), BF16)
    return kernel_call(
        functools.partial(ring_sum_kernel, len(pairs), rows, kind, step, size),
        "ring_sum",
        [out, out],
        (ids, *flat, *came),
    )


def ring_end_kernel(parts, splits, size, ids_ref, *refs):
    pairs = [(refs[2 * i], refs[2 * i + 1]) for i in range(parts)]
    up, down = refs[2 * parts : 2 * parts + 2]
    outs = refs[2 * parts + 2 :]
    rows = up.shape[0]
    at = pl.ds(pl.multiple_of(chip_near(ids_ref, 0, size) * rows, rows), rows)
    start, o = 0, 0
    for (mine, got), sizes in zip(pairs, splits):
        here = 0
        for count, cols in sizes:
            for i in range(count):
                to, own = slice(start, start + cols), slice(here, here + cols)
                total = mine[at, own].astype(F32) + got[at, own].astype(F32)
                total = total + up[:, to].astype(F32) + down[:, to].astype(F32)
                if count > 1:
                    outs[o][i] = total
                else:
                    outs[o][...] = total
                start, here = start + cols, here + cols
            o += 1


def ring_end(size, ids, pairs, came, splits):
    flat = [a for pair in pairs for a in pair]
    rows = came[0].shape[0]
    shapes = [
        (count, rows, cols) if count > 1 else (rows, cols) for sizes in splits for count, cols in sizes
    ]
    return kernel_call(
        functools.partial(ring_end_kernel, len(pairs), splits, size),
        "ring_end",
        [sds(shape, F32) for shape in shapes],
        (ids, *flat, *came),
    )


class Ring:
    def __init__(self, n_dp, ids):
        self.size = n_dp // 2
        self.ids = ids
        self.up = self.shift(1)
        self.down = self.shift(-1)
        self.cores = [(i, i ^ 1) for i in range(n_dp)]

    def shift(self, by):
        return [
            (2 * chip_of(p, self.size) + c, 2 * chip_of((p + by) % self.size, self.size) + c)
            for p in range(self.size)
            for c in range(2)
        ]


def swap_cores(ring, value):
    return lax.ppermute(value, "dp", ring.cores)


class Gather:
    def __init__(self, ring, piece):
        self.ring = ring
        self.pieces, self.places = [piece], [(0, 0)]
        self.step_now = 0
        self.up = self.down = piece

    def step(self, *deps):
        self.step_now += 1
        ring, step = self.ring, self.step_now
        up, down = self.up, self.down
        if deps:
            up, down = after(up, *deps), after(down, *deps)
        shift = 0
        if step == ring.size // 2:
            shift = up.shape[0] // 2
            up, down = split(up, down)
        self.up = lax.ppermute(up, "dp", ring.up)
        self.down = lax.ppermute(down, "dp", ring.down)
        self.pieces += [self.up, self.down]
        self.places += [(-step, 0), (step, shift)]
        return self.up, self.down

    def end(self, *deps):
        ids = after(self.ring.ids, *deps) if deps else self.ring.ids
        own = assemble(ids, self.places, self.pieces, self.ring.size)
        return own, swap_cores(self.ring, own)


class Reduce:
    def __init__(self, ring, pairs):
        self.ring, self.pairs = ring, pairs
        self.rows = pairs[0][0].shape[0] // ring.size
        self.step_now = ring.size // 2
        self.came = ()

    def step(self, *deps):
        ring, step = self.ring, self.step_now
        far = ring.size // 2
        kind = 0 if step == far else 1 if step == far - 1 else 2
        ids = after(ring.ids, *deps) if deps else ring.ids
        up, down = ring_sum(kind, self.rows, step, ring.size, ids, self.pairs, self.came)
        self.came = lax.ppermute(up, "dp", ring.up), lax.ppermute(down, "dp", ring.down)
        self.step_now -= 1
        return self.came

    def end(self, splits, *deps):
        ids = after(self.ring.ids, *deps) if deps else self.ring.ids
        return ring_end(self.ring.size, ids, self.pairs, self.came, splits)


def per_device(n_dp, tokens, seq_lengths, ln_gain, ln_bias, w_qkv, w_out, w_up, w_down, cotangent):
    ids = jnp.stack([lax.axis_index("dp"), lax.axis_index("mp")]).astype(jnp.int32)
    ring = Ring(n_dp, ids)
    count, width = tokens.shape
    rows = count // 2
    w_rows, units = w_up.shape
    cols = w_out.shape[0]

    def swap_sides(value):
        return lax.ppermute(value, "mp", [(0, 1), (1, 0)])

    g1 = Gather(ring, stage(after(w_qkv, ids), w_out.T))
    s1 = g1.step()
    cot_got = swap_sides(cotangent)
    stage2, stage3 = stage(w_up), stage(w_down.T)
    s2 = g1.step(stage2, stage3)
    x, a1, gain, bias = prepare(ids, tokens, ln_gain, ln_bias)
    s3 = g1.step(a1)
    cos, sin = rotary_pair(seq_lengths, count)
    cot = cotangent_rows(ids, cotangent, cot_got)
    s4 = g1.step(cos, sin, cot)
    g2 = Gather(ring, after(stage2, *s3))
    s21 = g2.step()
    w1 = g1.end()
    g3 = Gather(ring, after(stage3, w1[0]))
    s31 = g3.step()
    s22 = g2.step(w1[0])
    qkv = qkv_project(a1, *w1, cos, sin)
    probs, outs, ys, mids, zs, backs, mid_backs = [], [], [], [], [], [], []
    lengths = seq_lengths
    for c in range(2):
        p, o, part = attend(c * rows, rows, lengths, qkv, *w1)
        probs.append(p)
        outs.append(o)
        ys.append((part, swap_sides(part)))
        if c == 0:
            s32 = g3.step(part)
            lengths = after(lengths, part, *s22)
    s23 = g2.step(part)
    s33 = g3.step(*s23)
    s24 = g2.step()
    w2 = g2.end(ys[0][1])
    s34 = g3.step(w2[0])
    w3 = g3.end()
    for c in range(2):
        xc = after(x, *[m[0] for m in mids])
        mids.append(up_project(c, xc, *ys[c], gain, bias, *w2))
    for c in range(2):
        part = down_project(after(mids[c][1], *[z[0] for z in zs]), *w3)
        zs.append((part, swap_sides(part)))
    for c in range(2):
        xc = after(x, *[b[0] for b in backs])
        out, dz, du, part, gb = mlp_back(
            c, ids, xc, *ys[c], *zs[c], cot, gain, bias, mids[c][2], w3, w2,
            before=[b[0] for b in backs],
        )
        backs.append((out, dz, du, gb, (part, swap_sides(part))))
    output = backs[1][0]
    dzs, dus = [b[1] for b in backs], [b[2] for b in backs]
    a3s, gs = [m[0] for m in mids], [m[1] for m in mids]

    def mid(c, *deps):
        xc = after(x, *deps)
        return mid_back(c, xc, *ys[c], *backs[c][4], cot, gain, bias, *w1)

    down_other = weight_grad(1, [(dzs, gs)])
    down_got = swap_cores(ring, down_other)
    up_other = weight_grad(1, [([after(a3s[0], down_other), a3s[1]], dus)])
    up_got = swap_cores(ring, up_other)
    mid_backs.append(mid(0, up_other))
    down_mine = weight_grad(0, [([after(dzs[0], mid_backs[0][0]), dzs[1]], gs)])
    up_mine = weight_grad(0, [([after(a3s[0], down_mine), a3s[1]], dus)])
    mlp_ring = Reduce(ring, [(down_mine, down_got), (up_mine, up_got)])
    r1 = mlp_ring.step()
    mid_backs.append(mid(1, up_mine))
    grads = [m[2] for m in mid_backs]
    r2 = mlp_ring.step(*grads)
    g_qkv = attend_back(after(qkv, *r1), probs, outs, grads, cos, sin)
    r3 = mlp_ring.step(g_qkv)
    part_keep, part_give, gb0 = in_back(ids, after(g_qkv, *r2), *w1, x)
    part_got = swap_sides(part_give)
    extra = gain_pack(gb0, [m[3] for m in mid_backs], [b[3] for b in backs])
    dys = [m[1] for m in mid_backs]
    attn_other = weight_grad(1, [([a1], [g_qkv]), (dys, outs)], extra)
    attn_got = swap_cores(ring, attn_other)
    attn_mine = weight_grad(0, [([after(a1, attn_other)], [g_qkv]), (dys, outs)], extra)
    r4 = mlp_ring.step(attn_mine)
    attn_ring = Reduce(ring, [(attn_mine, attn_got)])
    q1 = attn_ring.step()
    q2 = attn_ring.step()
    q3 = attn_ring.step()
    grad_down, grad_up = mlp_ring.end([[(1, units)], [(1, units)]], *q1)
    grad_tokens = tokens_back(
        after(ids, *q1), x, part_keep, part_got, [m[0] for m in mid_backs], gain
    )
    q4 = attn_ring.step()
    grad_qkv, grad_out, gains = attn_ring.end([[(3, cols), (1, cols), (1, LANES)]])
    gains = gain_end(gains, swap_sides(gains))
    return output, grad_tokens, grad_qkv, grad_out.T, grad_up, grad_down.T, gains[0], gains[1]


def layer_norm(values, norm_gain, norm_bias):
    average = jnp.mean(values, axis=-1, keepdims=True)
    centred = values - average
    variance = jnp.mean(centred * centred, axis=-1, keepdims=True)
    return centred * lax.rsqrt(variance + NORM_EPS) * norm_gain + norm_bias


def norm_pull(values, norm_gain, norm_bias, grad_result):
    result, puller = jax.vjp(layer_norm, values, norm_gain, norm_bias)
    return puller(grad_result)


def seq_layout(lengths, block_size):
    block_count = lengths.shape[0]
    block_ids = jnp.arange(block_count, dtype=jnp.int32)
    starts = lengths > 0
    earlier = starts[None, :] & (block_ids[None, :] <= block_ids[:, None])
    owners = jnp.max(jnp.where(earlier, block_ids[None, :], 0), axis=1)
    owner_len = jnp.sum(
        jnp.where(block_ids[None, :] == owners[:, None], lengths[None, :], 0), axis=1
    )
    places = jnp.arange(block_count * block_size, dtype=jnp.int32)
    tok_owner = jnp.repeat(owners, block_size)
    position = places - tok_owner * block_size
    is_valid = position < jnp.repeat(owner_len, block_size)
    allowed = (
        (tok_owner[:, None] == tok_owner[None, :])
        & (places[None, :] <= places[:, None])
        & is_valid[None, :]
    )
    return (position, allowed)


def rotary_tables(position, width):
    frequency = ROPE_BASE ** (-jnp.arange(width // 2, dtype=jnp.float32) * 2.0 / width)
    angles = position.astype(jnp.float32)[:, None] * frequency[None, :]
    return (jnp.cos(angles), jnp.sin(angles))


def rotate(values, cos_table, sin_table):
    half_width = values.shape[-1] // 2
    front_half = values[..., :half_width]
    back_half = values[..., half_width:]
    cos_part = cos_table[:, None, :]
    sin_part = sin_table[:, None, :]
    return jnp.concatenate(
        [
            front_half * cos_part - back_half * sin_part,
            back_half * cos_part + front_half * sin_part,
        ],
        axis=-1,
    )


def attention_scores(queries, keys_rot, allowed, scale):
    raw_scores = (
        jnp.einsum("hqd,hkd->hqk", queries, keys_rot, preferred_element_type=jnp.float32) * scale
    )
    return jnp.where(allowed[None, :, :], raw_scores, MASK_FILL)


def plain_device(tokens, seq_lengths, ln_gain, ln_bias, w_qkv, w_out, w_up, w_down, cotangent):
    full_qkv, full_out, full_up, full_down = (
        lax.all_gather(w_qkv, "dp", axis=1, tiled=True),
        lax.all_gather(w_out, "dp", axis=1, tiled=True),
        lax.all_gather(w_up, "dp", axis=0, tiled=True),
        lax.all_gather(w_down, "dp", axis=1, tiled=True),
    )
    tok_count = tokens.shape[0]
    shard_rows = cotangent.shape[0]
    row_start = lax.axis_index("mp") * shard_rows
    heads_here = full_out.shape[0] // HD
    scale = HD ** (-0.5)
    position, allowed = seq_layout(seq_lengths, BLOCK)
    cos_table, sin_table = rotary_tables(position, HD)

    def to_heads(values):
        return jnp.transpose(values.reshape(tok_count, heads_here, HD), (1, 0, 2))

    def from_heads(values):
        return jnp.transpose(values, (1, 0, 2)).reshape(tok_count, heads_here * HD)

    def rotated(values):
        return rotate(values.reshape(tok_count, heads_here, HD), cos_table, sin_table)

    inputs = tokens.astype(jnp.float32)
    normed_in = layer_norm(inputs, ln_gain[0], ln_bias[0]).astype(jnp.bfloat16)
    projected = jnp.einsum("td,cde->cte", normed_in, full_qkv, preferred_element_type=jnp.float32)
    queries = jnp.transpose(rotated(projected[0]), (1, 0, 2)).astype(jnp.bfloat16)
    keys_rot = jnp.transpose(rotated(projected[1]), (1, 0, 2)).astype(jnp.bfloat16)
    values_h = to_heads(projected[2]).astype(jnp.bfloat16)
    scores = attention_scores(queries, keys_rot, allowed, scale)
    top_score = jnp.max(scores, axis=-1, keepdims=True)
    expo = jnp.exp(scores - top_score)
    row_total = jnp.sum(expo, axis=-1, keepdims=True)
    probs = expo / row_total
    log_total = top_score + jnp.log(row_total)
    attended = jnp.einsum(
        "hqk,hkd->hqd", probs.astype(jnp.bfloat16), values_h, preferred_element_type=jnp.float32
    )
    mixed_heads = from_heads(attended).astype(jnp.bfloat16)
    attn_part = jnp.dot(mixed_heads, full_out, preferred_element_type=jnp.float32)
    attn_sum = lax.psum_scatter(
        attn_part.astype(jnp.bfloat16), "mp", scatter_dimension=0, tiled=True
    ).astype(jnp.float32)
    resid_in = lax.dynamic_slice_in_dim(inputs, row_start, shard_rows, 0)
    hidden_state = resid_in + layer_norm(attn_sum, ln_gain[1], ln_bias[1])
    normed_mid = layer_norm(hidden_state, ln_gain[2], ln_bias[2]).astype(jnp.bfloat16)
    mlp_input = lax.all_gather(normed_mid, "mp", axis=0, tiled=True)
    pre_act = jnp.dot(mlp_input, full_up, preferred_element_type=jnp.float32)
    act_low = jax.nn.gelu(pre_act, approximate=True).astype(jnp.bfloat16)
    mlp_part = jnp.dot(act_low, full_down, preferred_element_type=jnp.float32)
    mlp_sum = lax.psum_scatter(
        mlp_part.astype(jnp.bfloat16), "mp", scatter_dimension=0, tiled=True
    ).astype(jnp.float32)
    output = (hidden_state + layer_norm(mlp_sum, ln_gain[3], ln_bias[3])).astype(jnp.bfloat16)
    grad_result = cotangent.astype(jnp.float32)
    grad_mlp_sum, grad_gain3, grad_bias3 = norm_pull(mlp_sum, ln_gain[3], ln_bias[3], grad_result)
    grad_mlp_rows = lax.all_gather(grad_mlp_sum.astype(jnp.bfloat16), "mp", axis=0, tiled=True)
    grad_down = jnp.einsum("tf,te->fe", act_low, grad_mlp_rows, preferred_element_type=jnp.float32)
    grad_act = jnp.einsum("te,fe->tf", grad_mlp_rows, full_down, preferred_element_type=jnp.float32)
    gelu_puller = jax.vjp(lambda values: jax.nn.gelu(values, approximate=True), pre_act)[1]
    grad_pre = gelu_puller(grad_act)[0].astype(jnp.bfloat16)
    grad_up = jnp.einsum("td,tf->df", mlp_input, grad_pre, preferred_element_type=jnp.float32)
    grad_mid_part = jnp.einsum("tf,df->td", grad_pre, full_up, preferred_element_type=jnp.float32)
    grad_mid = lax.psum_scatter(
        grad_mid_part.astype(jnp.bfloat16), "mp", scatter_dimension=0, tiled=True
    ).astype(jnp.float32)
    grad_hidden_norm, grad_gain2, grad_bias2 = norm_pull(
        hidden_state, ln_gain[2], ln_bias[2], grad_mid
    )
    grad_hidden = grad_result + grad_hidden_norm
    grad_attn_sum, grad_gain1, grad_bias1 = norm_pull(attn_sum, ln_gain[1], ln_bias[1], grad_hidden)
    grad_attn_rows = lax.all_gather(grad_attn_sum.astype(jnp.bfloat16), "mp", axis=0, tiled=True)
    grad_outproj = jnp.einsum(
        "tc,te->ce", mixed_heads, grad_attn_rows, preferred_element_type=jnp.float32
    )
    grad_mixed = jnp.einsum(
        "te,ce->tc", grad_attn_rows, full_out, preferred_element_type=jnp.float32
    ).astype(jnp.bfloat16)
    grad_heads = to_heads(grad_mixed)
    again_scores = attention_scores(queries, keys_rot, allowed, scale)
    again_probs = jnp.exp(again_scores - log_total)
    grad_probs = jnp.einsum(
        "hqd,hkd->hqk", grad_heads, values_h, preferred_element_type=jnp.float32
    )
    grad_values = jnp.einsum(
        "hqk,hqd->hkd",
        again_probs.astype(jnp.bfloat16),
        grad_heads,
        preferred_element_type=jnp.float32,
    )
    row_dot = jnp.sum(again_probs * grad_probs, axis=-1, keepdims=True)
    grad_scores = (again_probs * (grad_probs - row_dot) * scale).astype(jnp.bfloat16)
    grad_q_rot = jnp.einsum(
        "hqk,hkd->hqd", grad_scores, keys_rot, preferred_element_type=jnp.float32
    )
    grad_k_rot = jnp.einsum(
        "hqk,hqd->hkd", grad_scores, queries, preferred_element_type=jnp.float32
    )
    zero_heads = jnp.zeros((tok_count, heads_here, HD), jnp.float32)
    unrotate = jax.vjp(lambda values: rotate(values, cos_table, sin_table), zero_heads)[1]
    grad_query = unrotate(jnp.transpose(grad_q_rot, (1, 0, 2)))[0].reshape(
        tok_count, heads_here * HD
    )
    grad_key = unrotate(jnp.transpose(grad_k_rot, (1, 0, 2)))[0].reshape(tok_count, heads_here * HD)
    grad_value = from_heads(grad_values)
    grad_proj = jnp.stack(
        [
            grad_query.astype(jnp.bfloat16),
            grad_key.astype(jnp.bfloat16),
            grad_value.astype(jnp.bfloat16),
        ]
    )
    grad_qkv = jnp.einsum("td,cte->cde", normed_in, grad_proj, preferred_element_type=jnp.float32)
    grad_in_part = jnp.einsum(
        "cte,cde->td", grad_proj, full_qkv, preferred_element_type=jnp.float32
    )
    grad_in = lax.psum_scatter(
        grad_in_part.astype(jnp.bfloat16), "mp", scatter_dimension=0, tiled=True
    ).astype(jnp.float32)
    grad_norm_in, grad_gain0, grad_bias0 = norm_pull(resid_in, ln_gain[0], ln_bias[0], grad_in)
    grad_tokens = grad_hidden + grad_norm_in
    gain_grads = jnp.stack([grad_gain0, grad_gain1, grad_gain2, grad_gain3])
    bias_grads = jnp.stack([grad_bias0, grad_bias1, grad_bias2, grad_bias3])
    gain_grads, bias_grads = (
        lax.psum(gain_grads.astype(jnp.bfloat16), "mp").astype(jnp.float32),
        lax.psum(bias_grads.astype(jnp.bfloat16), "mp").astype(jnp.float32),
    )
    grad_qkv, grad_outproj, grad_up, grad_down, gain_grads, bias_grads = (
        lax.psum_scatter(
            grad_qkv.astype(jnp.bfloat16), "dp", scatter_dimension=1, tiled=True
        ).astype(jnp.float32),
        lax.psum_scatter(
            grad_outproj.astype(jnp.bfloat16), "dp", scatter_dimension=1, tiled=True
        ).astype(jnp.float32),
        lax.psum_scatter(
            grad_up.astype(jnp.bfloat16), "dp", scatter_dimension=0, tiled=True
        ).astype(jnp.float32),
        lax.psum_scatter(
            grad_down.astype(jnp.bfloat16), "dp", scatter_dimension=1, tiled=True
        ).astype(jnp.float32),
        lax.psum_scatter(
            gain_grads.astype(jnp.bfloat16), "dp", scatter_dimension=1, tiled=True
        ).astype(jnp.float32),
        lax.psum_scatter(
            bias_grads.astype(jnp.bfloat16), "dp", scatter_dimension=1, tiled=True
        ).astype(jnp.float32),
    )
    return (output, grad_tokens, grad_qkv, grad_outproj, grad_up, grad_down, gain_grads, bias_grads)


def solution(mesh):
    placed = (
        P("dp", None),
        P("dp"),
        P(),
        P(),
        P(None, "dp", "mp"),
        P("mp", "dp"),
        P("dp", "mp"),
        P("mp", "dp"),
        P(("dp", "mp"), None),
    )
    n_dp, n_mp = mesh.shape["dp"], mesh.shape["mp"]

    def layer(tokens, *rest):
        if n_mp == 2 and tokens.shape[1] == n_dp * LANES // 2:
            return per_device(n_dp, tokens, *rest)
        return plain_device(tokens, *rest)

    return jax.shard_map(
        layer,
        mesh=mesh,
        in_specs=placed,
        out_specs=(
            P(("dp", "mp"), None),
            P(("dp", "mp"), None),
            P(None, "dp", "mp"),
            P("mp", "dp"),
            P("dp", "mp"),
            P("mp", "dp"),
            P(None, "dp"),
            P(None, "dp"),
        ),
        check_vma=False,
    )
```

```python
import functools

import jax
import jax.numpy as jnp
from jax import lax
from jax.experimental import pallas as pl
from jax.experimental.pallas import tpu as pltpu
from jax.sharding import PartitionSpec as P

HD = 64
BLOCK = 128
LANES = 128
NORM_EPS = 1e-05
ROPE_BASE = 10000.0
MASK_FILL = -1e30
F32 = jnp.float32
BF16 = jnp.bfloat16
VMEM_LIMIT = 6 * 1024 * 1024
STEP = 128
NN = (((1,), (0,)), ((), ()))
NT = (((1,), (1,)), ((), ()))
TN = (((0,), (0,)), ((), ()))


def mm(left, right, dims):
    return lax.dot_general(left, right, dims, preferred_element_type=F32)


def sds(shape, dtype):
    return jax.ShapeDtypeStruct(shape, dtype)


def whole():
    return pl.BlockSpec(memory_space=pltpu.VMEM)


def smem():
    return pl.BlockSpec(memory_space=pltpu.SMEM)


def anywhere():
    return pl.BlockSpec(memory_space=pl.ANY)


TIMES = {
    "prepare": 3.3, "cotangent_rows": 1.5, "qkv_project": 2.0, "attend0": 2.5, "attend1": 4.4,
    "up_project": 4.3, "down_project": 1.3, "mlp_back": 5.4, "weight_grad": 1.3, "mid_back": 3.3,
    "attend_back": 5.0, "in_back": 3.6, "gain_pack": 0.4, "tokens_back": 3.9, "stage": 0.5,
    "assemble": 1.2, "ring_sum": 1.3, "ring_end": 2.0, "rotary": 2.0, "split": 0.4,
}
TIME_SHARE = 1.0


def cost_of(name):
    return pl.CostEstimate(
        flops=0, bytes_accessed=int(TIMES[name] * TIME_SHARE * 3.69e6), transcendentals=0
    )


def kernel_call(body, name, out_shape, args, smems=1, flops=0, nbytes=0, scratch=(), **extra):
    many = isinstance(out_shape, (list, tuple))
    return pl.pallas_call(
        body,
        in_specs=[smem()] * smems + [whole()] * (len(args) - smems),
        out_specs=[whole()] * len(out_shape) if many else whole(),
        out_shape=out_shape,
        scratch_shapes=list(scratch),
        compiler_params=pltpu.CompilerParams(vmem_limit_bytes=VMEM_LIMIT),
        cost_estimate=cost_of(name),
        name=name,
        **extra,
    )(*args)


def after(value, *others):
    return lax.optimization_barrier((value,) + others)[0]


def chip_of(place, size):
    if isinstance(place, int):
        return 2 * place if place < size // 2 else 2 * (size - 1 - place) + 1
    return jnp.where(place < size // 2, 2 * place, 2 * (size - 1 - place) + 1)


def chip_near(ids_ref, step, size):
    chip = ids_ref[0] // 2
    here = jnp.where(chip % 2 == 0, chip // 2, size - 1 - chip // 2)
    return chip_of((here + step + size) % size, size)


def ring_order(size):
    order = [size // 2]
    for step in range(size // 2 - 1, 0, -1):
        order += [step, -step]
    return order + [0]


def ring_index(ids_ref, chip, size):
    own = ids_ref[0] // 2
    here = jnp.where(own % 2 == 0, own // 2, size - 1 - own // 2)
    place = chip // 2 if chip % 2 == 0 else size - 1 - chip // 2
    step = (place - here + size) % size
    index = jnp.where(step >= size // 2, 2 * (step - size // 2), size - 1 - 2 * step)
    return jnp.where(step == 0, size - 1, index)


def split_cores(values, core):
    half = values.shape[1] // 2
    lane = lax.broadcasted_iota(jnp.int32, (values.shape[0], LANES), 1)
    low = lane < LANES // 2
    own, other = [], []
    for start in range(0, 2 * half, 2 * LANES):
        a = values[:, start : start + LANES]
        b = values[:, start + LANES : start + 2 * LANES]
        first = jnp.where(low, a, pltpu.roll(b, LANES // 2, 1))
        second = jnp.where(low, pltpu.roll(a, LANES // 2, 1), b)
        own.append(jnp.where(core == 0, first, second))
        other.append(jnp.where(core == 0, second, first))
    return jnp.concatenate(own + other, axis=1)


def join_cores(values, core):
    half = values.shape[1] // 2
    lane = lax.broadcasted_iota(jnp.int32, (values.shape[0], LANES), 1)
    low = lane < LANES // 2
    out = []
    for start in range(0, half, LANES):
        own = values[:, start : start + LANES]
        other = values[:, half + start : half + start + LANES]
        first = jnp.where(core == 0, own, other)
        second = jnp.where(core == 0, other, own)
        out.append(jnp.where(low, first, pltpu.roll(second, LANES // 2, 1)))
        out.append(jnp.where(low, pltpu.roll(first, LANES // 2, 1), second))
    return jnp.concatenate(out, axis=1)


def norm_stats(values):
    centred = values - jnp.mean(values, axis=-1, keepdims=True)
    rstd = lax.rsqrt(jnp.mean(centred * centred, axis=-1, keepdims=True) + NORM_EPS)
    return centred * rstd, rstd


def norm_back(normed, rstd, scaled_grad):
    first = jnp.mean(scaled_grad, axis=-1, keepdims=True)
    second = jnp.mean(scaled_grad * normed, axis=-1, keepdims=True)
    return (scaled_grad - first - normed * second) * rstd


def fold_rows(values):
    return jnp.sum(values.reshape(-1, 8, values.shape[-1]), axis=0)


def row_steps(rows, body):
    @pl.loop(0, rows // STEP)
    def _(i):
        body(pl.ds(pl.multiple_of(i * STEP, STEP), STEP))


def prepare_kernel(ids_ref, x_ref, gain_ref, bias_ref, xp_ref, a1_ref, gp_ref, bp_ref):
    core = ids_ref[0] % 2
    gp_ref[...] = split_cores(gain_ref[...], core)
    bp_ref[...] = split_cores(bias_ref[...], core)

    def body(at):
        x = split_cores(x_ref[at, :].astype(F32), core)
        xp_ref[at, :] = x.astype(BF16)
        normed, _ = norm_stats(x)
        a1_ref[at, :] = (normed * gp_ref[0:1, :] + bp_ref[0:1, :]).astype(BF16)

    row_steps(x_ref.shape[0], body)


def prepare(ids, x, gain, bias):
    return kernel_call(
        prepare_kernel,
        "prepare",
        [sds(x.shape, BF16), sds(x.shape, BF16), sds(gain.shape, F32), sds(bias.shape, F32)],
        (ids, x, gain, bias),
        nbytes=6 * x.size,
    )


def cotangent_kernel(ids_ref, own_ref, got_ref, out_ref):
    core, side = ids_ref[0] % 2, ids_ref[1]
    rows = own_ref.shape[0]
    for ref, base in ((own_ref, side * rows), (got_ref, (1 - side) * rows)):

        @pl.loop(0, rows // STEP)
        def _(i, ref=ref, base=base):
            at = pl.ds(pl.multiple_of(i * STEP, STEP), STEP)
            to = pl.ds(pl.multiple_of(base + i * STEP, STEP), STEP)
            out_ref[to, :] = split_cores(ref[at, :].astype(F32), core).astype(BF16)


def cotangent_rows(ids, own, got):
    rows, width = own.shape
    return kernel_call(
        cotangent_kernel, "cotangent_rows", sds((2 * rows, width), BF16), (ids, own, got),
        nbytes=8 * own.size,
    )


def partner(values):
    lane = lax.broadcasted_iota(jnp.int32, values.shape, 1)
    ahead = pltpu.roll(values, LANES - HD // 2, 1)
    behind = pltpu.roll(values, HD // 2, 1)
    return jnp.where(lax.rem(lane, HD) < HD // 2, ahead, behind)


def qkv_kernel(a_ref, wo_ref, wg_ref, cos_ref, sin_ref, out_ref):
    half = wo_ref.shape[0]
    cols = wo_ref.shape[1] // 4
    rows = 2 * BLOCK

    @pl.loop(0, a_ref.shape[0] // rows)
    def _(i):
        at = pl.ds(pl.multiple_of(i * rows, rows), rows)
        cos, sin = cos_ref[at, :], sin_ref[at, :]
        for which in range(3):
            to = slice(which * cols, (which + 1) * cols)
            proj = mm(a_ref[at, :half], wo_ref[:, to], NN) + mm(a_ref[at, half:], wg_ref[:, to], NN)
            for start in range(0, cols, LANES):
                part = proj[:, start : start + LANES]
                if which < 2:
                    part = part * cos + partner(part) * sin
                if which == 0:
                    part = part.astype(BF16).astype(F32) * HD ** (-0.5)
                out_ref[at, which * cols + start : which * cols + start + LANES] = part.astype(BF16)


def qkv_project(a1, wo, wg, cos, sin):
    count, width = a1.shape
    three = wo.shape[1] // 4 * 3
    return kernel_call(
        qkv_kernel, "qkv_project", sds((count, three), BF16), (a1, wo, wg, cos, sin), smems=0,
        flops=2 * count * width * three, nbytes=2 * width * three,
    )


def span_of(len_ref, block):
    start, size = jnp.int32(0), jnp.int32(0)
    for b in range(block + 1):
        here = len_ref[b]
        start = jnp.where(here > 0, b * BLOCK, start)
        size = jnp.where(here > 0, here, size)
    return start, start + size


def rotary_kernel(len_ref, cos_ref, sin_ref):
    lane = lax.broadcasted_iota(jnp.int32, (BLOCK, LANES), 1)
    row = lax.broadcasted_iota(jnp.int32, (BLOCK, LANES), 0)
    index = (lane % (HD // 2)).astype(F32)
    frequency = jnp.exp(index * (-2.0 / HD * 9.210340371976184))
    back = lane % HD >= HD // 2
    for b in range(cos_ref.shape[0] // BLOCK):
        start, _ = span_of(len_ref, b)
        angle = (row + (b * BLOCK - start)).astype(F32) * frequency
        sin = jnp.sin(angle)
        cos_ref[b * BLOCK : (b + 1) * BLOCK, :] = jnp.cos(angle)
        sin_ref[b * BLOCK : (b + 1) * BLOCK, :] = jnp.where(back, sin, -sin)


def rotary_pair(lengths, count):
    out = sds((count, LANES), F32)
    return kernel_call(rotary_kernel, "rotary", [out, out], (lengths,))


def head_lanes(rows, first):
    lane = lax.broadcasted_iota(jnp.int32, (rows, LANES), 1)
    return (lane < HD) == first


def attend_kernel(row0, len_ref, q_ref, wo_ref, wg_ref, p_ref, o_ref, part_ref):
    rows, cols = o_ref.shape
    ext = p_ref.shape[2]
    half = wo_ref.shape[0]
    key = lax.broadcasted_iota(jnp.int32, (BLOCK, ext), 1)
    query = lax.broadcasted_iota(jnp.int32, (BLOCK, ext), 0)
    masks = []
    for b in range(rows // BLOCK):
        lo, hi = span_of(len_ref, row0 // BLOCK + b)
        seen = (key >= lo) & (key < hi) & (key <= query + (row0 + b * BLOCK))
        masks.append(jnp.where(seen, 0.0, MASK_FILL))
    mask = jnp.concatenate(masks, axis=0)
    head = 0
    for start in range(0, cols, LANES):
        q = q_ref[row0 : row0 + rows, start : start + LANES]
        k = q_ref[0:ext, cols + start : cols + start + LANES]
        v = q_ref[0:ext, 2 * cols + start : 2 * cols + start + LANES]
        outs = []
        for first in (True, False):
            mine = head_lanes(rows, first)
            s = mm(jnp.where(mine, q, jnp.zeros_like(q)), k, NT) + mask
            e = jnp.exp(s - jnp.max(s, axis=-1, keepdims=True))
            p = (e * (1.0 / jnp.sum(e, axis=-1, keepdims=True))).astype(BF16)
            p_ref[head] = p
            head += 1
            outs.append(mm(p, v, NN))
        o_ref[:, start : start + LANES] = jnp.where(
            head_lanes(rows, True), outs[0], outs[1]
        ).astype(BF16)
    part_ref[:, :half] = mm(o_ref[...], wo_ref[:, 3 * cols :], NT).astype(BF16)
    part_ref[:, half:] = mm(o_ref[...], wg_ref[:, 3 * cols :], NT).astype(BF16)


def attend(row0, rows, lengths, qkv, wo, wg):
    ext = row0 + rows
    cols = qkv.shape[1] // 3
    heads = cols // HD
    width = 2 * wo.shape[0]
    return kernel_call(
        functools.partial(attend_kernel, row0),
        "attend0" if row0 == 0 else "attend1",
        [sds((heads, rows, ext), BF16), sds((rows, cols), BF16), sds((rows, width), BF16)],
        (lengths, qkv, wo, wg),
        flops=4 * heads * rows * ext * HD + 2 * rows * width * cols,
    )


def hidden_of(x, ya, yb, gain_ref, bias_ref):
    n1, r1 = norm_stats(ya.astype(F32) + yb.astype(F32))
    return x.astype(F32) + n1 * gain_ref[1:2, :] + bias_ref[1:2, :], n1, r1


def chunk_rows(chunk, rows, at):
    return pl.ds(pl.multiple_of(chunk * rows + at.start, STEP), STEP)


UNITS = 512


def up_kernel(chunk, x_ref, ya_ref, yb_ref, gain_ref, bias_ref, wo_ref, wg_ref, a3_ref, g_ref, gp_ref):
    rows = ya_ref.shape[0]
    half = wo_ref.shape[0]

    def body(at):
        x = x_ref[chunk_rows(chunk, rows, at), :]
        h, _, _ = hidden_of(x, ya_ref[at, :], yb_ref[at, :], gain_ref, bias_ref)
        n2, _ = norm_stats(h)
        a3_ref[at, :] = (n2 * gain_ref[2:3, :] + bias_ref[2:3, :]).astype(BF16)

    row_steps(rows, body)

    @pl.loop(0, wo_ref.shape[1] // UNITS)
    def _(i):
        to = pl.ds(pl.multiple_of(i * UNITS, UNITS), UNITS)
        u = mm(a3_ref[:, :half], wo_ref[:, to], NN) + mm(a3_ref[:, half:], wg_ref[:, to], NN)
        k0 = 0.7978845608028654
        k1 = 0.044715
        sq = u * u
        th = jnp.tanh(u * (k0 + (k0 * k1) * sq))
        plus = 0.5 + 0.5 * th
        g_ref[:, to] = (u * plus).astype(BF16)
        slope = plus + (u * (k0 + (3.0 * k0 * k1) * sq)) * (0.5 - (0.5 * th) * th)
        gp_ref[:, to] = slope.astype(BF16)


def up_project(chunk, x, ya, yb, gain, bias, wo, wg):
    rows, width = ya.shape
    units = wo.shape[1]
    return kernel_call(
        functools.partial(up_kernel, chunk),
        "up_project",
        [sds((rows, width), BF16), sds((rows, units), BF16), sds((rows, units), BF16)],
        (x, ya, yb, gain, bias, wo, wg),
        smems=0,
        flops=2 * rows * width * units,
    )


def down_kernel(g_ref, wo_ref, wg_ref, z_ref):
    half = wo_ref.shape[0]
    z_ref[:, :half] = mm(g_ref[...], wo_ref[...], NT).astype(BF16)
    z_ref[:, half:] = mm(g_ref[...], wg_ref[...], NT).astype(BF16)


def down_project(g, wo, wg):
    rows, units = g.shape
    width = 2 * wo.shape[0]
    return kernel_call(
        down_kernel, "down_project", sds((rows, width), BF16), (g, wo, wg), smems=0,
        flops=2 * rows * width * units,
    )


def mlp_back_kernel(
    chunk, ids_ref, x_ref, ya_ref, yb_ref, za_ref, zb_ref, cot_ref, gain_ref, bias_ref, gp_ref,
    w3o, w3g, w2o, w2g, *refs
):
    out_ref, dz_ref, du_ref, part_ref, gb_ref = refs[-5:]
    rows = ya_ref.shape[0]
    half = w3o.shape[0]
    core, side = ids_ref[0] % 2, ids_ref[1]
    gb_ref[...] = jnp.zeros_like(gb_ref)

    def body(at):
        far = chunk_rows(chunk, rows, at)
        h, _, _ = hidden_of(x_ref[far, :], ya_ref[at, :], yb_ref[at, :], gain_ref, bias_ref)
        n3, r3 = norm_stats(za_ref[at, :].astype(F32) + zb_ref[at, :].astype(F32))
        cot = cot_ref[far, :].astype(F32)
        gain = gain_ref[3:4, :]
        out = join_cores(h + (n3 * gain + bias_ref[3:4, :]), core)
        if chunk > 0:
            out = jnp.where(side == chunk, out, refs[0][at, :].astype(F32))
        out_ref[at, :] = out.astype(BF16)
        dz_ref[at, :] = norm_back(n3, r3, cot * gain).astype(BF16)
        gb_ref[0] += fold_rows(cot * n3)
        gb_ref[1] += fold_rows(cot)

    row_steps(rows, body)

    @pl.loop(0, w3o.shape[1] // UNITS)
    def _(i):
        to = pl.ds(pl.multiple_of(i * UNITS, UNITS), UNITS)
        dg = mm(dz_ref[:, :half], w3o[:, to], NN) + mm(dz_ref[:, half:], w3g[:, to], NN)
        du_ref[:, to] = (dg * gp_ref[:, to].astype(F32)).astype(BF16)

    part_ref[:, :half] = mm(du_ref[...], w2o[...], NT).astype(BF16)
    part_ref[:, half:] = mm(du_ref[...], w2g[...], NT).astype(BF16)


def mlp_back(chunk, ids, x, ya, yb, za, zb, cot, gain, bias, gp, w3, w2, before=()):
    rows, width = ya.shape
    units = w3[0].shape[1]
    return kernel_call(
        functools.partial(mlp_back_kernel, chunk),
        "mlp_back",
        [
            sds((rows, width), BF16),
            sds((rows, width), BF16),
            sds((rows, units), BF16),
            sds((rows, width), BF16),
            sds((2, 8, width), F32),
        ],
        (ids, x, ya, yb, za, zb, cot, gain, bias, gp, *w3, *w2, *before),
        flops=4 * rows * width * units,
    )


def weight_grad_kernel(which, sizes, size, ids_ref, *refs):
    far_ref, near_ref, ring_sc = refs[-3:]
    half, count = ring_sc.shape
    block = half // size
    start = 0
    for lefts, rights, cols in sizes:
        rows = 0
        for ref in refs[lefts[0] : lefts[1]]:
            part = ref[:, which * half : (which + 1) * half].T
            for chip in range(size):
                at = pl.multiple_of(ring_index(ids_ref, chip, size) * block, block)
                ring_sc[pl.ds(at, block), rows : rows + part.shape[1]] = part[
                    chip * block : (chip + 1) * block
                ]
            rows += part.shape[1]
        for c in range(0, cols, UNITS):
            total, rows = None, 0
            for ref in refs[rights[0] : rights[1]]:
                n = ref.shape[0]
                term = mm(ring_sc[:, rows : rows + n], ref[:, c : c + UNITS], NN)
                total = term if total is None else total + term
                rows += n
            total = total.astype(BF16)
            far_ref[:, start + c : start + c + UNITS] = total[:block]
            near_ref[:, start + c : start + c + UNITS] = total[block:]
        start += cols


def weight_grad(ids, which, size, products):
    args, sizes, total = [], [], 0
    for lefts, rights in products:
        cols = rights[0].shape[1]
        n = len(args)
        sizes.append(((n, n + len(lefts)), (n + len(lefts), n + len(lefts) + len(rights)), cols))
        args += list(lefts) + list(rights)
        total += cols
    half = args[0].shape[1] // 2
    count = sum(a.shape[0] for a in products[0][0])
    block = half // size
    return kernel_call(
        functools.partial(weight_grad_kernel, which, sizes, size),
        "weight_grad",
        [sds((block, total), BF16), sds((half - block, total), BF16)],
        (ids, *args),
        scratch=[pltpu.VMEM((half, count), BF16)],
    )


def mid_back_kernel(
    chunk, x_ref, ya_ref, yb_ref, ea_ref, eb_ref, cot_ref, gain_ref, bias_ref, wo_ref, wg_ref,
    dh_ref, dy_ref, do_ref, gb_ref,
):
    rows, cols = do_ref.shape
    half = wo_ref.shape[0]
    gb_ref[...] = jnp.zeros_like(gb_ref)

    def body(at):
        far = chunk_rows(chunk, rows, at)
        h, n1, r1 = hidden_of(x_ref[far, :], ya_ref[at, :], yb_ref[at, :], gain_ref, bias_ref)
        n2, r2 = norm_stats(h)
        e = ea_ref[at, :].astype(F32) + eb_ref[at, :].astype(F32)
        dh = cot_ref[far, :].astype(F32) + norm_back(n2, r2, e * gain_ref[2:3, :])
        dh_ref[at, :] = dh
        dy_ref[at, :] = norm_back(n1, r1, dh * gain_ref[1:2, :]).astype(BF16)
        gb_ref[0] += fold_rows(e * n2)
        gb_ref[1] += fold_rows(e)
        gb_ref[2] += fold_rows(dh * n1)
        gb_ref[3] += fold_rows(dh)

    row_steps(rows, body)
    do = mm(dy_ref[:, :half], wo_ref[:, 3 * cols :], NN)
    do_ref[...] = (do + mm(dy_ref[:, half:], wg_ref[:, 3 * cols :], NN)).astype(BF16)


def mid_back(chunk, x, ya, yb, ea, eb, cot, gain, bias, wo, wg):
    rows, width = ya.shape
    cols = wo.shape[1] // 4
    return kernel_call(
        functools.partial(mid_back_kernel, chunk),
        "mid_back",
        [
            sds((rows, width), F32),
            sds((rows, width), BF16),
            sds((rows, cols), BF16),
            sds((4, 8, width), F32),
        ],
        (x, ya, yb, ea, eb, cot, gain, bias, wo, wg),
        smems=0,
        flops=2 * rows * width * cols,
    )


def attend_back_kernel(q_ref, p0_ref, p1_ref, o0, o1, d0, d1, cos_ref, sin_ref, g_ref):
    rows, cols = o0.shape
    cos, sin = cos_ref[...], sin_ref[...]
    head = 0
    for start in range(0, cols, LANES):
        at = slice(start, start + LANES)
        q = q_ref[:, at]
        k = q_ref[:, cols + start : cols + start + LANES]
        v = q_ref[:, 2 * cols + start : 2 * cols + start + LANES]
        do = (d0[:, at], d1[:, at])
        prod = [a.astype(F32) * b[:, at].astype(F32) for a, b in zip(do, (o0, o1))]
        dq, dk, dv = [], [], []
        for first in (True, False):
            mine = head_lanes(rows, first)
            dqs = []
            for c, p_ref in enumerate((p0_ref, p1_ref)):
                ext = p_ref.shape[2]
                p = p_ref[head]
                dp = mm(jnp.where(mine, do[c], jnp.zeros_like(do[c])), v[:ext], NT)
                dot = jnp.sum(jnp.where(mine, prod[c], 0.0), axis=-1, keepdims=True)
                ds = (p.astype(F32) * (dp - dot)).astype(BF16)
                dqs.append(mm(ds, k[:ext], NN))
                dkc = mm(ds, q[c * rows : (c + 1) * rows], TN)
                dvc = mm(p, do[c], TN)
                if c == 0:
                    dk0, dv0 = dkc, dvc
            dk.append(jnp.concatenate([dk0 + dkc[:rows], dkc[rows:]], axis=0))
            dv.append(jnp.concatenate([dv0 + dvc[:rows], dvc[rows:]], axis=0))
            dq.append(jnp.concatenate(dqs, axis=0))
            head += 1
        low = head_lanes(2 * rows, True)
        gq = jnp.where(low, dq[0], dq[1]) * HD ** (-0.5)
        gk = jnp.where(low, dk[0], dk[1])
        gv = jnp.where(low, dv[0], dv[1])
        g_ref[:, at] = (gq * cos - partner(gq) * sin).astype(BF16)
        g_ref[:, cols + start : cols + start + LANES] = (gk * cos - partner(gk) * sin).astype(BF16)
        g_ref[:, 2 * cols + start : 2 * cols + start + LANES] = gv.astype(BF16)


def attend_back(qkv, probs, outs, grads, cos, sin):
    count, three = qkv.shape
    heads = probs[0].shape[0]
    return kernel_call(
        attend_back_kernel,
        "attend_back",
        sds((count, three), BF16),
        (qkv, *probs, *outs, *grads, cos, sin),
        smems=0,
        flops=10 * heads * count * count * HD,
    )


def in_back_kernel(ids_ref, g_ref, wo_ref, wg_ref, x_ref, keep_ref, give_ref, gb_ref):
    three = g_ref.shape[1]
    half = wo_ref.shape[0]
    rows = keep_ref.shape[0]
    gb_ref[...] = jnp.zeros_like(gb_ref)
    for turn, out_ref in enumerate((give_ref, keep_ref)):
        base = (1 - ids_ref[1] if turn == 0 else ids_ref[1]) * rows
        g = g_ref[pl.ds(pl.multiple_of(base, rows), rows), :]
        out_ref[:, :half] = mm(g, wo_ref[:, :three], NT).astype(BF16)
        out_ref[:, half:] = mm(g, wg_ref[:, :three], NT).astype(BF16)

        @pl.loop(0, rows // STEP)
        def _(i, base=base, out_ref=out_ref):
            e = out_ref[pl.ds(pl.multiple_of(i * STEP, STEP), STEP), :].astype(F32)
            far = pl.ds(pl.multiple_of(base + i * STEP, STEP), STEP)
            n0, _ = norm_stats(x_ref[far, :].astype(F32))
            gb_ref[0] += fold_rows(e * n0)
            gb_ref[1] += fold_rows(e)


def in_back(ids, g, wo, wg, x):
    count, three = g.shape
    width = x.shape[1]
    part = sds((count // 2, width), BF16)
    return kernel_call(
        in_back_kernel, "in_back", [part, part, sds((2, 8, width), F32)], (ids, g, wo, wg, x),
    )


def gain_sum_kernel(gb0_ref, g12a, g12b, g3a, g3b, mine_ref, other_ref):
    share = 0.5
    rows = []
    for kind in range(2):
        rows += [
            gb0_ref[kind],
            share * (g12a[2 + kind] + g12b[2 + kind]),
            share * (g12a[kind] + g12b[kind]),
            share * (g3a[kind] + g3b[kind]),
        ]
    half = mine_ref.shape[1]
    for i, row in enumerate(rows):
        row = jnp.sum(row, axis=0, keepdims=True)
        mine_ref[i : i + 1, :] = row[:, :half]
        other_ref[i : i + 1, :] = row[:, half:]


def gain_sum(gb0, g12, g3):
    out = sds((8, gb0.shape[-1] // 2), F32)
    return kernel_call(gain_sum_kernel, "gain_pack", [out, out], (gb0, *g12, *g3), smems=0)


def gain_pack_kernel(size, ids_ref, *refs):
    out_ref, columns = refs[-2:]
    half = out_ref.shape[0]
    block = half // size
    total = refs[0][...] + refs[1][...] + refs[2][...] + refs[3][...]
    filler = jnp.zeros((LANES - total.shape[0], half), F32)
    columns[...] = jnp.concatenate([total, filler], axis=0).T
    for i, step in enumerate(ring_order(size)):
        at = pl.multiple_of(chip_near(ids_ref, step, size) * block, block)
        out_ref[i * block : (i + 1) * block, :] = columns[pl.ds(at, block), :].astype(BF16)


def gain_pack(ids, size, parts):
    half = parts[0].shape[1]
    return kernel_call(
        functools.partial(gain_pack_kernel, size), "gain_pack", sds((half, LANES), BF16),
        (ids, *parts), scratch=[pltpu.VMEM((half, LANES), F32)],
    )


def tokens_back_kernel(ids_ref, x_ref, keep_ref, got_ref, dh0_ref, dh1_ref, gain_ref, out_ref):
    core, side = ids_ref[0] % 2, ids_ref[1]
    rows = got_ref.shape[0]

    def body(at):
        far = pl.ds(pl.multiple_of(side * rows + at.start, STEP), STEP)
        e = keep_ref[at, :].astype(F32) + got_ref[at, :].astype(F32)
        n0, r0 = norm_stats(x_ref[far, :].astype(F32))
        dh = jnp.where(side == 0, dh0_ref[at, :], dh1_ref[at, :])
        out_ref[at, :] = join_cores(dh + norm_back(n0, r0, e * gain_ref[0:1, :]), core)

    row_steps(rows, body)


def tokens_back(ids, x, keep, got, dhs, gain):
    return kernel_call(
        tokens_back_kernel, "tokens_back", sds(got.shape, F32), (ids, x, keep, got, *dhs, gain),
    )


def split_kernel(up_ref, down_ref, up_out, down_out):
    half = up_out.shape[0]
    up_out[...] = up_ref[:half, :]
    down_out[...] = down_ref[half:, :]


def split(up, down):
    out = sds((up.shape[0] // 2, up.shape[1]), BF16)
    return kernel_call(split_kernel, "split", [out, out], (up, down), smems=0)


def stage_kernel(*refs):
    ins, out_ref, sem = refs[:-2], refs[-2], refs[-1]
    copies, start = [], 0
    for ref in ins:
        parts = [ref.at[i] for i in range(ref.shape[0])] if len(ref.shape) == 3 else [ref]
        for part in parts:
            cols = part.shape[1]
            dst = out_ref.at[:, pl.ds(start, cols)]
            copies.append(pltpu.make_async_copy(part, dst, sem.at[len(copies)]))
            start += cols
    for copy in copies:
        copy.start()
    for copy in copies:
        copy.wait()


def stage(*arrays):
    rows = arrays[0].shape[-2]
    cols = sum(a.size // rows for a in arrays)
    return pl.pallas_call(
        stage_kernel,
        in_specs=[pl.BlockSpec(memory_space=pltpu.HBM)] * len(arrays),
        out_specs=whole(),
        out_shape=sds((rows, cols), BF16),
        scratch_shapes=[pltpu.SemaphoreType.DMA((4 * len(arrays),))],
        compiler_params=pltpu.CompilerParams(vmem_limit_bytes=VMEM_LIMIT),
        cost_estimate=cost_of("stage"),
        name="stage",
    )(*arrays)


def assemble_kernel(places, size, ids_ref, *refs):
    ins, out, sem = refs[:-2], refs[-2], refs[-1]
    rows, unit = ins[0].shape[0], ins[-1].shape[0]
    copies = []
    for i, (src, (step, shift)) in enumerate(zip(ins, places)):
        at = pl.multiple_of(chip_near(ids_ref, step, size) * rows + shift, unit)
        copies.append(pltpu.make_async_copy(src, out.at[pl.ds(at, src.shape[0])], sem.at[i]))
    for copy in copies:
        copy.start()
    for copy in copies:
        copy.wait()


def assemble(ids, places, pieces, size):
    rows, width = pieces[0].shape
    return pl.pallas_call(
        functools.partial(assemble_kernel, places, size),
        in_specs=[smem()] + [anywhere()] * len(pieces),
        out_specs=whole(),
        out_shape=sds((rows * size, width), BF16),
        scratch_shapes=[pltpu.SemaphoreType.DMA((len(pieces),))],
        compiler_params=pltpu.CompilerParams(vmem_limit_bytes=VMEM_LIMIT),
        cost_estimate=cost_of("assemble"),
        name="assemble",
    )(ids, *pieces)


def term_rows(groups, block, index, to):
    total = None
    for refs in groups:
        if len(refs) == 2:
            ref, first = (refs[0], 0) if index == 0 else (refs[1], (index - 1) * block)
        else:
            ref, first = refs[0], index * block
        part = ref[first : first + block, to].astype(F32)
        total = part if total is None else total + part
    return total


def unflatten(refs, layout):
    groups, n = [], 0
    for terms in layout:
        group = []
        for count in terms:
            group.append(refs[n : n + count])
            n += count
        groups.append(group)
    return groups, refs[n:]


def ring_sum_kernel(layout, block, index, *refs):
    groups, refs = unflatten(refs, layout)
    outs, came = refs[-2:], refs[:-2]
    half = block // 2
    start = 0
    for group in groups:
        cols = group[0][0].shape[1]
        for c in range(0, cols, UNITS):
            n = min(UNITS, cols - c)
            own, to = slice(c, c + n), slice(start + c, start + c + n)
            if index == 0:
                total = sum(term[0][0:block, own].astype(F32) for term in group)
                outs[0][:, to] = total[:half].astype(BF16)
                outs[1][:, to] = total[half:].astype(BF16)
                continue
            for way in range(2):
                total = term_rows(group, block, index + way, own)
                part = came[way][:, to].astype(F32)
                if part.shape[0] == block:
                    outs[way][:, to] = (total + part).astype(BF16)
                else:
                    hit = slice(0, half) if way == 0 else slice(half, block)
                    rest = slice(half, block) if way == 0 else slice(0, half)
                    outs[way][hit, to] = (total[hit] + part).astype(BF16)
                    outs[way][rest, to] = total[rest].astype(BF16)
        start += cols


def ring_sum(index, block, groups, came=()):
    layout = [[len(term) for term in group] for group in groups]
    flat = [a for group in groups for term in group for a in term]
    cols = sum(group[0][0].shape[1] for group in groups)
    out = sds((block // 2 if index == 0 else block, cols), BF16)
    return kernel_call(
        functools.partial(ring_sum_kernel, layout, block, index), "ring_sum", [out, out],
        (*flat, *came), smems=0,
    )


def ring_end_kernel(layout, splits, index, *refs):
    groups, refs = unflatten(refs, layout)
    (up, down), outs = refs[:2], refs[2:]
    block = up.shape[0]
    start, o = 0, 0
    for group, sizes in zip(groups, splits):
        here = 0
        for count, cols in sizes:
            for i in range(max(count, 1)):
                to, own = slice(start, start + cols), slice(here, here + cols)
                total = term_rows(group, block, index, own)
                total = total + up[:, to].astype(F32) + down[:, to].astype(F32)
                if count == 0:
                    turned = total.T
                    outs[o][...] = turned[0:4, :]
                    outs[o + 1][...] = turned[4:8, :]
                elif count > 1:
                    outs[o][i] = total
                else:
                    outs[o][...] = total
                start, here = start + cols, here + cols
            o += 2 if count == 0 else 1


def ring_end(size, groups, came, splits):
    layout = [[len(term) for term in group] for group in groups]
    flat = [a for group in groups for term in group for a in term]
    block = came[0].shape[0]
    shapes = []
    for sizes in splits:
        for count, cols in sizes:
            if count == 0:
                shapes += [(4, block)] * 2
            else:
                shapes.append((count, block, cols) if count > 1 else (block, cols))
    return kernel_call(
        functools.partial(ring_end_kernel, layout, splits, size - 1), "ring_end",
        [sds(shape, F32) for shape in shapes], (*flat, *came), smems=0,
    )


class Ring:
    def __init__(self, n_dp, ids):
        self.size = n_dp // 2
        self.ids = ids
        self.up = self.shift(1)
        self.down = self.shift(-1)
        self.cores = [(i, i ^ 1) for i in range(n_dp)]

    def shift(self, by):
        return [
            (2 * chip_of(p, self.size) + c, 2 * chip_of((p + by) % self.size, self.size) + c)
            for p in range(self.size)
            for c in range(2)
        ]


def swap_cores(ring, value):
    return lax.ppermute(value, "dp", ring.cores)


class Gather:
    def __init__(self, ring, piece):
        self.ring = ring
        self.pieces, self.places = [piece], [(0, 0)]
        self.step_now = 0
        self.up = self.down = piece

    def step(self, *deps):
        self.step_now += 1
        ring, step = self.ring, self.step_now
        up, down = self.up, self.down
        if deps:
            up, down = after(up, *deps), after(down, *deps)
        shift = 0
        if step == ring.size // 2:
            shift = up.shape[0] // 2
            up, down = split(up, down)
            self.sent = up, down
        self.up = lax.ppermute(up, "dp", ring.up)
        self.down = lax.ppermute(down, "dp", ring.down)
        self.pieces += [self.up, self.down]
        self.places += [(-step, 0), (step, shift)]
        return self.up, self.down

    def end(self, *deps):
        ids = after(self.ring.ids, *deps) if deps else self.ring.ids
        return assemble(ids, self.places, self.pieces, self.ring.size)


class Reduce:
    def __init__(self, ring, block, groups):
        self.ring, self.block, self.groups = ring, block, groups
        self.index = 0
        self.came = ()

    def step(self, *deps):
        groups = self.groups
        if deps:
            first = groups[0][0]
            groups = [[(after(first[0], *deps), *first[1:]), *groups[0][1:]], *groups[1:]]
        if self.index == 0:
            groups = [[(term[0],) for term in group] for group in groups]
        self.sent = ring_sum(self.index, self.block, groups, self.came)
        up, down = self.sent
        self.came = lax.ppermute(up, "dp", self.ring.up), lax.ppermute(down, "dp", self.ring.down)
        self.index += 2 if self.index else 1
        return self.came

    def end(self, splits, *deps):
        came = self.came
        if deps:
            came = after(came[0], *deps), came[1]
        return ring_end(self.ring.size, self.groups, came, splits)


def per_device(n_dp, tokens, seq_lengths, ln_gain, ln_bias, w_qkv, w_out, w_up, w_down, cotangent):
    ids = jnp.stack([lax.axis_index("dp"), lax.axis_index("mp")]).astype(jnp.int32)
    ring = Ring(n_dp, ids)
    count, width = tokens.shape
    rows = count // 2
    w_rows, units = w_up.shape
    cols = w_out.shape[0]

    def swap_sides(value):
        return lax.ppermute(value, "mp", [(0, 1), (1, 0)])

    g1 = Gather(ring, stage(after(w_qkv, ids), w_out.T))
    s1 = g1.step()
    cot_got = swap_sides(cotangent)
    stage2, stage3 = stage(w_up), stage(w_down.T)
    s2 = g1.step(stage2, stage3)
    x, a1, gain, bias = prepare(ids, tokens, ln_gain, ln_bias)
    s3 = g1.step(a1)
    s4 = g1.step(cot_got)
    g2 = Gather(ring, after(stage2, *g1.sent))
    s21 = g2.step()
    g3 = Gather(ring, after(stage3, *s4))
    s31 = g3.step()
    own = g1.end()
    w1 = own, swap_cores(ring, after(own, *s21))
    cos, sin = rotary_pair(after(seq_lengths, own), count)
    cot = cotangent_rows(after(ids, own), cotangent, cot_got)
    s22 = g2.step(own)
    qkv = qkv_project(after(a1, cot), *w1, cos, sin)
    probs, outs, ys, mids, zs, backs, mid_backs = [], [], [], [], [], [], []
    lengths = seq_lengths
    for c in range(2):
        p, o, part = attend(c * rows, rows, lengths, qkv, *w1)
        probs.append(p)
        outs.append(o)
        ys.append((part, swap_sides(part)))
        if c == 0:
            lengths = after(lengths, part, *s31)
    s32 = g3.step()
    s23 = g2.step(part)
    s33 = g3.step()
    s24 = g2.step(ys[0][1])
    own = g2.end()
    w2 = own, swap_cores(ring, own)
    s34 = g3.step(own, ys[1][1])
    own = g3.end()
    w3 = own, swap_cores(ring, own)
    for c in range(2):
        xc = after(x, *[m[0] for m in mids])
        mids.append(up_project(c, xc, *ys[c], gain, bias, *w2))
    for c in range(2):
        part = down_project(after(mids[c][1], *[z[0] for z in zs]), *w3)
        zs.append((part, swap_sides(part)))
    for c in range(2):
        xc = after(x, *[b[0] for b in backs])
        out, dz, du, part, gb = mlp_back(
            c, ids, xc, *ys[c], *zs[c], cot, gain, bias, mids[c][2], w3, w2,
            before=[b[0] for b in backs],
        )
        backs.append((out, dz, du, gb, (part, swap_sides(part))))
    output = backs[1][0]
    dzs, dus = [b[1] for b in backs], [b[2] for b in backs]
    a3s, gs = [m[0] for m in mids], [m[1] for m in mids]

    def mid(c, *deps):
        xc = after(x, *deps)
        return mid_back(c, xc, *ys[c], *backs[c][4], cot, gain, bias, *w1)

    def grad(which, products, *deps):
        return weight_grad(after(ids, *deps) if deps else ids, which, ring.size, products)

    def swap_term(term, *deps):
        far = swap_cores(ring, term[0])
        return far, swap_cores(ring, after(term[1], far, *deps))

    down_other = grad(1, [(dzs, gs)])
    up_other = grad(1, [(a3s, dus)], down_other[0])
    down_mine = grad(0, [(dzs, gs)], up_other[0])
    came = backs[0][4][1]
    down_got = swap_term(down_other, came)
    up_mine = grad(0, [(a3s, dus)], down_mine[0], down_got[0])
    up_got = swap_term(up_other, came, up_mine[0])
    mlp_ring = Reduce(ring, w_rows, [[down_mine, down_got], [up_mine, up_got]])
    r1 = mlp_ring.step()
    mid_backs.append(mid(0, *mlp_ring.sent))
    r2 = mlp_ring.step(mid_backs[0][0])
    mid_backs.append(mid(1, *mlp_ring.sent))
    grads = [m[2] for m in mid_backs]
    g_qkv = attend_back(qkv, probs, outs, grads, cos, sin)
    dys = [m[1] for m in mid_backs]
    attn_other = grad(1, [([a1], [g_qkv]), (dys, outs)])
    attn_got = swap_term(attn_other, *r2)
    r3 = mlp_ring.step(attn_other[0])
    attn_mine = grad(0, [([a1], [g_qkv]), (dys, outs)], *mlp_ring.sent)
    part_keep, part_give, gb0 = in_back(ids, after(g_qkv, attn_mine[0]), *w1, x)
    gain_mine, gain_other = gain_sum(gb0, [m[3] for m in mid_backs], [b[3] for b in backs])
    gain_terms = [
        gain_mine,
        swap_cores(ring, gain_other),
        swap_sides(gain_mine),
        lax.ppermute(gain_other, ("dp", "mp"), [(i, i ^ 3) for i in range(2 * n_dp)]),
    ]
    gains = gain_pack(ids, ring.size, gain_terms)
    part_got = swap_sides(after(part_give, gains))
    attn_ring = Reduce(ring, w_rows, [[attn_mine, attn_got], [(gains,)]])
    q1 = attn_ring.step()
    q2 = attn_ring.step(*r3)
    r4 = mlp_ring.step(*attn_ring.sent)
    grad_tokens = tokens_back(
        after(ids, *mlp_ring.sent), x, part_keep, part_got, [m[0] for m in mid_backs], gain
    )
    q3 = attn_ring.step(grad_tokens)
    q4 = attn_ring.step()
    grad_down, grad_up = mlp_ring.end([[(1, units)], [(1, units)]], *attn_ring.sent)
    grad_qkv, grad_out, grad_gain, grad_bias = attn_ring.end(
        [[(3, cols), (1, cols)], [(0, LANES)]], grad_up
    )
    return output, grad_tokens, grad_qkv, grad_out.T, grad_up, grad_down.T, grad_gain, grad_bias


def layer_norm(values, norm_gain, norm_bias):
    average = jnp.mean(values, axis=-1, keepdims=True)
    centred = values - average
    variance = jnp.mean(centred * centred, axis=-1, keepdims=True)
    return centred * lax.rsqrt(variance + NORM_EPS) * norm_gain + norm_bias


def norm_pull(values, norm_gain, norm_bias, grad_result):
    result, puller = jax.vjp(layer_norm, values, norm_gain, norm_bias)
    return puller(grad_result)


def seq_layout(lengths, block_size):
    block_count = lengths.shape[0]
    block_ids = jnp.arange(block_count, dtype=jnp.int32)
    starts = lengths > 0
    earlier = starts[None, :] & (block_ids[None, :] <= block_ids[:, None])
    owners = jnp.max(jnp.where(earlier, block_ids[None, :], 0), axis=1)
    owner_len = jnp.sum(
        jnp.where(block_ids[None, :] == owners[:, None], lengths[None, :], 0), axis=1
    )
    places = jnp.arange(block_count * block_size, dtype=jnp.int32)
    tok_owner = jnp.repeat(owners, block_size)
    position = places - tok_owner * block_size
    is_valid = position < jnp.repeat(owner_len, block_size)
    allowed = (
        (tok_owner[:, None] == tok_owner[None, :])
        & (places[None, :] <= places[:, None])
        & is_valid[None, :]
    )
    return (position, allowed)


def rotary_tables(position, width):
    frequency = ROPE_BASE ** (-jnp.arange(width // 2, dtype=jnp.float32) * 2.0 / width)
    angles = position.astype(jnp.float32)[:, None] * frequency[None, :]
    return (jnp.cos(angles), jnp.sin(angles))


def rotate(values, cos_table, sin_table):
    half_width = values.shape[-1] // 2
    front_half = values[..., :half_width]
    back_half = values[..., half_width:]
    cos_part = cos_table[:, None, :]
    sin_part = sin_table[:, None, :]
    return jnp.concatenate(
        [
            front_half * cos_part - back_half * sin_part,
            back_half * cos_part + front_half * sin_part,
        ],
        axis=-1,
    )


def attention_scores(queries, keys_rot, allowed, scale):
    raw_scores = (
        jnp.einsum("hqd,hkd->hqk", queries, keys_rot, preferred_element_type=jnp.float32) * scale
    )
    return jnp.where(allowed[None, :, :], raw_scores, MASK_FILL)


def plain_device(tokens, seq_lengths, ln_gain, ln_bias, w_qkv, w_out, w_up, w_down, cotangent):
    full_qkv, full_out, full_up, full_down = (
        lax.all_gather(w_qkv, "dp", axis=1, tiled=True),
        lax.all_gather(w_out, "dp", axis=1, tiled=True),
        lax.all_gather(w_up, "dp", axis=0, tiled=True),
        lax.all_gather(w_down, "dp", axis=1, tiled=True),
    )
    tok_count = tokens.shape[0]
    shard_rows = cotangent.shape[0]
    row_start = lax.axis_index("mp") * shard_rows
    heads_here = full_out.shape[0] // HD
    scale = HD ** (-0.5)
    position, allowed = seq_layout(seq_lengths, BLOCK)
    cos_table, sin_table = rotary_tables(position, HD)

    def to_heads(values):
        return jnp.transpose(values.reshape(tok_count, heads_here, HD), (1, 0, 2))

    def from_heads(values):
        return jnp.transpose(values, (1, 0, 2)).reshape(tok_count, heads_here * HD)

    def rotated(values):
        return rotate(values.reshape(tok_count, heads_here, HD), cos_table, sin_table)

    inputs = tokens.astype(jnp.float32)
    normed_in = layer_norm(inputs, ln_gain[0], ln_bias[0]).astype(jnp.bfloat16)
    projected = jnp.einsum("td,cde->cte", normed_in, full_qkv, preferred_element_type=jnp.float32)
    queries = jnp.transpose(rotated(projected[0]), (1, 0, 2)).astype(jnp.bfloat16)
    keys_rot = jnp.transpose(rotated(projected[1]), (1, 0, 2)).astype(jnp.bfloat16)
    values_h = to_heads(projected[2]).astype(jnp.bfloat16)
    scores = attention_scores(queries, keys_rot, allowed, scale)
    top_score = jnp.max(scores, axis=-1, keepdims=True)
    expo = jnp.exp(scores - top_score)
    row_total = jnp.sum(expo, axis=-1, keepdims=True)
    probs = expo / row_total
    log_total = top_score + jnp.log(row_total)
    attended = jnp.einsum(
        "hqk,hkd->hqd", probs.astype(jnp.bfloat16), values_h, preferred_element_type=jnp.float32
    )
    mixed_heads = from_heads(attended).astype(jnp.bfloat16)
    attn_part = jnp.dot(mixed_heads, full_out, preferred_element_type=jnp.float32)
    attn_sum = lax.psum_scatter(
        attn_part.astype(jnp.bfloat16), "mp", scatter_dimension=0, tiled=True
    ).astype(jnp.float32)
    resid_in = lax.dynamic_slice_in_dim(inputs, row_start, shard_rows, 0)
    hidden_state = resid_in + layer_norm(attn_sum, ln_gain[1], ln_bias[1])
    normed_mid = layer_norm(hidden_state, ln_gain[2], ln_bias[2]).astype(jnp.bfloat16)
    mlp_input = lax.all_gather(normed_mid, "mp", axis=0, tiled=True)
    pre_act = jnp.dot(mlp_input, full_up, preferred_element_type=jnp.float32)
    act_low = jax.nn.gelu(pre_act, approximate=True).astype(jnp.bfloat16)
    mlp_part = jnp.dot(act_low, full_down, preferred_element_type=jnp.float32)
    mlp_sum = lax.psum_scatter(
        mlp_part.astype(jnp.bfloat16), "mp", scatter_dimension=0, tiled=True
    ).astype(jnp.float32)
    output = (hidden_state + layer_norm(mlp_sum, ln_gain[3], ln_bias[3])).astype(jnp.bfloat16)
    grad_result = cotangent.astype(jnp.float32)
    grad_mlp_sum, grad_gain3, grad_bias3 = norm_pull(mlp_sum, ln_gain[3], ln_bias[3], grad_result)
    grad_mlp_rows = lax.all_gather(grad_mlp_sum.astype(jnp.bfloat16), "mp", axis=0, tiled=True)
    grad_down = jnp.einsum("tf,te->fe", act_low, grad_mlp_rows, preferred_element_type=jnp.float32)
    grad_act = jnp.einsum("te,fe->tf", grad_mlp_rows, full_down, preferred_element_type=jnp.float32)
    gelu_puller = jax.vjp(lambda values: jax.nn.gelu(values, approximate=True), pre_act)[1]
    grad_pre = gelu_puller(grad_act)[0].astype(jnp.bfloat16)
    grad_up = jnp.einsum("td,tf->df", mlp_input, grad_pre, preferred_element_type=jnp.float32)
    grad_mid_part = jnp.einsum("tf,df->td", grad_pre, full_up, preferred_element_type=jnp.float32)
    grad_mid = lax.psum_scatter(
        grad_mid_part.astype(jnp.bfloat16), "mp", scatter_dimension=0, tiled=True
    ).astype(jnp.float32)
    grad_hidden_norm, grad_gain2, grad_bias2 = norm_pull(
        hidden_state, ln_gain[2], ln_bias[2], grad_mid
    )
    grad_hidden = grad_result + grad_hidden_norm
    grad_attn_sum, grad_gain1, grad_bias1 = norm_pull(attn_sum, ln_gain[1], ln_bias[1], grad_hidden)
    grad_attn_rows = lax.all_gather(grad_attn_sum.astype(jnp.bfloat16), "mp", axis=0, tiled=True)
    grad_outproj = jnp.einsum(
        "tc,te->ce", mixed_heads, grad_attn_rows, preferred_element_type=jnp.float32
    )
    grad_mixed = jnp.einsum(
        "te,ce->tc", grad_attn_rows, full_out, preferred_element_type=jnp.float32
    ).astype(jnp.bfloat16)
    grad_heads = to_heads(grad_mixed)
    again_scores = attention_scores(queries, keys_rot, allowed, scale)
    again_probs = jnp.exp(again_scores - log_total)
    grad_probs = jnp.einsum(
        "hqd,hkd->hqk", grad_heads, values_h, preferred_element_type=jnp.float32
    )
    grad_values = jnp.einsum(
        "hqk,hqd->hkd",
        again_probs.astype(jnp.bfloat16),
        grad_heads,
        preferred_element_type=jnp.float32,
    )
    row_dot = jnp.sum(again_probs * grad_probs, axis=-1, keepdims=True)
    grad_scores = (again_probs * (grad_probs - row_dot) * scale).astype(jnp.bfloat16)
    grad_q_rot = jnp.einsum(
        "hqk,hkd->hqd", grad_scores, keys_rot, preferred_element_type=jnp.float32
    )
    grad_k_rot = jnp.einsum(
        "hqk,hqd->hkd", grad_scores, queries, preferred_element_type=jnp.float32
    )
    zero_heads = jnp.zeros((tok_count, heads_here, HD), jnp.float32)
    unrotate = jax.vjp(lambda values: rotate(values, cos_table, sin_table), zero_heads)[1]
    grad_query = unrotate(jnp.transpose(grad_q_rot, (1, 0, 2)))[0].reshape(
        tok_count, heads_here * HD
    )
    grad_key = unrotate(jnp.transpose(grad_k_rot, (1, 0, 2)))[0].reshape(tok_count, heads_here * HD)
    grad_value = from_heads(grad_values)
    grad_proj = jnp.stack(
        [
            grad_query.astype(jnp.bfloat16),
            grad_key.astype(jnp.bfloat16),
            grad_value.astype(jnp.bfloat16),
        ]
    )
    grad_qkv = jnp.einsum("td,cte->cde", normed_in, grad_proj, preferred_element_type=jnp.float32)
    grad_in_part = jnp.einsum(
        "cte,cde->td", grad_proj, full_qkv, preferred_element_type=jnp.float32
    )
    grad_in = lax.psum_scatter(
        grad_in_part.astype(jnp.bfloat16), "mp", scatter_dimension=0, tiled=True
    ).astype(jnp.float32)
    grad_norm_in, grad_gain0, grad_bias0 = norm_pull(resid_in, ln_gain[0], ln_bias[0], grad_in)
    grad_tokens = grad_hidden + grad_norm_in
    gain_grads = jnp.stack([grad_gain0, grad_gain1, grad_gain2, grad_gain3])
    bias_grads = jnp.stack([grad_bias0, grad_bias1, grad_bias2, grad_bias3])
    gain_grads, bias_grads = (
        lax.psum(gain_grads.astype(jnp.bfloat16), "mp").astype(jnp.float32),
        lax.psum(bias_grads.astype(jnp.bfloat16), "mp").astype(jnp.float32),
    )
    grad_qkv, grad_outproj, grad_up, grad_down, gain_grads, bias_grads = (
        lax.psum_scatter(
            grad_qkv.astype(jnp.bfloat16), "dp", scatter_dimension=1, tiled=True
        ).astype(jnp.float32),
        lax.psum_scatter(
            grad_outproj.astype(jnp.bfloat16), "dp", scatter_dimension=1, tiled=True
        ).astype(jnp.float32),
        lax.psum_scatter(
            grad_up.astype(jnp.bfloat16), "dp", scatter_dimension=0, tiled=True
        ).astype(jnp.float32),
        lax.psum_scatter(
            grad_down.astype(jnp.bfloat16), "dp", scatter_dimension=1, tiled=True
        ).astype(jnp.float32),
        lax.psum_scatter(
            gain_grads.astype(jnp.bfloat16), "dp", scatter_dimension=1, tiled=True
        ).astype(jnp.float32),
        lax.psum_scatter(
            bias_grads.astype(jnp.bfloat16), "dp", scatter_dimension=1, tiled=True
        ).astype(jnp.float32),
    )
    return (output, grad_tokens, grad_qkv, grad_outproj, grad_up, grad_down, gain_grads, bias_grads)


def solution(mesh):
    placed = (
        P("dp", None),
        P("dp"),
        P(),
        P(),
        P(None, "dp", "mp"),
        P("mp", "dp"),
        P("dp", "mp"),
        P("mp", "dp"),
        P(("dp", "mp"), None),
    )
    n_dp, n_mp = mesh.shape["dp"], mesh.shape["mp"]

    def layer(tokens, *rest):
        if n_mp == 2 and tokens.shape[1] == n_dp * LANES // 2:
            return per_device(n_dp, tokens, *rest)
        return plain_device(tokens, *rest)

    return jax.shard_map(
        layer,
        mesh=mesh,
        in_specs=placed,
        out_specs=(
            P(("dp", "mp"), None),
            P(("dp", "mp"), None),
            P(None, "dp", "mp"),
            P("mp", "dp"),
            P("dp", "mp"),
            P("mp", "dp"),
            P(None, "dp"),
            P(None, "dp"),
        ),
        check_vma=False,
    )
```

```python
import functools

import jax
import jax.numpy as jnp
from jax import lax
from jax.experimental import pallas as pl
from jax.experimental.pallas import tpu as pltpu
from jax.sharding import PartitionSpec as P

HD = 64
BLOCK = 128
LANES = 128
NORM_EPS = 1e-05
ROPE_BASE = 10000.0
MASK_FILL = -1e30
F32 = jnp.float32
BF16 = jnp.bfloat16
VMEM_LIMIT = 6 * 1024 * 1024
STEP = 128
NN = (((1,), (0,)), ((), ()))
NT = (((1,), (1,)), ((), ()))
TN = (((0,), (0,)), ((), ()))


def mm(left, right, dims):
    return lax.dot_general(left, right, dims, preferred_element_type=F32)


def sds(shape, dtype):
    return jax.ShapeDtypeStruct(shape, dtype)


def whole():
    return pl.BlockSpec(memory_space=pltpu.VMEM)


def smem():
    return pl.BlockSpec(memory_space=pltpu.SMEM)


def anywhere():
    return pl.BlockSpec(memory_space=pl.ANY)


TIMES = {
    "prepare": 3.3, "cotangent_rows": 1.5, "qkv_project": 2.0, "attend0": 2.5, "attend1": 4.4,
    "up_project": 4.3, "down_project": 1.3, "mlp_back": 5.4, "weight_grad": 1.3, "mid_back": 3.3,
    "attend_back": 5.0, "in_back": 3.6, "gain_pack": 0.4, "tokens_back": 3.9, "stage": 0.5,
    "assemble": 1.2, "ring_sum": 1.3, "ring_end": 2.0, "rotary": 2.0, "split": 0.4,
}
TIME_SHARE = 1.0


def cost_of(name):
    return pl.CostEstimate(
        flops=0, bytes_accessed=int(TIMES[name] * TIME_SHARE * 3.69e6), transcendentals=0
    )


def kernel_call(body, name, out_shape, args, smems=1, flops=0, nbytes=0, scratch=(), **extra):
    many = isinstance(out_shape, (list, tuple))
    return pl.pallas_call(
        body,
        in_specs=[smem()] * smems + [whole()] * (len(args) - smems),
        out_specs=[whole()] * len(out_shape) if many else whole(),
        out_shape=out_shape,
        scratch_shapes=list(scratch),
        compiler_params=pltpu.CompilerParams(vmem_limit_bytes=VMEM_LIMIT),
        cost_estimate=cost_of(name),
        name=name,
        **extra,
    )(*args)


def after(value, *others):
    return lax.optimization_barrier((value,) + others)[0]


def chip_of(place, size):
    if isinstance(place, int):
        return 2 * place if place < size // 2 else 2 * (size - 1 - place) + 1
    return jnp.where(place < size // 2, 2 * place, 2 * (size - 1 - place) + 1)


def ring_order(size):
    order = [size // 2]
    for step in range(size // 2 - 1, 0, -1):
        order += [step, -step]
    return order + [0]


def chip_lanes(ids_ref, width):
    size = width // LANES
    own = ids_ref[0] // 2
    here = jnp.where(own % 2 == 0, own // 2, size - 1 - own // 2)
    starts = [chip_of((here + step + size) % size, size) * LANES for step in ring_order(size)]
    return [pl.ds(pl.multiple_of(start, LANES), LANES) for start in starts]


def split_cores(ids_ref, ref, rows):
    places = chip_lanes(ids_ref, ref.shape[1])
    core = ids_ref[0] % 2
    own, other = [], []
    for i in range(0, len(places), 2):
        a, b = (ref[rows, place].astype(F32) for place in places[i : i + 2])
        low = lax.broadcasted_iota(jnp.int32, a.shape, 1) < LANES // 2
        first = jnp.where(low, a, pltpu.roll(b, LANES // 2, 1))
        second = jnp.where(low, pltpu.roll(a, LANES // 2, 1), b)
        own.append(jnp.where(core == 0, first, second))
        other.append(jnp.where(core == 0, second, first))
    return jnp.concatenate(own + other, axis=1)


def join_cores(ids_ref, values, out_ref, rows, chosen=None, other_ref=None):
    places = chip_lanes(ids_ref, values.shape[1])
    core = ids_ref[0] % 2
    half = values.shape[1] // 2
    for i in range(0, len(places), 2):
        own = values[:, i * LANES // 2 : i * LANES // 2 + LANES]
        other = values[:, half + i * LANES // 2 : half + i * LANES // 2 + LANES]
        low = lax.broadcasted_iota(jnp.int32, own.shape, 1) < LANES // 2
        first = jnp.where(core == 0, own, other)
        second = jnp.where(core == 0, other, own)
        joined = (
            jnp.where(low, first, pltpu.roll(second, LANES // 2, 1)),
            jnp.where(low, pltpu.roll(first, LANES // 2, 1), second),
        )
        for place, part in zip(places[i : i + 2], joined):
            if chosen is not None:
                part = jnp.where(chosen, part, other_ref[rows, place].astype(F32))
            out_ref[rows, place] = part.astype(out_ref.dtype)


def norm_stats(values):
    centred = values - jnp.mean(values, axis=-1, keepdims=True)
    rstd = lax.rsqrt(jnp.mean(centred * centred, axis=-1, keepdims=True) + NORM_EPS)
    return centred * rstd, rstd


def norm_back(normed, rstd, scaled_grad):
    first = jnp.mean(scaled_grad, axis=-1, keepdims=True)
    second = jnp.mean(scaled_grad * normed, axis=-1, keepdims=True)
    return (scaled_grad - first - normed * second) * rstd


def fold_rows(values):
    return jnp.sum(values.reshape(-1, 8, values.shape[-1]), axis=0)


def lanes_at(start, count):
    return pl.ds(pl.multiple_of(start, LANES), count)


def row_steps(rows, body):
    @pl.loop(0, rows // STEP)
    def _(i):
        body(pl.ds(pl.multiple_of(i * STEP, STEP), STEP))


def prepare_kernel(ids_ref, x_ref, gain_ref, bias_ref, xp_ref, a1_ref, gp_ref, bp_ref):
    every = slice(0, gain_ref.shape[0])
    gp_ref[...] = split_cores(ids_ref, gain_ref, every)
    bp_ref[...] = split_cores(ids_ref, bias_ref, every)

    def body(at):
        x = split_cores(ids_ref, x_ref, at)
        xp_ref[at, :] = x.astype(BF16)
        normed, _ = norm_stats(x)
        a1_ref[at, :] = (normed * gp_ref[0:1, :] + bp_ref[0:1, :]).astype(BF16)

    row_steps(x_ref.shape[0], body)


def prepare(ids, x, gain, bias):
    return kernel_call(
        prepare_kernel,
        "prepare",
        [sds(x.shape, BF16), sds(x.shape, BF16), sds(gain.shape, F32), sds(bias.shape, F32)],
        (ids, x, gain, bias),
        nbytes=6 * x.size,
    )


def cotangent_kernel(ids_ref, own_ref, got_ref, out_ref):
    side = ids_ref[1]
    rows = own_ref.shape[0]
    for ref, base in ((own_ref, side * rows), (got_ref, (1 - side) * rows)):

        @pl.loop(0, rows // STEP)
        def _(i, ref=ref, base=base):
            at = pl.ds(pl.multiple_of(i * STEP, STEP), STEP)
            to = pl.ds(pl.multiple_of(base + i * STEP, STEP), STEP)
            out_ref[to, :] = split_cores(ids_ref, ref, at).astype(BF16)


def cotangent_rows(ids, own, got):
    rows, width = own.shape
    return kernel_call(
        cotangent_kernel, "cotangent_rows", sds((2 * rows, width), BF16), (ids, own, got),
        nbytes=8 * own.size,
    )


def partner(values):
    lane = lax.broadcasted_iota(jnp.int32, values.shape, 1)
    ahead = pltpu.roll(values, LANES - HD // 2, 1)
    behind = pltpu.roll(values, HD // 2, 1)
    return jnp.where(lax.rem(lane, HD) < HD // 2, ahead, behind)


def qkv_kernel(a_ref, wo_ref, wg_ref, cos_ref, sin_ref, out_ref):
    half = wo_ref.shape[0]
    cols = wo_ref.shape[1] // 4
    rows = 2 * BLOCK

    @pl.loop(0, a_ref.shape[0] // rows)
    def _(i):
        at = pl.ds(pl.multiple_of(i * rows, rows), rows)
        cos, sin = cos_ref[at, :], sin_ref[at, :]
        for which in range(3):
            to = slice(which * cols, (which + 1) * cols)
            proj = mm(a_ref[at, :half], wo_ref[:, to], NN) + mm(a_ref[at, half:], wg_ref[:, to], NN)
            for start in range(0, cols, LANES):
                part = proj[:, start : start + LANES]
                if which < 2:
                    part = part * cos + partner(part) * sin
                if which == 0:
                    part = part.astype(BF16).astype(F32) * HD ** (-0.5)
                out_ref[at, which * cols + start : which * cols + start + LANES] = part.astype(BF16)


def qkv_project(a1, wo, wg, cos, sin):
    count, width = a1.shape
    three = wo.shape[1] // 4 * 3
    return kernel_call(
        qkv_kernel, "qkv_project", sds((count, three), BF16), (a1, wo, wg, cos, sin), smems=0,
        flops=2 * count * width * three, nbytes=2 * width * three,
    )


def span_of(len_ref, block):
    start, size = jnp.int32(0), jnp.int32(0)
    for b in range(block + 1):
        here = len_ref[b]
        start = jnp.where(here > 0, b * BLOCK, start)
        size = jnp.where(here > 0, here, size)
    return start, start + size


def rotary_kernel(len_ref, cos_ref, sin_ref):
    lane = lax.broadcasted_iota(jnp.int32, (BLOCK, LANES), 1)
    row = lax.broadcasted_iota(jnp.int32, (BLOCK, LANES), 0)
    index = (lane % (HD // 2)).astype(F32)
    frequency = jnp.exp(index * (-2.0 / HD * 9.210340371976184))
    back = lane % HD >= HD // 2
    for b in range(cos_ref.shape[0] // BLOCK):
        start, _ = span_of(len_ref, b)
        angle = (row + (b * BLOCK - start)).astype(F32) * frequency
        sin = jnp.sin(angle)
        cos_ref[b * BLOCK : (b + 1) * BLOCK, :] = jnp.cos(angle)
        sin_ref[b * BLOCK : (b + 1) * BLOCK, :] = jnp.where(back, sin, -sin)


def rotary_pair(lengths, count):
    out = sds((count, LANES), F32)
    return kernel_call(rotary_kernel, "rotary", [out, out], (lengths,))


def head_lanes(rows, first):
    lane = lax.broadcasted_iota(jnp.int32, (rows, LANES), 1)
    return (lane < HD) == first


def attend_kernel(row0, len_ref, q_ref, wo_ref, wg_ref, p_ref, o_ref, part_ref):
    rows, cols = o_ref.shape
    ext = p_ref.shape[2]
    half = wo_ref.shape[0]
    key = lax.broadcasted_iota(jnp.int32, (BLOCK, ext), 1)
    query = lax.broadcasted_iota(jnp.int32, (BLOCK, ext), 0)
    masks = []
    for b in range(rows // BLOCK):
        lo, hi = span_of(len_ref, row0 // BLOCK + b)
        seen = (key >= lo) & (key < hi) & (key <= query + (row0 + b * BLOCK))
        masks.append(jnp.where(seen, 0.0, MASK_FILL))
    mask = jnp.concatenate(masks, axis=0)
    head = 0
    for start in range(0, cols, LANES):
        q = q_ref[row0 : row0 + rows, start : start + LANES]
        k = q_ref[0:ext, cols + start : cols + start + LANES]
        v = q_ref[0:ext, 2 * cols + start : 2 * cols + start + LANES]
        outs = []
        for first in (True, False):
            mine = head_lanes(rows, first)
            s = mm(jnp.where(mine, q, jnp.zeros_like(q)), k, NT) + mask
            e = jnp.exp(s - jnp.max(s, axis=-1, keepdims=True))
            p = (e * (1.0 / jnp.sum(e, axis=-1, keepdims=True))).astype(BF16)
            p_ref[head] = p
            head += 1
            outs.append(mm(p, v, NN))
        o_ref[:, start : start + LANES] = jnp.where(
            head_lanes(rows, True), outs[0], outs[1]
        ).astype(BF16)
    part_ref[:, :half] = mm(o_ref[...], wo_ref[:, 3 * cols :], NT).astype(BF16)
    part_ref[:, half:] = mm(o_ref[...], wg_ref[:, 3 * cols :], NT).astype(BF16)


def attend(row0, rows, lengths, qkv, wo, wg):
    ext = row0 + rows
    cols = qkv.shape[1] // 3
    heads = cols // HD
    width = 2 * wo.shape[0]
    return kernel_call(
        functools.partial(attend_kernel, row0),
        "attend0" if row0 == 0 else "attend1",
        [sds((heads, rows, ext), BF16), sds((rows, cols), BF16), sds((rows, width), BF16)],
        (lengths, qkv, wo, wg),
        flops=4 * heads * rows * ext * HD + 2 * rows * width * cols,
    )


def hidden_of(x, ya, yb, gain_ref, bias_ref):
    n1, r1 = norm_stats(ya.astype(F32) + yb.astype(F32))
    return x.astype(F32) + n1 * gain_ref[1:2, :] + bias_ref[1:2, :], n1, r1


def chunk_rows(chunk, rows, at):
    return pl.ds(pl.multiple_of(chunk * rows + at.start, STEP), STEP)


UNITS = 512


def up_kernel(chunk, x_ref, ya_ref, yb_ref, gain_ref, bias_ref, wo_ref, wg_ref, a3_ref, g_ref, gp_ref):
    rows = ya_ref.shape[0]
    half = wo_ref.shape[0]

    def body(at):
        x = x_ref[chunk_rows(chunk, rows, at), :]
        h, _, _ = hidden_of(x, ya_ref[at, :], yb_ref[at, :], gain_ref, bias_ref)
        n2, _ = norm_stats(h)
        a3_ref[at, :] = (n2 * gain_ref[2:3, :] + bias_ref[2:3, :]).astype(BF16)

    row_steps(rows, body)

    @pl.loop(0, wo_ref.shape[1] // UNITS)
    def _(i):
        to = pl.ds(pl.multiple_of(i * UNITS, UNITS), UNITS)
        u = mm(a3_ref[:, :half], wo_ref[:, to], NN) + mm(a3_ref[:, half:], wg_ref[:, to], NN)
        k0 = 0.7978845608028654
        k1 = 0.044715
        sq = u * u
        th = jnp.tanh(u * (k0 + (k0 * k1) * sq))
        plus = 0.5 + 0.5 * th
        g_ref[:, to] = (u * plus).astype(BF16)
        slope = plus + (u * (k0 + (3.0 * k0 * k1) * sq)) * (0.5 - (0.5 * th) * th)
        gp_ref[:, to] = slope.astype(BF16)


def up_project(chunk, x, ya, yb, gain, bias, wo, wg):
    rows, width = ya.shape
    units = wo.shape[1]
    return kernel_call(
        functools.partial(up_kernel, chunk),
        "up_project",
        [sds((rows, width), BF16), sds((rows, units), BF16), sds((rows, units), BF16)],
        (x, ya, yb, gain, bias, wo, wg),
        smems=0,
        flops=2 * rows * width * units,
    )


def down_kernel(g_ref, wo_ref, wg_ref, z_ref):
    half = wo_ref.shape[0]
    z_ref[:, :half] = mm(g_ref[...], wo_ref[...], NT).astype(BF16)
    z_ref[:, half:] = mm(g_ref[...], wg_ref[...], NT).astype(BF16)


def down_project(g, wo, wg):
    rows, units = g.shape
    width = 2 * wo.shape[0]
    return kernel_call(
        down_kernel, "down_project", sds((rows, width), BF16), (g, wo, wg), smems=0,
        flops=2 * rows * width * units,
    )


def mlp_back_kernel(
    chunk, ids_ref, x_ref, ya_ref, yb_ref, za_ref, zb_ref, cot_ref, gain_ref, bias_ref, gp_ref,
    w3o, w3g, w2o, w2g, *refs
):
    out_ref, dz_ref, du_ref, part_ref, gb_ref = refs[-5:]
    rows = ya_ref.shape[0]
    half = w3o.shape[0]
    gb_ref[...] = jnp.zeros_like(gb_ref)

    def body(at):
        far = chunk_rows(chunk, rows, at)
        h, _, _ = hidden_of(x_ref[far, :], ya_ref[at, :], yb_ref[at, :], gain_ref, bias_ref)
        n3, r3 = norm_stats(za_ref[at, :].astype(F32) + zb_ref[at, :].astype(F32))
        cot = cot_ref[far, :].astype(F32)
        gain = gain_ref[3:4, :]
        out = h + (n3 * gain + bias_ref[3:4, :])
        if chunk > 0:
            join_cores(ids_ref, out, out_ref, at, ids_ref[1] == chunk, refs[0])
        else:
            join_cores(ids_ref, out, out_ref, at)
        dz_ref[at, :] = norm_back(n3, r3, cot * gain).astype(BF16)
        gb_ref[0] += fold_rows(cot * n3)
        gb_ref[1] += fold_rows(cot)

    row_steps(rows, body)

    @pl.loop(0, w3o.shape[1] // UNITS)
    def _(i):
        to = pl.ds(pl.multiple_of(i * UNITS, UNITS), UNITS)
        dg = mm(dz_ref[:, :half], w3o[:, to], NN) + mm(dz_ref[:, half:], w3g[:, to], NN)
        du_ref[:, to] = (dg * gp_ref[:, to].astype(F32)).astype(BF16)

    part_ref[:, :half] = mm(du_ref[...], w2o[...], NT).astype(BF16)
    part_ref[:, half:] = mm(du_ref[...], w2g[...], NT).astype(BF16)


def mlp_back(chunk, ids, x, ya, yb, za, zb, cot, gain, bias, gp, w3, w2, before=()):
    rows, width = ya.shape
    units = w3[0].shape[1]
    return kernel_call(
        functools.partial(mlp_back_kernel, chunk),
        "mlp_back",
        [
            sds((rows, width), BF16),
            sds((rows, width), BF16),
            sds((rows, units), BF16),
            sds((rows, width), BF16),
            sds((2, 8, width), F32),
        ],
        (ids, x, ya, yb, za, zb, cot, gain, bias, gp, *w3, *w2, *before),
        flops=4 * rows * width * units,
    )


def weight_grad_kernel(which, sizes, *refs):
    far_ref, near_ref, left_sc = refs[-3:]
    half, block = left_sc.shape[0], far_ref.shape[0]
    start = 0
    for lefts, rights, cols in sizes:
        rows = 0
        for ref in refs[lefts[0] : lefts[1]]:
            part = ref[:, which * half : (which + 1) * half]
            left_sc[:, rows : rows + part.shape[0]] = part.T
            rows += part.shape[0]
        for c in range(0, cols, UNITS):
            total, rows = None, 0
            for ref in refs[rights[0] : rights[1]]:
                n = ref.shape[0]
                term = mm(left_sc[:, rows : rows + n], ref[:, c : c + UNITS], NN)
                total = term if total is None else total + term
                rows += n
            total = total.astype(BF16)
            far_ref[:, start + c : start + c + UNITS] = total[:block]
            near_ref[:, start + c : start + c + UNITS] = total[block:]
        start += cols


def weight_grad(which, size, products):
    args, sizes, total = [], [], 0
    for lefts, rights in products:
        cols = rights[0].shape[1]
        n = len(args)
        sizes.append(((n, n + len(lefts)), (n + len(lefts), n + len(lefts) + len(rights)), cols))
        args += list(lefts) + list(rights)
        total += cols
    half = args[0].shape[1] // 2
    count = sum(a.shape[0] for a in products[0][0])
    block = half // size
    return kernel_call(
        functools.partial(weight_grad_kernel, which, sizes),
        "weight_grad",
        [sds((block, total), BF16), sds((half - block, total), BF16)],
        tuple(args),
        smems=0,
        scratch=[pltpu.VMEM((half, count), BF16)],
    )


def mid_back_kernel(
    chunk, x_ref, ya_ref, yb_ref, ea_ref, eb_ref, cot_ref, gain_ref, bias_ref, wo_ref, wg_ref,
    dh_ref, dy_ref, do_ref, gb_ref,
):
    rows, cols = do_ref.shape
    half = wo_ref.shape[0]
    gb_ref[...] = jnp.zeros_like(gb_ref)

    def body(at):
        far = chunk_rows(chunk, rows, at)
        h, n1, r1 = hidden_of(x_ref[far, :], ya_ref[at, :], yb_ref[at, :], gain_ref, bias_ref)
        n2, r2 = norm_stats(h)
        e = ea_ref[at, :].astype(F32) + eb_ref[at, :].astype(F32)
        dh = cot_ref[far, :].astype(F32) + norm_back(n2, r2, e * gain_ref[2:3, :])
        dh_ref[at, :] = dh
        dy_ref[at, :] = norm_back(n1, r1, dh * gain_ref[1:2, :]).astype(BF16)
        gb_ref[0] += fold_rows(e * n2)
        gb_ref[1] += fold_rows(e)
        gb_ref[2] += fold_rows(dh * n1)
        gb_ref[3] += fold_rows(dh)

    row_steps(rows, body)
    do = mm(dy_ref[:, :half], wo_ref[:, 3 * cols :], NN)
    do_ref[...] = (do + mm(dy_ref[:, half:], wg_ref[:, 3 * cols :], NN)).astype(BF16)


def mid_back(chunk, x, ya, yb, ea, eb, cot, gain, bias, wo, wg):
    rows, width = ya.shape
    cols = wo.shape[1] // 4
    return kernel_call(
        functools.partial(mid_back_kernel, chunk),
        "mid_back",
        [
            sds((rows, width), F32),
            sds((rows, width), BF16),
            sds((rows, cols), BF16),
            sds((4, 8, width), F32),
        ],
        (x, ya, yb, ea, eb, cot, gain, bias, wo, wg),
        smems=0,
        flops=2 * rows * width * cols,
    )


def attend_back_kernel(q_ref, p0_ref, p1_ref, o0, o1, d0, d1, cos_ref, sin_ref, g_ref):
    rows, cols = o0.shape

    @pl.loop(0, cols // LANES)
    def _(i):
        cos, sin = cos_ref[...], sin_ref[...]
        start = i * LANES
        at = lanes_at(start, LANES)
        q = q_ref[:, at]
        k = q_ref[:, lanes_at(cols + start, LANES)]
        v = q_ref[:, lanes_at(2 * cols + start, LANES)]
        do = (d0[:, at], d1[:, at])
        prod = [a.astype(F32) * b[:, at].astype(F32) for a, b in zip(do, (o0, o1))]
        dq, dk, dv = [], [], []
        for turn, first in enumerate((True, False)):
            mine = head_lanes(rows, first)
            dqs = []
            for c, p_ref in enumerate((p0_ref, p1_ref)):
                ext = p_ref.shape[2]
                p = p_ref[2 * i + turn]
                dp = mm(jnp.where(mine, do[c], jnp.zeros_like(do[c])), v[:ext], NT)
                dot = jnp.sum(jnp.where(mine, prod[c], 0.0), axis=-1, keepdims=True)
                ds = (p.astype(F32) * (dp - dot)).astype(BF16)
                dqs.append(mm(ds, k[:ext], NN))
                dkc = mm(ds, q[c * rows : (c + 1) * rows], TN)
                dvc = mm(p, do[c], TN)
                if c == 0:
                    dk0, dv0 = dkc, dvc
            dk.append(jnp.concatenate([dk0 + dkc[:rows], dkc[rows:]], axis=0))
            dv.append(jnp.concatenate([dv0 + dvc[:rows], dvc[rows:]], axis=0))
            dq.append(jnp.concatenate(dqs, axis=0))
        low = head_lanes(2 * rows, True)
        gq = jnp.where(low, dq[0], dq[1]) * HD ** (-0.5)
        gk = jnp.where(low, dk[0], dk[1])
        gv = jnp.where(low, dv[0], dv[1])
        g_ref[:, at] = (gq * cos - partner(gq) * sin).astype(BF16)
        g_ref[:, lanes_at(cols + start, LANES)] = (gk * cos - partner(gk) * sin).astype(BF16)
        g_ref[:, lanes_at(2 * cols + start, LANES)] = gv.astype(BF16)


def attend_back(qkv, probs, outs, grads, cos, sin):
    count, three = qkv.shape
    heads = probs[0].shape[0]
    return kernel_call(
        attend_back_kernel,
        "attend_back",
        sds((count, three), BF16),
        (qkv, *probs, *outs, *grads, cos, sin),
        smems=0,
        flops=10 * heads * count * count * HD,
    )


def in_back_kernel(ids_ref, g_ref, wo_ref, wg_ref, x_ref, keep_ref, give_ref, gb_ref):
    three = g_ref.shape[1]
    half = wo_ref.shape[0]
    rows = keep_ref.shape[0]
    gb_ref[...] = jnp.zeros_like(gb_ref)
    for turn, out_ref in enumerate((give_ref, keep_ref)):
        base = (1 - ids_ref[1] if turn == 0 else ids_ref[1]) * rows
        g = g_ref[pl.ds(pl.multiple_of(base, rows), rows), :]
        out_ref[:, :half] = mm(g, wo_ref[:, :three], NT).astype(BF16)
        out_ref[:, half:] = mm(g, wg_ref[:, :three], NT).astype(BF16)

        @pl.loop(0, rows // STEP)
        def _(i, base=base, out_ref=out_ref):
            e = out_ref[pl.ds(pl.multiple_of(i * STEP, STEP), STEP), :].astype(F32)
            far = pl.ds(pl.multiple_of(base + i * STEP, STEP), STEP)
            n0, _ = norm_stats(x_ref[far, :].astype(F32))
            gb_ref[0] += fold_rows(e * n0)
            gb_ref[1] += fold_rows(e)


def in_back(ids, g, wo, wg, x):
    count, three = g.shape
    width = x.shape[1]
    part = sds((count // 2, width), BF16)
    return kernel_call(
        in_back_kernel, "in_back", [part, part, sds((2, 8, width), F32)], (ids, g, wo, wg, x),
    )


def gain_sum_kernel(gb0_ref, g12a, g12b, g3a, g3b, mine_ref, other_ref):
    share = 0.5
    rows = []
    for kind in range(2):
        rows += [
            gb0_ref[kind],
            share * (g12a[2 + kind] + g12b[2 + kind]),
            share * (g12a[kind] + g12b[kind]),
            share * (g3a[kind] + g3b[kind]),
        ]
    half = mine_ref.shape[1]
    for i, row in enumerate(rows):
        row = jnp.sum(row, axis=0, keepdims=True)
        mine_ref[i : i + 1, :] = row[:, :half]
        other_ref[i : i + 1, :] = row[:, half:]


def gain_sum(gb0, g12, g3):
    out = sds((8, gb0.shape[-1] // 2), F32)
    return kernel_call(gain_sum_kernel, "gain_pack", [out, out], (gb0, *g12, *g3), smems=0)


def gain_pack_kernel(*refs):
    out_ref = refs[-1]
    total = refs[0][...] + refs[1][...] + refs[2][...] + refs[3][...]
    filler = jnp.zeros((LANES - total.shape[0], total.shape[1]), F32)
    out_ref[...] = jnp.concatenate([total, filler], axis=0).T.astype(BF16)


def gain_pack(parts):
    out = sds((parts[0].shape[1], LANES), BF16)
    return kernel_call(gain_pack_kernel, "gain_pack", out, tuple(parts), smems=0)


def tokens_back_kernel(ids_ref, x_ref, keep_ref, got_ref, dh0_ref, dh1_ref, gain_ref, out_ref):
    side = ids_ref[1]
    rows = got_ref.shape[0]

    def body(at):
        far = pl.ds(pl.multiple_of(side * rows + at.start, STEP), STEP)
        e = keep_ref[at, :].astype(F32) + got_ref[at, :].astype(F32)
        n0, r0 = norm_stats(x_ref[far, :].astype(F32))
        dh = jnp.where(side == 0, dh0_ref[at, :], dh1_ref[at, :])
        join_cores(ids_ref, dh + norm_back(n0, r0, e * gain_ref[0:1, :]), out_ref, at)

    row_steps(rows, body)


def tokens_back(ids, x, keep, got, dhs, gain):
    return kernel_call(
        tokens_back_kernel, "tokens_back", sds(got.shape, F32), (ids, x, keep, got, *dhs, gain),
    )


def split_kernel(up_ref, down_ref, up_out, down_out):
    half = up_out.shape[0]
    up_out[...] = up_ref[:half, :]
    down_out[...] = down_ref[half:, :]


def split(up, down):
    out = sds((up.shape[0] // 2, up.shape[1]), BF16)
    return kernel_call(split_kernel, "split", [out, out], (up, down), smems=0)


def stage_kernel(*refs):
    ins, out_ref, sem = refs[:-2], refs[-2], refs[-1]
    copies, start = [], 0
    for ref in ins:
        parts = [ref.at[i] for i in range(ref.shape[0])] if len(ref.shape) == 3 else [ref]
        for part in parts:
            cols = part.shape[1]
            dst = out_ref.at[:, pl.ds(start, cols)]
            copies.append(pltpu.make_async_copy(part, dst, sem.at[len(copies)]))
            start += cols
    for copy in copies:
        copy.start()
    for copy in copies:
        copy.wait()


def stage(*arrays):
    rows = arrays[0].shape[-2]
    cols = sum(a.size // rows for a in arrays)
    return pl.pallas_call(
        stage_kernel,
        in_specs=[pl.BlockSpec(memory_space=pltpu.HBM)] * len(arrays),
        out_specs=whole(),
        out_shape=sds((rows, cols), BF16),
        scratch_shapes=[pltpu.SemaphoreType.DMA((4 * len(arrays),))],
        compiler_params=pltpu.CompilerParams(vmem_limit_bytes=VMEM_LIMIT),
        cost_estimate=cost_of("stage"),
        name="stage",
    )(*arrays)


def assemble_kernel(places, *refs):
    ins, out, sem = refs[: len(places)], refs[-2], refs[-1]
    copies = []
    for i, (src, at) in enumerate(zip(ins, places)):
        copies.append(pltpu.make_async_copy(src, out.at[pl.ds(at, src.shape[0])], sem.at[i]))
    for copy in copies:
        copy.start()
    for copy in copies:
        copy.wait()


def assemble(places, pieces, size):
    rows, width = pieces[0].shape
    return pl.pallas_call(
        functools.partial(assemble_kernel, places),
        in_specs=[anywhere()] * len(pieces),
        out_specs=whole(),
        out_shape=sds((rows * size, width), BF16),
        scratch_shapes=[pltpu.SemaphoreType.DMA((len(pieces),))],
        compiler_params=pltpu.CompilerParams(vmem_limit_bytes=VMEM_LIMIT),
        cost_estimate=cost_of("assemble"),
        name="assemble",
    )(*pieces)


def term_rows(groups, block, index, to):
    total = None
    for refs in groups:
        if len(refs) == 2:
            ref, first = (refs[0], 0) if index == 0 else (refs[1], (index - 1) * block)
        else:
            ref, first = refs[0], index * block
        part = ref[first : first + block, to].astype(F32)
        total = part if total is None else total + part
    return total


def unflatten(refs, layout):
    groups, n = [], 0
    for terms in layout:
        group = []
        for count in terms:
            group.append(refs[n : n + count])
            n += count
        groups.append(group)
    return groups, refs[n:]


def ring_sum_kernel(layout, block, index, *refs):
    groups, refs = unflatten(refs, layout)
    outs, came = refs[-2:], refs[:-2]
    half = block // 2
    start = 0
    for group in groups:
        cols = group[0][0].shape[1]
        for c in range(0, cols, UNITS):
            n = min(UNITS, cols - c)
            own, to = slice(c, c + n), slice(start + c, start + c + n)
            if index == 0:
                total = sum(term[0][0:block, own].astype(F32) for term in group)
                outs[0][:, to] = total[:half].astype(BF16)
                outs[1][:, to] = total[half:].astype(BF16)
                continue
            for way in range(2):
                total = term_rows(group, block, index + way, own)
                part = came[way][:, to].astype(F32)
                if part.shape[0] == block:
                    outs[way][:, to] = (total + part).astype(BF16)
                else:
                    hit = slice(0, half) if way == 0 else slice(half, block)
                    rest = slice(half, block) if way == 0 else slice(0, half)
                    outs[way][hit, to] = (total[hit] + part).astype(BF16)
                    outs[way][rest, to] = total[rest].astype(BF16)
        start += cols


def ring_sum(index, block, groups, came=()):
    layout = [[len(term) for term in group] for group in groups]
    flat = [a for group in groups for term in group for a in term]
    cols = sum(group[0][0].shape[1] for group in groups)
    out = sds((block // 2 if index == 0 else block, cols), BF16)
    return kernel_call(
        functools.partial(ring_sum_kernel, layout, block, index), "ring_sum", [out, out],
        (*flat, *came), smems=0,
    )


def ring_end_kernel(layout, splits, index, *refs):
    groups, refs = unflatten(refs, layout)
    (up, down), outs = refs[:2], refs[2:]
    block = up.shape[0]
    start, o = 0, 0
    for group, sizes in zip(groups, splits):
        here = 0
        for count, cols in sizes:
            for i in range(max(count, 1)):
                to, own = slice(start, start + cols), slice(here, here + cols)
                total = term_rows(group, block, index, own)
                total = total + up[:, to].astype(F32) + down[:, to].astype(F32)
                if count == 0:
                    turned = total.T
                    outs[o][...] = turned[0:4, :]
                    outs[o + 1][...] = turned[4:8, :]
                elif count > 1:
                    outs[o][i] = total
                else:
                    outs[o][...] = total
                start, here = start + cols, here + cols
            o += 2 if count == 0 else 1


def ring_end(size, groups, came, splits):
    layout = [[len(term) for term in group] for group in groups]
    flat = [a for group in groups for term in group for a in term]
    block = came[0].shape[0]
    shapes = []
    for sizes in splits:
        for count, cols in sizes:
            if count == 0:
                shapes += [(4, block)] * 2
            else:
                shapes.append((count, block, cols) if count > 1 else (block, cols))
    return kernel_call(
        functools.partial(ring_end_kernel, layout, splits, size - 1), "ring_end",
        [sds(shape, F32) for shape in shapes], (*flat, *came), smems=0,
    )


class Ring:
    def __init__(self, n_dp, ids):
        self.size = n_dp // 2
        self.ids = ids
        self.up = self.shift(1)
        self.down = self.shift(-1)
        self.cores = [(i, i ^ 1) for i in range(n_dp)]

    def shift(self, by):
        return [
            (2 * chip_of(p, self.size) + c, 2 * chip_of((p + by) % self.size, self.size) + c)
            for p in range(self.size)
            for c in range(2)
        ]


def swap_cores(ring, value):
    return lax.ppermute(value, "dp", ring.cores)


class Gather:
    def __init__(self, ring, piece):
        self.ring = ring
        self.rows = piece.shape[0]
        self.pieces, self.places = [piece], [ring_order(ring.size).index(0) * self.rows]
        self.step_now = 0
        self.up = self.down = piece

    def step(self, *deps):
        self.step_now += 1
        ring, step = self.ring, self.step_now
        up, down = self.up, self.down
        if deps:
            up, down = after(up, *deps), after(down, *deps)
        shift = 0
        if step == ring.size // 2:
            shift = up.shape[0] // 2
            up, down = split(up, down)
            self.sent = up, down
        self.up = lax.ppermute(up, "dp", ring.up)
        self.down = lax.ppermute(down, "dp", ring.down)
        self.pieces += [self.up, self.down]
        order = ring_order(ring.size)
        self.places += [
            order.index(step if shift else -step) * self.rows,
            order.index(step) * self.rows + shift,
        ]
        return self.up, self.down

    def end(self, *deps):
        pieces = self.pieces
        if deps:
            pieces = [after(pieces[0], *deps), *pieces[1:]]
        return assemble(self.places, pieces, self.ring.size)


class Reduce:
    def __init__(self, ring, block, groups):
        self.ring, self.block, self.groups = ring, block, groups
        self.index = 0
        self.came = ()

    def step(self, *deps):
        groups = self.groups
        if deps:
            first = groups[0][0]
            groups = [[(after(first[0], *deps), *first[1:]), *groups[0][1:]], *groups[1:]]
        if self.index == 0:
            groups = [[(term[0],) for term in group] for group in groups]
        self.sent = ring_sum(self.index, self.block, groups, self.came)
        up, down = self.sent
        self.came = lax.ppermute(up, "dp", self.ring.up), lax.ppermute(down, "dp", self.ring.down)
        self.index += 2 if self.index else 1
        return self.came

    def end(self, splits, *deps):
        came = self.came
        if deps:
            came = after(came[0], *deps), came[1]
        return ring_end(self.ring.size, self.groups, came, splits)


def per_device(n_dp, tokens, seq_lengths, ln_gain, ln_bias, w_qkv, w_out, w_up, w_down, cotangent):
    ids = jnp.stack([lax.axis_index("dp"), lax.axis_index("mp")]).astype(jnp.int32)
    ring = Ring(n_dp, ids)
    count, width = tokens.shape
    rows = count // 2
    w_rows, units = w_up.shape
    cols = w_out.shape[0]

    def swap_sides(value):
        return lax.ppermute(value, "mp", [(0, 1), (1, 0)])

    g1 = Gather(ring, stage(after(w_qkv, ids), w_out.T))
    s1 = g1.step()
    cot_got = swap_sides(cotangent)
    stage2, stage3 = stage(w_up), stage(w_down.T)
    s2 = g1.step(stage2, stage3)
    x, a1, gain, bias = prepare(ids, tokens, ln_gain, ln_bias)
    s3 = g1.step(a1)
    s4 = g1.step(cot_got)
    g2 = Gather(ring, after(stage2, *g1.sent))
    s21 = g2.step()
    g3 = Gather(ring, after(stage3, *s4))
    s31 = g3.step()
    own = g1.end()
    w1 = own, swap_cores(ring, after(own, *s21))
    cos, sin = rotary_pair(after(seq_lengths, own), count)
    cot = cotangent_rows(after(ids, own), cotangent, cot_got)
    s22 = g2.step(own)
    qkv = qkv_project(after(a1, cot), *w1, cos, sin)
    probs, outs, ys, mids, zs, backs, mid_backs = [], [], [], [], [], [], []
    lengths = seq_lengths
    for c in range(2):
        p, o, part = attend(c * rows, rows, lengths, qkv, *w1)
        probs.append(p)
        outs.append(o)
        ys.append((part, swap_sides(part)))
        if c == 0:
            lengths = after(lengths, part, *s31)
    s32 = g3.step()
    s23 = g2.step(part)
    s33 = g3.step()
    s24 = g2.step(ys[0][1])
    own = g2.end()
    w2 = own, swap_cores(ring, own)
    s34 = g3.step(own, ys[1][1])
    own = g3.end()
    w3 = own, swap_cores(ring, own)
    for c in range(2):
        xc = after(x, *[m[0] for m in mids])
        mids.append(up_project(c, xc, *ys[c], gain, bias, *w2))
    for c in range(2):
        part = down_project(after(mids[c][1], *[z[0] for z in zs]), *w3)
        zs.append((part, swap_sides(part)))
    for c in range(2):
        xc = after(x, *[b[0] for b in backs])
        out, dz, du, part, gb = mlp_back(
            c, ids, xc, *ys[c], *zs[c], cot, gain, bias, mids[c][2], w3, w2,
            before=[b[0] for b in backs],
        )
        backs.append((out, dz, du, gb, (part, swap_sides(part))))
    output = backs[1][0]
    dzs, dus = [b[1] for b in backs], [b[2] for b in backs]
    a3s, gs = [m[0] for m in mids], [m[1] for m in mids]

    def mid(c, *deps):
        xc = after(x, *deps)
        return mid_back(c, xc, *ys[c], *backs[c][4], cot, gain, bias, *w1)

    def grad(which, products, *deps):
        if deps:
            (lefts, rights), rest = products[0], products[1:]
            products = [([after(lefts[0], *deps), *lefts[1:]], rights), *rest]
        return weight_grad(which, ring.size, products)

    def swap_term(term, *deps):
        far = swap_cores(ring, term[0])
        return far, swap_cores(ring, after(term[1], far, *deps))

    down_other = grad(1, [(dzs, gs)])
    up_other = grad(1, [(a3s, dus)], down_other[0])
    down_mine = grad(0, [(dzs, gs)], up_other[0])
    came = backs[0][4][1]
    down_got = swap_term(down_other, came)
    up_mine = grad(0, [(a3s, dus)], down_mine[0], down_got[0])
    up_got = swap_term(up_other, came, up_mine[0])
    mlp_ring = Reduce(ring, w_rows, [[down_mine, down_got], [up_mine, up_got]])
    r1 = mlp_ring.step()
    mid_backs.append(mid(0, *mlp_ring.sent))
    r2 = mlp_ring.step(mid_backs[0][0])
    mid_backs.append(mid(1, *mlp_ring.sent))
    grads = [m[2] for m in mid_backs]
    g_qkv = attend_back(qkv, probs, outs, grads, cos, sin)
    dys = [m[1] for m in mid_backs]
    attn_other = grad(1, [([a1], [g_qkv]), (dys, outs)])
    attn_got = swap_term(attn_other, *r2)
    r3 = mlp_ring.step(attn_other[0])
    attn_mine = grad(0, [([a1], [g_qkv]), (dys, outs)], *mlp_ring.sent)
    part_keep, part_give, gb0 = in_back(ids, after(g_qkv, attn_mine[0]), *w1, x)
    gain_mine, gain_other = gain_sum(gb0, [m[3] for m in mid_backs], [b[3] for b in backs])
    gain_terms = [
        gain_mine,
        swap_cores(ring, gain_other),
        swap_sides(gain_mine),
        lax.ppermute(gain_other, ("dp", "mp"), [(i, i ^ 3) for i in range(2 * n_dp)]),
    ]
    gains = gain_pack(gain_terms)
    part_got = swap_sides(after(part_give, gains))
    attn_ring = Reduce(ring, w_rows, [[attn_mine, attn_got], [(gains,)]])
    q1 = attn_ring.step()
    q2 = attn_ring.step(*r3)
    r4 = mlp_ring.step(*attn_ring.sent)
    grad_tokens = tokens_back(
        after(ids, *mlp_ring.sent), x, part_keep, part_got, [m[0] for m in mid_backs], gain
    )
    q3 = attn_ring.step(grad_tokens)
    q4 = attn_ring.step()
    grad_down, grad_up = mlp_ring.end([[(1, units)], [(1, units)]], *attn_ring.sent)
    grad_qkv, grad_out, grad_gain, grad_bias = attn_ring.end(
        [[(3, cols), (1, cols)], [(0, LANES)]], grad_up
    )
    return output, grad_tokens, grad_qkv, grad_out.T, grad_up, grad_down.T, grad_gain, grad_bias


def layer_norm(values, norm_gain, norm_bias):
    average = jnp.mean(values, axis=-1, keepdims=True)
    centred = values - average
    variance = jnp.mean(centred * centred, axis=-1, keepdims=True)
    return centred * lax.rsqrt(variance + NORM_EPS) * norm_gain + norm_bias


def norm_pull(values, norm_gain, norm_bias, grad_result):
    result, puller = jax.vjp(layer_norm, values, norm_gain, norm_bias)
    return puller(grad_result)


def seq_layout(lengths, block_size):
    block_count = lengths.shape[0]
    block_ids = jnp.arange(block_count, dtype=jnp.int32)
    starts = lengths > 0
    earlier = starts[None, :] & (block_ids[None, :] <= block_ids[:, None])
    owners = jnp.max(jnp.where(earlier, block_ids[None, :], 0), axis=1)
    owner_len = jnp.sum(
        jnp.where(block_ids[None, :] == owners[:, None], lengths[None, :], 0), axis=1
    )
    places = jnp.arange(block_count * block_size, dtype=jnp.int32)
    tok_owner = jnp.repeat(owners, block_size)
    position = places - tok_owner * block_size
    is_valid = position < jnp.repeat(owner_len, block_size)
    allowed = (
        (tok_owner[:, None] == tok_owner[None, :])
        & (places[None, :] <= places[:, None])
        & is_valid[None, :]
    )
    return (position, allowed)


def rotary_tables(position, width):
    frequency = ROPE_BASE ** (-jnp.arange(width // 2, dtype=jnp.float32) * 2.0 / width)
    angles = position.astype(jnp.float32)[:, None] * frequency[None, :]
    return (jnp.cos(angles), jnp.sin(angles))


def rotate(values, cos_table, sin_table):
    half_width = values.shape[-1] // 2
    front_half = values[..., :half_width]
    back_half = values[..., half_width:]
    cos_part = cos_table[:, None, :]
    sin_part = sin_table[:, None, :]
    return jnp.concatenate(
        [
            front_half * cos_part - back_half * sin_part,
            back_half * cos_part + front_half * sin_part,
        ],
        axis=-1,
    )


def attention_scores(queries, keys_rot, allowed, scale):
    raw_scores = (
        jnp.einsum("hqd,hkd->hqk", queries, keys_rot, preferred_element_type=jnp.float32) * scale
    )
    return jnp.where(allowed[None, :, :], raw_scores, MASK_FILL)


def plain_device(tokens, seq_lengths, ln_gain, ln_bias, w_qkv, w_out, w_up, w_down, cotangent):
    full_qkv, full_out, full_up, full_down = (
        lax.all_gather(w_qkv, "dp", axis=1, tiled=True),
        lax.all_gather(w_out, "dp", axis=1, tiled=True),
        lax.all_gather(w_up, "dp", axis=0, tiled=True),
        lax.all_gather(w_down, "dp", axis=1, tiled=True),
    )
    tok_count = tokens.shape[0]
    shard_rows = cotangent.shape[0]
    row_start = lax.axis_index("mp") * shard_rows
    heads_here = full_out.shape[0] // HD
    scale = HD ** (-0.5)
    position, allowed = seq_layout(seq_lengths, BLOCK)
    cos_table, sin_table = rotary_tables(position, HD)

    def to_heads(values):
        return jnp.transpose(values.reshape(tok_count, heads_here, HD), (1, 0, 2))

    def from_heads(values):
        return jnp.transpose(values, (1, 0, 2)).reshape(tok_count, heads_here * HD)

    def rotated(values):
        return rotate(values.reshape(tok_count, heads_here, HD), cos_table, sin_table)

    inputs = tokens.astype(jnp.float32)
    normed_in = layer_norm(inputs, ln_gain[0], ln_bias[0]).astype(jnp.bfloat16)
    projected = jnp.einsum("td,cde->cte", normed_in, full_qkv, preferred_element_type=jnp.float32)
    queries = jnp.transpose(rotated(projected[0]), (1, 0, 2)).astype(jnp.bfloat16)
    keys_rot = jnp.transpose(rotated(projected[1]), (1, 0, 2)).astype(jnp.bfloat16)
    values_h = to_heads(projected[2]).astype(jnp.bfloat16)
    scores = attention_scores(queries, keys_rot, allowed, scale)
    top_score = jnp.max(scores, axis=-1, keepdims=True)
    expo = jnp.exp(scores - top_score)
    row_total = jnp.sum(expo, axis=-1, keepdims=True)
    probs = expo / row_total
    log_total = top_score + jnp.log(row_total)
    attended = jnp.einsum(
        "hqk,hkd->hqd", probs.astype(jnp.bfloat16), values_h, preferred_element_type=jnp.float32
    )
    mixed_heads = from_heads(attended).astype(jnp.bfloat16)
    attn_part = jnp.dot(mixed_heads, full_out, preferred_element_type=jnp.float32)
    attn_sum = lax.psum_scatter(
        attn_part.astype(jnp.bfloat16), "mp", scatter_dimension=0, tiled=True
    ).astype(jnp.float32)
    resid_in = lax.dynamic_slice_in_dim(inputs, row_start, shard_rows, 0)
    hidden_state = resid_in + layer_norm(attn_sum, ln_gain[1], ln_bias[1])
    normed_mid = layer_norm(hidden_state, ln_gain[2], ln_bias[2]).astype(jnp.bfloat16)
    mlp_input = lax.all_gather(normed_mid, "mp", axis=0, tiled=True)
    pre_act = jnp.dot(mlp_input, full_up, preferred_element_type=jnp.float32)
    act_low = jax.nn.gelu(pre_act, approximate=True).astype(jnp.bfloat16)
    mlp_part = jnp.dot(act_low, full_down, preferred_element_type=jnp.float32)
    mlp_sum = lax.psum_scatter(
        mlp_part.astype(jnp.bfloat16), "mp", scatter_dimension=0, tiled=True
    ).astype(jnp.float32)
    output = (hidden_state + layer_norm(mlp_sum, ln_gain[3], ln_bias[3])).astype(jnp.bfloat16)
    grad_result = cotangent.astype(jnp.float32)
    grad_mlp_sum, grad_gain3, grad_bias3 = norm_pull(mlp_sum, ln_gain[3], ln_bias[3], grad_result)
    grad_mlp_rows = lax.all_gather(grad_mlp_sum.astype(jnp.bfloat16), "mp", axis=0, tiled=True)
    grad_down = jnp.einsum("tf,te->fe", act_low, grad_mlp_rows, preferred_element_type=jnp.float32)
    grad_act = jnp.einsum("te,fe->tf", grad_mlp_rows, full_down, preferred_element_type=jnp.float32)
    gelu_puller = jax.vjp(lambda values: jax.nn.gelu(values, approximate=True), pre_act)[1]
    grad_pre = gelu_puller(grad_act)[0].astype(jnp.bfloat16)
    grad_up = jnp.einsum("td,tf->df", mlp_input, grad_pre, preferred_element_type=jnp.float32)
    grad_mid_part = jnp.einsum("tf,df->td", grad_pre, full_up, preferred_element_type=jnp.float32)
    grad_mid = lax.psum_scatter(
        grad_mid_part.astype(jnp.bfloat16), "mp", scatter_dimension=0, tiled=True
    ).astype(jnp.float32)
    grad_hidden_norm, grad_gain2, grad_bias2 = norm_pull(
        hidden_state, ln_gain[2], ln_bias[2], grad_mid
    )
    grad_hidden = grad_result + grad_hidden_norm
    grad_attn_sum, grad_gain1, grad_bias1 = norm_pull(attn_sum, ln_gain[1], ln_bias[1], grad_hidden)
    grad_attn_rows = lax.all_gather(grad_attn_sum.astype(jnp.bfloat16), "mp", axis=0, tiled=True)
    grad_outproj = jnp.einsum(
        "tc,te->ce", mixed_heads, grad_attn_rows, preferred_element_type=jnp.float32
    )
    grad_mixed = jnp.einsum(
        "te,ce->tc", grad_attn_rows, full_out, preferred_element_type=jnp.float32
    ).astype(jnp.bfloat16)
    grad_heads = to_heads(grad_mixed)
    again_scores = attention_scores(queries, keys_rot, allowed, scale)
    again_probs = jnp.exp(again_scores - log_total)
    grad_probs = jnp.einsum(
        "hqd,hkd->hqk", grad_heads, values_h, preferred_element_type=jnp.float32
    )
    grad_values = jnp.einsum(
        "hqk,hqd->hkd",
        again_probs.astype(jnp.bfloat16),
        grad_heads,
        preferred_element_type=jnp.float32,
    )
    row_dot = jnp.sum(again_probs * grad_probs, axis=-1, keepdims=True)
    grad_scores = (again_probs * (grad_probs - row_dot) * scale).astype(jnp.bfloat16)
    grad_q_rot = jnp.einsum(
        "hqk,hkd->hqd", grad_scores, keys_rot, preferred_element_type=jnp.float32
    )
    grad_k_rot = jnp.einsum(
        "hqk,hqd->hkd", grad_scores, queries, preferred_element_type=jnp.float32
    )
    zero_heads = jnp.zeros((tok_count, heads_here, HD), jnp.float32)
    unrotate = jax.vjp(lambda values: rotate(values, cos_table, sin_table), zero_heads)[1]
    grad_query = unrotate(jnp.transpose(grad_q_rot, (1, 0, 2)))[0].reshape(
        tok_count, heads_here * HD
    )
    grad_key = unrotate(jnp.transpose(grad_k_rot, (1, 0, 2)))[0].reshape(tok_count, heads_here * HD)
    grad_value = from_heads(grad_values)
    grad_proj = jnp.stack(
        [
            grad_query.astype(jnp.bfloat16),
            grad_key.astype(jnp.bfloat16),
            grad_value.astype(jnp.bfloat16),
        ]
    )
    grad_qkv = jnp.einsum("td,cte->cde", normed_in, grad_proj, preferred_element_type=jnp.float32)
    grad_in_part = jnp.einsum(
        "cte,cde->td", grad_proj, full_qkv, preferred_element_type=jnp.float32
    )
    grad_in = lax.psum_scatter(
        grad_in_part.astype(jnp.bfloat16), "mp", scatter_dimension=0, tiled=True
    ).astype(jnp.float32)
    grad_norm_in, grad_gain0, grad_bias0 = norm_pull(resid_in, ln_gain[0], ln_bias[0], grad_in)
    grad_tokens = grad_hidden + grad_norm_in
    gain_grads = jnp.stack([grad_gain0, grad_gain1, grad_gain2, grad_gain3])
    bias_grads = jnp.stack([grad_bias0, grad_bias1, grad_bias2, grad_bias3])
    gain_grads, bias_grads = (
        lax.psum(gain_grads.astype(jnp.bfloat16), "mp").astype(jnp.float32),
        lax.psum(bias_grads.astype(jnp.bfloat16), "mp").astype(jnp.float32),
    )
    grad_qkv, grad_outproj, grad_up, grad_down, gain_grads, bias_grads = (
        lax.psum_scatter(
            grad_qkv.astype(jnp.bfloat16), "dp", scatter_dimension=1, tiled=True
        ).astype(jnp.float32),
        lax.psum_scatter(
            grad_outproj.astype(jnp.bfloat16), "dp", scatter_dimension=1, tiled=True
        ).astype(jnp.float32),
        lax.psum_scatter(
            grad_up.astype(jnp.bfloat16), "dp", scatter_dimension=0, tiled=True
        ).astype(jnp.float32),
        lax.psum_scatter(
            grad_down.astype(jnp.bfloat16), "dp", scatter_dimension=1, tiled=True
        ).astype(jnp.float32),
        lax.psum_scatter(
            gain_grads.astype(jnp.bfloat16), "dp", scatter_dimension=1, tiled=True
        ).astype(jnp.float32),
        lax.psum_scatter(
            bias_grads.astype(jnp.bfloat16), "dp", scatter_dimension=1, tiled=True
        ).astype(jnp.float32),
    )
    return (output, grad_tokens, grad_qkv, grad_outproj, grad_up, grad_down, gain_grads, bias_grads)


def solution(mesh):
    placed = (
        P("dp", None),
        P("dp"),
        P(),
        P(),
        P(None, "dp", "mp"),
        P("mp", "dp"),
        P("dp", "mp"),
        P("mp", "dp"),
        P(("dp", "mp"), None),
    )
    n_dp, n_mp = mesh.shape["dp"], mesh.shape["mp"]

    def layer(tokens, *rest):
        if n_mp == 2 and tokens.shape[1] == n_dp * LANES // 2:
            return per_device(n_dp, tokens, *rest)
        return plain_device(tokens, *rest)

    return jax.shard_map(
        layer,
        mesh=mesh,
        in_specs=placed,
        out_specs=(
            P(("dp", "mp"), None),
            P(("dp", "mp"), None),
            P(None, "dp", "mp"),
            P("mp", "dp"),
            P("dp", "mp"),
            P("mp", "dp"),
            P(None, "dp"),
            P(None, "dp"),
        ),
        check_vma=False,
    )
```

```python
import functools

import jax
import jax.numpy as jnp
from jax import lax
from jax.experimental import pallas as pl
from jax.experimental.pallas import tpu as pltpu
from jax.sharding import PartitionSpec as P

HD = 64
BLOCK = 128
LANES = 128
NORM_EPS = 1e-05
ROPE_BASE = 10000.0
MASK_FILL = -1e30
F32 = jnp.float32
BF16 = jnp.bfloat16
VMEM_LIMIT = 6 * 1024 * 1024
STEP = 128
NN = (((1,), (0,)), ((), ()))
NT = (((1,), (1,)), ((), ()))
TN = (((0,), (0,)), ((), ()))


def mm(left, right, dims):
    return lax.dot_general(left, right, dims, preferred_element_type=F32)


def sds(shape, dtype):
    return jax.ShapeDtypeStruct(shape, dtype)


def whole():
    return pl.BlockSpec(memory_space=pltpu.VMEM)


def smem():
    return pl.BlockSpec(memory_space=pltpu.SMEM)


def anywhere():
    return pl.BlockSpec(memory_space=pl.ANY)


TIMES = {
    "prepare": 3.3, "cotangent_rows": 1.5, "qkv_project": 2.0, "attend0": 2.5, "attend1": 4.4,
    "up_project": 4.3, "down_project": 1.3, "mlp_back": 5.4, "mid_norm": 2.5, "weight_grad": 1.3, "mid_back": 3.3,
    "attend_back": 5.0, "in_back": 3.6, "gain_pack": 0.4, "tokens_back": 3.9, "stage": 0.5,
    "assemble": 1.2, "ring_sum": 1.3, "ring_end": 2.0, "rotary": 2.0, "split": 0.4,
}
TIME_SHARE = 1.0


def cost_of(name):
    return pl.CostEstimate(
        flops=0, bytes_accessed=int(TIMES[name] * TIME_SHARE * 3.69e6), transcendentals=0
    )


ORDER = {
    "s12": ("stages",), "s13": ("a1",), "s14": ("cot_got",), "s21": ("s14_sent",), "s31": ("s14",),
    "cot_swap": ("s11",), "w1": ("s21",), "rotary": ("own1",), "cot": ("own1",), "s22": ("own1",),
    "qkv": ("cot",), "attend1": ("part0", "s31"), "s23": ("part1",), "s24": ("y0",),
    "norm0": ("own2",), "s34": ("own2", "y1"), "up1": ("down0",), "down1": ("down0",),
    "back1": ("back0",), "up_other": ("down_other",), "down_mine": ("up_other",),
    "up_mine": ("down_mine", "down_far"), "up_near": ("da0", "up_mine"), "mid0": ("m1_sent",),
    "m2": ("mid0",), "mid1": ("m2_sent",), "attn_near": ("m2",), "m3": ("attn_other",),
    "in_back": ("m3_sent",), "attn_mine": ("gain_sum",), "gains": ("attn_mine",),
    "part_give": ("gains",), "m4": ("q1_sent",), "q2": ("m4_sent",), "tokens": ("q2_sent",),
    "q3": ("tokens",), "m_end": ("q3_sent",), "q4": ("m_end",),
}


def kernel_call(body, name, out_shape, args, smems=1, flops=0, nbytes=0, scratch=(), **extra):
    many = isinstance(out_shape, (list, tuple))
    return pl.pallas_call(
        body,
        in_specs=[smem()] * smems + [whole()] * (len(args) - smems),
        out_specs=[whole()] * len(out_shape) if many else whole(),
        out_shape=out_shape,
        scratch_shapes=list(scratch),
        compiler_params=pltpu.CompilerParams(vmem_limit_bytes=VMEM_LIMIT),
        cost_estimate=cost_of(name),
        name=name,
        **extra,
    )(*args)


def after(value, *others):
    return lax.optimization_barrier((value,) + others)[0]


def chip_of(place, size):
    if isinstance(place, int):
        return 2 * place if place < size // 2 else 2 * (size - 1 - place) + 1
    return jnp.where(place < size // 2, 2 * place, 2 * (size - 1 - place) + 1)


def ring_order(size):
    order = [size // 2]
    for step in range(size // 2 - 1, 0, -1):
        order += [step, -step]
    return order + [0]


def chip_lanes(ids_ref, width):
    size = width // LANES
    own = ids_ref[0] // 2
    here = jnp.where(own % 2 == 0, own // 2, size - 1 - own // 2)
    starts = [chip_of((here + step + size) % size, size) * LANES for step in ring_order(size)]
    return [pl.ds(pl.multiple_of(start, LANES), LANES) for start in starts]


def split_cores(ids_ref, ref, rows):
    places = chip_lanes(ids_ref, ref.shape[1])
    core = ids_ref[0] % 2
    own, other = [], []
    for i in range(0, len(places), 2):
        a, b = (ref[rows, place].astype(F32) for place in places[i : i + 2])
        low = lax.broadcasted_iota(jnp.int32, a.shape, 1) < LANES // 2
        first = jnp.where(low, a, pltpu.roll(b, LANES // 2, 1))
        second = jnp.where(low, pltpu.roll(a, LANES // 2, 1), b)
        own.append(jnp.where(core == 0, first, second))
        other.append(jnp.where(core == 0, second, first))
    return jnp.concatenate(own + other, axis=1)


def join_cores(ids_ref, values, out_ref, rows):
    places = chip_lanes(ids_ref, values.shape[1])
    core = ids_ref[0] % 2
    half = values.shape[1] // 2
    for i in range(0, len(places), 2):
        own = values[:, i * LANES // 2 : i * LANES // 2 + LANES]
        other = values[:, half + i * LANES // 2 : half + i * LANES // 2 + LANES]
        low = lax.broadcasted_iota(jnp.int32, own.shape, 1) < LANES // 2
        first = jnp.where(core == 0, own, other)
        second = jnp.where(core == 0, other, own)
        joined = (
            jnp.where(low, first, pltpu.roll(second, LANES // 2, 1)),
            jnp.where(low, pltpu.roll(first, LANES // 2, 1), second),
        )
        for place, part in zip(places[i : i + 2], joined):
            out_ref[rows, place] = part.astype(out_ref.dtype)


def norm_stats(values):
    centred = values - jnp.mean(values, axis=-1, keepdims=True)
    rstd = lax.rsqrt(jnp.mean(centred * centred, axis=-1, keepdims=True) + NORM_EPS)
    return centred * rstd, rstd


def norm_back(normed, rstd, scaled_grad):
    first = jnp.mean(scaled_grad, axis=-1, keepdims=True)
    second = jnp.mean(scaled_grad * normed, axis=-1, keepdims=True)
    return (scaled_grad - first - normed * second) * rstd


def fold_rows(values):
    return jnp.sum(values.reshape(-1, 8, values.shape[-1]), axis=0)


def lanes_at(start, count):
    return pl.ds(pl.multiple_of(start, LANES), count)


def from_features(left, w_refs, cols):
    total, start = None, 0
    for ref in w_refs:
        term = mm(left[:, start : start + ref.shape[0]], ref[:, cols], NN)
        total = term if total is None else total + term
        start += ref.shape[0]
    return total


def into_features(out_ref, rows, left, w_refs, cols):
    start = 0
    for ref in w_refs:
        part = mm(left, ref[:, cols], NT).astype(BF16)
        out_ref[rows, start : start + ref.shape[0]] = part
        start += ref.shape[0]


def row_steps(rows, body):
    @pl.loop(0, rows // STEP)
    def _(i):
        body(pl.ds(pl.multiple_of(i * STEP, STEP), STEP))


def prepare_kernel(ids_ref, x_ref, gain_ref, bias_ref, xp_ref, a1_ref, gp_ref, bp_ref):
    every = slice(0, gain_ref.shape[0])
    gp_ref[...] = split_cores(ids_ref, gain_ref, every)
    bp_ref[...] = split_cores(ids_ref, bias_ref, every)

    def body(at):
        x = split_cores(ids_ref, x_ref, at)
        xp_ref[at, :] = x.astype(BF16)
        normed, _ = norm_stats(x)
        a1_ref[at, :] = (normed * gp_ref[0:1, :] + bp_ref[0:1, :]).astype(BF16)

    row_steps(x_ref.shape[0], body)


def prepare(ids, x, gain, bias):
    return kernel_call(
        prepare_kernel,
        "prepare",
        [sds(x.shape, BF16), sds(x.shape, BF16), sds(gain.shape, F32), sds(bias.shape, F32)],
        (ids, x, gain, bias),
        nbytes=6 * x.size,
    )


def cotangent_kernel(ids_ref, own_ref, got_ref, out_ref):
    side = ids_ref[1]
    rows = own_ref.shape[0]
    for ref, base in ((own_ref, side * rows), (got_ref, (1 - side) * rows)):

        @pl.loop(0, rows // STEP)
        def _(i, ref=ref, base=base):
            at = pl.ds(pl.multiple_of(i * STEP, STEP), STEP)
            to = pl.ds(pl.multiple_of(base + i * STEP, STEP), STEP)
            out_ref[to, :] = split_cores(ids_ref, ref, at).astype(BF16)


def cotangent_rows(ids, own, got):
    rows, width = own.shape
    return kernel_call(
        cotangent_kernel, "cotangent_rows", sds((2 * rows, width), BF16), (ids, own, got),
        nbytes=8 * own.size,
    )


def partner(values):
    lane = lax.broadcasted_iota(jnp.int32, values.shape, 1)
    ahead = pltpu.roll(values, LANES - HD // 2, 1)
    behind = pltpu.roll(values, HD // 2, 1)
    return jnp.where(lax.rem(lane, HD) < HD // 2, ahead, behind)


def qkv_kernel(a_ref, cos_ref, sin_ref, *refs):
    w_refs, out_ref = refs[:-1], refs[-1]
    cols = w_refs[0].shape[1] // 4
    rows = 2 * BLOCK

    @pl.loop(0, a_ref.shape[0] // rows)
    def _(i):
        at = pl.ds(pl.multiple_of(i * rows, rows), rows)
        cos, sin = cos_ref[at, :], sin_ref[at, :]
        a = a_ref[at, :]
        for which in range(3):
            proj = from_features(a, w_refs, slice(which * cols, (which + 1) * cols))
            for start in range(0, cols, LANES):
                part = proj[:, start : start + LANES]
                if which < 2:
                    part = part * cos + partner(part) * sin
                if which == 0:
                    part = part.astype(BF16).astype(F32) * HD ** (-0.5)
                out_ref[at, which * cols + start : which * cols + start + LANES] = part.astype(BF16)


def qkv_project(a1, w, cos, sin):
    out = sds((a1.shape[0], w[0].shape[1] // 4 * 3), BF16)
    return kernel_call(qkv_kernel, "qkv_project", out, (a1, cos, sin, *w), smems=0)


def span_of(len_ref, block):
    start, size = jnp.int32(0), jnp.int32(0)
    for b in range(block + 1):
        here = len_ref[b]
        start = jnp.where(here > 0, b * BLOCK, start)
        size = jnp.where(here > 0, here, size)
    return start, start + size


def rotary_kernel(len_ref, cos_ref, sin_ref):
    lane = lax.broadcasted_iota(jnp.int32, (BLOCK, LANES), 1)
    row = lax.broadcasted_iota(jnp.int32, (BLOCK, LANES), 0)
    index = (lane % (HD // 2)).astype(F32)
    frequency = jnp.exp(index * (-2.0 / HD * 9.210340371976184))
    back = lane % HD >= HD // 2
    for b in range(cos_ref.shape[0] // BLOCK):
        start, _ = span_of(len_ref, b)
        angle = (row + (b * BLOCK - start)).astype(F32) * frequency
        sin = jnp.sin(angle)
        cos_ref[b * BLOCK : (b + 1) * BLOCK, :] = jnp.cos(angle)
        sin_ref[b * BLOCK : (b + 1) * BLOCK, :] = jnp.where(back, sin, -sin)


def rotary_pair(lengths, count):
    out = sds((count, LANES), F32)
    return kernel_call(rotary_kernel, "rotary", [out, out], (lengths,))


def head_lanes(rows, first):
    lane = lax.broadcasted_iota(jnp.int32, (rows, LANES), 1)
    return (lane < HD) == first


def attend_kernel(row0, len_ref, q_ref, *refs):
    w_refs, (p_ref, o_ref, part_ref) = refs[:-3], refs[-3:]
    rows, cols = o_ref.shape
    ext = p_ref.shape[2]
    key = lax.broadcasted_iota(jnp.int32, (BLOCK, ext), 1)
    query = lax.broadcasted_iota(jnp.int32, (BLOCK, ext), 0)
    masks = []
    for b in range(rows // BLOCK):
        lo, hi = span_of(len_ref, row0 // BLOCK + b)
        seen = (key >= lo) & (key < hi) & (key <= query + (row0 + b * BLOCK))
        masks.append(jnp.where(seen, 0.0, MASK_FILL))
    mask = jnp.concatenate(masks, axis=0)
    head = 0
    for start in range(0, cols, LANES):
        q = q_ref[row0 : row0 + rows, start : start + LANES]
        k = q_ref[0:ext, cols + start : cols + start + LANES]
        v = q_ref[0:ext, 2 * cols + start : 2 * cols + start + LANES]
        outs = []
        for first in (True, False):
            mine = head_lanes(rows, first)
            s = mm(jnp.where(mine, q, jnp.zeros_like(q)), k, NT) + mask
            e = jnp.exp(s - jnp.max(s, axis=-1, keepdims=True))
            p = (e * (1.0 / jnp.sum(e, axis=-1, keepdims=True))).astype(BF16)
            p_ref[head] = p
            head += 1
            outs.append(mm(p, v, NN))
        o_ref[:, start : start + LANES] = jnp.where(
            head_lanes(rows, True), outs[0], outs[1]
        ).astype(BF16)
    into_features(part_ref, slice(None), o_ref[...], w_refs, slice(3 * cols, 4 * cols))


def attend(row0, rows, lengths, qkv, w):
    ext = row0 + rows
    cols = qkv.shape[1] // 3
    width = sum(piece.shape[0] for piece in w)
    return kernel_call(
        functools.partial(attend_kernel, row0),
        "attend0" if row0 == 0 else "attend1",
        [sds((cols // HD, rows, ext), BF16), sds((rows, cols), BF16), sds((rows, width), BF16)],
        (lengths, qkv, *w),
    )


def hidden_of(x, ya, yb, gain_ref, bias_ref):
    n1, r1 = norm_stats(ya.astype(F32) + yb.astype(F32))
    return x.astype(F32) + n1 * gain_ref[1:2, :] + bias_ref[1:2, :], n1, r1


def chunk_rows(chunk, rows, at):
    return pl.ds(pl.multiple_of(chunk * rows + at.start, STEP), STEP)


UNITS = 512


def mid_norm_kernel(chunk, x_ref, ya_ref, yb_ref, gain_ref, bias_ref, a3_ref):
    rows = a3_ref.shape[0]

    def body(at):
        x = x_ref[chunk_rows(chunk, rows, at), :]
        h, _, _ = hidden_of(x, ya_ref[at, :], yb_ref[at, :], gain_ref, bias_ref)
        n2, _ = norm_stats(h)
        a3_ref[at, :] = (n2 * gain_ref[2:3, :] + bias_ref[2:3, :]).astype(BF16)

    row_steps(rows, body)


def mid_norm(chunk, x, ya, yb, gain, bias):
    body = functools.partial(mid_norm_kernel, chunk)
    return kernel_call(body, "mid_norm", sds(ya.shape, BF16), (x, ya, yb, gain, bias), smems=0)


def up_kernel(a3_ref, *refs):
    w_refs, (g_ref, gp_ref) = refs[:-2], refs[-2:]

    @pl.loop(0, w_refs[0].shape[1] // UNITS)
    def _(i):
        to = pl.ds(pl.multiple_of(i * UNITS, UNITS), UNITS)
        u = from_features(a3_ref[...], w_refs, to)
        k0 = 0.7978845608028654
        k1 = 0.044715
        sq = u * u
        th = jnp.tanh(u * (k0 + (k0 * k1) * sq))
        plus = 0.5 + 0.5 * th
        g_ref[:, to] = (u * plus).astype(BF16)
        slope = plus + (u * (k0 + (3.0 * k0 * k1) * sq)) * (0.5 - (0.5 * th) * th)
        gp_ref[:, to] = slope.astype(BF16)


def up_project(a3, w):
    out = sds((a3.shape[0], w[0].shape[1]), BF16)
    return kernel_call(up_kernel, "up_project", [out, out], (a3, *w), smems=0)


def down_kernel(g_ref, *refs):
    into_features(refs[-1], slice(None), g_ref[...], refs[:-1], slice(None))


def down_project(g, w):
    out = sds((g.shape[0], sum(piece.shape[0] for piece in w)), BF16)
    return kernel_call(down_kernel, "down_project", out, (g, *w), smems=0)


def mlp_back_kernel(
    chunk, ids_ref, x_ref, ya_ref, yb_ref, za_ref, zb_ref, cot_ref, gain_ref, bias_ref, gp_ref,
    *refs
):
    out_ref, dz_ref, du_ref, part_ref, gb_ref = refs[-5:]
    pieces = (len(refs) - 5) // 2
    w3, w2 = refs[:pieces], refs[pieces : 2 * pieces]
    rows = za_ref.shape[0]
    gb_ref[...] = jnp.zeros_like(gb_ref)

    def body(at):
        far = chunk_rows(chunk, rows, at)
        h, _, _ = hidden_of(x_ref[far, :], ya_ref[at, :], yb_ref[at, :], gain_ref, bias_ref)
        n3, r3 = norm_stats(za_ref[at, :].astype(F32) + zb_ref[at, :].astype(F32))
        cot = cot_ref[far, :].astype(F32)
        gain = gain_ref[3:4, :]
        out = h + (n3 * gain + bias_ref[3:4, :])
        if chunk == 0:
            join_cores(ids_ref, out, out_ref, at)
        else:

            @pl.when(ids_ref[1] == chunk)
            def _():
                join_cores(ids_ref, out, out_ref, at)

            @pl.when(ids_ref[1] != chunk)
            def _():
                out_ref[at, :] = refs[-6][at, :]

        dz_ref[at, :] = norm_back(n3, r3, cot * gain).astype(BF16)
        gb_ref[0] += fold_rows(cot * n3)
        gb_ref[1] += fold_rows(cot)

    row_steps(rows, body)

    @pl.loop(0, w3[0].shape[1] // UNITS)
    def _(i):
        to = pl.ds(pl.multiple_of(i * UNITS, UNITS), UNITS)
        dg = from_features(dz_ref[...], w3, to)
        du_ref[:, to] = (dg * gp_ref[:, to].astype(F32)).astype(BF16)

    into_features(part_ref, slice(None), du_ref[...], w2, slice(None))


def mlp_back(chunk, ids, x, ya, yb, za, zb, cot, gain, bias, gp, w3, w2, before=()):
    rows, width = za.shape
    units = w3[0].shape[1]
    return kernel_call(
        functools.partial(mlp_back_kernel, chunk),
        "mlp_back",
        [
            sds((rows, width), BF16),
            sds((rows, width), BF16),
            sds((rows, units), BF16),
            sds((rows, width), BF16),
            sds((2, 8, width), F32),
        ],
        (ids, x, ya, yb, za, zb, cot, gain, bias, gp, *w3, *w2, *before),
        flops=4 * rows * width * units,
    )


def weight_grad_kernel(which, sizes, *refs):
    far_ref, near_ref, left_sc = refs[-3:]
    half, block = left_sc.shape[0], far_ref.shape[0]
    start = 0
    for lefts, rights, cols in sizes:
        rows = 0
        for ref in refs[lefts[0] : lefts[1]]:
            part = ref[:, which * half : (which + 1) * half]
            left_sc[:, rows : rows + part.shape[0]] = part.T
            rows += part.shape[0]
        for c in range(0, cols, UNITS):
            total, rows = None, 0
            for ref in refs[rights[0] : rights[1]]:
                n = ref.shape[0]
                term = mm(left_sc[:, rows : rows + n], ref[:, c : c + UNITS], NN)
                total = term if total is None else total + term
                rows += n
            total = total.astype(BF16)
            far_ref[:, start + c : start + c + UNITS] = total[:block]
            near_ref[:, start + c : start + c + UNITS] = total[block:]
        start += cols


def weight_grad(which, size, products):
    args, sizes, total = [], [], 0
    for lefts, rights in products:
        cols = rights[0].shape[1]
        n = len(args)
        sizes.append(((n, n + len(lefts)), (n + len(lefts), n + len(lefts) + len(rights)), cols))
        args += list(lefts) + list(rights)
        total += cols
    half = args[0].shape[1] // 2
    count = sum(a.shape[0] for a in products[0][0])
    block = half // size
    return kernel_call(
        functools.partial(weight_grad_kernel, which, sizes),
        "weight_grad",
        [sds((block, total), BF16), sds((half - block, total), BF16)],
        tuple(args),
        smems=0,
        scratch=[pltpu.VMEM((half, count), BF16)],
    )


def mid_back_kernel(
    chunk, x_ref, ya_ref, yb_ref, ea_ref, eb_ref, cot_ref, gain_ref, bias_ref, *refs
):
    w_refs, (dh_ref, dy_ref, do_ref, gb_ref) = refs[:-4], refs[-4:]
    rows, cols = do_ref.shape
    gb_ref[...] = jnp.zeros_like(gb_ref)

    def body(at):
        far = chunk_rows(chunk, rows, at)
        h, n1, r1 = hidden_of(x_ref[far, :], ya_ref[at, :], yb_ref[at, :], gain_ref, bias_ref)
        n2, r2 = norm_stats(h)
        e = ea_ref[at, :].astype(F32) + eb_ref[at, :].astype(F32)
        dh = cot_ref[far, :].astype(F32) + norm_back(n2, r2, e * gain_ref[2:3, :])
        dh_ref[at, :] = dh
        dy_ref[at, :] = norm_back(n1, r1, dh * gain_ref[1:2, :]).astype(BF16)
        gb_ref[0] += fold_rows(e * n2)
        gb_ref[1] += fold_rows(e)
        gb_ref[2] += fold_rows(dh * n1)
        gb_ref[3] += fold_rows(dh)

    row_steps(rows, body)
    do = from_features(dy_ref[...], w_refs, slice(3 * cols, 4 * cols))
    do_ref[...] = do.astype(BF16)


def mid_back(chunk, x, ya, yb, ea, eb, cot, gain, bias, w):
    rows, width = ea.shape
    cols = w[0].shape[1] // 4
    return kernel_call(
        functools.partial(mid_back_kernel, chunk),
        "mid_back",
        [
            sds((rows, width), F32),
            sds((rows, width), BF16),
            sds((rows, cols), BF16),
            sds((4, 8, width), F32),
        ],
        (x, ya, yb, ea, eb, cot, gain, bias, *w),
        smems=0,
        flops=2 * rows * width * cols,
    )


def attend_back_kernel(q_ref, p0_ref, p1_ref, o0, o1, d0, d1, cos_ref, sin_ref, g_ref):
    rows, cols = o0.shape

    @pl.loop(0, cols // LANES)
    def _(i):
        cos, sin = cos_ref[...], sin_ref[...]
        start = i * LANES
        at = lanes_at(start, LANES)
        q = q_ref[:, at]
        k = q_ref[:, lanes_at(cols + start, LANES)]
        v = q_ref[:, lanes_at(2 * cols + start, LANES)]
        do = (d0[:, at], d1[:, at])
        prod = [a.astype(F32) * b[:, at].astype(F32) for a, b in zip(do, (o0, o1))]
        dq, dk, dv = [], [], []
        for turn, first in enumerate((True, False)):
            mine = head_lanes(rows, first)
            dqs = []
            for c, p_ref in enumerate((p0_ref, p1_ref)):
                ext = p_ref.shape[2]
                p = p_ref[2 * i + turn]
                dp = mm(jnp.where(mine, do[c], jnp.zeros_like(do[c])), v[:ext], NT)
                dot = jnp.sum(jnp.where(mine, prod[c], 0.0), axis=-1, keepdims=True)
                ds = (p.astype(F32) * (dp - dot)).astype(BF16)
                dqs.append(mm(ds, k[:ext], NN))
                dkc = mm(ds, q[c * rows : (c + 1) * rows], TN)
                dvc = mm(p, do[c], TN)
                if c == 0:
                    dk0, dv0 = dkc, dvc
            dk.append(jnp.concatenate([dk0 + dkc[:rows], dkc[rows:]], axis=0))
            dv.append(jnp.concatenate([dv0 + dvc[:rows], dvc[rows:]], axis=0))
            dq.append(jnp.concatenate(dqs, axis=0))
        low = head_lanes(2 * rows, True)
        gq = jnp.where(low, dq[0], dq[1]) * HD ** (-0.5)
        gk = jnp.where(low, dk[0], dk[1])
        gv = jnp.where(low, dv[0], dv[1])
        g_ref[:, at] = (gq * cos - partner(gq) * sin).astype(BF16)
        g_ref[:, lanes_at(cols + start, LANES)] = (gk * cos - partner(gk) * sin).astype(BF16)
        g_ref[:, lanes_at(2 * cols + start, LANES)] = gv.astype(BF16)


def attend_back(qkv, probs, outs, grads, cos, sin):
    count, three = qkv.shape
    heads = probs[0].shape[0]
    return kernel_call(
        attend_back_kernel,
        "attend_back",
        sds((count, three), BF16),
        (qkv, *probs, *outs, *grads, cos, sin),
        smems=0,
        flops=10 * heads * count * count * HD,
    )


def in_back_kernel(ids_ref, g_ref, x_ref, *refs):
    w_refs, (keep_ref, give_ref, gb_ref) = refs[:-3], refs[-3:]
    three = g_ref.shape[1]
    rows = keep_ref.shape[0]
    gb_ref[...] = jnp.zeros_like(gb_ref)
    for turn, out_ref in enumerate((give_ref, keep_ref)):
        base = (1 - ids_ref[1] if turn == 0 else ids_ref[1]) * rows
        g = g_ref[pl.ds(pl.multiple_of(base, rows), rows), :]
        into_features(out_ref, slice(None), g, w_refs, slice(0, three))

        @pl.loop(0, rows // STEP)
        def _(i, base=base, out_ref=out_ref):
            e = out_ref[pl.ds(pl.multiple_of(i * STEP, STEP), STEP), :].astype(F32)
            far = pl.ds(pl.multiple_of(base + i * STEP, STEP), STEP)
            n0, _ = norm_stats(x_ref[far, :].astype(F32))
            gb_ref[0] += fold_rows(e * n0)
            gb_ref[1] += fold_rows(e)


def in_back(ids, g, x, w):
    count, three = g.shape
    width = x.shape[1]
    part = sds((count // 2, width), BF16)
    return kernel_call(
        in_back_kernel, "in_back", [part, part, sds((2, 8, width), F32)], (ids, g, x, *w),
    )


def gain_sum_kernel(gb0_ref, g12a, g12b, g3a, g3b, mine_ref, other_ref):
    share = 0.5
    rows = []
    for kind in range(2):
        rows += [
            gb0_ref[kind],
            share * (g12a[2 + kind] + g12b[2 + kind]),
            share * (g12a[kind] + g12b[kind]),
            share * (g3a[kind] + g3b[kind]),
        ]
    half = mine_ref.shape[1]
    for i, row in enumerate(rows):
        row = jnp.sum(row, axis=0, keepdims=True)
        mine_ref[i : i + 1, :] = row[:, :half]
        other_ref[i : i + 1, :] = row[:, half:]


def gain_sum(gb0, g12, g3):
    out = sds((8, gb0.shape[-1] // 2), F32)
    return kernel_call(gain_sum_kernel, "gain_pack", [out, out], (gb0, *g12, *g3), smems=0)


def gain_pack_kernel(*refs):
    out_ref = refs[-1]
    total = refs[0][...] + refs[1][...] + refs[2][...] + refs[3][...]
    filler = jnp.zeros((LANES - total.shape[0], total.shape[1]), F32)
    out_ref[...] = jnp.concatenate([total, filler], axis=0).T.astype(BF16)


def gain_pack(parts):
    out = sds((parts[0].shape[1], LANES), BF16)
    return kernel_call(gain_pack_kernel, "gain_pack", out, tuple(parts), smems=0)


def tokens_back_kernel(ids_ref, x_ref, keep_ref, got_ref, dh0_ref, dh1_ref, gain_ref, out_ref):
    side = ids_ref[1]
    rows = got_ref.shape[0]

    def body(at):
        far = pl.ds(pl.multiple_of(side * rows + at.start, STEP), STEP)
        e = keep_ref[at, :].astype(F32) + got_ref[at, :].astype(F32)
        n0, r0 = norm_stats(x_ref[far, :].astype(F32))
        dh = jnp.where(side == 0, dh0_ref[at, :], dh1_ref[at, :])
        join_cores(ids_ref, dh + norm_back(n0, r0, e * gain_ref[0:1, :]), out_ref, at)

    row_steps(rows, body)


def tokens_back(ids, x, keep, got, dhs, gain):
    return kernel_call(
        tokens_back_kernel, "tokens_back", sds(got.shape, F32), (ids, x, keep, got, *dhs, gain),
    )


def split_kernel(up_ref, down_ref, up_out, down_out):
    half = up_out.shape[0]
    up_out[...] = up_ref[:half, :]
    down_out[...] = down_ref[half:, :]


def split(up, down):
    out = sds((up.shape[0] // 2, up.shape[1]), BF16)
    return kernel_call(split_kernel, "split", [out, out], (up, down), smems=0)


def stage_kernel(*refs):
    ins, out_ref, sem = refs[:-2], refs[-2], refs[-1]
    copies, start = [], 0
    for ref in ins:
        parts = [ref.at[i] for i in range(ref.shape[0])] if len(ref.shape) == 3 else [ref]
        for part in parts:
            cols = part.shape[1]
            dst = out_ref.at[:, pl.ds(start, cols)]
            copies.append(pltpu.make_async_copy(part, dst, sem.at[len(copies)]))
            start += cols
    for copy in copies:
        copy.start()
    for copy in copies:
        copy.wait()


def stage(*arrays):
    rows = arrays[0].shape[-2]
    cols = sum(a.size // rows for a in arrays)
    return pl.pallas_call(
        stage_kernel,
        in_specs=[pl.BlockSpec(memory_space=pltpu.HBM)] * len(arrays),
        out_specs=whole(),
        out_shape=sds((rows, cols), BF16),
        scratch_shapes=[pltpu.SemaphoreType.DMA((4 * len(arrays),))],
        compiler_params=pltpu.CompilerParams(vmem_limit_bytes=VMEM_LIMIT),
        cost_estimate=cost_of("stage"),
        name="stage",
    )(*arrays)


def assemble_kernel(places, *refs):
    ins, out, sem = refs[: len(places)], refs[-2], refs[-1]
    copies = []
    for i, (src, at) in enumerate(zip(ins, places)):
        copies.append(pltpu.make_async_copy(src, out.at[pl.ds(at, src.shape[0])], sem.at[i]))
    for copy in copies:
        copy.start()
    for copy in copies:
        copy.wait()


def assemble(places, pieces):
    rows = sum(piece.shape[0] for piece in pieces)
    return pl.pallas_call(
        functools.partial(assemble_kernel, places),
        in_specs=[anywhere()] * len(pieces),
        out_specs=whole(),
        out_shape=sds((rows, pieces[0].shape[1]), BF16),
        scratch_shapes=[pltpu.SemaphoreType.DMA((len(pieces),))],
        compiler_params=pltpu.CompilerParams(vmem_limit_bytes=VMEM_LIMIT),
        cost_estimate=cost_of("assemble"),
        name="assemble",
    )(*pieces)


def term_rows(groups, block, index, to):
    total = None
    for refs in groups:
        if len(refs) == 2:
            ref, first = (refs[0], 0) if index == 0 else (refs[1], (index - 1) * block)
        else:
            ref, first = refs[0], index * block
        part = ref[first : first + block, to].astype(F32)
        total = part if total is None else total + part
    return total


def unflatten(refs, layout):
    groups, n = [], 0
    for terms in layout:
        group = []
        for count in terms:
            group.append(refs[n : n + count])
            n += count
        groups.append(group)
    return groups, refs[n:]


def ring_sum_kernel(layout, block, index, *refs):
    groups, refs = unflatten(refs, layout)
    outs, came = refs[-2:], refs[:-2]
    half = block // 2
    start = 0
    for g, group in enumerate(groups):
        cols = group[0][0].shape[1]
        for c in range(0, cols, UNITS):
            n = min(UNITS, cols - c)
            own, to = slice(c, c + n), slice(start + c, start + c + n)
            if index == 0:
                total = sum(term[0][0:block, own].astype(F32) for term in group)
                outs[0][:, to] = total[:half].astype(BF16)
                outs[1][:, to] = total[half:].astype(BF16)
                continue
            for way in range(2):
                total = term_rows(group, block, index + way, own)
                if len(came) == 2:
                    part = came[way][:, to].astype(F32)
                else:
                    part = came[2 * g + way][:, own].astype(F32)
                if part.shape[0] == block:
                    outs[way][:, to] = (total + part).astype(BF16)
                else:
                    hit = slice(0, half) if way == 0 else slice(half, block)
                    rest = slice(half, block) if way == 0 else slice(0, half)
                    outs[way][hit, to] = (total[hit] + part).astype(BF16)
                    outs[way][rest, to] = total[rest].astype(BF16)
        start += cols


def ring_sum(index, block, groups, came=()):
    layout = [[len(term) for term in group] for group in groups]
    flat = [a for group in groups for term in group for a in term]
    cols = sum(group[0][0].shape[1] for group in groups)
    out = sds((block // 2 if index == 0 else block, cols), BF16)
    return kernel_call(
        functools.partial(ring_sum_kernel, layout, block, index), "ring_sum", [out, out],
        (*flat, *came), smems=0,
    )


def ring_end_kernel(layout, splits, index, *refs):
    groups, refs = unflatten(refs, layout)
    (up, down), outs = refs[:2], refs[2:]
    block = up.shape[0]
    start, o = 0, 0
    for group, sizes in zip(groups, splits):
        here = 0
        for count, cols in sizes:
            for i in range(max(count, 1)):
                to, own = slice(start, start + cols), slice(here, here + cols)
                total = term_rows(group, block, index, own)
                total = total + up[:, to].astype(F32) + down[:, to].astype(F32)
                if count == 0:
                    turned = total.T
                    outs[o][...] = turned[0:4, :]
                    outs[o + 1][...] = turned[4:8, :]
                elif count > 1:
                    outs[o][i] = total
                else:
                    outs[o][...] = total
                start, here = start + cols, here + cols
            o += 2 if count == 0 else 1


def ring_end(size, groups, came, splits):
    layout = [[len(term) for term in group] for group in groups]
    flat = [a for group in groups for term in group for a in term]
    block = came[0].shape[0]
    shapes = []
    for sizes in splits:
        for count, cols in sizes:
            if count == 0:
                shapes += [(4, block)] * 2
            else:
                shapes.append((count, block, cols) if count > 1 else (block, cols))
    return kernel_call(
        functools.partial(ring_end_kernel, layout, splits, size - 1), "ring_end",
        [sds(shape, F32) for shape in shapes], (*flat, *came), smems=0,
    )


class Ring:
    def __init__(self, n_dp, ids):
        self.size = n_dp // 2
        self.ids = ids
        self.up = self.shift(1)
        self.down = self.shift(-1)
        self.cores = [(i, i ^ 1) for i in range(n_dp)]

    def shift(self, by):
        return [
            (2 * chip_of(p, self.size) + c, 2 * chip_of((p + by) % self.size, self.size) + c)
            for p in range(self.size)
            for c in range(2)
        ]


def swap_cores(ring, value):
    return lax.ppermute(value, "dp", ring.cores)


class Gather:
    def __init__(self, ring, piece):
        self.ring = ring
        self.rows = piece.shape[0]
        self.pieces, self.places = [piece], [ring_order(ring.size).index(0) * self.rows]
        self.step_now = 0
        self.up = self.down = piece

    def step(self, *deps):
        self.step_now += 1
        ring, step = self.ring, self.step_now
        up, down = self.up, self.down
        if deps:
            up, down = after(up, *deps), after(down, *deps)
        shift = 0
        if step == ring.size // 2:
            shift = up.shape[0] // 2
            up, down = split(up, down)
            self.sent = up, down
        self.up = lax.ppermute(up, "dp", ring.up)
        self.down = lax.ppermute(down, "dp", ring.down)
        self.pieces += [self.up, self.down]
        order = ring_order(ring.size)
        self.places += [
            order.index(step if shift else -step) * self.rows,
            order.index(step) * self.rows + shift,
        ]
        return self.up, self.down

    def end(self, *deps):
        pieces = self.pieces
        if deps:
            pieces = [after(pieces[0], *deps), *pieces[1:]]
        return assemble(self.places, pieces)


class Reduce:
    def __init__(self, ring, block, groups):
        self.ring, self.block, self.groups = ring, block, groups
        self.index = 0
        self.came = ()

    def step(self, *deps):
        groups = self.groups
        if deps:
            first = groups[0][0]
            groups = [[(after(first[0], *deps), *first[1:]), *groups[0][1:]], *groups[1:]]
        if self.index == 0:
            groups = [[(term[0],) for term in group] for group in groups]
        self.sent = ring_sum(self.index, self.block, groups, self.came)
        up, down = self.sent
        self.came = lax.ppermute(up, "dp", self.ring.up), lax.ppermute(down, "dp", self.ring.down)
        self.index += 2 if self.index else 1
        return self.came

    @classmethod
    def join(cls, *rings):
        first = rings[0]
        ring = cls(first.ring, first.block, [group for r in rings for group in r.groups])
        ring.index, ring.came = 1, tuple(value for r in rings for value in r.came)
        return ring

    def end(self, splits, *deps):
        came = self.came
        if deps:
            came = after(came[0], *deps), came[1]
        return ring_end(self.ring.size, self.groups, came, splits)


def per_device(n_dp, tokens, seq_lengths, ln_gain, ln_bias, w_qkv, w_out, w_up, w_down, cotangent):
    ids = jnp.stack([lax.axis_index("dp"), lax.axis_index("mp")]).astype(jnp.int32)
    ring = Ring(n_dp, ids)
    count, width = tokens.shape
    rows = count // 2
    w_rows, units = w_up.shape
    cols = w_out.shape[0]

    def swap_sides(value):
        return lax.ppermute(value, "mp", [(0, 1), (1, 0)])

    done = {}

    def dep(name):
        found = []
        for other in ORDER.get(name, ()):
            value = done[other]
            found += list(value) if isinstance(value, (tuple, list)) else [value]
        return found

    def tie(value, name):
        others = dep(name)
        return after(value, *others) if others else value

    def both(own, name):
        return [own, swap_cores(ring, tie(own, name))]

    g1 = Gather(ring, stage(after(w_qkv, ids), w_out.T))
    done["s11"] = g1.step()
    cot_got = done["cot_got"] = swap_sides(tie(cotangent, "cot_swap"))
    stage2, stage3 = stage(w_up), stage(w_down.T)
    done["stages"] = stage2, stage3
    done["s12"] = g1.step(*dep("s12"))
    x, a1, gain, bias = prepare(ids, tokens, ln_gain, ln_bias)
    done["a1"] = a1
    done["s13"] = g1.step(*dep("s13"))
    done["s14"] = g1.step(*dep("s14"))
    done["s14_sent"] = g1.sent
    g2 = Gather(ring, tie(stage2, "s21"))
    done["s21"] = g2.step()
    g3 = Gather(ring, tie(stage3, "s31"))
    done["s31"] = g3.step()
    own = done["own1"] = g1.end(*dep("own1"))
    w1 = both(own, "w1")
    cos, sin = rotary_pair(tie(seq_lengths, "rotary"), count)
    cot = done["cot"] = cotangent_rows(tie(ids, "cot"), cotangent, cot_got)
    done["s22"] = g2.step(*dep("s22"))
    qkv = done["qkv"] = qkv_project(tie(a1, "qkv"), w1, cos, sin)
    probs, outs, ys, a3s, mids, zs, backs, mid_backs = [], [], [], [], [], [], [], []
    for c in range(2):
        p, o, part = attend(c * rows, rows, tie(seq_lengths, f"attend{c}"), qkv, w1)
        probs.append(p)
        outs.append(o)
        done[f"part{c}"] = part
        if c == 0:
            ys.append((part, swap_sides(part)))
            done["y0"] = ys[0][1]
    done["s32"] = g3.step(*dep("s32"))
    done["s23"] = g2.step(*dep("s23"))
    ys.append((part, swap_sides(tie(part, "y1"))))
    done["y1"] = ys[1][1]
    done["s33"] = g3.step(*dep("s33"))
    done["s24"] = g2.step(*dep("s24"))
    own = done["own2"] = g2.end(*dep("own2"))
    w2 = both(own, "w2")
    a3s.append(mid_norm(0, tie(x, "norm0"), *ys[0], gain, bias))
    done["norm0"] = a3s[0]
    done["s34"] = g3.step(*dep("s34"))
    own = done["own3"] = g3.end(*dep("own3"))
    w3 = both(own, "w3")
    mids.append(up_project(tie(a3s[0], "up0"), w2))
    done["up0"] = mids[0][0]
    part = down_project(tie(mids[0][0], "down0"), w3)
    done["down0"] = part
    zs.append((part, swap_sides(part)))
    a3s.append(mid_norm(1, tie(x, "norm1"), *ys[1], gain, bias))
    done["norm1"] = a3s[1]
    mids.append(up_project(tie(a3s[1], "up1"), w2))
    done["up1"] = mids[1][0]
    part = down_project(tie(mids[1][0], "down1"), w3)
    done["down1"] = part
    zs.append((part, swap_sides(part)))
    for c in range(2):
        out, dz, du, part, gb = mlp_back(
            c, ids, tie(x, f"back{c}"), *ys[c], *zs[c], cot, gain, bias, mids[c][1], w3, w2,
            before=[b[0] for b in backs],
        )
        backs.append((out, dz, du, gb, (part, swap_sides(part))))
        done[f"back{c}"], done[f"da{c}"] = out, backs[c][4][1]
    output = backs[1][0]
    dzs, dus = [b[1] for b in backs], [b[2] for b in backs]
    gs = [m[0] for m in mids]

    def mid(c):
        w = mid_back(c, tie(x, f"mid{c}"), *ys[c], *backs[c][4], cot, gain, bias, w1)
        done[f"mid{c}"] = w[0]
        mid_backs.append(w)

    def grad(which, products, name):
        others = dep(name)
        if others:
            (lefts, rights), rest = products[0], products[1:]
            products = [([after(lefts[0], *others), *lefts[1:]], rights), *rest]
        term = weight_grad(which, ring.size, products)
        done[name] = term[0]
        return term

    def swap_term(term, name):
        far = swap_cores(ring, term[0])
        done[name + "_far"] = far
        return far, swap_cores(ring, after(term[1], far, *dep(name + "_near")))

    def ring_step(reduce, name):
        done[name] = reduce.step(*dep(name))
        done[name + "_sent"] = reduce.sent

    down_other = grad(1, [(dzs, gs)], "down_other")
    up_other = grad(1, [(a3s, dus)], "up_other")
    down_mine = grad(0, [(dzs, gs)], "down_mine")
    down_got = swap_term(down_other, "down")
    up_mine = grad(0, [(a3s, dus)], "up_mine")
    up_got = swap_term(up_other, "up")
    mlp_ring = Reduce(ring, w_rows, [[down_mine, down_got], [up_mine, up_got]])
    ring_step(mlp_ring, "m1")
    mid(0)
    ring_step(mlp_ring, "m2")
    mid(1)
    grads = [m[2] for m in mid_backs]
    g_qkv = done["g_qkv"] = attend_back(tie(qkv, "g_qkv"), probs, outs, grads, cos, sin)
    attn_products = [([a1], [g_qkv]), ([m[1] for m in mid_backs], outs)]
    attn_other = grad(1, attn_products, "attn_other")
    attn_got = swap_term(attn_other, "attn")
    ring_step(mlp_ring, "m3")
    part_keep, part_give, gb0 = in_back(ids, tie(g_qkv, "in_back"), x, w1)
    done["in_back"] = part_keep
    gain_mine, gain_other = gain_sum(gb0, [m[3] for m in mid_backs], [b[3] for b in backs])
    done["gain_sum"] = gain_mine
    gain_terms = [
        gain_mine,
        swap_cores(ring, gain_other),
        swap_sides(gain_mine),
        lax.ppermute(gain_other, ("dp", "mp"), [(i, i ^ 3) for i in range(2 * n_dp)]),
    ]
    attn_mine = grad(0, attn_products, "attn_mine")
    gains = gain_pack([tie(gain_terms[0], "gains"), *gain_terms[1:]])
    done["gains"] = gains
    part_got = done["part_got"] = swap_sides(tie(part_give, "part_give"))
    attn_ring = Reduce(ring, w_rows, [[attn_mine, attn_got], [(gains,)]])
    ring_step(attn_ring, "q1")
    ring_step(mlp_ring, "m4")
    ring_step(attn_ring, "q2")
    grad_tokens = done["tokens"] = tokens_back(
        tie(ids, "tokens"), x, part_keep, part_got, [m[0] for m in mid_backs], gain
    )
    ring_step(attn_ring, "q3")
    grad_down, grad_up = mlp_ring.end([[(1, units)], [(1, units)]], *dep("m_end"))
    done["m_end"] = grad_down
    ring_step(attn_ring, "q4")
    grad_qkv, grad_out, grad_gain, grad_bias = attn_ring.end([[(3, cols), (1, cols)], [(0, LANES)]])
    return output, grad_tokens, grad_qkv, grad_out.T, grad_up, grad_down.T, grad_gain, grad_bias


def layer_norm(values, norm_gain, norm_bias):
    average = jnp.mean(values, axis=-1, keepdims=True)
    centred = values - average
    variance = jnp.mean(centred * centred, axis=-1, keepdims=True)
    return centred * lax.rsqrt(variance + NORM_EPS) * norm_gain + norm_bias


def norm_pull(values, norm_gain, norm_bias, grad_result):
    result, puller = jax.vjp(layer_norm, values, norm_gain, norm_bias)
    return puller(grad_result)


def seq_layout(lengths, block_size):
    block_count = lengths.shape[0]
    block_ids = jnp.arange(block_count, dtype=jnp.int32)
    starts = lengths > 0
    earlier = starts[None, :] & (block_ids[None, :] <= block_ids[:, None])
    owners = jnp.max(jnp.where(earlier, block_ids[None, :], 0), axis=1)
    owner_len = jnp.sum(
        jnp.where(block_ids[None, :] == owners[:, None], lengths[None, :], 0), axis=1
    )
    places = jnp.arange(block_count * block_size, dtype=jnp.int32)
    tok_owner = jnp.repeat(owners, block_size)
    position = places - tok_owner * block_size
    is_valid = position < jnp.repeat(owner_len, block_size)
    allowed = (
        (tok_owner[:, None] == tok_owner[None, :])
        & (places[None, :] <= places[:, None])
        & is_valid[None, :]
    )
    return (position, allowed)


def rotary_tables(position, width):
    frequency = ROPE_BASE ** (-jnp.arange(width // 2, dtype=jnp.float32) * 2.0 / width)
    angles = position.astype(jnp.float32)[:, None] * frequency[None, :]
    return (jnp.cos(angles), jnp.sin(angles))


def rotate(values, cos_table, sin_table):
    half_width = values.shape[-1] // 2
    front_half = values[..., :half_width]
    back_half = values[..., half_width:]
    cos_part = cos_table[:, None, :]
    sin_part = sin_table[:, None, :]
    return jnp.concatenate(
        [
            front_half * cos_part - back_half * sin_part,
            back_half * cos_part + front_half * sin_part,
        ],
        axis=-1,
    )


def attention_scores(queries, keys_rot, allowed, scale):
    raw_scores = (
        jnp.einsum("hqd,hkd->hqk", queries, keys_rot, preferred_element_type=jnp.float32) * scale
    )
    return jnp.where(allowed[None, :, :], raw_scores, MASK_FILL)


def plain_device(tokens, seq_lengths, ln_gain, ln_bias, w_qkv, w_out, w_up, w_down, cotangent):
    full_qkv, full_out, full_up, full_down = (
        lax.all_gather(w_qkv, "dp", axis=1, tiled=True),
        lax.all_gather(w_out, "dp", axis=1, tiled=True),
        lax.all_gather(w_up, "dp", axis=0, tiled=True),
        lax.all_gather(w_down, "dp", axis=1, tiled=True),
    )
    tok_count = tokens.shape[0]
    shard_rows = cotangent.shape[0]
    row_start = lax.axis_index("mp") * shard_rows
    heads_here = full_out.shape[0] // HD
    scale = HD ** (-0.5)
    position, allowed = seq_layout(seq_lengths, BLOCK)
    cos_table, sin_table = rotary_tables(position, HD)

    def to_heads(values):
        return jnp.transpose(values.reshape(tok_count, heads_here, HD), (1, 0, 2))

    def from_heads(values):
        return jnp.transpose(values, (1, 0, 2)).reshape(tok_count, heads_here * HD)

    def rotated(values):
        return rotate(values.reshape(tok_count, heads_here, HD), cos_table, sin_table)

    inputs = tokens.astype(jnp.float32)
    normed_in = layer_norm(inputs, ln_gain[0], ln_bias[0]).astype(jnp.bfloat16)
    projected = jnp.einsum("td,cde->cte", normed_in, full_qkv, preferred_element_type=jnp.float32)
    queries = jnp.transpose(rotated(projected[0]), (1, 0, 2)).astype(jnp.bfloat16)
    keys_rot = jnp.transpose(rotated(projected[1]), (1, 0, 2)).astype(jnp.bfloat16)
    values_h = to_heads(projected[2]).astype(jnp.bfloat16)
    scores = attention_scores(queries, keys_rot, allowed, scale)
    top_score = jnp.max(scores, axis=-1, keepdims=True)
    expo = jnp.exp(scores - top_score)
    row_total = jnp.sum(expo, axis=-1, keepdims=True)
    probs = expo / row_total
    log_total = top_score + jnp.log(row_total)
    attended = jnp.einsum(
        "hqk,hkd->hqd", probs.astype(jnp.bfloat16), values_h, preferred_element_type=jnp.float32
    )
    mixed_heads = from_heads(attended).astype(jnp.bfloat16)
    attn_part = jnp.dot(mixed_heads, full_out, preferred_element_type=jnp.float32)
    attn_sum = lax.psum_scatter(
        attn_part.astype(jnp.bfloat16), "mp", scatter_dimension=0, tiled=True
    ).astype(jnp.float32)
    resid_in = lax.dynamic_slice_in_dim(inputs, row_start, shard_rows, 0)
    hidden_state = resid_in + layer_norm(attn_sum, ln_gain[1], ln_bias[1])
    normed_mid = layer_norm(hidden_state, ln_gain[2], ln_bias[2]).astype(jnp.bfloat16)
    mlp_input = lax.all_gather(normed_mid, "mp", axis=0, tiled=True)
    pre_act = jnp.dot(mlp_input, full_up, preferred_element_type=jnp.float32)
    act_low = jax.nn.gelu(pre_act, approximate=True).astype(jnp.bfloat16)
    mlp_part = jnp.dot(act_low, full_down, preferred_element_type=jnp.float32)
    mlp_sum = lax.psum_scatter(
        mlp_part.astype(jnp.bfloat16), "mp", scatter_dimension=0, tiled=True
    ).astype(jnp.float32)
    output = (hidden_state + layer_norm(mlp_sum, ln_gain[3], ln_bias[3])).astype(jnp.bfloat16)
    grad_result = cotangent.astype(jnp.float32)
    grad_mlp_sum, grad_gain3, grad_bias3 = norm_pull(mlp_sum, ln_gain[3], ln_bias[3], grad_result)
    grad_mlp_rows = lax.all_gather(grad_mlp_sum.astype(jnp.bfloat16), "mp", axis=0, tiled=True)
    grad_down = jnp.einsum("tf,te->fe", act_low, grad_mlp_rows, preferred_element_type=jnp.float32)
    grad_act = jnp.einsum("te,fe->tf", grad_mlp_rows, full_down, preferred_element_type=jnp.float32)
    gelu_puller = jax.vjp(lambda values: jax.nn.gelu(values, approximate=True), pre_act)[1]
    grad_pre = gelu_puller(grad_act)[0].astype(jnp.bfloat16)
    grad_up = jnp.einsum("td,tf->df", mlp_input, grad_pre, preferred_element_type=jnp.float32)
    grad_mid_part = jnp.einsum("tf,df->td", grad_pre, full_up, preferred_element_type=jnp.float32)
    grad_mid = lax.psum_scatter(
        grad_mid_part.astype(jnp.bfloat16), "mp", scatter_dimension=0, tiled=True
    ).astype(jnp.float32)
    grad_hidden_norm, grad_gain2, grad_bias2 = norm_pull(
        hidden_state, ln_gain[2], ln_bias[2], grad_mid
    )
    grad_hidden = grad_result + grad_hidden_norm
    grad_attn_sum, grad_gain1, grad_bias1 = norm_pull(attn_sum, ln_gain[1], ln_bias[1], grad_hidden)
    grad_attn_rows = lax.all_gather(grad_attn_sum.astype(jnp.bfloat16), "mp", axis=0, tiled=True)
    grad_outproj = jnp.einsum(
        "tc,te->ce", mixed_heads, grad_attn_rows, preferred_element_type=jnp.float32
    )
    grad_mixed = jnp.einsum(
        "te,ce->tc", grad_attn_rows, full_out, preferred_element_type=jnp.float32
    ).astype(jnp.bfloat16)
    grad_heads = to_heads(grad_mixed)
    again_scores = attention_scores(queries, keys_rot, allowed, scale)
    again_probs = jnp.exp(again_scores - log_total)
    grad_probs = jnp.einsum(
        "hqd,hkd->hqk", grad_heads, values_h, preferred_element_type=jnp.float32
    )
    grad_values = jnp.einsum(
        "hqk,hqd->hkd",
        again_probs.astype(jnp.bfloat16),
        grad_heads,
        preferred_element_type=jnp.float32,
    )
    row_dot = jnp.sum(again_probs * grad_probs, axis=-1, keepdims=True)
    grad_scores = (again_probs * (grad_probs - row_dot) * scale).astype(jnp.bfloat16)
    grad_q_rot = jnp.einsum(
        "hqk,hkd->hqd", grad_scores, keys_rot, preferred_element_type=jnp.float32
    )
    grad_k_rot = jnp.einsum(
        "hqk,hqd->hkd", grad_scores, queries, preferred_element_type=jnp.float32
    )
    zero_heads = jnp.zeros((tok_count, heads_here, HD), jnp.float32)
    unrotate = jax.vjp(lambda values: rotate(values, cos_table, sin_table), zero_heads)[1]
    grad_query = unrotate(jnp.transpose(grad_q_rot, (1, 0, 2)))[0].reshape(
        tok_count, heads_here * HD
    )
    grad_key = unrotate(jnp.transpose(grad_k_rot, (1, 0, 2)))[0].reshape(tok_count, heads_here * HD)
    grad_value = from_heads(grad_values)
    grad_proj = jnp.stack(
        [
            grad_query.astype(jnp.bfloat16),
            grad_key.astype(jnp.bfloat16),
            grad_value.astype(jnp.bfloat16),
        ]
    )
    grad_qkv = jnp.einsum("td,cte->cde", normed_in, grad_proj, preferred_element_type=jnp.float32)
    grad_in_part = jnp.einsum(
        "cte,cde->td", grad_proj, full_qkv, preferred_element_type=jnp.float32
    )
    grad_in = lax.psum_scatter(
        grad_in_part.astype(jnp.bfloat16), "mp", scatter_dimension=0, tiled=True
    ).astype(jnp.float32)
    grad_norm_in, grad_gain0, grad_bias0 = norm_pull(resid_in, ln_gain[0], ln_bias[0], grad_in)
    grad_tokens = grad_hidden + grad_norm_in
    gain_grads = jnp.stack([grad_gain0, grad_gain1, grad_gain2, grad_gain3])
    bias_grads = jnp.stack([grad_bias0, grad_bias1, grad_bias2, grad_bias3])
    gain_grads, bias_grads = (
        lax.psum(gain_grads.astype(jnp.bfloat16), "mp").astype(jnp.float32),
        lax.psum(bias_grads.astype(jnp.bfloat16), "mp").astype(jnp.float32),
    )
    grad_qkv, grad_outproj, grad_up, grad_down, gain_grads, bias_grads = (
        lax.psum_scatter(
            grad_qkv.astype(jnp.bfloat16), "dp", scatter_dimension=1, tiled=True
        ).astype(jnp.float32),
        lax.psum_scatter(
            grad_outproj.astype(jnp.bfloat16), "dp", scatter_dimension=1, tiled=True
        ).astype(jnp.float32),
        lax.psum_scatter(
            grad_up.astype(jnp.bfloat16), "dp", scatter_dimension=0, tiled=True
        ).astype(jnp.float32),
        lax.psum_scatter(
            grad_down.astype(jnp.bfloat16), "dp", scatter_dimension=1, tiled=True
        ).astype(jnp.float32),
        lax.psum_scatter(
            gain_grads.astype(jnp.bfloat16), "dp", scatter_dimension=1, tiled=True
        ).astype(jnp.float32),
        lax.psum_scatter(
            bias_grads.astype(jnp.bfloat16), "dp", scatter_dimension=1, tiled=True
        ).astype(jnp.float32),
    )
    return (output, grad_tokens, grad_qkv, grad_outproj, grad_up, grad_down, gain_grads, bias_grads)


def solution(mesh):
    placed = (
        P("dp", None),
        P("dp"),
        P(),
        P(),
        P(None, "dp", "mp"),
        P("mp", "dp"),
        P("dp", "mp"),
        P("mp", "dp"),
        P(("dp", "mp"), None),
    )
    n_dp, n_mp = mesh.shape["dp"], mesh.shape["mp"]

    def layer(tokens, *rest):
        if n_mp == 2 and tokens.shape[1] == n_dp * LANES // 2:
            return per_device(n_dp, tokens, *rest)
        return plain_device(tokens, *rest)

    return jax.shard_map(
        layer,
        mesh=mesh,
        in_specs=placed,
        out_specs=(
            P(("dp", "mp"), None),
            P(("dp", "mp"), None),
            P(None, "dp", "mp"),
            P("mp", "dp"),
            P("dp", "mp"),
            P("mp", "dp"),
            P(None, "dp"),
            P(None, "dp"),
        ),
        check_vma=False,
    )
```

```python
import functools

import jax
import jax.numpy as jnp
from jax import lax
from jax.experimental import pallas as pl
from jax.experimental.pallas import tpu as pltpu
from jax.sharding import PartitionSpec as P

HD = 64
BLOCK = 128
LANES = 128
NORM_EPS = 1e-05
ROPE_BASE = 10000.0
MASK_FILL = -1e30
F32 = jnp.float32
BF16 = jnp.bfloat16
VMEM_LIMIT = 6 * 1024 * 1024
STEP = 128
NN = (((1,), (0,)), ((), ()))
NT = (((1,), (1,)), ((), ()))
TN = (((0,), (0,)), ((), ()))


def mm(left, right, dims):
    return lax.dot_general(left, right, dims, preferred_element_type=F32)


def sds(shape, dtype):
    return jax.ShapeDtypeStruct(shape, dtype)


def whole():
    return pl.BlockSpec(memory_space=pltpu.VMEM)


def smem():
    return pl.BlockSpec(memory_space=pltpu.SMEM)


def anywhere():
    return pl.BlockSpec(memory_space=pl.ANY)


TIMES = {
    "prepare": 3.3, "cotangent_rows": 1.5, "qkv_project": 2.0, "attend0": 2.5, "attend1": 4.4,
    "up_project": 4.3, "down_project": 1.3, "mlp_back": 5.4, "mid_norm": 2.5, "last_norm": 3.0, "weight_grad": 1.3, "mid_back": 3.3,
    "attend_back": 5.0, "in_back": 3.6, "gain_pack": 0.4, "tokens_back": 3.9, "stage": 0.5,
    "assemble": 1.2, "ring_sum": 1.3, "ring_end": 2.0, "rotary": 2.0, "split": 0.4,
}
TIME_SHARE = 1.0


def cost_of(name):
    return pl.CostEstimate(
        flops=0, bytes_accessed=int(TIMES[name] * TIME_SHARE * 3.69e6), transcendentals=0
    )


ORDER = {
    "s12": ("stages",), "s13": ("a1",), "s14": ("cot_got",), "s21": ("s14_sent",), "s31": ("s14",),
    "cot_swap": ("s11",), "w1": ("s21",), "rotary": ("own1",), "cot": ("own1",), "s22": ("own1",),
    "qkv": ("cot",), "attend1": ("part0", "s31"), "s23": ("part1",), "s24": ("y0",),
    "norm0": ("own2",), "s34": ("own2", "y1"), "up1": ("down0",), "down1": ("down0",),
    "back1": ("back0",), "up_other": ("down_other",), "down_mine": ("up_other",),
    "up_mine": ("down_mine", "down_far"), "up_near": ("da0", "up_mine"), "mid0": ("m1_sent",),
    "last": ("mid0",), "m2": ("last",), "mid1": ("m2_sent",), "attn_near": ("m2",), "m3": ("attn_other",),
    "in_back": ("m3_sent",), "attn_mine": ("gain_sum",), "gains": ("attn_mine",),
    "part_give": ("gains",), "m4": ("q1_sent",), "q2": ("m4_sent",), "tokens": ("q2_sent",),
    "q3": ("tokens",), "m_end": ("q3_sent",), "q4": ("m_end",),
}


def kernel_call(body, name, out_shape, args, smems=1, flops=0, nbytes=0, scratch=(), **extra):
    many = isinstance(out_shape, (list, tuple))
    return pl.pallas_call(
        body,
        in_specs=[smem()] * smems + [whole()] * (len(args) - smems),
        out_specs=[whole()] * len(out_shape) if many else whole(),
        out_shape=out_shape,
        scratch_shapes=list(scratch),
        compiler_params=pltpu.CompilerParams(vmem_limit_bytes=VMEM_LIMIT),
        cost_estimate=cost_of(name),
        name=name,
        **extra,
    )(*args)


def after(value, *others):
    return lax.optimization_barrier((value,) + others)[0]


def chip_of(place, size):
    if isinstance(place, int):
        return 2 * place if place < size // 2 else 2 * (size - 1 - place) + 1
    return jnp.where(place < size // 2, 2 * place, 2 * (size - 1 - place) + 1)


def ring_order(size):
    order = [size // 2]
    for step in range(size // 2 - 1, 0, -1):
        order += [step, -step]
    return order + [0]


def chip_lanes(ids_ref, width):
    size = width // LANES
    own = ids_ref[0] // 2
    here = jnp.where(own % 2 == 0, own // 2, size - 1 - own // 2)
    starts = [chip_of((here + step + size) % size, size) * LANES for step in ring_order(size)]
    return [pl.ds(pl.multiple_of(start, LANES), LANES) for start in starts]


def split_cores(ids_ref, ref, rows):
    places = chip_lanes(ids_ref, ref.shape[1])
    core = ids_ref[0] % 2
    own, other = [], []
    for i in range(0, len(places), 2):
        a, b = (ref[rows, place].astype(F32) for place in places[i : i + 2])
        low = lax.broadcasted_iota(jnp.int32, a.shape, 1) < LANES // 2
        first = jnp.where(low, a, pltpu.roll(b, LANES // 2, 1))
        second = jnp.where(low, pltpu.roll(a, LANES // 2, 1), b)
        own.append(jnp.where(core == 0, first, second))
        other.append(jnp.where(core == 0, second, first))
    return jnp.concatenate(own + other, axis=1)


def join_cores(ids_ref, values, out_ref, rows):
    places = chip_lanes(ids_ref, values.shape[1])
    core = ids_ref[0] % 2
    half = values.shape[1] // 2
    for i in range(0, len(places), 2):
        own = values[:, i * LANES // 2 : i * LANES // 2 + LANES]
        other = values[:, half + i * LANES // 2 : half + i * LANES // 2 + LANES]
        low = lax.broadcasted_iota(jnp.int32, own.shape, 1) < LANES // 2
        first = jnp.where(core == 0, own, other)
        second = jnp.where(core == 0, other, own)
        joined = (
            jnp.where(low, first, pltpu.roll(second, LANES // 2, 1)),
            jnp.where(low, pltpu.roll(first, LANES // 2, 1), second),
        )
        for place, part in zip(places[i : i + 2], joined):
            out_ref[rows, place] = part.astype(out_ref.dtype)


def norm_stats(values):
    centred = values - jnp.mean(values, axis=-1, keepdims=True)
    rstd = lax.rsqrt(jnp.mean(centred * centred, axis=-1, keepdims=True) + NORM_EPS)
    return centred * rstd, rstd


def norm_back(normed, rstd, scaled_grad):
    first = jnp.mean(scaled_grad, axis=-1, keepdims=True)
    second = jnp.mean(scaled_grad * normed, axis=-1, keepdims=True)
    return (scaled_grad - first - normed * second) * rstd


def fold_rows(values):
    return jnp.sum(values.reshape(-1, 8, values.shape[-1]), axis=0)


def lanes_at(start, count):
    if isinstance(start, int):
        return slice(start, start + count)
    return pl.ds(pl.multiple_of(start, LANES), count)


def from_features(left, w_refs, cols):
    total, start = None, 0
    for ref in w_refs:
        term = mm(left[:, start : start + ref.shape[0]], ref[:, cols], NN)
        total = term if total is None else total + term
        start += ref.shape[0]
    return total


def into_features(out_ref, rows, left, w_refs, cols):
    start = 0
    for ref in w_refs:
        part = mm(left, ref[:, cols], NT).astype(BF16)
        out_ref[rows, start : start + ref.shape[0]] = part
        start += ref.shape[0]


def row_steps(rows, body):
    @pl.loop(0, rows // STEP)
    def _(i):
        body(pl.ds(pl.multiple_of(i * STEP, STEP), STEP))


def prepare_kernel(ids_ref, x_ref, gain_ref, bias_ref, xp_ref, a1_ref, gp_ref, bp_ref):
    every = slice(0, gain_ref.shape[0])
    gp_ref[...] = split_cores(ids_ref, gain_ref, every)
    bp_ref[...] = split_cores(ids_ref, bias_ref, every)

    def body(at):
        x = split_cores(ids_ref, x_ref, at)
        xp_ref[at, :] = x.astype(BF16)
        normed, _ = norm_stats(x)
        a1_ref[at, :] = (normed * gp_ref[0:1, :] + bp_ref[0:1, :]).astype(BF16)

    row_steps(x_ref.shape[0], body)


def prepare(ids, x, gain, bias):
    return kernel_call(
        prepare_kernel,
        "prepare",
        [sds(x.shape, BF16), sds(x.shape, BF16), sds(gain.shape, F32), sds(bias.shape, F32)],
        (ids, x, gain, bias),
        nbytes=6 * x.size,
    )


def cotangent_kernel(ids_ref, own_ref, got_ref, out_ref):
    side = ids_ref[1]
    rows = own_ref.shape[0]
    for ref, base in ((own_ref, side * rows), (got_ref, (1 - side) * rows)):

        @pl.loop(0, rows // STEP)
        def _(i, ref=ref, base=base):
            at = pl.ds(pl.multiple_of(i * STEP, STEP), STEP)
            to = pl.ds(pl.multiple_of(base + i * STEP, STEP), STEP)
            out_ref[to, :] = split_cores(ids_ref, ref, at).astype(BF16)


def cotangent_rows(ids, own, got):
    rows, width = own.shape
    return kernel_call(
        cotangent_kernel, "cotangent_rows", sds((2 * rows, width), BF16), (ids, own, got),
        nbytes=8 * own.size,
    )


def partner(values):
    lane = lax.broadcasted_iota(jnp.int32, values.shape, 1)
    ahead = pltpu.roll(values, LANES - HD // 2, 1)
    behind = pltpu.roll(values, HD // 2, 1)
    return jnp.where(lax.rem(lane, HD) < HD // 2, ahead, behind)


def qkv_kernel(a_ref, cos_ref, sin_ref, *refs):
    w_refs, out_ref = refs[:-1], refs[-1]
    cols = w_refs[0].shape[1] // 4
    rows = 2 * BLOCK

    @pl.loop(0, a_ref.shape[0] // rows)
    def _(i):
        at = pl.ds(pl.multiple_of(i * rows, rows), rows)
        cos, sin = cos_ref[at, :], sin_ref[at, :]
        a = a_ref[at, :]
        for which in range(3):
            proj = from_features(a, w_refs, slice(which * cols, (which + 1) * cols))
            for start in range(0, cols, LANES):
                part = proj[:, start : start + LANES]
                if which < 2:
                    part = part * cos + partner(part) * sin
                if which == 0:
                    part = part.astype(BF16).astype(F32) * HD ** (-0.5)
                out_ref[at, which * cols + start : which * cols + start + LANES] = part.astype(BF16)


def qkv_project(a1, w, cos, sin):
    out = sds((a1.shape[0], w[0].shape[1] // 4 * 3), BF16)
    return kernel_call(qkv_kernel, "qkv_project", out, (a1, cos, sin, *w), smems=0)


def span_of(len_ref, block):
    start, size = jnp.int32(0), jnp.int32(0)
    for b in range(block + 1):
        here = len_ref[b]
        start = jnp.where(here > 0, b * BLOCK, start)
        size = jnp.where(here > 0, here, size)
    return start, start + size


def rotary_kernel(len_ref, cos_ref, sin_ref):
    lane = lax.broadcasted_iota(jnp.int32, (BLOCK, LANES), 1)
    row = lax.broadcasted_iota(jnp.int32, (BLOCK, LANES), 0)
    index = (lane % (HD // 2)).astype(F32)
    frequency = jnp.exp(index * (-2.0 / HD * 9.210340371976184))
    back = lane % HD >= HD // 2
    blocks = cos_ref.shape[0] // BLOCK

    @pl.loop(0, blocks)
    def _(b):
        start = jnp.int32(0)
        for k in range(blocks):
            start = jnp.where((k <= b) & (len_ref[k] > 0), k * BLOCK, start)
        at = pl.ds(pl.multiple_of(b * BLOCK, BLOCK), BLOCK)
        angle = (row + (b * BLOCK - start)).astype(F32) * frequency
        sin = jnp.sin(angle)
        cos_ref[at, :] = jnp.cos(angle)
        sin_ref[at, :] = jnp.where(back, sin, -sin)


def rotary_pair(lengths, count):
    out = sds((count, LANES), F32)
    return kernel_call(rotary_kernel, "rotary", [out, out], (lengths,))


def head_lanes(rows, first):
    lane = lax.broadcasted_iota(jnp.int32, (rows, LANES), 1)
    return (lane < HD) == first


def attend_kernel(row0, len_ref, q_ref, *refs):
    w_refs, (p_ref, o_ref, part_ref) = refs[:-3], refs[-3:]
    rows, cols = o_ref.shape
    ext = p_ref.shape[2]
    key = lax.broadcasted_iota(jnp.int32, (BLOCK, ext), 1)
    query = lax.broadcasted_iota(jnp.int32, (BLOCK, ext), 0)
    masks = []
    for b in range(rows // BLOCK):
        lo, hi = span_of(len_ref, row0 // BLOCK + b)
        seen = (key >= lo) & (key < hi) & (key <= query + (row0 + b * BLOCK))
        masks.append(jnp.where(seen, 0.0, MASK_FILL))
    mask = jnp.concatenate(masks, axis=0)
    head = 0
    for start in range(0, cols, LANES):
        q = q_ref[row0 : row0 + rows, start : start + LANES]
        k = q_ref[0:ext, cols + start : cols + start + LANES]
        v = q_ref[0:ext, 2 * cols + start : 2 * cols + start + LANES]
        outs = []
        for first in (True, False):
            mine = head_lanes(rows, first)
            s = mm(jnp.where(mine, q, jnp.zeros_like(q)), k, NT) + mask
            e = jnp.exp(s - jnp.max(s, axis=-1, keepdims=True))
            p = (e * (1.0 / jnp.sum(e, axis=-1, keepdims=True))).astype(BF16)
            p_ref[head] = p
            head += 1
            outs.append(mm(p, v, NN))
        o_ref[:, start : start + LANES] = jnp.where(
            head_lanes(rows, True), outs[0], outs[1]
        ).astype(BF16)
    into_features(part_ref, slice(None), o_ref[...], w_refs, slice(3 * cols, 4 * cols))


def attend(row0, rows, lengths, qkv, w):
    ext = row0 + rows
    cols = qkv.shape[1] // 3
    width = sum(piece.shape[0] for piece in w)
    return kernel_call(
        functools.partial(attend_kernel, row0),
        "attend0" if row0 == 0 else "attend1",
        [sds((cols // HD, rows, ext), BF16), sds((rows, cols), BF16), sds((rows, width), BF16)],
        (lengths, qkv, *w),
    )


def hidden_of(x, ya, yb, gain_ref, bias_ref):
    n1, r1 = norm_stats(ya.astype(F32) + yb.astype(F32))
    return x.astype(F32) + n1 * gain_ref[1:2, :] + bias_ref[1:2, :], n1, r1


def chunk_rows(chunk, rows, at):
    return pl.ds(pl.multiple_of(chunk * rows + at.start, STEP), STEP)


UNITS = 512


def mid_norm_kernel(chunk, x_ref, ya_ref, yb_ref, gain_ref, bias_ref, a3_ref):
    rows = a3_ref.shape[0]

    def body(at):
        x = x_ref[chunk_rows(chunk, rows, at), :]
        h, _, _ = hidden_of(x, ya_ref[at, :], yb_ref[at, :], gain_ref, bias_ref)
        n2, _ = norm_stats(h)
        a3_ref[at, :] = (n2 * gain_ref[2:3, :] + bias_ref[2:3, :]).astype(BF16)

    row_steps(rows, body)


def mid_norm(chunk, x, ya, yb, gain, bias):
    body = functools.partial(mid_norm_kernel, chunk)
    return kernel_call(body, "mid_norm", sds(ya.shape, BF16), (x, ya, yb, gain, bias), smems=0)


def up_kernel(a3_ref, *refs):
    w_refs, (g_ref, gp_ref) = refs[:-2], refs[-2:]

    @pl.loop(0, w_refs[0].shape[1] // UNITS)
    def _(i):
        to = pl.ds(pl.multiple_of(i * UNITS, UNITS), UNITS)
        u = from_features(a3_ref[...], w_refs, to)
        k0 = 0.7978845608028654
        k1 = 0.044715
        sq = u * u
        th = jnp.tanh(u * (k0 + (k0 * k1) * sq))
        plus = 0.5 + 0.5 * th
        g_ref[:, to] = (u * plus).astype(BF16)
        slope = plus + (u * (k0 + (3.0 * k0 * k1) * sq)) * (0.5 - (0.5 * th) * th)
        gp_ref[:, to] = slope.astype(BF16)


def up_project(a3, w):
    out = sds((a3.shape[0], w[0].shape[1]), BF16)
    return kernel_call(up_kernel, "up_project", [out, out], (a3, *w), smems=0)


def down_kernel(g_ref, *refs):
    into_features(refs[-1], slice(None), g_ref[...], refs[:-1], slice(None))


def down_project(g, w):
    out = sds((g.shape[0], sum(piece.shape[0] for piece in w)), BF16)
    return kernel_call(down_kernel, "down_project", out, (g, *w), smems=0)


def mlp_back_kernel(chunk, za_ref, zb_ref, cot_ref, gain_ref, gp_ref, *refs):
    dz_ref, du_ref, part_ref = refs[-3:]
    pieces = (len(refs) - 3) // 2
    w3, w2 = refs[:pieces], refs[pieces : 2 * pieces]
    rows = za_ref.shape[0]

    def body(at):
        n3, r3 = norm_stats(za_ref[at, :].astype(F32) + zb_ref[at, :].astype(F32))
        cot = cot_ref[chunk_rows(chunk, rows, at), :].astype(F32)
        dz_ref[at, :] = norm_back(n3, r3, cot * gain_ref[3:4, :]).astype(BF16)

    row_steps(rows, body)

    @pl.loop(0, w3[0].shape[1] // UNITS)
    def _(i):
        to = pl.ds(pl.multiple_of(i * UNITS, UNITS), UNITS)
        dg = from_features(dz_ref[...], w3, to)
        du_ref[:, to] = (dg * gp_ref[:, to].astype(F32)).astype(BF16)

    into_features(part_ref, slice(None), du_ref[...], w2, slice(None))


def mlp_back(chunk, za, zb, cot, gain, gp, w3, w2):
    rows, width = za.shape
    units = gp.shape[1]
    return kernel_call(
        functools.partial(mlp_back_kernel, chunk),
        "mlp_back",
        [sds((rows, width), BF16), sds((rows, units), BF16), sds((rows, width), BF16)],
        (za, zb, cot, gain, gp, *w3, *w2),
        smems=0,
    )


def last_norm_kernel(ids_ref, x_ref, cot_ref, gain_ref, bias_ref, *refs):
    ys, zs, (out_ref, gb_ref) = refs[0:4], refs[4:8], refs[8:]
    rows = out_ref.shape[0]
    gb_ref[...] = jnp.zeros_like(gb_ref)
    for chunk in range(2):
        ya_ref, yb_ref = ys[2 * chunk : 2 * chunk + 2]
        za_ref, zb_ref = zs[2 * chunk : 2 * chunk + 2]

        def body(at, chunk=chunk, ya_ref=ya_ref, yb_ref=yb_ref, za_ref=za_ref, zb_ref=zb_ref):
            far = chunk_rows(chunk, rows, at)
            n3, _ = norm_stats(za_ref[at, :].astype(F32) + zb_ref[at, :].astype(F32))
            cot = cot_ref[far, :].astype(F32)
            gb_ref[0] += fold_rows(cot * n3)
            gb_ref[1] += fold_rows(cot)

            @pl.when(ids_ref[1] == chunk)
            def _():
                h, _, _ = hidden_of(x_ref[far, :], ya_ref[at, :], yb_ref[at, :], gain_ref, bias_ref)
                out = h + (n3 * gain_ref[3:4, :] + bias_ref[3:4, :])
                join_cores(ids_ref, out, out_ref, at)

        row_steps(rows, body)


def last_norm(ids, x, cot, gain, bias, ys, zs):
    rows, width = ys[0][0].shape
    return kernel_call(
        last_norm_kernel,
        "last_norm",
        [sds((rows, width), BF16), sds((2, 8, width), F32)],
        (ids, x, cot, gain, bias, *ys[0], *ys[1], *zs[0], *zs[1]),
    )


def weight_grad_kernel(which, sizes, *refs):
    far_ref, near_ref, left_sc = refs[-3:]
    half, block = left_sc.shape[0], far_ref.shape[0]
    start = 0
    for lefts, rights, cols in sizes:
        rows = 0
        for ref in refs[lefts[0] : lefts[1]]:
            part = ref[:, which * half : (which + 1) * half]
            left_sc[:, rows : rows + part.shape[0]] = part.T
            rows += part.shape[0]

        def blocks(first, count, rights=rights, start=start):
            for i in range(count):
                c = (first + i) * UNITS
                total, rows = None, 0
                for ref in refs[rights[0] : rights[1]]:
                    n = ref.shape[0]
                    term = mm(left_sc[:, rows : rows + n], ref[:, lanes_at(c, UNITS)], NN)
                    total = term if total is None else total + term
                    rows += n
                total = total.astype(BF16)
                far_ref[:, lanes_at(start + c, UNITS)] = total[:block]
                near_ref[:, lanes_at(start + c, UNITS)] = total[block:]

        pairs = cols // (2 * UNITS)
        if pairs > 1:
            pl.loop(0, pairs)(lambda i: blocks(2 * i, 2))
        else:
            blocks(0, cols // UNITS)
        start += cols


def weight_grad(which, size, products):
    args, sizes, total = [], [], 0
    for lefts, rights in products:
        cols = rights[0].shape[1]
        n = len(args)
        sizes.append(((n, n + len(lefts)), (n + len(lefts), n + len(lefts) + len(rights)), cols))
        args += list(lefts) + list(rights)
        total += cols
    half = args[0].shape[1] // 2
    count = sum(a.shape[0] for a in products[0][0])
    block = half // size
    return kernel_call(
        functools.partial(weight_grad_kernel, which, sizes),
        "weight_grad",
        [sds((block, total), BF16), sds((half - block, total), BF16)],
        tuple(args),
        smems=0,
        scratch=[pltpu.VMEM((half, count), BF16)],
    )


def mid_back_kernel(
    chunk, x_ref, ya_ref, yb_ref, ea_ref, eb_ref, cot_ref, gain_ref, bias_ref, *refs
):
    w_refs, (dh_ref, dy_ref, do_ref, gb_ref) = refs[:-4], refs[-4:]
    rows, cols = do_ref.shape
    gb_ref[...] = jnp.zeros_like(gb_ref)

    def body(at):
        far = chunk_rows(chunk, rows, at)
        h, n1, r1 = hidden_of(x_ref[far, :], ya_ref[at, :], yb_ref[at, :], gain_ref, bias_ref)
        n2, r2 = norm_stats(h)
        e = ea_ref[at, :].astype(F32) + eb_ref[at, :].astype(F32)
        dh = cot_ref[far, :].astype(F32) + norm_back(n2, r2, e * gain_ref[2:3, :])
        dh_ref[at, :] = dh
        dy_ref[at, :] = norm_back(n1, r1, dh * gain_ref[1:2, :]).astype(BF16)
        gb_ref[0] += fold_rows(e * n2)
        gb_ref[1] += fold_rows(e)
        gb_ref[2] += fold_rows(dh * n1)
        gb_ref[3] += fold_rows(dh)

    row_steps(rows, body)
    do = from_features(dy_ref[...], w_refs, slice(3 * cols, 4 * cols))
    do_ref[...] = do.astype(BF16)


def mid_back(chunk, x, ya, yb, ea, eb, cot, gain, bias, w):
    rows, width = ea.shape
    cols = w[0].shape[1] // 4
    return kernel_call(
        functools.partial(mid_back_kernel, chunk),
        "mid_back",
        [
            sds((rows, width), F32),
            sds((rows, width), BF16),
            sds((rows, cols), BF16),
            sds((4, 8, width), F32),
        ],
        (x, ya, yb, ea, eb, cot, gain, bias, *w),
        smems=0,
        flops=2 * rows * width * cols,
    )


def attend_back_kernel(q_ref, p0_ref, p1_ref, o0, o1, d0, d1, cos_ref, sin_ref, g_ref):
    rows, cols = o0.shape

    @pl.loop(0, cols // LANES)
    def _(i):
        cos, sin = cos_ref[...], sin_ref[...]
        start = i * LANES
        at = lanes_at(start, LANES)
        q = q_ref[:, at]
        k = q_ref[:, lanes_at(cols + start, LANES)]
        v = q_ref[:, lanes_at(2 * cols + start, LANES)]
        do = (d0[:, at], d1[:, at])
        prod = [a.astype(F32) * b[:, at].astype(F32) for a, b in zip(do, (o0, o1))]
        dq, dk, dv = [], [], []
        for turn, first in enumerate((True, False)):
            mine = head_lanes(rows, first)
            dqs = []
            for c, p_ref in enumerate((p0_ref, p1_ref)):
                ext = p_ref.shape[2]
                p = p_ref[2 * i + turn]
                dp = mm(jnp.where(mine, do[c], jnp.zeros_like(do[c])), v[:ext], NT)
                dot = jnp.sum(jnp.where(mine, prod[c], 0.0), axis=-1, keepdims=True)
                ds = (p.astype(F32) * (dp - dot)).astype(BF16)
                dqs.append(mm(ds, k[:ext], NN))
                dkc = mm(ds, q[c * rows : (c + 1) * rows], TN)
                dvc = mm(p, do[c], TN)
                if c == 0:
                    dk0, dv0 = dkc, dvc
            dk.append(jnp.concatenate([dk0 + dkc[:rows], dkc[rows:]], axis=0))
            dv.append(jnp.concatenate([dv0 + dvc[:rows], dvc[rows:]], axis=0))
            dq.append(jnp.concatenate(dqs, axis=0))
        low = head_lanes(2 * rows, True)
        gq = jnp.where(low, dq[0], dq[1]) * HD ** (-0.5)
        gk = jnp.where(low, dk[0], dk[1])
        gv = jnp.where(low, dv[0], dv[1])
        g_ref[:, at] = (gq * cos - partner(gq) * sin).astype(BF16)
        g_ref[:, lanes_at(cols + start, LANES)] = (gk * cos - partner(gk) * sin).astype(BF16)
        g_ref[:, lanes_at(2 * cols + start, LANES)] = gv.astype(BF16)


def attend_back(qkv, probs, outs, grads, cos, sin):
    count, three = qkv.shape
    heads = probs[0].shape[0]
    return kernel_call(
        attend_back_kernel,
        "attend_back",
        sds((count, three), BF16),
        (qkv, *probs, *outs, *grads, cos, sin),
        smems=0,
        flops=10 * heads * count * count * HD,
    )


def in_back_kernel(ids_ref, g_ref, x_ref, *refs):
    w_refs, (keep_ref, give_ref, gb_ref) = refs[:-3], refs[-3:]
    three = g_ref.shape[1]
    rows = keep_ref.shape[0]
    gb_ref[...] = jnp.zeros_like(gb_ref)
    for turn, out_ref in enumerate((give_ref, keep_ref)):
        base = (1 - ids_ref[1] if turn == 0 else ids_ref[1]) * rows
        g = g_ref[pl.ds(pl.multiple_of(base, rows), rows), :]
        into_features(out_ref, slice(None), g, w_refs, slice(0, three))

        @pl.loop(0, rows // STEP)
        def _(i, base=base, out_ref=out_ref):
            e = out_ref[pl.ds(pl.multiple_of(i * STEP, STEP), STEP), :].astype(F32)
            far = pl.ds(pl.multiple_of(base + i * STEP, STEP), STEP)
            n0, _ = norm_stats(x_ref[far, :].astype(F32))
            gb_ref[0] += fold_rows(e * n0)
            gb_ref[1] += fold_rows(e)


def in_back(ids, g, x, w):
    count, three = g.shape
    width = x.shape[1]
    part = sds((count // 2, width), BF16)
    return kernel_call(
        in_back_kernel, "in_back", [part, part, sds((2, 8, width), F32)], (ids, g, x, *w),
    )


def gain_sum_kernel(gb0_ref, g12a, g12b, g3, mine_ref, other_ref):
    share = 0.5
    rows = []
    for kind in range(2):
        rows += [
            gb0_ref[kind],
            share * (g12a[2 + kind] + g12b[2 + kind]),
            share * (g12a[kind] + g12b[kind]),
            share * g3[kind],
        ]
    half = mine_ref.shape[1]
    for i, row in enumerate(rows):
        row = jnp.sum(row, axis=0, keepdims=True)
        mine_ref[i : i + 1, :] = row[:, :half]
        other_ref[i : i + 1, :] = row[:, half:]


def gain_sum(gb0, g12, g3):
    out = sds((8, gb0.shape[-1] // 2), F32)
    return kernel_call(gain_sum_kernel, "gain_pack", [out, out], (gb0, *g12, g3), smems=0)


def gain_pack_kernel(*refs):
    out_ref = refs[-1]
    total = refs[0][...] + refs[1][...] + refs[2][...] + refs[3][...]
    filler = jnp.zeros((LANES - total.shape[0], total.shape[1]), F32)
    out_ref[...] = jnp.concatenate([total, filler], axis=0).T.astype(BF16)


def gain_pack(parts):
    out = sds((parts[0].shape[1], LANES), BF16)
    return kernel_call(gain_pack_kernel, "gain_pack", out, tuple(parts), smems=0)


def tokens_back_kernel(ids_ref, x_ref, keep_ref, got_ref, dh0_ref, dh1_ref, gain_ref, out_ref):
    side = ids_ref[1]
    rows = got_ref.shape[0]

    def body(at):
        far = pl.ds(pl.multiple_of(side * rows + at.start, STEP), STEP)
        e = keep_ref[at, :].astype(F32) + got_ref[at, :].astype(F32)
        n0, r0 = norm_stats(x_ref[far, :].astype(F32))
        dh = jnp.where(side == 0, dh0_ref[at, :], dh1_ref[at, :])
        join_cores(ids_ref, dh + norm_back(n0, r0, e * gain_ref[0:1, :]), out_ref, at)

    row_steps(rows, body)


def tokens_back(ids, x, keep, got, dhs, gain):
    return kernel_call(
        tokens_back_kernel, "tokens_back", sds(got.shape, F32), (ids, x, keep, got, *dhs, gain),
    )


def split_kernel(up_ref, down_ref, up_out, down_out):
    half = up_out.shape[0]
    up_out[...] = up_ref[:half, :]
    down_out[...] = down_ref[half:, :]


def split(up, down):
    out = sds((up.shape[0] // 2, up.shape[1]), BF16)
    return kernel_call(split_kernel, "split", [out, out], (up, down), smems=0)


def stage_kernel(*refs):
    ins, out_ref, sem = refs[:-2], refs[-2], refs[-1]
    copies, start = [], 0
    for ref in ins:
        parts = [ref.at[i] for i in range(ref.shape[0])] if len(ref.shape) == 3 else [ref]
        for part in parts:
            cols = part.shape[1]
            dst = out_ref.at[:, pl.ds(start, cols)]
            copies.append(pltpu.make_async_copy(part, dst, sem.at[len(copies)]))
            start += cols
    for copy in copies:
        copy.start()
    for copy in copies:
        copy.wait()


def stage(*arrays):
    rows = arrays[0].shape[-2]
    cols = sum(a.size // rows for a in arrays)
    return pl.pallas_call(
        stage_kernel,
        in_specs=[pl.BlockSpec(memory_space=pltpu.HBM)] * len(arrays),
        out_specs=whole(),
        out_shape=sds((rows, cols), BF16),
        scratch_shapes=[pltpu.SemaphoreType.DMA((4 * len(arrays),))],
        compiler_params=pltpu.CompilerParams(vmem_limit_bytes=VMEM_LIMIT),
        cost_estimate=cost_of("stage"),
        name="stage",
    )(*arrays)


def assemble_kernel(places, *refs):
    ins, out, sem = refs[: len(places)], refs[-2], refs[-1]
    copies = []
    for i, (src, at) in enumerate(zip(ins, places)):
        copies.append(pltpu.make_async_copy(src, out.at[pl.ds(at, src.shape[0])], sem.at[i]))
    for copy in copies:
        copy.start()
    for copy in copies:
        copy.wait()


def assemble(places, pieces):
    rows = sum(piece.shape[0] for piece in pieces)
    return pl.pallas_call(
        functools.partial(assemble_kernel, places),
        in_specs=[anywhere()] * len(pieces),
        out_specs=whole(),
        out_shape=sds((rows, pieces[0].shape[1]), BF16),
        scratch_shapes=[pltpu.SemaphoreType.DMA((len(pieces),))],
        compiler_params=pltpu.CompilerParams(vmem_limit_bytes=VMEM_LIMIT),
        cost_estimate=cost_of("assemble"),
        name="assemble",
    )(*pieces)


def term_rows(groups, block, index, to):
    total = None
    for refs in groups:
        if len(refs) == 2:
            ref, first = (refs[0], 0) if index == 0 else (refs[1], (index - 1) * block)
        else:
            ref, first = refs[0], index * block
        part = ref[first : first + block, to].astype(F32)
        total = part if total is None else total + part
    return total


def unflatten(refs, layout):
    groups, n = [], 0
    for terms in layout:
        group = []
        for count in terms:
            group.append(refs[n : n + count])
            n += count
        groups.append(group)
    return groups, refs[n:]


def ring_sum_kernel(layout, block, index, way, *refs):
    groups, refs = unflatten(refs, layout)
    out_ref, came = refs[-1], refs[:-1]
    half = block // 2
    start = 0
    for group in groups:
        cols = group[0][0].shape[1]
        for c in range(0, cols, UNITS):
            n = min(UNITS, cols - c)
            own, to = slice(c, c + n), slice(start + c, start + c + n)
            if index == 0:
                rows = slice(way * half, (way + 1) * half)
                total = sum(term[0][rows, own].astype(F32) for term in group)
                out_ref[:, to] = total.astype(BF16)
                continue
            total = term_rows(group, block, index + way, own)
            part = came[0][:, to].astype(F32)
            if part.shape[0] == block:
                out_ref[:, to] = (total + part).astype(BF16)
            else:
                hit = slice(0, half) if way == 0 else slice(half, block)
                rest = slice(half, block) if way == 0 else slice(0, half)
                out_ref[hit, to] = (total[hit] + part).astype(BF16)
                out_ref[rest, to] = total[rest].astype(BF16)
        start += cols


def ring_sum(index, way, block, groups, came=()):
    layout = [[len(term) for term in group] for group in groups]
    flat = [a for group in groups for term in group for a in term]
    cols = sum(group[0][0].shape[1] for group in groups)
    return kernel_call(
        functools.partial(ring_sum_kernel, layout, block, index, way), "ring_sum",
        sds((block // 2 if index == 0 else block, cols), BF16), (*flat, *came), smems=0,
    )


def ring_end_kernel(layout, splits, index, *refs):
    groups, refs = unflatten(refs, layout)
    (up, down), outs = refs[:2], refs[2:]
    block = up.shape[0]
    start, o = 0, 0
    for group, sizes in zip(groups, splits):
        here = 0
        for count, cols in sizes:
            for i in range(max(count, 1)):
                to, own = slice(start, start + cols), slice(here, here + cols)
                total = term_rows(group, block, index, own)
                total = total + up[:, to].astype(F32) + down[:, to].astype(F32)
                if count == 0:
                    turned = total.T
                    outs[o][...] = turned[0:4, :]
                    outs[o + 1][...] = turned[4:8, :]
                elif count > 1:
                    outs[o][i] = total
                else:
                    outs[o][...] = total
                start, here = start + cols, here + cols
            o += 2 if count == 0 else 1


def ring_end(size, groups, came, splits):
    layout = [[len(term) for term in group] for group in groups]
    flat = [a for group in groups for term in group for a in term]
    block = came[0].shape[0]
    shapes = []
    for sizes in splits:
        for count, cols in sizes:
            if count == 0:
                shapes += [(4, block)] * 2
            else:
                shapes.append((count, block, cols) if count > 1 else (block, cols))
    return kernel_call(
        functools.partial(ring_end_kernel, layout, splits, size - 1), "ring_end",
        [sds(shape, F32) for shape in shapes], (*flat, *came), smems=0,
    )


class Ring:
    def __init__(self, n_dp, ids):
        self.size = n_dp // 2
        self.ids = ids
        self.up = self.shift(1)
        self.down = self.shift(-1)
        self.cores = [(i, i ^ 1) for i in range(n_dp)]

    def shift(self, by):
        return [
            (2 * chip_of(p, self.size) + c, 2 * chip_of((p + by) % self.size, self.size) + c)
            for p in range(self.size)
            for c in range(2)
        ]


def swap_cores(ring, value):
    return lax.ppermute(value, "dp", ring.cores)


class Gather:
    def __init__(self, ring, piece):
        self.ring = ring
        self.rows = piece.shape[0]
        self.pieces, self.places = [piece], [ring_order(ring.size).index(0) * self.rows]
        self.step_now = 0
        self.up = self.down = piece

    def step(self, *deps):
        self.step_now += 1
        ring, step = self.ring, self.step_now
        up, down = self.up, self.down
        if deps:
            up, down = after(up, *deps), after(down, *deps)
        shift = 0
        if step == ring.size // 2:
            shift = up.shape[0] // 2
            up, down = split(up, down)
            self.sent = up, down
        self.up = lax.ppermute(up, "dp", ring.up)
        self.down = lax.ppermute(down, "dp", ring.down)
        self.pieces += [self.up, self.down]
        order = ring_order(ring.size)
        self.places += [
            order.index(step if shift else -step) * self.rows,
            order.index(step) * self.rows + shift,
        ]
        return self.up, self.down

    def end(self, *deps):
        pieces = self.pieces
        if deps:
            pieces = [after(pieces[0], *deps), *pieces[1:]]
        return assemble(self.places, pieces)


class Reduce:
    def __init__(self, ring, block, groups):
        self.ring, self.block, self.groups = ring, block, groups
        self.index = 0
        self.came = ()

    def step(self, *deps):
        groups = self.groups
        if deps:
            first = groups[0][0]
            groups = [[(after(first[0], *deps), *first[1:]), *groups[0][1:]], *groups[1:]]
        if self.index == 0:
            groups = [[(term[0],) for term in group] for group in groups]
        sent, came = [], []
        for way, perm in enumerate((self.ring.up, self.ring.down)):
            sent.append(ring_sum(self.index, way, self.block, groups, self.came[way : way + 1]))
            came.append(lax.ppermute(sent[way], "dp", perm))
        self.sent, self.came = tuple(sent), tuple(came)
        self.index += 2 if self.index else 1
        return self.came

    def end(self, splits, *deps):
        came = self.came
        if deps:
            came = after(came[0], *deps), came[1]
        return ring_end(self.ring.size, self.groups, came, splits)


def per_device(n_dp, tokens, seq_lengths, ln_gain, ln_bias, w_qkv, w_out, w_up, w_down, cotangent):
    ids = jnp.stack([lax.axis_index("dp"), lax.axis_index("mp")]).astype(jnp.int32)
    ring = Ring(n_dp, ids)
    count, width = tokens.shape
    rows = count // 2
    w_rows, units = w_up.shape
    cols = w_out.shape[0]

    def swap_sides(value):
        return lax.ppermute(value, "mp", [(0, 1), (1, 0)])

    done = {}

    def dep(name):
        found = []
        for other in ORDER.get(name, ()):
            value = done[other]
            found += list(value) if isinstance(value, (tuple, list)) else [value]
        return found

    def tie(value, name):
        others = dep(name)
        return after(value, *others) if others else value

    def both(own, name):
        return [own, swap_cores(ring, tie(own, name))]

    g1 = Gather(ring, stage(after(w_qkv, ids), w_out.T))
    done["s11"] = g1.step()
    cot_got = done["cot_got"] = swap_sides(tie(cotangent, "cot_swap"))
    stage2, stage3 = stage(w_up), stage(w_down.T)
    done["stages"] = stage2, stage3
    done["s12"] = g1.step(*dep("s12"))
    x, a1, gain, bias = prepare(ids, tokens, ln_gain, ln_bias)
    done["a1"] = a1
    done["s13"] = g1.step(*dep("s13"))
    done["s14"] = g1.step(*dep("s14"))
    done["s14_sent"] = g1.sent
    g2 = Gather(ring, tie(stage2, "s21"))
    done["s21"] = g2.step()
    g3 = Gather(ring, tie(stage3, "s31"))
    done["s31"] = g3.step()
    own = done["own1"] = g1.end(*dep("own1"))
    w1 = both(own, "w1")
    cos, sin = rotary_pair(tie(seq_lengths, "rotary"), count)
    cot = done["cot"] = cotangent_rows(tie(ids, "cot"), cotangent, cot_got)
    done["s22"] = g2.step(*dep("s22"))
    qkv = done["qkv"] = qkv_project(tie(a1, "qkv"), w1, cos, sin)
    probs, outs, ys, a3s, mids, zs, backs, mid_backs = [], [], [], [], [], [], [], []
    for c in range(2):
        p, o, part = attend(c * rows, rows, tie(seq_lengths, f"attend{c}"), qkv, w1)
        probs.append(p)
        outs.append(o)
        done[f"part{c}"] = part
        if c == 0:
            ys.append((part, swap_sides(part)))
            done["y0"] = ys[0][1]
    done["s32"] = g3.step(*dep("s32"))
    done["s23"] = g2.step(*dep("s23"))
    ys.append((part, swap_sides(tie(part, "y1"))))
    done["y1"] = ys[1][1]
    done["s33"] = g3.step(*dep("s33"))
    done["s24"] = g2.step(*dep("s24"))
    own = done["own2"] = g2.end(*dep("own2"))
    w2 = both(own, "w2")
    a3s.append(mid_norm(0, tie(x, "norm0"), *ys[0], gain, bias))
    done["norm0"] = a3s[0]
    done["s34"] = g3.step(*dep("s34"))
    own = done["own3"] = g3.end(*dep("own3"))
    w3 = both(own, "w3")
    mids.append(up_project(tie(a3s[0], "up0"), w2))
    done["up0"] = mids[0][0]
    part = down_project(tie(mids[0][0], "down0"), w3)
    done["down0"] = part
    zs.append((part, swap_sides(part)))
    a3s.append(mid_norm(1, tie(x, "norm1"), *ys[1], gain, bias))
    done["norm1"] = a3s[1]
    mids.append(up_project(tie(a3s[1], "up1"), w2))
    done["up1"] = mids[1][0]
    part = down_project(tie(mids[1][0], "down1"), w3)
    done["down1"] = part
    zs.append((part, swap_sides(part)))
    for c in range(2):
        z = zs[c][0], tie(zs[c][1], f"back{c}")
        dz, du, part = mlp_back(c, *z, cot, gain, mids[c][1], w3, w2)
        backs.append((dz, du, (part, swap_sides(part))))
        done[f"back{c}"], done[f"da{c}"] = dz, backs[c][2][1]
    dzs, dus = [b[0] for b in backs], [b[1] for b in backs]
    gs = [m[0] for m in mids]

    def mid(c):
        w = mid_back(c, tie(x, f"mid{c}"), *ys[c], *backs[c][2], cot, gain, bias, w1)
        done[f"mid{c}"] = w[0]
        mid_backs.append(w)

    def grad(which, products, name):
        others = dep(name)
        if others:
            (lefts, rights), rest = products[0], products[1:]
            products = [([after(lefts[0], *others), *lefts[1:]], rights), *rest]
        term = weight_grad(which, ring.size, products)
        done[name] = term[0]
        return term

    def swap_term(term, name):
        far = swap_cores(ring, term[0])
        done[name + "_far"] = far
        return far, swap_cores(ring, after(term[1], far, *dep(name + "_near")))

    def ring_step(reduce, name):
        done[name] = reduce.step(*dep(name))
        done[name + "_sent"] = reduce.sent

    down_other = grad(1, [(dzs, gs)], "down_other")
    up_other = grad(1, [(a3s, dus)], "up_other")
    down_mine = grad(0, [(dzs, gs)], "down_mine")
    down_got = swap_term(down_other, "down")
    up_mine = grad(0, [(a3s, dus)], "up_mine")
    up_got = swap_term(up_other, "up")
    mlp_ring = Reduce(ring, w_rows, [[down_mine, down_got], [up_mine, up_got]])
    ring_step(mlp_ring, "m1")
    mid(0)
    output, gb3 = last_norm(tie(ids, "last"), x, cot, gain, bias, ys, zs)
    done["last"] = output
    ring_step(mlp_ring, "m2")
    mid(1)
    grads = [m[2] for m in mid_backs]
    g_qkv = done["g_qkv"] = attend_back(tie(qkv, "g_qkv"), probs, outs, grads, cos, sin)
    attn_products = [([a1], [g_qkv]), ([m[1] for m in mid_backs], outs)]
    attn_other = grad(1, attn_products, "attn_other")
    attn_got = swap_term(attn_other, "attn")
    ring_step(mlp_ring, "m3")
    part_keep, part_give, gb0 = in_back(ids, tie(g_qkv, "in_back"), x, w1)
    done["in_back"] = part_keep
    gain_mine, gain_other = gain_sum(gb0, [m[3] for m in mid_backs], gb3)
    done["gain_sum"] = gain_mine
    gain_terms = [
        gain_mine,
        swap_cores(ring, gain_other),
        swap_sides(gain_mine),
        lax.ppermute(gain_other, ("dp", "mp"), [(i, i ^ 3) for i in range(2 * n_dp)]),
    ]
    attn_mine = grad(0, attn_products, "attn_mine")
    gains = gain_pack([tie(gain_terms[0], "gains"), *gain_terms[1:]])
    done["gains"] = gains
    part_got = done["part_got"] = swap_sides(tie(part_give, "part_give"))
    attn_ring = Reduce(ring, w_rows, [[attn_mine, attn_got], [(gains,)]])
    ring_step(attn_ring, "q1")
    ring_step(mlp_ring, "m4")
    ring_step(attn_ring, "q2")
    grad_tokens = done["tokens"] = tokens_back(
        tie(ids, "tokens"), x, part_keep, part_got, [m[0] for m in mid_backs], gain
    )
    ring_step(attn_ring, "q3")
    grad_down, grad_up = mlp_ring.end([[(1, units)], [(1, units)]], *dep("m_end"))
    done["m_end"] = grad_down
    ring_step(attn_ring, "q4")
    grad_qkv, grad_out, grad_gain, grad_bias = attn_ring.end([[(3, cols), (1, cols)], [(0, LANES)]])
    return output, grad_tokens, grad_qkv, grad_out.T, grad_up, grad_down.T, grad_gain, grad_bias


def layer_norm(values, norm_gain, norm_bias):
    average = jnp.mean(values, axis=-1, keepdims=True)
    centred = values - average
    variance = jnp.mean(centred * centred, axis=-1, keepdims=True)
    return centred * lax.rsqrt(variance + NORM_EPS) * norm_gain + norm_bias


def norm_pull(values, norm_gain, norm_bias, grad_result):
    result, puller = jax.vjp(layer_norm, values, norm_gain, norm_bias)
    return puller(grad_result)


def seq_layout(lengths, block_size):
    block_count = lengths.shape[0]
    block_ids = jnp.arange(block_count, dtype=jnp.int32)
    starts = lengths > 0
    earlier = starts[None, :] & (block_ids[None, :] <= block_ids[:, None])
    owners = jnp.max(jnp.where(earlier, block_ids[None, :], 0), axis=1)
    owner_len = jnp.sum(
        jnp.where(block_ids[None, :] == owners[:, None], lengths[None, :], 0), axis=1
    )
    places = jnp.arange(block_count * block_size, dtype=jnp.int32)
    tok_owner = jnp.repeat(owners, block_size)
    position = places - tok_owner * block_size
    is_valid = position < jnp.repeat(owner_len, block_size)
    allowed = (
        (tok_owner[:, None] == tok_owner[None, :])
        & (places[None, :] <= places[:, None])
        & is_valid[None, :]
    )
    return (position, allowed)


def rotary_tables(position, width):
    frequency = ROPE_BASE ** (-jnp.arange(width // 2, dtype=jnp.float32) * 2.0 / width)
    angles = position.astype(jnp.float32)[:, None] * frequency[None, :]
    return (jnp.cos(angles), jnp.sin(angles))


def rotate(values, cos_table, sin_table):
    half_width = values.shape[-1] // 2
    front_half = values[..., :half_width]
    back_half = values[..., half_width:]
    cos_part = cos_table[:, None, :]
    sin_part = sin_table[:, None, :]
    return jnp.concatenate(
        [
            front_half * cos_part - back_half * sin_part,
            back_half * cos_part + front_half * sin_part,
        ],
        axis=-1,
    )


def attention_scores(queries, keys_rot, allowed, scale):
    raw_scores = (
        jnp.einsum("hqd,hkd->hqk", queries, keys_rot, preferred_element_type=jnp.float32) * scale
    )
    return jnp.where(allowed[None, :, :], raw_scores, MASK_FILL)


def plain_device(tokens, seq_lengths, ln_gain, ln_bias, w_qkv, w_out, w_up, w_down, cotangent):
    full_qkv, full_out, full_up, full_down = (
        lax.all_gather(w_qkv, "dp", axis=1, tiled=True),
        lax.all_gather(w_out, "dp", axis=1, tiled=True),
        lax.all_gather(w_up, "dp", axis=0, tiled=True),
        lax.all_gather(w_down, "dp", axis=1, tiled=True),
    )
    tok_count = tokens.shape[0]
    shard_rows = cotangent.shape[0]
    row_start = lax.axis_index("mp") * shard_rows
    heads_here = full_out.shape[0] // HD
    scale = HD ** (-0.5)
    position, allowed = seq_layout(seq_lengths, BLOCK)
    cos_table, sin_table = rotary_tables(position, HD)

    def to_heads(values):
        return jnp.transpose(values.reshape(tok_count, heads_here, HD), (1, 0, 2))

    def from_heads(values):
        return jnp.transpose(values, (1, 0, 2)).reshape(tok_count, heads_here * HD)

    def rotated(values):
        return rotate(values.reshape(tok_count, heads_here, HD), cos_table, sin_table)

    inputs = tokens.astype(jnp.float32)
    normed_in = layer_norm(inputs, ln_gain[0], ln_bias[0]).astype(jnp.bfloat16)
    projected = jnp.einsum("td,cde->cte", normed_in, full_qkv, preferred_element_type=jnp.float32)
    queries = jnp.transpose(rotated(projected[0]), (1, 0, 2)).astype(jnp.bfloat16)
    keys_rot = jnp.transpose(rotated(projected[1]), (1, 0, 2)).astype(jnp.bfloat16)
    values_h = to_heads(projected[2]).astype(jnp.bfloat16)
    scores = attention_scores(queries, keys_rot, allowed, scale)
    top_score = jnp.max(scores, axis=-1, keepdims=True)
    expo = jnp.exp(scores - top_score)
    row_total = jnp.sum(expo, axis=-1, keepdims=True)
    probs = expo / row_total
    log_total = top_score + jnp.log(row_total)
    attended = jnp.einsum(
        "hqk,hkd->hqd", probs.astype(jnp.bfloat16), values_h, preferred_element_type=jnp.float32
    )
    mixed_heads = from_heads(attended).astype(jnp.bfloat16)
    attn_part = jnp.dot(mixed_heads, full_out, preferred_element_type=jnp.float32)
    attn_sum = lax.psum_scatter(
        attn_part.astype(jnp.bfloat16), "mp", scatter_dimension=0, tiled=True
    ).astype(jnp.float32)
    resid_in = lax.dynamic_slice_in_dim(inputs, row_start, shard_rows, 0)
    hidden_state = resid_in + layer_norm(attn_sum, ln_gain[1], ln_bias[1])
    normed_mid = layer_norm(hidden_state, ln_gain[2], ln_bias[2]).astype(jnp.bfloat16)
    mlp_input = lax.all_gather(normed_mid, "mp", axis=0, tiled=True)
    pre_act = jnp.dot(mlp_input, full_up, preferred_element_type=jnp.float32)
    act_low = jax.nn.gelu(pre_act, approximate=True).astype(jnp.bfloat16)
    mlp_part = jnp.dot(act_low, full_down, preferred_element_type=jnp.float32)
    mlp_sum = lax.psum_scatter(
        mlp_part.astype(jnp.bfloat16), "mp", scatter_dimension=0, tiled=True
    ).astype(jnp.float32)
    output = (hidden_state + layer_norm(mlp_sum, ln_gain[3], ln_bias[3])).astype(jnp.bfloat16)
    grad_result = cotangent.astype(jnp.float32)
    grad_mlp_sum, grad_gain3, grad_bias3 = norm_pull(mlp_sum, ln_gain[3], ln_bias[3], grad_result)
    grad_mlp_rows = lax.all_gather(grad_mlp_sum.astype(jnp.bfloat16), "mp", axis=0, tiled=True)
    grad_down = jnp.einsum("tf,te->fe", act_low, grad_mlp_rows, preferred_element_type=jnp.float32)
    grad_act = jnp.einsum("te,fe->tf", grad_mlp_rows, full_down, preferred_element_type=jnp.float32)
    gelu_puller = jax.vjp(lambda values: jax.nn.gelu(values, approximate=True), pre_act)[1]
    grad_pre = gelu_puller(grad_act)[0].astype(jnp.bfloat16)
    grad_up = jnp.einsum("td,tf->df", mlp_input, grad_pre, preferred_element_type=jnp.float32)
    grad_mid_part = jnp.einsum("tf,df->td", grad_pre, full_up, preferred_element_type=jnp.float32)
    grad_mid = lax.psum_scatter(
        grad_mid_part.astype(jnp.bfloat16), "mp", scatter_dimension=0, tiled=True
    ).astype(jnp.float32)
    grad_hidden_norm, grad_gain2, grad_bias2 = norm_pull(
        hidden_state, ln_gain[2], ln_bias[2], grad_mid
    )
    grad_hidden = grad_result + grad_hidden_norm
    grad_attn_sum, grad_gain1, grad_bias1 = norm_pull(attn_sum, ln_gain[1], ln_bias[1], grad_hidden)
    grad_attn_rows = lax.all_gather(grad_attn_sum.astype(jnp.bfloat16), "mp", axis=0, tiled=True)
    grad_outproj = jnp.einsum(
        "tc,te->ce", mixed_heads, grad_attn_rows, preferred_element_type=jnp.float32
    )
    grad_mixed = jnp.einsum(
        "te,ce->tc", grad_attn_rows, full_out, preferred_element_type=jnp.float32
    ).astype(jnp.bfloat16)
    grad_heads = to_heads(grad_mixed)
    again_scores = attention_scores(queries, keys_rot, allowed, scale)
    again_probs = jnp.exp(again_scores - log_total)
    grad_probs = jnp.einsum(
        "hqd,hkd->hqk", grad_heads, values_h, preferred_element_type=jnp.float32
    )
    grad_values = jnp.einsum(
        "hqk,hqd->hkd",
        again_probs.astype(jnp.bfloat16),
        grad_heads,
        preferred_element_type=jnp.float32,
    )
    row_dot = jnp.sum(again_probs * grad_probs, axis=-1, keepdims=True)
    grad_scores = (again_probs * (grad_probs - row_dot) * scale).astype(jnp.bfloat16)
    grad_q_rot = jnp.einsum(
        "hqk,hkd->hqd", grad_scores, keys_rot, preferred_element_type=jnp.float32
    )
    grad_k_rot = jnp.einsum(
        "hqk,hqd->hkd", grad_scores, queries, preferred_element_type=jnp.float32
    )
    zero_heads = jnp.zeros((tok_count, heads_here, HD), jnp.float32)
    unrotate = jax.vjp(lambda values: rotate(values, cos_table, sin_table), zero_heads)[1]
    grad_query = unrotate(jnp.transpose(grad_q_rot, (1, 0, 2)))[0].reshape(
        tok_count, heads_here * HD
    )
    grad_key = unrotate(jnp.transpose(grad_k_rot, (1, 0, 2)))[0].reshape(tok_count, heads_here * HD)
    grad_value = from_heads(grad_values)
    grad_proj = jnp.stack(
        [
            grad_query.astype(jnp.bfloat16),
            grad_key.astype(jnp.bfloat16),
            grad_value.astype(jnp.bfloat16),
        ]
    )
    grad_qkv = jnp.einsum("td,cte->cde", normed_in, grad_proj, preferred_element_type=jnp.float32)
    grad_in_part = jnp.einsum(
        "cte,cde->td", grad_proj, full_qkv, preferred_element_type=jnp.float32
    )
    grad_in = lax.psum_scatter(
        grad_in_part.astype(jnp.bfloat16), "mp", scatter_dimension=0, tiled=True
    ).astype(jnp.float32)
    grad_norm_in, grad_gain0, grad_bias0 = norm_pull(resid_in, ln_gain[0], ln_bias[0], grad_in)
    grad_tokens = grad_hidden + grad_norm_in
    gain_grads = jnp.stack([grad_gain0, grad_gain1, grad_gain2, grad_gain3])
    bias_grads = jnp.stack([grad_bias0, grad_bias1, grad_bias2, grad_bias3])
    gain_grads, bias_grads = (
        lax.psum(gain_grads.astype(jnp.bfloat16), "mp").astype(jnp.float32),
        lax.psum(bias_grads.astype(jnp.bfloat16), "mp").astype(jnp.float32),
    )
    grad_qkv, grad_outproj, grad_up, grad_down, gain_grads, bias_grads = (
        lax.psum_scatter(
            grad_qkv.astype(jnp.bfloat16), "dp", scatter_dimension=1, tiled=True
        ).astype(jnp.float32),
        lax.psum_scatter(
            grad_outproj.astype(jnp.bfloat16), "dp", scatter_dimension=1, tiled=True
        ).astype(jnp.float32),
        lax.psum_scatter(
            grad_up.astype(jnp.bfloat16), "dp", scatter_dimension=0, tiled=True
        ).astype(jnp.float32),
        lax.psum_scatter(
            grad_down.astype(jnp.bfloat16), "dp", scatter_dimension=1, tiled=True
        ).astype(jnp.float32),
        lax.psum_scatter(
            gain_grads.astype(jnp.bfloat16), "dp", scatter_dimension=1, tiled=True
        ).astype(jnp.float32),
        lax.psum_scatter(
            bias_grads.astype(jnp.bfloat16), "dp", scatter_dimension=1, tiled=True
        ).astype(jnp.float32),
    )
    return (output, grad_tokens, grad_qkv, grad_outproj, grad_up, grad_down, gain_grads, bias_grads)


def solution(mesh):
    placed = (
        P("dp", None),
        P("dp"),
        P(),
        P(),
        P(None, "dp", "mp"),
        P("mp", "dp"),
        P("dp", "mp"),
        P("mp", "dp"),
        P(("dp", "mp"), None),
    )
    n_dp, n_mp = mesh.shape["dp"], mesh.shape["mp"]

    def layer(tokens, *rest):
        if n_mp == 2 and tokens.shape[1] == n_dp * LANES // 2:
            return per_device(n_dp, tokens, *rest)
        return plain_device(tokens, *rest)

    return jax.shard_map(
        layer,
        mesh=mesh,
        in_specs=placed,
        out_specs=(
            P(("dp", "mp"), None),
            P(("dp", "mp"), None),
            P(None, "dp", "mp"),
            P("mp", "dp"),
            P("dp", "mp"),
            P("mp", "dp"),
            P(None, "dp"),
            P(None, "dp"),
        ),
        check_vma=False,
    )
```

```python
import functools

import jax
import jax.numpy as jnp
from jax import lax
from jax.experimental import pallas as pl
from jax.experimental.pallas import tpu as pltpu
from jax.sharding import PartitionSpec as P

HD = 64
BLOCK = 128
LANES = 128
NORM_EPS = 1e-05
ROPE_BASE = 10000.0
MASK_FILL = -1e30
F32 = jnp.float32
BF16 = jnp.bfloat16
VMEM_LIMIT = 6 * 1024 * 1024
STEP = 128
NN = (((1,), (0,)), ((), ()))
NT = (((1,), (1,)), ((), ()))
TN = (((0,), (0,)), ((), ()))


def mm(left, right, dims):
    return lax.dot_general(left, right, dims, preferred_element_type=F32)


def sds(shape, dtype):
    return jax.ShapeDtypeStruct(shape, dtype)


def whole():
    return pl.BlockSpec(memory_space=pltpu.VMEM)


def smem():
    return pl.BlockSpec(memory_space=pltpu.SMEM)


def anywhere():
    return pl.BlockSpec(memory_space=pl.ANY)


TIMES = {
    "prepare": 3.3, "cotangent_rows": 1.5, "qkv_project": 2.0, "attend0": 2.5, "attend1": 4.4,
    "up_project": 4.3, "down_project": 1.3, "mlp_back": 5.4, "mid_norm": 2.5, "last_norm": 3.0, "weight_grad": 1.3, "mid_back": 3.3,
    "attend_back": 5.0, "in_back": 3.6, "gain_pack": 0.4, "tokens_back": 3.9, "stage": 0.5,
    "assemble": 1.2, "ring_sum": 1.3, "ring_end": 2.0, "rotary": 2.0, "split": 0.4,
}
TIME_SHARE = 1.0


def cost_of(name):
    return pl.CostEstimate(
        flops=0, bytes_accessed=int(TIMES[name] * TIME_SHARE * 3.69e6), transcendentals=0
    )


ORDER = {
    "s12": ("stages",), "s13": ("a1",), "s14": ("cot_got", "s11"), "s21": ("s14_sent",),
    "s31": ("s14",), "cot_swap": ("s11",), "w1": ("s21",), "rotary": ("own1",), "cot": ("own1",),
    "s22": ("own1",), "qkv": ("cot",), "attend1": ("part0", "s31"), "s23": ("part1",), "s24": ("y0",),
    "norm0": ("own2",), "y1": ("s32",), "s34": ("own2",), "own3": ("y1",), "up1": ("down0",),
    "down1": ("down0",), "back1": ("back0",), "up_other": ("down_other", "up1"),
    "down_mine": ("up_other",), "up_mine": ("down_mine", "down_far"), "up_near": ("da0", "up_mine"),
    "mid0": ("m1_sent",), "last": ("mid0",), "m2": ("last",), "mid1": ("m2_sent",),
    "attn_near": ("m2",), "m3": ("attn_other",), "in_back": ("m3_sent",), "attn_mine": ("gain_sum",),
    "gains": ("attn_mine",), "part_give": ("gains",), "m4": ("q1_sent",), "q2": ("m4_sent",),
    "tokens": ("q2_sent",), "q3": ("tokens",), "m_end": ("q3_sent",), "q4": ("m_end",),
    "q1": ("m3_sent",), "attn_other": ("m1_sent",),
}


def kernel_call(body, name, out_shape, args, smems=1, flops=0, nbytes=0, scratch=(), **extra):
    many = isinstance(out_shape, (list, tuple))
    return pl.pallas_call(
        body,
        in_specs=[smem()] * smems + [whole()] * (len(args) - smems),
        out_specs=[whole()] * len(out_shape) if many else whole(),
        out_shape=out_shape,
        scratch_shapes=list(scratch),
        compiler_params=pltpu.CompilerParams(vmem_limit_bytes=VMEM_LIMIT),
        cost_estimate=cost_of(name),
        name=name,
        **extra,
    )(*args)


def after(value, *others):
    return lax.optimization_barrier((value,) + others)[0]


def chip_of(place, size):
    if isinstance(place, int):
        return 2 * place if place < size // 2 else 2 * (size - 1 - place) + 1
    return jnp.where(place < size // 2, 2 * place, 2 * (size - 1 - place) + 1)


def ring_order(size):
    order = [size // 2]
    for step in range(size // 2 - 1, 0, -1):
        order += [step, -step]
    return order + [0]


def chip_lanes(ids_ref, width):
    size = width // LANES
    own = ids_ref[0] // 2
    here = jnp.where(own % 2 == 0, own // 2, size - 1 - own // 2)
    starts = [chip_of((here + step + size) % size, size) * LANES for step in ring_order(size)]
    return [pl.ds(pl.multiple_of(start, LANES), LANES) for start in starts]


def split_cores(ids_ref, ref, rows):
    places = chip_lanes(ids_ref, ref.shape[1])
    core = ids_ref[0] % 2
    own, other = [], []
    for i in range(0, len(places), 2):
        a, b = (ref[rows, place].astype(F32) for place in places[i : i + 2])
        low = lax.broadcasted_iota(jnp.int32, a.shape, 1) < LANES // 2
        first = jnp.where(low, a, pltpu.roll(b, LANES // 2, 1))
        second = jnp.where(low, pltpu.roll(a, LANES // 2, 1), b)
        own.append(jnp.where(core == 0, first, second))
        other.append(jnp.where(core == 0, second, first))
    return jnp.concatenate(own + other, axis=1)


def join_cores(ids_ref, values, out_ref, rows):
    places = chip_lanes(ids_ref, values.shape[1])
    core = ids_ref[0] % 2
    half = values.shape[1] // 2
    for i in range(0, len(places), 2):
        own = values[:, i * LANES // 2 : i * LANES // 2 + LANES]
        other = values[:, half + i * LANES // 2 : half + i * LANES // 2 + LANES]
        low = lax.broadcasted_iota(jnp.int32, own.shape, 1) < LANES // 2
        first = jnp.where(core == 0, own, other)
        second = jnp.where(core == 0, other, own)
        joined = (
            jnp.where(low, first, pltpu.roll(second, LANES // 2, 1)),
            jnp.where(low, pltpu.roll(first, LANES // 2, 1), second),
        )
        for place, part in zip(places[i : i + 2], joined):
            out_ref[rows, place] = part.astype(out_ref.dtype)


def norm_stats(values):
    centred = values - jnp.mean(values, axis=-1, keepdims=True)
    rstd = lax.rsqrt(jnp.mean(centred * centred, axis=-1, keepdims=True) + NORM_EPS)
    return centred * rstd, rstd


def norm_back(normed, rstd, scaled_grad):
    first = jnp.mean(scaled_grad, axis=-1, keepdims=True)
    second = jnp.mean(scaled_grad * normed, axis=-1, keepdims=True)
    return (scaled_grad - first - normed * second) * rstd


def fold_rows(values):
    return jnp.sum(values.reshape(-1, 8, values.shape[-1]), axis=0)


def lanes_at(start, count):
    if isinstance(start, int):
        return slice(start, start + count)
    return pl.ds(pl.multiple_of(start, LANES), count)


def from_features(left, w_refs, cols):
    total, start = None, 0
    for ref in w_refs:
        term = mm(left[:, start : start + ref.shape[0]], ref[:, cols], NN)
        total = term if total is None else total + term
        start += ref.shape[0]
    return total


def into_features(out_ref, rows, left, w_refs, cols):
    start = 0
    for ref in w_refs:
        part = mm(left, ref[:, cols], NT).astype(BF16)
        out_ref[rows, start : start + ref.shape[0]] = part
        start += ref.shape[0]


def row_steps(rows, body):
    @pl.loop(0, rows // STEP)
    def _(i):
        body(pl.ds(pl.multiple_of(i * STEP, STEP), STEP))


def prepare_kernel(ids_ref, x_ref, gain_ref, bias_ref, xp_ref, a1_ref, gp_ref, bp_ref):
    every = slice(0, gain_ref.shape[0])
    gp_ref[...] = split_cores(ids_ref, gain_ref, every)
    bp_ref[...] = split_cores(ids_ref, bias_ref, every)

    def body(at):
        x = split_cores(ids_ref, x_ref, at)
        xp_ref[at, :] = x.astype(BF16)
        normed, _ = norm_stats(x)
        a1_ref[at, :] = (normed * gp_ref[0:1, :] + bp_ref[0:1, :]).astype(BF16)

    row_steps(x_ref.shape[0], body)


def prepare(ids, x, gain, bias):
    return kernel_call(
        prepare_kernel,
        "prepare",
        [sds(x.shape, BF16), sds(x.shape, BF16), sds(gain.shape, F32), sds(bias.shape, F32)],
        (ids, x, gain, bias),
        nbytes=6 * x.size,
    )


def cotangent_kernel(ids_ref, own_ref, got_ref, out_ref):
    side = ids_ref[1]
    rows = own_ref.shape[0]
    for ref, base in ((own_ref, side * rows), (got_ref, (1 - side) * rows)):

        @pl.loop(0, rows // STEP)
        def _(i, ref=ref, base=base):
            at = pl.ds(pl.multiple_of(i * STEP, STEP), STEP)
            to = pl.ds(pl.multiple_of(base + i * STEP, STEP), STEP)
            out_ref[to, :] = split_cores(ids_ref, ref, at).astype(BF16)


def cotangent_rows(ids, own, got):
    rows, width = own.shape
    return kernel_call(
        cotangent_kernel, "cotangent_rows", sds((2 * rows, width), BF16), (ids, own, got),
        nbytes=8 * own.size,
    )


def partner(values):
    lane = lax.broadcasted_iota(jnp.int32, values.shape, 1)
    ahead = pltpu.roll(values, LANES - HD // 2, 1)
    behind = pltpu.roll(values, HD // 2, 1)
    return jnp.where(lax.rem(lane, HD) < HD // 2, ahead, behind)


def qkv_kernel(a_ref, cos_ref, sin_ref, *refs):
    w_refs, out_ref = refs[:-1], refs[-1]
    cols = w_refs[0].shape[1] // 4
    rows = 2 * BLOCK

    @pl.loop(0, a_ref.shape[0] // rows)
    def _(i):
        at = pl.ds(pl.multiple_of(i * rows, rows), rows)
        cos, sin = cos_ref[at, :], sin_ref[at, :]
        a = a_ref[at, :]
        for which in range(3):
            proj = from_features(a, w_refs, slice(which * cols, (which + 1) * cols))
            for start in range(0, cols, LANES):
                part = proj[:, start : start + LANES]
                if which < 2:
                    part = part * cos + partner(part) * sin
                if which == 0:
                    part = part.astype(BF16).astype(F32) * HD ** (-0.5)
                out_ref[at, which * cols + start : which * cols + start + LANES] = part.astype(BF16)


def qkv_project(a1, w, cos, sin):
    out = sds((a1.shape[0], w[0].shape[1] // 4 * 3), BF16)
    return kernel_call(qkv_kernel, "qkv_project", out, (a1, cos, sin, *w), smems=0)


def span_of(len_ref, block):
    start, size = jnp.int32(0), jnp.int32(0)
    for b in range(block + 1):
        here = len_ref[b]
        start = jnp.where(here > 0, b * BLOCK, start)
        size = jnp.where(here > 0, here, size)
    return start, start + size


def rotary_kernel(len_ref, cos_ref, sin_ref):
    lane = lax.broadcasted_iota(jnp.int32, (BLOCK, LANES), 1)
    row = lax.broadcasted_iota(jnp.int32, (BLOCK, LANES), 0)
    index = (lane % (HD // 2)).astype(F32)
    frequency = jnp.exp(index * (-2.0 / HD * 9.210340371976184))
    back = lane % HD >= HD // 2
    blocks = cos_ref.shape[0] // BLOCK

    @pl.loop(0, blocks)
    def _(b):
        start = jnp.int32(0)
        for k in range(blocks):
            start = jnp.where((k <= b) & (len_ref[k] > 0), k * BLOCK, start)
        at = pl.ds(pl.multiple_of(b * BLOCK, BLOCK), BLOCK)
        angle = (row + (b * BLOCK - start)).astype(F32) * frequency
        sin = jnp.sin(angle)
        cos_ref[at, :] = jnp.cos(angle)
        sin_ref[at, :] = jnp.where(back, sin, -sin)


def rotary_pair(lengths, count):
    out = sds((count, LANES), F32)
    return kernel_call(rotary_kernel, "rotary", [out, out], (lengths,))


def head_lanes(rows, first):
    lane = lax.broadcasted_iota(jnp.int32, (rows, LANES), 1)
    return (lane < HD) == first


def attend_kernel(row0, len_ref, q_ref, *refs):
    w_refs, (p_ref, o_ref, part_ref) = refs[:-3], refs[-3:]
    rows, cols = o_ref.shape
    ext = p_ref.shape[2]
    key = lax.broadcasted_iota(jnp.int32, (BLOCK, ext), 1)
    query = lax.broadcasted_iota(jnp.int32, (BLOCK, ext), 0)
    masks = []
    for b in range(rows // BLOCK):
        lo, hi = span_of(len_ref, row0 // BLOCK + b)
        seen = (key >= lo) & (key < hi) & (key <= query + (row0 + b * BLOCK))
        masks.append(jnp.where(seen, 0.0, MASK_FILL))
    mask = jnp.concatenate(masks, axis=0)
    head = 0
    for start in range(0, cols, LANES):
        q = q_ref[row0 : row0 + rows, start : start + LANES]
        k = q_ref[0:ext, cols + start : cols + start + LANES]
        v = q_ref[0:ext, 2 * cols + start : 2 * cols + start + LANES]
        outs = []
        for first in (True, False):
            mine = head_lanes(rows, first)
            s = mm(jnp.where(mine, q, jnp.zeros_like(q)), k, NT) + mask
            e = jnp.exp(s - jnp.max(s, axis=-1, keepdims=True))
            p = (e * (1.0 / jnp.sum(e, axis=-1, keepdims=True))).astype(BF16)
            p_ref[head] = p
            head += 1
            outs.append(mm(p, v, NN))
        o_ref[:, start : start + LANES] = jnp.where(
            head_lanes(rows, True), outs[0], outs[1]
        ).astype(BF16)
    into_features(part_ref, slice(None), o_ref[...], w_refs, slice(3 * cols, 4 * cols))


def attend(row0, rows, lengths, qkv, w):
    ext = row0 + rows
    cols = qkv.shape[1] // 3
    width = sum(piece.shape[0] for piece in w)
    return kernel_call(
        functools.partial(attend_kernel, row0),
        "attend0" if row0 == 0 else "attend1",
        [sds((cols // HD, rows, ext), BF16), sds((rows, cols), BF16), sds((rows, width), BF16)],
        (lengths, qkv, *w),
    )


def hidden_of(x, ya, yb, gain_ref, bias_ref):
    n1, r1 = norm_stats(ya.astype(F32) + yb.astype(F32))
    return x.astype(F32) + n1 * gain_ref[1:2, :] + bias_ref[1:2, :], n1, r1


def chunk_rows(chunk, rows, at):
    return pl.ds(pl.multiple_of(chunk * rows + at.start, STEP), STEP)


UNITS = 512


def mid_norm_kernel(chunk, x_ref, ya_ref, yb_ref, gain_ref, bias_ref, a3_ref):
    rows = a3_ref.shape[0]

    def body(at):
        x = x_ref[chunk_rows(chunk, rows, at), :]
        h, _, _ = hidden_of(x, ya_ref[at, :], yb_ref[at, :], gain_ref, bias_ref)
        n2, _ = norm_stats(h)
        a3_ref[at, :] = (n2 * gain_ref[2:3, :] + bias_ref[2:3, :]).astype(BF16)

    row_steps(rows, body)


def mid_norm(chunk, x, ya, yb, gain, bias):
    body = functools.partial(mid_norm_kernel, chunk)
    return kernel_call(body, "mid_norm", sds(ya.shape, BF16), (x, ya, yb, gain, bias), smems=0)


def up_kernel(a3_ref, *refs):
    w_refs, (g_ref, gp_ref) = refs[:-2], refs[-2:]

    @pl.loop(0, w_refs[0].shape[1] // UNITS)
    def _(i):
        to = pl.ds(pl.multiple_of(i * UNITS, UNITS), UNITS)
        u = from_features(a3_ref[...], w_refs, to)
        k0 = 0.7978845608028654
        k1 = 0.044715
        sq = u * u
        th = jnp.tanh(u * (k0 + (k0 * k1) * sq))
        plus = 0.5 + 0.5 * th
        g_ref[:, to] = (u * plus).astype(BF16)
        slope = plus + (u * (k0 + (3.0 * k0 * k1) * sq)) * (0.5 - (0.5 * th) * th)
        gp_ref[:, to] = slope.astype(BF16)


def up_project(a3, w):
    out = sds((a3.shape[0], w[0].shape[1]), BF16)
    return kernel_call(up_kernel, "up_project", [out, out], (a3, *w), smems=0)


def down_kernel(g_ref, *refs):
    into_features(refs[-1], slice(None), g_ref[...], refs[:-1], slice(None))


def down_project(g, w):
    out = sds((g.shape[0], sum(piece.shape[0] for piece in w)), BF16)
    return kernel_call(down_kernel, "down_project", out, (g, *w), smems=0)


def mlp_back_kernel(chunk, za_ref, zb_ref, cot_ref, gain_ref, gp_ref, *refs):
    dz_ref, du_ref, part_ref = refs[-3:]
    pieces = (len(refs) - 3) // 2
    w3, w2 = refs[:pieces], refs[pieces : 2 * pieces]
    rows = za_ref.shape[0]

    def body(at):
        n3, r3 = norm_stats(za_ref[at, :].astype(F32) + zb_ref[at, :].astype(F32))
        cot = cot_ref[chunk_rows(chunk, rows, at), :].astype(F32)
        dz_ref[at, :] = norm_back(n3, r3, cot * gain_ref[3:4, :]).astype(BF16)

    row_steps(rows, body)

    @pl.loop(0, w3[0].shape[1] // UNITS)
    def _(i):
        to = pl.ds(pl.multiple_of(i * UNITS, UNITS), UNITS)
        dg = from_features(dz_ref[...], w3, to)
        du_ref[:, to] = (dg * gp_ref[:, to].astype(F32)).astype(BF16)

    into_features(part_ref, slice(None), du_ref[...], w2, slice(None))


def mlp_back(chunk, za, zb, cot, gain, gp, w3, w2):
    rows, width = za.shape
    units = gp.shape[1]
    return kernel_call(
        functools.partial(mlp_back_kernel, chunk),
        "mlp_back",
        [sds((rows, width), BF16), sds((rows, units), BF16), sds((rows, width), BF16)],
        (za, zb, cot, gain, gp, *w3, *w2),
        smems=0,
    )


def last_norm_kernel(ids_ref, x_ref, cot_ref, gain_ref, bias_ref, *refs):
    ys, zs, (out_ref, gb_ref) = refs[0:4], refs[4:8], refs[8:]
    rows = out_ref.shape[0]
    gb_ref[...] = jnp.zeros_like(gb_ref)
    for chunk in range(2):
        ya_ref, yb_ref = ys[2 * chunk : 2 * chunk + 2]
        za_ref, zb_ref = zs[2 * chunk : 2 * chunk + 2]

        def body(at, chunk=chunk, ya_ref=ya_ref, yb_ref=yb_ref, za_ref=za_ref, zb_ref=zb_ref):
            far = chunk_rows(chunk, rows, at)
            n3, _ = norm_stats(za_ref[at, :].astype(F32) + zb_ref[at, :].astype(F32))
            cot = cot_ref[far, :].astype(F32)
            gb_ref[0] += fold_rows(cot * n3)
            gb_ref[1] += fold_rows(cot)

            @pl.when(ids_ref[1] == chunk)
            def _():
                h, _, _ = hidden_of(x_ref[far, :], ya_ref[at, :], yb_ref[at, :], gain_ref, bias_ref)
                out = h + (n3 * gain_ref[3:4, :] + bias_ref[3:4, :])
                join_cores(ids_ref, out, out_ref, at)

        row_steps(rows, body)


def last_norm(ids, x, cot, gain, bias, ys, zs):
    rows, width = ys[0][0].shape
    return kernel_call(
        last_norm_kernel,
        "last_norm",
        [sds((rows, width), BF16), sds((2, 8, width), F32)],
        (ids, x, cot, gain, bias, *ys[0], *ys[1], *zs[0], *zs[1]),
    )


def weight_grad_kernel(which, sizes, *refs):
    far_ref, near_ref, left_sc = refs[-3:]
    half, block = left_sc.shape[0], far_ref.shape[0]
    start = 0
    for lefts, rights, cols in sizes:
        rows = 0
        for ref in refs[lefts[0] : lefts[1]]:
            part = ref[:, which * half : (which + 1) * half]
            left_sc[:, rows : rows + part.shape[0]] = part.T
            rows += part.shape[0]

        def blocks(first, count, rights=rights, start=start):
            for i in range(count):
                c = (first + i) * UNITS
                total, rows = None, 0
                for ref in refs[rights[0] : rights[1]]:
                    n = ref.shape[0]
                    term = mm(left_sc[:, rows : rows + n], ref[:, lanes_at(c, UNITS)], NN)
                    total = term if total is None else total + term
                    rows += n
                total = total.astype(BF16)
                far_ref[:, lanes_at(start + c, UNITS)] = total[:block]
                near_ref[:, lanes_at(start + c, UNITS)] = total[block:]

        pairs = cols // (2 * UNITS)
        if pairs > 1:
            pl.loop(0, pairs)(lambda i: blocks(2 * i, 2))
        else:
            blocks(0, cols // UNITS)
        start += cols


def weight_grad(which, size, products):
    args, sizes, total = [], [], 0
    for lefts, rights in products:
        cols = rights[0].shape[1]
        n = len(args)
        sizes.append(((n, n + len(lefts)), (n + len(lefts), n + len(lefts) + len(rights)), cols))
        args += list(lefts) + list(rights)
        total += cols
    half = args[0].shape[1] // 2
    count = sum(a.shape[0] for a in products[0][0])
    block = half // size
    return kernel_call(
        functools.partial(weight_grad_kernel, which, sizes),
        "weight_grad",
        [sds((block, total), BF16), sds((half - block, total), BF16)],
        tuple(args),
        smems=0,
        scratch=[pltpu.VMEM((half, count), BF16)],
    )


def mid_back_kernel(
    chunk, x_ref, ya_ref, yb_ref, ea_ref, eb_ref, cot_ref, gain_ref, bias_ref, *refs
):
    w_refs, (dh_ref, dy_ref, do_ref, gb_ref) = refs[:-4], refs[-4:]
    rows, cols = do_ref.shape
    gb_ref[...] = jnp.zeros_like(gb_ref)

    def body(at):
        far = chunk_rows(chunk, rows, at)
        h, n1, r1 = hidden_of(x_ref[far, :], ya_ref[at, :], yb_ref[at, :], gain_ref, bias_ref)
        n2, r2 = norm_stats(h)
        e = ea_ref[at, :].astype(F32) + eb_ref[at, :].astype(F32)
        dh = cot_ref[far, :].astype(F32) + norm_back(n2, r2, e * gain_ref[2:3, :])
        dh_ref[at, :] = dh
        dy_ref[at, :] = norm_back(n1, r1, dh * gain_ref[1:2, :]).astype(BF16)
        gb_ref[0] += fold_rows(e * n2)
        gb_ref[1] += fold_rows(e)
        gb_ref[2] += fold_rows(dh * n1)
        gb_ref[3] += fold_rows(dh)

    row_steps(rows, body)
    do = from_features(dy_ref[...], w_refs, slice(3 * cols, 4 * cols))
    do_ref[...] = do.astype(BF16)


def mid_back(chunk, x, ya, yb, ea, eb, cot, gain, bias, w):
    rows, width = ea.shape
    cols = w[0].shape[1] // 4
    return kernel_call(
        functools.partial(mid_back_kernel, chunk),
        "mid_back",
        [
            sds((rows, width), F32),
            sds((rows, width), BF16),
            sds((rows, cols), BF16),
            sds((4, 8, width), F32),
        ],
        (x, ya, yb, ea, eb, cot, gain, bias, *w),
        smems=0,
        flops=2 * rows * width * cols,
    )


def attend_back_kernel(q_ref, p0_ref, p1_ref, o0, o1, d0, d1, cos_ref, sin_ref, g_ref):
    rows, cols = o0.shape

    @pl.loop(0, cols // LANES)
    def _(i):
        cos, sin = cos_ref[...], sin_ref[...]
        start = i * LANES
        at = lanes_at(start, LANES)
        q = q_ref[:, at]
        k = q_ref[:, lanes_at(cols + start, LANES)]
        v = q_ref[:, lanes_at(2 * cols + start, LANES)]
        do = (d0[:, at], d1[:, at])
        prod = [a.astype(F32) * b[:, at].astype(F32) for a, b in zip(do, (o0, o1))]
        dq, dk, dv = [], [], []
        for turn, first in enumerate((True, False)):
            mine = head_lanes(rows, first)
            dqs = []
            for c, p_ref in enumerate((p0_ref, p1_ref)):
                ext = p_ref.shape[2]
                p = p_ref[2 * i + turn]
                dp = mm(jnp.where(mine, do[c], jnp.zeros_like(do[c])), v[:ext], NT)
                dot = jnp.sum(jnp.where(mine, prod[c], 0.0), axis=-1, keepdims=True)
                ds = (p.astype(F32) * (dp - dot)).astype(BF16)
                dqs.append(mm(ds, k[:ext], NN))
                dkc = mm(ds, q[c * rows : (c + 1) * rows], TN)
                dvc = mm(p, do[c], TN)
                if c == 0:
                    dk0, dv0 = dkc, dvc
            dk.append(jnp.concatenate([dk0 + dkc[:rows], dkc[rows:]], axis=0))
            dv.append(jnp.concatenate([dv0 + dvc[:rows], dvc[rows:]], axis=0))
            dq.append(jnp.concatenate(dqs, axis=0))
        low = head_lanes(2 * rows, True)
        gq = jnp.where(low, dq[0], dq[1]) * HD ** (-0.5)
        gk = jnp.where(low, dk[0], dk[1])
        gv = jnp.where(low, dv[0], dv[1])
        g_ref[:, at] = (gq * cos - partner(gq) * sin).astype(BF16)
        g_ref[:, lanes_at(cols + start, LANES)] = (gk * cos - partner(gk) * sin).astype(BF16)
        g_ref[:, lanes_at(2 * cols + start, LANES)] = gv.astype(BF16)


def attend_back(qkv, probs, outs, grads, cos, sin):
    count, three = qkv.shape
    heads = probs[0].shape[0]
    return kernel_call(
        attend_back_kernel,
        "attend_back",
        sds((count, three), BF16),
        (qkv, *probs, *outs, *grads, cos, sin),
        smems=0,
        flops=10 * heads * count * count * HD,
    )


def in_back_kernel(ids_ref, g_ref, x_ref, *refs):
    w_refs, (keep_ref, give_ref, gb_ref) = refs[:-3], refs[-3:]
    three = g_ref.shape[1]
    rows = keep_ref.shape[0]
    gb_ref[...] = jnp.zeros_like(gb_ref)
    for turn, out_ref in enumerate((give_ref, keep_ref)):
        base = (1 - ids_ref[1] if turn == 0 else ids_ref[1]) * rows
        g = g_ref[pl.ds(pl.multiple_of(base, rows), rows), :]
        into_features(out_ref, slice(None), g, w_refs, slice(0, three))

        @pl.loop(0, rows // STEP)
        def _(i, base=base, out_ref=out_ref):
            e = out_ref[pl.ds(pl.multiple_of(i * STEP, STEP), STEP), :].astype(F32)
            far = pl.ds(pl.multiple_of(base + i * STEP, STEP), STEP)
            n0, _ = norm_stats(x_ref[far, :].astype(F32))
            gb_ref[0] += fold_rows(e * n0)
            gb_ref[1] += fold_rows(e)


def in_back(ids, g, x, w):
    count, three = g.shape
    width = x.shape[1]
    part = sds((count // 2, width), BF16)
    return kernel_call(
        in_back_kernel, "in_back", [part, part, sds((2, 8, width), F32)], (ids, g, x, *w),
    )


def gain_sum_kernel(gb0_ref, g12a, g12b, g3, mine_ref, other_ref):
    share = 0.5
    rows = []
    for kind in range(2):
        rows += [
            gb0_ref[kind],
            share * (g12a[2 + kind] + g12b[2 + kind]),
            share * (g12a[kind] + g12b[kind]),
            share * g3[kind],
        ]
    half = mine_ref.shape[1]
    for i, row in enumerate(rows):
        row = jnp.sum(row, axis=0, keepdims=True)
        mine_ref[i : i + 1, :] = row[:, :half]
        other_ref[i : i + 1, :] = row[:, half:]


def gain_sum(gb0, g12, g3):
    out = sds((8, gb0.shape[-1] // 2), F32)
    return kernel_call(gain_sum_kernel, "gain_pack", [out, out], (gb0, *g12, g3), smems=0)


def gain_pack_kernel(*refs):
    out_ref = refs[-1]
    total = refs[0][...] + refs[1][...] + refs[2][...] + refs[3][...]
    filler = jnp.zeros((LANES - total.shape[0], total.shape[1]), F32)
    out_ref[...] = jnp.concatenate([total, filler], axis=0).T.astype(BF16)


def gain_pack(parts):
    out = sds((parts[0].shape[1], LANES), BF16)
    return kernel_call(gain_pack_kernel, "gain_pack", out, tuple(parts), smems=0)


def tokens_back_kernel(ids_ref, x_ref, keep_ref, got_ref, dh0_ref, dh1_ref, gain_ref, out_ref):
    side = ids_ref[1]
    rows = got_ref.shape[0]

    def body(at):
        far = pl.ds(pl.multiple_of(side * rows + at.start, STEP), STEP)
        e = keep_ref[at, :].astype(F32) + got_ref[at, :].astype(F32)
        n0, r0 = norm_stats(x_ref[far, :].astype(F32))
        dh = jnp.where(side == 0, dh0_ref[at, :], dh1_ref[at, :])
        join_cores(ids_ref, dh + norm_back(n0, r0, e * gain_ref[0:1, :]), out_ref, at)

    row_steps(rows, body)


def tokens_back(ids, x, keep, got, dhs, gain):
    return kernel_call(
        tokens_back_kernel, "tokens_back", sds(got.shape, F32), (ids, x, keep, got, *dhs, gain),
    )


def split_kernel(up_ref, down_ref, up_out, down_out):
    half = up_out.shape[0]
    up_out[...] = up_ref[:half, :]
    down_out[...] = down_ref[half:, :]


def split(up, down):
    out = sds((up.shape[0] // 2, up.shape[1]), BF16)
    return kernel_call(split_kernel, "split", [out, out], (up, down), smems=0)


def stage_kernel(*refs):
    ins, out_ref, sem = refs[:-2], refs[-2], refs[-1]
    copies, start = [], 0
    for ref in ins:
        parts = [ref.at[i] for i in range(ref.shape[0])] if len(ref.shape) == 3 else [ref]
        for part in parts:
            cols = part.shape[1]
            dst = out_ref.at[:, pl.ds(start, cols)]
            copies.append(pltpu.make_async_copy(part, dst, sem.at[len(copies)]))
            start += cols
    for copy in copies:
        copy.start()
    for copy in copies:
        copy.wait()


def stage(*arrays):
    rows = arrays[0].shape[-2]
    cols = sum(a.size // rows for a in arrays)
    return pl.pallas_call(
        stage_kernel,
        in_specs=[pl.BlockSpec(memory_space=pltpu.HBM)] * len(arrays),
        out_specs=whole(),
        out_shape=sds((rows, cols), BF16),
        scratch_shapes=[pltpu.SemaphoreType.DMA((4 * len(arrays),))],
        compiler_params=pltpu.CompilerParams(vmem_limit_bytes=VMEM_LIMIT),
        cost_estimate=cost_of("stage"),
        name="stage",
    )(*arrays)


def assemble_kernel(places, *refs):
    ins, out, sem = refs[: len(places)], refs[-2], refs[-1]
    copies = []
    for i, (src, at) in enumerate(zip(ins, places)):
        copies.append(pltpu.make_async_copy(src, out.at[pl.ds(at, src.shape[0])], sem.at[i]))
    for copy in copies:
        copy.start()
    for copy in copies:
        copy.wait()


def assemble(places, pieces):
    rows = sum(piece.shape[0] for piece in pieces)
    return pl.pallas_call(
        functools.partial(assemble_kernel, places),
        in_specs=[anywhere()] * len(pieces),
        out_specs=whole(),
        out_shape=sds((rows, pieces[0].shape[1]), BF16),
        scratch_shapes=[pltpu.SemaphoreType.DMA((len(pieces),))],
        compiler_params=pltpu.CompilerParams(vmem_limit_bytes=VMEM_LIMIT),
        cost_estimate=cost_of("assemble"),
        name="assemble",
    )(*pieces)


def term_rows(groups, block, index, to):
    total = None
    for refs in groups:
        if len(refs) == 2:
            ref, first = (refs[0], 0) if index == 0 else (refs[1], (index - 1) * block)
        else:
            ref, first = refs[0], index * block
        part = ref[first : first + block, to].astype(F32)
        total = part if total is None else total + part
    return total


def unflatten(refs, layout):
    groups, n = [], 0
    for terms in layout:
        group = []
        for count in terms:
            group.append(refs[n : n + count])
            n += count
        groups.append(group)
    return groups, refs[n:]


def ring_sum_kernel(layout, block, index, way, *refs):
    groups, refs = unflatten(refs, layout)
    out_ref, came = refs[-1], refs[:-1]
    half = block // 2
    start = 0
    for group in groups:
        cols = group[0][0].shape[1]
        for c in range(0, cols, UNITS):
            n = min(UNITS, cols - c)
            own, to = slice(c, c + n), slice(start + c, start + c + n)
            if index == 0:
                rows = slice(way * half, (way + 1) * half)
                total = sum(term[0][rows, own].astype(F32) for term in group)
                out_ref[:, to] = total.astype(BF16)
                continue
            total = term_rows(group, block, index + way, own)
            part = came[0][:, to].astype(F32)
            if part.shape[0] == block:
                out_ref[:, to] = (total + part).astype(BF16)
            else:
                hit = slice(0, half) if way == 0 else slice(half, block)
                rest = slice(half, block) if way == 0 else slice(0, half)
                out_ref[hit, to] = (total[hit] + part).astype(BF16)
                out_ref[rest, to] = total[rest].astype(BF16)
        start += cols


def ring_sum(index, way, block, groups, came=()):
    layout = [[len(term) for term in group] for group in groups]
    flat = [a for group in groups for term in group for a in term]
    cols = sum(group[0][0].shape[1] for group in groups)
    return kernel_call(
        functools.partial(ring_sum_kernel, layout, block, index, way), "ring_sum",
        sds((block // 2 if index == 0 else block, cols), BF16), (*flat, *came), smems=0,
    )


def ring_end_kernel(layout, splits, index, *refs):
    groups, refs = unflatten(refs, layout)
    (up, down), outs = refs[:2], refs[2:]
    block = up.shape[0]
    start, o = 0, 0
    for group, sizes in zip(groups, splits):
        here = 0
        for count, cols in sizes:
            for i in range(max(count, 1)):
                to, own = slice(start, start + cols), slice(here, here + cols)
                total = term_rows(group, block, index, own)
                total = total + up[:, to].astype(F32) + down[:, to].astype(F32)
                if count == 0:
                    turned = total.T
                    outs[o][...] = turned[0:4, :]
                    outs[o + 1][...] = turned[4:8, :]
                elif count > 1:
                    outs[o][i] = total
                else:
                    outs[o][...] = total
                start, here = start + cols, here + cols
            o += 2 if count == 0 else 1


def ring_end(size, groups, came, splits):
    layout = [[len(term) for term in group] for group in groups]
    flat = [a for group in groups for term in group for a in term]
    block = came[0].shape[0]
    shapes = []
    for sizes in splits:
        for count, cols in sizes:
            if count == 0:
                shapes += [(4, block)] * 2
            else:
                shapes.append((count, block, cols) if count > 1 else (block, cols))
    return kernel_call(
        functools.partial(ring_end_kernel, layout, splits, size - 1), "ring_end",
        [sds(shape, F32) for shape in shapes], (*flat, *came), smems=0,
    )


class Ring:
    def __init__(self, n_dp, ids):
        self.size = n_dp // 2
        self.ids = ids
        self.up = self.shift(1)
        self.down = self.shift(-1)
        self.cores = [(i, i ^ 1) for i in range(n_dp)]

    def shift(self, by):
        return [
            (2 * chip_of(p, self.size) + c, 2 * chip_of((p + by) % self.size, self.size) + c)
            for p in range(self.size)
            for c in range(2)
        ]


def swap_cores(ring, value):
    return lax.ppermute(value, "dp", ring.cores)


class Gather:
    def __init__(self, ring, piece):
        self.ring = ring
        self.rows = piece.shape[0]
        self.pieces, self.places = [piece], [ring_order(ring.size).index(0) * self.rows]
        self.step_now = 0
        self.up = self.down = piece

    def step(self, *deps):
        self.step_now += 1
        ring, step = self.ring, self.step_now
        up, down = self.up, self.down
        if deps:
            up, down = after(up, *deps), after(down, *deps)
        shift = 0
        if step == ring.size // 2:
            shift = up.shape[0] // 2
            up, down = split(up, down)
            self.sent = up, down
        self.up = lax.ppermute(up, "dp", ring.up)
        self.down = lax.ppermute(down, "dp", ring.down)
        self.pieces += [self.up, self.down]
        order = ring_order(ring.size)
        self.places += [
            order.index(step if shift else -step) * self.rows,
            order.index(step) * self.rows + shift,
        ]
        return self.up, self.down

    def end(self, *deps):
        pieces = self.pieces
        if deps:
            pieces = [after(pieces[0], *deps), *pieces[1:]]
        return assemble(self.places, pieces)


class Reduce:
    def __init__(self, ring, block, groups):
        self.ring, self.block, self.groups = ring, block, groups
        self.index = 0
        self.came = ()

    def step(self, *deps):
        groups = self.groups
        if deps:
            first = groups[0][0]
            groups = [[(after(first[0], *deps), *first[1:]), *groups[0][1:]], *groups[1:]]
        if self.index == 0:
            groups = [[(term[0],) for term in group] for group in groups]
        sent, came = [], []
        for way, perm in enumerate((self.ring.up, self.ring.down)):
            sent.append(ring_sum(self.index, way, self.block, groups, self.came[way : way + 1]))
            came.append(lax.ppermute(sent[way], "dp", perm))
        self.sent, self.came = tuple(sent), tuple(came)
        self.index += 2 if self.index else 1
        return self.came

    def end(self, splits, *deps):
        came = self.came
        if deps:
            came = after(came[0], *deps), came[1]
        return ring_end(self.ring.size, self.groups, came, splits)


def per_device(n_dp, tokens, seq_lengths, ln_gain, ln_bias, w_qkv, w_out, w_up, w_down, cotangent):
    ids = jnp.stack([lax.axis_index("dp"), lax.axis_index("mp")]).astype(jnp.int32)
    ring = Ring(n_dp, ids)
    count, width = tokens.shape
    rows = count // 2
    w_rows, units = w_up.shape
    cols = w_out.shape[0]

    def swap_sides(value):
        return lax.ppermute(value, "mp", [(0, 1), (1, 0)])

    done = {}

    def dep(name):
        found = []
        for other in ORDER.get(name, ()):
            value = done[other]
            found += list(value) if isinstance(value, (tuple, list)) else [value]
        return found

    def tie(value, name):
        others = dep(name)
        return after(value, *others) if others else value

    def both(own, name):
        return [own, swap_cores(ring, tie(own, name))]

    g1 = Gather(ring, stage(after(w_qkv, ids), w_out.T))
    done["s11"] = g1.step()
    cot_got = done["cot_got"] = swap_sides(tie(cotangent, "cot_swap"))
    stage2, stage3 = stage(w_up), stage(w_down.T)
    done["stages"] = stage2, stage3
    done["s12"] = g1.step(*dep("s12"))
    x, a1, gain, bias = prepare(ids, tokens, ln_gain, ln_bias)
    done["a1"] = a1
    done["s13"] = g1.step(*dep("s13"))
    done["s14"] = g1.step(*dep("s14"))
    done["s14_sent"] = g1.sent
    g2 = Gather(ring, tie(stage2, "s21"))
    done["s21"] = g2.step()
    g3 = Gather(ring, tie(stage3, "s31"))
    done["s31"] = g3.step()
    own = done["own1"] = g1.end(*dep("own1"))
    w1 = both(own, "w1")
    cos, sin = rotary_pair(tie(seq_lengths, "rotary"), count)
    cot = done["cot"] = cotangent_rows(tie(ids, "cot"), cotangent, cot_got)
    done["s22"] = g2.step(*dep("s22"))
    qkv = done["qkv"] = qkv_project(tie(a1, "qkv"), w1, cos, sin)
    probs, outs, ys, a3s, mids, zs, backs, mid_backs = [], [], [], [], [], [], [], []
    for c in range(2):
        p, o, part = attend(c * rows, rows, tie(seq_lengths, f"attend{c}"), qkv, w1)
        probs.append(p)
        outs.append(o)
        done[f"part{c}"] = part
        if c == 0:
            ys.append((part, swap_sides(part)))
            done["y0"] = ys[0][1]
    done["s32"] = g3.step(*dep("s32"))
    done["s23"] = g2.step(*dep("s23"))
    ys.append((part, swap_sides(tie(part, "y1"))))
    done["y1"] = ys[1][1]
    done["s33"] = g3.step(*dep("s33"))
    done["s24"] = g2.step(*dep("s24"))
    own = done["own2"] = g2.end(*dep("own2"))
    w2 = both(own, "w2")
    a3s.append(mid_norm(0, tie(x, "norm0"), *ys[0], gain, bias))
    done["norm0"] = a3s[0]
    done["s34"] = g3.step(*dep("s34"))
    own = done["own3"] = g3.end(*dep("own3"))
    w3 = both(own, "w3")
    mids.append(up_project(tie(a3s[0], "up0"), w2))
    done["up0"] = mids[0][0]
    part = down_project(tie(mids[0][0], "down0"), w3)
    done["down0"] = part
    zs.append((part, swap_sides(part)))
    a3s.append(mid_norm(1, tie(x, "norm1"), *ys[1], gain, bias))
    done["norm1"] = a3s[1]
    mids.append(up_project(tie(a3s[1], "up1"), w2))
    done["up1"] = mids[1][0]
    part = down_project(tie(mids[1][0], "down1"), w3)
    done["down1"] = part
    zs.append((part, swap_sides(part)))
    for c in range(2):
        z = zs[c][0], tie(zs[c][1], f"back{c}")
        dz, du, part = mlp_back(c, *z, cot, gain, mids[c][1], w3, w2)
        backs.append((dz, du, (part, swap_sides(part))))
        done[f"back{c}"], done[f"da{c}"] = dz, backs[c][2][1]
    dzs, dus = [b[0] for b in backs], [b[1] for b in backs]
    gs = [m[0] for m in mids]

    def mid(c):
        w = mid_back(c, tie(x, f"mid{c}"), *ys[c], *backs[c][2], cot, gain, bias, w1)
        done[f"mid{c}"] = w[0]
        mid_backs.append(w)

    def grad(which, products, name):
        others = dep(name)
        if others:
            (lefts, rights), rest = products[0], products[1:]
            products = [([after(lefts[0], *others), *lefts[1:]], rights), *rest]
        term = weight_grad(which, ring.size, products)
        done[name] = term[0]
        return term

    def swap_term(term, name):
        far = swap_cores(ring, term[0])
        done[name + "_far"] = far
        return far, swap_cores(ring, after(term[1], far, *dep(name + "_near")))

    def ring_step(reduce, name):
        done[name] = reduce.step(*dep(name))
        done[name + "_sent"] = reduce.sent

    down_other = grad(1, [(dzs, gs)], "down_other")
    up_other = grad(1, [(a3s, dus)], "up_other")
    down_mine = grad(0, [(dzs, gs)], "down_mine")
    down_got = swap_term(down_other, "down")
    up_mine = grad(0, [(a3s, dus)], "up_mine")
    up_got = swap_term(up_other, "up")
    mlp_ring = Reduce(ring, w_rows, [[down_mine, down_got], [up_mine, up_got]])
    ring_step(mlp_ring, "m1")
    mid(0)
    output, gb3 = last_norm(tie(ids, "last"), x, cot, gain, bias, ys, zs)
    done["last"] = output
    ring_step(mlp_ring, "m2")
    mid(1)
    grads = [m[2] for m in mid_backs]
    g_qkv = done["g_qkv"] = attend_back(tie(qkv, "g_qkv"), probs, outs, grads, cos, sin)
    attn_products = [([a1], [g_qkv]), ([m[1] for m in mid_backs], outs)]
    attn_other = grad(1, attn_products, "attn_other")
    attn_got = swap_term(attn_other, "attn")
    ring_step(mlp_ring, "m3")
    part_keep, part_give, gb0 = in_back(ids, tie(g_qkv, "in_back"), x, w1)
    done["in_back"] = part_keep
    gain_mine, gain_other = gain_sum(gb0, [m[3] for m in mid_backs], gb3)
    done["gain_sum"] = gain_mine
    gain_terms = [
        gain_mine,
        swap_cores(ring, gain_other),
        swap_sides(gain_mine),
        lax.ppermute(gain_other, ("dp", "mp"), [(i, i ^ 3) for i in range(2 * n_dp)]),
    ]
    attn_mine = grad(0, attn_products, "attn_mine")
    gains = gain_pack([tie(gain_terms[0], "gains"), *gain_terms[1:]])
    done["gains"] = gains
    part_got = done["part_got"] = swap_sides(tie(part_give, "part_give"))
    attn_ring = Reduce(ring, w_rows, [[attn_mine, attn_got], [(gains,)]])
    ring_step(attn_ring, "q1")
    ring_step(mlp_ring, "m4")
    ring_step(attn_ring, "q2")
    grad_tokens = done["tokens"] = tokens_back(
        tie(ids, "tokens"), x, part_keep, part_got, [m[0] for m in mid_backs], gain
    )
    ring_step(attn_ring, "q3")
    grad_down, grad_up = mlp_ring.end([[(1, units)], [(1, units)]], *dep("m_end"))
    done["m_end"] = grad_down
    ring_step(attn_ring, "q4")
    grad_qkv, grad_out, grad_gain, grad_bias = attn_ring.end([[(3, cols), (1, cols)], [(0, LANES)]])
    return output, grad_tokens, grad_qkv, grad_out.T, grad_up, grad_down.T, grad_gain, grad_bias


def layer_norm(values, norm_gain, norm_bias):
    average = jnp.mean(values, axis=-1, keepdims=True)
    centred = values - average
    variance = jnp.mean(centred * centred, axis=-1, keepdims=True)
    return centred * lax.rsqrt(variance + NORM_EPS) * norm_gain + norm_bias


def norm_pull(values, norm_gain, norm_bias, grad_result):
    result, puller = jax.vjp(layer_norm, values, norm_gain, norm_bias)
    return puller(grad_result)


def seq_layout(lengths, block_size):
    block_count = lengths.shape[0]
    block_ids = jnp.arange(block_count, dtype=jnp.int32)
    starts = lengths > 0
    earlier = starts[None, :] & (block_ids[None, :] <= block_ids[:, None])
    owners = jnp.max(jnp.where(earlier, block_ids[None, :], 0), axis=1)
    owner_len = jnp.sum(
        jnp.where(block_ids[None, :] == owners[:, None], lengths[None, :], 0), axis=1
    )
    places = jnp.arange(block_count * block_size, dtype=jnp.int32)
    tok_owner = jnp.repeat(owners, block_size)
    position = places - tok_owner * block_size
    is_valid = position < jnp.repeat(owner_len, block_size)
    allowed = (
        (tok_owner[:, None] == tok_owner[None, :])
        & (places[None, :] <= places[:, None])
        & is_valid[None, :]
    )
    return (position, allowed)


def rotary_tables(position, width):
    frequency = ROPE_BASE ** (-jnp.arange(width // 2, dtype=jnp.float32) * 2.0 / width)
    angles = position.astype(jnp.float32)[:, None] * frequency[None, :]
    return (jnp.cos(angles), jnp.sin(angles))


def rotate(values, cos_table, sin_table):
    half_width = values.shape[-1] // 2
    front_half = values[..., :half_width]
    back_half = values[..., half_width:]
    cos_part = cos_table[:, None, :]
    sin_part = sin_table[:, None, :]
    return jnp.concatenate(
        [
            front_half * cos_part - back_half * sin_part,
            back_half * cos_part + front_half * sin_part,
        ],
        axis=-1,
    )


def attention_scores(queries, keys_rot, allowed, scale):
    raw_scores = (
        jnp.einsum("hqd,hkd->hqk", queries, keys_rot, preferred_element_type=jnp.float32) * scale
    )
    return jnp.where(allowed[None, :, :], raw_scores, MASK_FILL)


def plain_device(tokens, seq_lengths, ln_gain, ln_bias, w_qkv, w_out, w_up, w_down, cotangent):
    full_qkv, full_out, full_up, full_down = (
        lax.all_gather(w_qkv, "dp", axis=1, tiled=True),
        lax.all_gather(w_out, "dp", axis=1, tiled=True),
        lax.all_gather(w_up, "dp", axis=0, tiled=True),
        lax.all_gather(w_down, "dp", axis=1, tiled=True),
    )
    tok_count = tokens.shape[0]
    shard_rows = cotangent.shape[0]
    row_start = lax.axis_index("mp") * shard_rows
    heads_here = full_out.shape[0] // HD
    scale = HD ** (-0.5)
    position, allowed = seq_layout(seq_lengths, BLOCK)
    cos_table, sin_table = rotary_tables(position, HD)

    def to_heads(values):
        return jnp.transpose(values.reshape(tok_count, heads_here, HD), (1, 0, 2))

    def from_heads(values):
        return jnp.transpose(values, (1, 0, 2)).reshape(tok_count, heads_here * HD)

    def rotated(values):
        return rotate(values.reshape(tok_count, heads_here, HD), cos_table, sin_table)

    inputs = tokens.astype(jnp.float32)
    normed_in = layer_norm(inputs, ln_gain[0], ln_bias[0]).astype(jnp.bfloat16)
    projected = jnp.einsum("td,cde->cte", normed_in, full_qkv, preferred_element_type=jnp.float32)
    queries = jnp.transpose(rotated(projected[0]), (1, 0, 2)).astype(jnp.bfloat16)
    keys_rot = jnp.transpose(rotated(projected[1]), (1, 0, 2)).astype(jnp.bfloat16)
    values_h = to_heads(projected[2]).astype(jnp.bfloat16)
    scores = attention_scores(queries, keys_rot, allowed, scale)
    top_score = jnp.max(scores, axis=-1, keepdims=True)
    expo = jnp.exp(scores - top_score)
    row_total = jnp.sum(expo, axis=-1, keepdims=True)
    probs = expo / row_total
    log_total = top_score + jnp.log(row_total)
    attended = jnp.einsum(
        "hqk,hkd->hqd", probs.astype(jnp.bfloat16), values_h, preferred_element_type=jnp.float32
    )
    mixed_heads = from_heads(attended).astype(jnp.bfloat16)
    attn_part = jnp.dot(mixed_heads, full_out, preferred_element_type=jnp.float32)
    attn_sum = lax.psum_scatter(
        attn_part.astype(jnp.bfloat16), "mp", scatter_dimension=0, tiled=True
    ).astype(jnp.float32)
    resid_in = lax.dynamic_slice_in_dim(inputs, row_start, shard_rows, 0)
    hidden_state = resid_in + layer_norm(attn_sum, ln_gain[1], ln_bias[1])
    normed_mid = layer_norm(hidden_state, ln_gain[2], ln_bias[2]).astype(jnp.bfloat16)
    mlp_input = lax.all_gather(normed_mid, "mp", axis=0, tiled=True)
    pre_act = jnp.dot(mlp_input, full_up, preferred_element_type=jnp.float32)
    act_low = jax.nn.gelu(pre_act, approximate=True).astype(jnp.bfloat16)
    mlp_part = jnp.dot(act_low, full_down, preferred_element_type=jnp.float32)
    mlp_sum = lax.psum_scatter(
        mlp_part.astype(jnp.bfloat16), "mp", scatter_dimension=0, tiled=True
    ).astype(jnp.float32)
    output = (hidden_state + layer_norm(mlp_sum, ln_gain[3], ln_bias[3])).astype(jnp.bfloat16)
    grad_result = cotangent.astype(jnp.float32)
    grad_mlp_sum, grad_gain3, grad_bias3 = norm_pull(mlp_sum, ln_gain[3], ln_bias[3], grad_result)
    grad_mlp_rows = lax.all_gather(grad_mlp_sum.astype(jnp.bfloat16), "mp", axis=0, tiled=True)
    grad_down = jnp.einsum("tf,te->fe", act_low, grad_mlp_rows, preferred_element_type=jnp.float32)
    grad_act = jnp.einsum("te,fe->tf", grad_mlp_rows, full_down, preferred_element_type=jnp.float32)
    gelu_puller = jax.vjp(lambda values: jax.nn.gelu(values, approximate=True), pre_act)[1]
    grad_pre = gelu_puller(grad_act)[0].astype(jnp.bfloat16)
    grad_up = jnp.einsum("td,tf->df", mlp_input, grad_pre, preferred_element_type=jnp.float32)
    grad_mid_part = jnp.einsum("tf,df->td", grad_pre, full_up, preferred_element_type=jnp.float32)
    grad_mid = lax.psum_scatter(
        grad_mid_part.astype(jnp.bfloat16), "mp", scatter_dimension=0, tiled=True
    ).astype(jnp.float32)
    grad_hidden_norm, grad_gain2, grad_bias2 = norm_pull(
        hidden_state, ln_gain[2], ln_bias[2], grad_mid
    )
    grad_hidden = grad_result + grad_hidden_norm
    grad_attn_sum, grad_gain1, grad_bias1 = norm_pull(attn_sum, ln_gain[1], ln_bias[1], grad_hidden)
    grad_attn_rows = lax.all_gather(grad_attn_sum.astype(jnp.bfloat16), "mp", axis=0, tiled=True)
    grad_outproj = jnp.einsum(
        "tc,te->ce", mixed_heads, grad_attn_rows, preferred_element_type=jnp.float32
    )
    grad_mixed = jnp.einsum(
        "te,ce->tc", grad_attn_rows, full_out, preferred_element_type=jnp.float32
    ).astype(jnp.bfloat16)
    grad_heads = to_heads(grad_mixed)
    again_scores = attention_scores(queries, keys_rot, allowed, scale)
    again_probs = jnp.exp(again_scores - log_total)
    grad_probs = jnp.einsum(
        "hqd,hkd->hqk", grad_heads, values_h, preferred_element_type=jnp.float32
    )
    grad_values = jnp.einsum(
        "hqk,hqd->hkd",
        again_probs.astype(jnp.bfloat16),
        grad_heads,
        preferred_element_type=jnp.float32,
    )
    row_dot = jnp.sum(again_probs * grad_probs, axis=-1, keepdims=True)
    grad_scores = (again_probs * (grad_probs - row_dot) * scale).astype(jnp.bfloat16)
    grad_q_rot = jnp.einsum(
        "hqk,hkd->hqd", grad_scores, keys_rot, preferred_element_type=jnp.float32
    )
    grad_k_rot = jnp.einsum(
        "hqk,hqd->hkd", grad_scores, queries, preferred_element_type=jnp.float32
    )
    zero_heads = jnp.zeros((tok_count, heads_here, HD), jnp.float32)
    unrotate = jax.vjp(lambda values: rotate(values, cos_table, sin_table), zero_heads)[1]
    grad_query = unrotate(jnp.transpose(grad_q_rot, (1, 0, 2)))[0].reshape(
        tok_count, heads_here * HD
    )
    grad_key = unrotate(jnp.transpose(grad_k_rot, (1, 0, 2)))[0].reshape(tok_count, heads_here * HD)
    grad_value = from_heads(grad_values)
    grad_proj = jnp.stack(
        [
            grad_query.astype(jnp.bfloat16),
            grad_key.astype(jnp.bfloat16),
            grad_value.astype(jnp.bfloat16),
        ]
    )
    grad_qkv = jnp.einsum("td,cte->cde", normed_in, grad_proj, preferred_element_type=jnp.float32)
    grad_in_part = jnp.einsum(
        "cte,cde->td", grad_proj, full_qkv, preferred_element_type=jnp.float32
    )
    grad_in = lax.psum_scatter(
        grad_in_part.astype(jnp.bfloat16), "mp", scatter_dimension=0, tiled=True
    ).astype(jnp.float32)
    grad_norm_in, grad_gain0, grad_bias0 = norm_pull(resid_in, ln_gain[0], ln_bias[0], grad_in)
    grad_tokens = grad_hidden + grad_norm_in
    gain_grads = jnp.stack([grad_gain0, grad_gain1, grad_gain2, grad_gain3])
    bias_grads = jnp.stack([grad_bias0, grad_bias1, grad_bias2, grad_bias3])
    gain_grads, bias_grads = (
        lax.psum(gain_grads.astype(jnp.bfloat16), "mp").astype(jnp.float32),
        lax.psum(bias_grads.astype(jnp.bfloat16), "mp").astype(jnp.float32),
    )
    grad_qkv, grad_outproj, grad_up, grad_down, gain_grads, bias_grads = (
        lax.psum_scatter(
            grad_qkv.astype(jnp.bfloat16), "dp", scatter_dimension=1, tiled=True
        ).astype(jnp.float32),
        lax.psum_scatter(
            grad_outproj.astype(jnp.bfloat16), "dp", scatter_dimension=1, tiled=True
        ).astype(jnp.float32),
        lax.psum_scatter(
            grad_up.astype(jnp.bfloat16), "dp", scatter_dimension=0, tiled=True
        ).astype(jnp.float32),
        lax.psum_scatter(
            grad_down.astype(jnp.bfloat16), "dp", scatter_dimension=1, tiled=True
        ).astype(jnp.float32),
        lax.psum_scatter(
            gain_grads.astype(jnp.bfloat16), "dp", scatter_dimension=1, tiled=True
        ).astype(jnp.float32),
        lax.psum_scatter(
            bias_grads.astype(jnp.bfloat16), "dp", scatter_dimension=1, tiled=True
        ).astype(jnp.float32),
    )
    return (output, grad_tokens, grad_qkv, grad_outproj, grad_up, grad_down, gain_grads, bias_grads)


def solution(mesh):
    placed = (
        P("dp", None),
        P("dp"),
        P(),
        P(),
        P(None, "dp", "mp"),
        P("mp", "dp"),
        P("dp", "mp"),
        P("mp", "dp"),
        P(("dp", "mp"), None),
    )
    n_dp, n_mp = mesh.shape["dp"], mesh.shape["mp"]

    def layer(tokens, *rest):
        if n_mp == 2 and tokens.shape[1] == n_dp * LANES // 2:
            return per_device(n_dp, tokens, *rest)
        return plain_device(tokens, *rest)

    return jax.shard_map(
        layer,
        mesh=mesh,
        in_specs=placed,
        out_specs=(
            P(("dp", "mp"), None),
            P(("dp", "mp"), None),
            P(None, "dp", "mp"),
            P("mp", "dp"),
            P("dp", "mp"),
            P("mp", "dp"),
            P(None, "dp"),
            P(None, "dp"),
        ),
        check_vma=False,
    )
```

```python
import functools

import jax
import jax.numpy as jnp
from jax import lax
from jax.experimental import pallas as pl
from jax.experimental.pallas import tpu as pltpu
from jax.sharding import PartitionSpec as P

HD = 64
BLOCK = 128
LANES = 128
NORM_EPS = 1e-05
ROPE_BASE = 10000.0
MASK_FILL = -1e30
F32 = jnp.float32
BF16 = jnp.bfloat16
VMEM_LIMIT = 6 * 1024 * 1024
STEP = 128
NN = (((1,), (0,)), ((), ()))
NT = (((1,), (1,)), ((), ()))
TN = (((0,), (0,)), ((), ()))


def mm(left, right, dims):
    return lax.dot_general(left, right, dims, preferred_element_type=F32)


def sds(shape, dtype):
    return jax.ShapeDtypeStruct(shape, dtype)


def whole():
    return pl.BlockSpec(memory_space=pltpu.VMEM)


def smem():
    return pl.BlockSpec(memory_space=pltpu.SMEM)


def anywhere():
    return pl.BlockSpec(memory_space=pl.ANY)


TIMES = {
    "prepare": 3.3, "cotangent_rows": 1.5, "qkv_project": 2.0, "attend0": 2.5, "attend1": 4.4,
    "up_project": 4.3, "down_project": 1.3, "mlp_back": 5.4, "mid_norm": 2.5, "last_norm": 3.0, "weight_grad": 1.3, "mid_back": 3.3,
    "attend_back": 5.0, "in_back": 3.6, "gain_pack": 0.4, "tokens_back": 3.9, "stage": 0.5,
    "assemble": 1.2, "ring_sum": 1.3, "ring_end": 2.0, "rotary": 2.0, "split": 0.4,
}
TIME_SHARE = 1.0


def cost_of(name):
    return pl.CostEstimate(
        flops=0, bytes_accessed=int(TIMES[name] * TIME_SHARE * 3.69e6), transcendentals=0
    )


ORDER = {
    "s12": ("stages",), "s13": ("a1",), "s14": ("cot_got", "s11"), "s21": ("s14_sent",),
    "s31": ("s14",), "cot_swap": ("s11",), "w1": ("s21",), "rotary": ("own1",), "cot": ("own1",),
    "s22": ("own1",), "qkv": ("cot",), "attend1": ("part0", "s31"), "s23": ("part1",), "s24": ("y0",),
    "norm0": ("own2",), "y1": ("s32",), "s34": ("own2",), "own3": ("y1",), "up1": ("down0",),
    "down1": ("down0",), "back1": ("back0",), "up_other": ("down_other", "up1"),
    "down_mine": ("up_other",), "up_mine": ("down_mine", "down_far"), "up_near": ("da0", "up_mine"),
    "mid0": ("m1_sent",), "last": ("mid0",), "m2": ("last",), "mid1": ("m2_sent",),
    "attn_near": ("m2",), "m3": ("attn_other",), "in_back": ("m3_sent",), "attn_mine": ("gain_sum",),
    "gains": ("attn_mine",), "part_give": ("gains",), "m4": ("q1_sent",), "q2": ("m4_sent",),
    "tokens": ("q2_sent",), "q3": ("tokens",), "m_end": ("q3_sent",), "q4": ("m_end",),
    "q1": ("m3_sent",), "attn_other": ("m1_sent",),
}


def kernel_call(body, name, out_shape, args, smems=1, flops=0, nbytes=0, scratch=(), **extra):
    many = isinstance(out_shape, (list, tuple))
    return pl.pallas_call(
        body,
        in_specs=[smem()] * smems + [whole()] * (len(args) - smems),
        out_specs=[whole()] * len(out_shape) if many else whole(),
        out_shape=out_shape,
        scratch_shapes=list(scratch),
        compiler_params=pltpu.CompilerParams(vmem_limit_bytes=VMEM_LIMIT),
        cost_estimate=cost_of(name),
        name=name,
        **extra,
    )(*args)


def after(value, *others):
    return lax.optimization_barrier((value,) + others)[0]


def chip_of(place, size):
    if isinstance(place, int):
        return 2 * place if place < size // 2 else 2 * (size - 1 - place) + 1
    return jnp.where(place < size // 2, 2 * place, 2 * (size - 1 - place) + 1)


def ring_order(size):
    order = [size // 2]
    for step in range(size // 2 - 1, 0, -1):
        order += [step, -step]
    return order + [0]


def chip_lanes(ids_ref, width):
    size = width // LANES
    own = ids_ref[0] // 2
    here = jnp.where(own % 2 == 0, own // 2, size - 1 - own // 2)
    starts = [chip_of((here + step + size) % size, size) * LANES for step in ring_order(size)]
    return [pl.ds(pl.multiple_of(start, LANES), LANES) for start in starts]


def split_cores(ids_ref, ref, rows):
    places = chip_lanes(ids_ref, ref.shape[1])
    core = ids_ref[0] % 2
    own, other = [], []
    for i in range(0, len(places), 2):
        a, b = (ref[rows, place].astype(F32) for place in places[i : i + 2])
        low = lax.broadcasted_iota(jnp.int32, a.shape, 1) < LANES // 2
        first = jnp.where(low, a, pltpu.roll(b, LANES // 2, 1))
        second = jnp.where(low, pltpu.roll(a, LANES // 2, 1), b)
        own.append(jnp.where(core == 0, first, second))
        other.append(jnp.where(core == 0, second, first))
    return jnp.concatenate(own + other, axis=1)


def join_cores(ids_ref, values, out_ref, rows):
    places = chip_lanes(ids_ref, values.shape[1])
    core = ids_ref[0] % 2
    half = values.shape[1] // 2
    for i in range(0, len(places), 2):
        own = values[:, i * LANES // 2 : i * LANES // 2 + LANES]
        other = values[:, half + i * LANES // 2 : half + i * LANES // 2 + LANES]
        low = lax.broadcasted_iota(jnp.int32, own.shape, 1) < LANES // 2
        first = jnp.where(core == 0, own, other)
        second = jnp.where(core == 0, other, own)
        joined = (
            jnp.where(low, first, pltpu.roll(second, LANES // 2, 1)),
            jnp.where(low, pltpu.roll(first, LANES // 2, 1), second),
        )
        for place, part in zip(places[i : i + 2], joined):
            out_ref[rows, place] = part.astype(out_ref.dtype)


def norm_stats(values):
    centred = values - jnp.mean(values, axis=-1, keepdims=True)
    rstd = lax.rsqrt(jnp.mean(centred * centred, axis=-1, keepdims=True) + NORM_EPS)
    return centred * rstd, rstd


def norm_back(normed, rstd, scaled_grad):
    first = jnp.mean(scaled_grad, axis=-1, keepdims=True)
    second = jnp.mean(scaled_grad * normed, axis=-1, keepdims=True)
    return (scaled_grad - first - normed * second) * rstd


def fold_rows(values):
    return jnp.sum(values.reshape(-1, 8, values.shape[-1]), axis=0)


def lanes_at(start, count):
    if isinstance(start, int):
        return slice(start, start + count)
    return pl.ds(pl.multiple_of(start, LANES), count)


def from_features(left, w_refs, cols):
    total, start = None, 0
    for ref in w_refs:
        term = mm(left[:, start : start + ref.shape[0]], ref[:, cols], NN)
        total = term if total is None else total + term
        start += ref.shape[0]
    return total


def into_features(out_ref, rows, left, w_refs, cols):
    start = 0
    for ref in w_refs:
        part = mm(left, ref[:, cols], NT).astype(BF16)
        out_ref[rows, start : start + ref.shape[0]] = part
        start += ref.shape[0]


def row_steps(rows, body):
    @pl.loop(0, rows // STEP)
    def _(i):
        body(pl.ds(pl.multiple_of(i * STEP, STEP), STEP))


def prepare_kernel(ids_ref, x_ref, gain_ref, bias_ref, xp_ref, a1_ref, gp_ref, bp_ref):
    every = slice(0, gain_ref.shape[0])
    gp_ref[...] = split_cores(ids_ref, gain_ref, every)
    bp_ref[...] = split_cores(ids_ref, bias_ref, every)

    def body(at):
        x = split_cores(ids_ref, x_ref, at)
        xp_ref[at, :] = x.astype(BF16)
        normed, _ = norm_stats(x)
        a1_ref[at, :] = (normed * gp_ref[0:1, :] + bp_ref[0:1, :]).astype(BF16)

    row_steps(x_ref.shape[0], body)


def prepare(ids, x, gain, bias):
    return kernel_call(
        prepare_kernel,
        "prepare",
        [sds(x.shape, BF16), sds(x.shape, BF16), sds(gain.shape, F32), sds(bias.shape, F32)],
        (ids, x, gain, bias),
        nbytes=6 * x.size,
    )


def cotangent_kernel(ids_ref, own_ref, got_ref, out_ref):
    side = ids_ref[1]
    rows = own_ref.shape[0]
    for ref, base in ((own_ref, side * rows), (got_ref, (1 - side) * rows)):

        @pl.loop(0, rows // STEP)
        def _(i, ref=ref, base=base):
            at = pl.ds(pl.multiple_of(i * STEP, STEP), STEP)
            to = pl.ds(pl.multiple_of(base + i * STEP, STEP), STEP)
            out_ref[to, :] = split_cores(ids_ref, ref, at).astype(BF16)


def cotangent_rows(ids, own, got):
    rows, width = own.shape
    return kernel_call(
        cotangent_kernel, "cotangent_rows", sds((2 * rows, width), BF16), (ids, own, got),
        nbytes=8 * own.size,
    )


def partner(values):
    lane = lax.broadcasted_iota(jnp.int32, values.shape, 1)
    ahead = pltpu.roll(values, LANES - HD // 2, 1)
    behind = pltpu.roll(values, HD // 2, 1)
    return jnp.where(lax.rem(lane, HD) < HD // 2, ahead, behind)


def qkv_kernel(a_ref, cos_ref, sin_ref, *refs):
    w_refs, out_ref = refs[:-1], refs[-1]
    cols = w_refs[0].shape[1] // 4
    rows = 2 * BLOCK

    @pl.loop(0, a_ref.shape[0] // rows)
    def _(i):
        at = pl.ds(pl.multiple_of(i * rows, rows), rows)
        cos, sin = cos_ref[at, :], sin_ref[at, :]
        a = a_ref[at, :]
        for which in range(3):
            proj = from_features(a, w_refs, slice(which * cols, (which + 1) * cols))
            for start in range(0, cols, LANES):
                part = proj[:, start : start + LANES]
                if which < 2:
                    part = part * cos + partner(part) * sin
                if which == 0:
                    part = part.astype(BF16).astype(F32) * HD ** (-0.5)
                out_ref[at, which * cols + start : which * cols + start + LANES] = part.astype(BF16)


def qkv_project(a1, w, cos, sin):
    out = sds((a1.shape[0], w[0].shape[1] // 4 * 3), BF16)
    return kernel_call(qkv_kernel, "qkv_project", out, (a1, cos, sin, *w), smems=0)


def span_of(len_ref, block):
    start, size = jnp.int32(0), jnp.int32(0)
    for b in range(block + 1):
        here = len_ref[b]
        start = jnp.where(here > 0, b * BLOCK, start)
        size = jnp.where(here > 0, here, size)
    return start, start + size


def rotary_kernel(len_ref, cos_ref, sin_ref):
    lane = lax.broadcasted_iota(jnp.int32, (BLOCK, LANES), 1)
    row = lax.broadcasted_iota(jnp.int32, (BLOCK, LANES), 0)
    index = (lane % (HD // 2)).astype(F32)
    frequency = jnp.exp(index * (-2.0 / HD * 9.210340371976184))
    back = lane % HD >= HD // 2
    blocks = cos_ref.shape[0] // BLOCK

    @pl.loop(0, blocks)
    def _(b):
        start = jnp.int32(0)
        for k in range(blocks):
            start = jnp.where((k <= b) & (len_ref[k] > 0), k * BLOCK, start)
        at = pl.ds(pl.multiple_of(b * BLOCK, BLOCK), BLOCK)
        angle = (row + (b * BLOCK - start)).astype(F32) * frequency
        sin = jnp.sin(angle)
        cos_ref[at, :] = jnp.cos(angle)
        sin_ref[at, :] = jnp.where(back, sin, -sin)


def rotary_pair(lengths, count):
    out = sds((count, LANES), F32)
    return kernel_call(rotary_kernel, "rotary", [out, out], (lengths,))


def head_lanes(rows, first):
    lane = lax.broadcasted_iota(jnp.int32, (rows, LANES), 1)
    return (lane < HD) == first


def attend_kernel(row0, len_ref, q_ref, *refs):
    w_refs, (p_ref, o_ref, part_ref) = refs[:-3], refs[-3:]
    rows, cols = o_ref.shape
    ext = p_ref.shape[2]
    key = lax.broadcasted_iota(jnp.int32, (BLOCK, ext), 1)
    query = lax.broadcasted_iota(jnp.int32, (BLOCK, ext), 0)
    masks = []
    for b in range(rows // BLOCK):
        lo, hi = span_of(len_ref, row0 // BLOCK + b)
        seen = (key >= lo) & (key < hi) & (key <= query + (row0 + b * BLOCK))
        masks.append(jnp.where(seen, 0.0, MASK_FILL))
    mask = jnp.concatenate(masks, axis=0)
    head = 0
    for start in range(0, cols, LANES):
        q = q_ref[row0 : row0 + rows, start : start + LANES]
        k = q_ref[0:ext, cols + start : cols + start + LANES]
        v = q_ref[0:ext, 2 * cols + start : 2 * cols + start + LANES]
        outs = []
        for first in (True, False):
            mine = head_lanes(rows, first)
            s = mm(jnp.where(mine, q, jnp.zeros_like(q)), k, NT) + mask
            e = jnp.exp(s - jnp.max(s, axis=-1, keepdims=True))
            p = (e * (1.0 / jnp.sum(e, axis=-1, keepdims=True))).astype(BF16)
            p_ref[head] = p
            head += 1
            outs.append(mm(p, v, NN))
        o_ref[:, start : start + LANES] = jnp.where(
            head_lanes(rows, True), outs[0], outs[1]
        ).astype(BF16)
    into_features(part_ref, slice(None), o_ref[...], w_refs, slice(3 * cols, 4 * cols))


def attend(row0, rows, lengths, qkv, w):
    ext = row0 + rows
    cols = qkv.shape[1] // 3
    width = sum(piece.shape[0] for piece in w)
    return kernel_call(
        functools.partial(attend_kernel, row0),
        "attend0" if row0 == 0 else "attend1",
        [sds((cols // HD, rows, ext), BF16), sds((rows, cols), BF16), sds((rows, width), BF16)],
        (lengths, qkv, *w),
    )


def hidden_of(x, ya, yb, gain_ref, bias_ref):
    n1, r1 = norm_stats(ya.astype(F32) + yb.astype(F32))
    return x.astype(F32) + n1 * gain_ref[1:2, :] + bias_ref[1:2, :], n1, r1


def chunk_rows(chunk, rows, at):
    return pl.ds(pl.multiple_of(chunk * rows + at.start, STEP), STEP)


UNITS = 512


def mid_norm_kernel(chunk, x_ref, ya_ref, yb_ref, gain_ref, bias_ref, a3_ref):
    rows = a3_ref.shape[0]

    def body(at):
        x = x_ref[chunk_rows(chunk, rows, at), :]
        h, _, _ = hidden_of(x, ya_ref[at, :], yb_ref[at, :], gain_ref, bias_ref)
        n2, _ = norm_stats(h)
        a3_ref[at, :] = (n2 * gain_ref[2:3, :] + bias_ref[2:3, :]).astype(BF16)

    row_steps(rows, body)


def mid_norm(chunk, x, ya, yb, gain, bias):
    body = functools.partial(mid_norm_kernel, chunk)
    return kernel_call(body, "mid_norm", sds(ya.shape, BF16), (x, ya, yb, gain, bias), smems=0)


def up_kernel(a3_ref, *refs):
    w_refs, (g_ref, gp_ref) = refs[:-2], refs[-2:]

    @pl.loop(0, w_refs[0].shape[1] // UNITS)
    def _(i):
        to = pl.ds(pl.multiple_of(i * UNITS, UNITS), UNITS)
        u = from_features(a3_ref[...], w_refs, to)
        k0 = 0.7978845608028654
        k1 = 0.044715
        sq = u * u
        th = jnp.tanh(u * (k0 + (k0 * k1) * sq))
        plus = 0.5 + 0.5 * th
        g_ref[:, to] = (u * plus).astype(BF16)
        slope = plus + (u * (k0 + (3.0 * k0 * k1) * sq)) * (0.5 - (0.5 * th) * th)
        gp_ref[:, to] = slope.astype(BF16)


def up_project(a3, w):
    out = sds((a3.shape[0], w[0].shape[1]), BF16)
    return kernel_call(up_kernel, "up_project", [out, out], (a3, *w), smems=0)


def down_kernel(g_ref, *refs):
    into_features(refs[-1], slice(None), g_ref[...], refs[:-1], slice(None))


def down_project(g, w):
    out = sds((g.shape[0], sum(piece.shape[0] for piece in w)), BF16)
    return kernel_call(down_kernel, "down_project", out, (g, *w), smems=0)


def mlp_back_kernel(chunk, za_ref, zb_ref, cot_ref, gain_ref, gp_ref, *refs):
    dz_ref, du_ref, part_ref = refs[-3:]
    pieces = (len(refs) - 3) // 2
    w3, w2 = refs[:pieces], refs[pieces : 2 * pieces]
    rows = za_ref.shape[0]

    def body(at):
        n3, r3 = norm_stats(za_ref[at, :].astype(F32) + zb_ref[at, :].astype(F32))
        cot = cot_ref[chunk_rows(chunk, rows, at), :].astype(F32)
        dz_ref[at, :] = norm_back(n3, r3, cot * gain_ref[3:4, :]).astype(BF16)

    row_steps(rows, body)

    @pl.loop(0, w3[0].shape[1] // UNITS)
    def _(i):
        to = pl.ds(pl.multiple_of(i * UNITS, UNITS), UNITS)
        dg = from_features(dz_ref[...], w3, to)
        du_ref[:, to] = (dg * gp_ref[:, to].astype(F32)).astype(BF16)

    into_features(part_ref, slice(None), du_ref[...], w2, slice(None))


def mlp_back(chunk, za, zb, cot, gain, gp, w3, w2):
    rows, width = za.shape
    units = gp.shape[1]
    return kernel_call(
        functools.partial(mlp_back_kernel, chunk),
        "mlp_back",
        [sds((rows, width), BF16), sds((rows, units), BF16), sds((rows, width), BF16)],
        (za, zb, cot, gain, gp, *w3, *w2),
        smems=0,
    )


def last_norm_kernel(ids_ref, x_ref, cot_ref, gain_ref, bias_ref, *refs):
    ys, zs, (out_ref, gb_ref) = refs[0:4], refs[4:8], refs[8:]
    rows = out_ref.shape[0]
    gb_ref[...] = jnp.zeros_like(gb_ref)
    for chunk in range(2):
        ya_ref, yb_ref = ys[2 * chunk : 2 * chunk + 2]
        za_ref, zb_ref = zs[2 * chunk : 2 * chunk + 2]

        def body(at, chunk=chunk, ya_ref=ya_ref, yb_ref=yb_ref, za_ref=za_ref, zb_ref=zb_ref):
            far = chunk_rows(chunk, rows, at)
            n3, _ = norm_stats(za_ref[at, :].astype(F32) + zb_ref[at, :].astype(F32))
            cot = cot_ref[far, :].astype(F32)
            gb_ref[0] += fold_rows(cot * n3)
            gb_ref[1] += fold_rows(cot)

            @pl.when(ids_ref[1] == chunk)
            def _():
                h, _, _ = hidden_of(x_ref[far, :], ya_ref[at, :], yb_ref[at, :], gain_ref, bias_ref)
                out = h + (n3 * gain_ref[3:4, :] + bias_ref[3:4, :])
                join_cores(ids_ref, out, out_ref, at)

        row_steps(rows, body)


def last_norm(ids, x, cot, gain, bias, ys, zs):
    rows, width = ys[0][0].shape
    return kernel_call(
        last_norm_kernel,
        "last_norm",
        [sds((rows, width), BF16), sds((2, 8, width), F32)],
        (ids, x, cot, gain, bias, *ys[0], *ys[1], *zs[0], *zs[1]),
    )


def weight_grad_kernel(which, sizes, *refs):
    far_ref, near_ref, left_sc = refs[-3:]
    half, block = left_sc.shape[0], far_ref.shape[0]
    start = 0
    for lefts, rights, cols in sizes:
        rows = 0
        for ref in refs[lefts[0] : lefts[1]]:
            part = ref[:, which * half : (which + 1) * half]
            left_sc[:, rows : rows + part.shape[0]] = part.T
            rows += part.shape[0]

        def blocks(first, count, rights=rights, start=start):
            for i in range(count):
                c = (first + i) * UNITS
                total, rows = None, 0
                for ref in refs[rights[0] : rights[1]]:
                    n = ref.shape[0]
                    term = mm(left_sc[:, rows : rows + n], ref[:, lanes_at(c, UNITS)], NN)
                    total = term if total is None else total + term
                    rows += n
                total = total.astype(BF16)
                far_ref[:, lanes_at(start + c, UNITS)] = total[:block]
                near_ref[:, lanes_at(start + c, UNITS)] = total[block:]

        pairs = cols // (2 * UNITS)
        if pairs > 1:
            pl.loop(0, pairs)(lambda i: blocks(2 * i, 2))
        else:
            blocks(0, cols // UNITS)
        start += cols


def weight_grad(which, size, products):
    args, sizes, total = [], [], 0
    for lefts, rights in products:
        cols = rights[0].shape[1]
        n = len(args)
        sizes.append(((n, n + len(lefts)), (n + len(lefts), n + len(lefts) + len(rights)), cols))
        args += list(lefts) + list(rights)
        total += cols
    half = args[0].shape[1] // 2
    count = sum(a.shape[0] for a in products[0][0])
    block = half // size
    return kernel_call(
        functools.partial(weight_grad_kernel, which, sizes),
        "weight_grad",
        [sds((block, total), BF16), sds((half - block, total), BF16)],
        tuple(args),
        smems=0,
        scratch=[pltpu.VMEM((half, count), BF16)],
    )


def mid_back_kernel(
    chunk, x_ref, ya_ref, yb_ref, ea_ref, eb_ref, cot_ref, gain_ref, bias_ref, *refs
):
    w_refs, (dh_ref, dy_ref, do_ref, gb_ref) = refs[:-4], refs[-4:]
    rows, cols = do_ref.shape
    gb_ref[...] = jnp.zeros_like(gb_ref)

    def body(at):
        far = chunk_rows(chunk, rows, at)
        h, n1, r1 = hidden_of(x_ref[far, :], ya_ref[at, :], yb_ref[at, :], gain_ref, bias_ref)
        n2, r2 = norm_stats(h)
        e = ea_ref[at, :].astype(F32) + eb_ref[at, :].astype(F32)
        dh = cot_ref[far, :].astype(F32) + norm_back(n2, r2, e * gain_ref[2:3, :])
        dh_ref[at, :] = dh
        dy_ref[at, :] = norm_back(n1, r1, dh * gain_ref[1:2, :]).astype(BF16)
        gb_ref[0] += fold_rows(e * n2)
        gb_ref[1] += fold_rows(e)
        gb_ref[2] += fold_rows(dh * n1)
        gb_ref[3] += fold_rows(dh)

    row_steps(rows, body)
    do = from_features(dy_ref[...], w_refs, slice(3 * cols, 4 * cols))
    do_ref[...] = do.astype(BF16)


def mid_back(chunk, x, ya, yb, ea, eb, cot, gain, bias, w):
    rows, width = ea.shape
    cols = w[0].shape[1] // 4
    return kernel_call(
        functools.partial(mid_back_kernel, chunk),
        "mid_back",
        [
            sds((rows, width), F32),
            sds((rows, width), BF16),
            sds((rows, cols), BF16),
            sds((4, 8, width), F32),
        ],
        (x, ya, yb, ea, eb, cot, gain, bias, *w),
        smems=0,
        flops=2 * rows * width * cols,
    )


def attend_back_kernel(q_ref, p0_ref, p1_ref, o0, o1, d0, d1, cos_ref, sin_ref, g_ref):
    rows, cols = o0.shape

    def pair(i):
        cos, sin = cos_ref[...], sin_ref[...]
        start = i * LANES
        at = lanes_at(start, LANES)
        q = q_ref[:, at]
        k = q_ref[:, lanes_at(cols + start, LANES)]
        v = q_ref[:, lanes_at(2 * cols + start, LANES)]
        do = (d0[:, at], d1[:, at])
        prod = [a.astype(F32) * b[:, at].astype(F32) for a, b in zip(do, (o0, o1))]
        dq, dk, dv = [], [], []
        for turn, first in enumerate((True, False)):
            mine = head_lanes(rows, first)
            dqs = []
            for c, p_ref in enumerate((p0_ref, p1_ref)):
                ext = p_ref.shape[2]
                p = p_ref[2 * i + turn]
                dp = mm(jnp.where(mine, do[c], jnp.zeros_like(do[c])), v[:ext], NT)
                dot = jnp.sum(jnp.where(mine, prod[c], 0.0), axis=-1, keepdims=True)
                ds = (p.astype(F32) * (dp - dot)).astype(BF16)
                dqs.append(mm(ds, k[:ext], NN))
                dkc = mm(ds, q[c * rows : (c + 1) * rows], TN)
                dvc = mm(p, do[c], TN)
                if c == 0:
                    dk0, dv0 = dkc, dvc
            dk.append(jnp.concatenate([dk0 + dkc[:rows], dkc[rows:]], axis=0))
            dv.append(jnp.concatenate([dv0 + dvc[:rows], dvc[rows:]], axis=0))
            dq.append(jnp.concatenate(dqs, axis=0))
        low = head_lanes(2 * rows, True)
        gq = jnp.where(low, dq[0], dq[1]) * HD ** (-0.5)
        gk = jnp.where(low, dk[0], dk[1])
        gv = jnp.where(low, dv[0], dv[1])
        g_ref[:, at] = (gq * cos - partner(gq) * sin).astype(BF16)
        g_ref[:, lanes_at(cols + start, LANES)] = (gk * cos - partner(gk) * sin).astype(BF16)
        g_ref[:, lanes_at(2 * cols + start, LANES)] = gv.astype(BF16)

    @pl.loop(0, cols // (2 * LANES))
    def _(i):
        pair(2 * i)
        pair(2 * i + 1)


def attend_back(qkv, probs, outs, grads, cos, sin):
    count, three = qkv.shape
    heads = probs[0].shape[0]
    return kernel_call(
        attend_back_kernel,
        "attend_back",
        sds((count, three), BF16),
        (qkv, *probs, *outs, *grads, cos, sin),
        smems=0,
        flops=10 * heads * count * count * HD,
    )


def in_back_kernel(ids_ref, g_ref, x_ref, *refs):
    w_refs, (keep_ref, give_ref, gb_ref) = refs[:-3], refs[-3:]
    three = g_ref.shape[1]
    rows = keep_ref.shape[0]
    gb_ref[...] = jnp.zeros_like(gb_ref)
    for turn, out_ref in enumerate((give_ref, keep_ref)):
        base = (1 - ids_ref[1] if turn == 0 else ids_ref[1]) * rows
        g = g_ref[pl.ds(pl.multiple_of(base, rows), rows), :]
        into_features(out_ref, slice(None), g, w_refs, slice(0, three))

        @pl.loop(0, rows // STEP)
        def _(i, base=base, out_ref=out_ref):
            e = out_ref[pl.ds(pl.multiple_of(i * STEP, STEP), STEP), :].astype(F32)
            far = pl.ds(pl.multiple_of(base + i * STEP, STEP), STEP)
            n0, _ = norm_stats(x_ref[far, :].astype(F32))
            gb_ref[0] += fold_rows(e * n0)
            gb_ref[1] += fold_rows(e)


def in_back(ids, g, x, w):
    count, three = g.shape
    width = x.shape[1]
    part = sds((count // 2, width), BF16)
    return kernel_call(
        in_back_kernel, "in_back", [part, part, sds((2, 8, width), F32)], (ids, g, x, *w),
    )


def gain_sum_kernel(gb0_ref, g12a, g12b, g3, mine_ref, other_ref):
    share = 0.5
    rows = []
    for kind in range(2):
        rows += [
            gb0_ref[kind],
            share * (g12a[2 + kind] + g12b[2 + kind]),
            share * (g12a[kind] + g12b[kind]),
            share * g3[kind],
        ]
    half = mine_ref.shape[1]
    for i, row in enumerate(rows):
        row = jnp.sum(row, axis=0, keepdims=True)
        mine_ref[i : i + 1, :] = row[:, :half]
        other_ref[i : i + 1, :] = row[:, half:]


def gain_sum(gb0, g12, g3):
    out = sds((8, gb0.shape[-1] // 2), F32)
    return kernel_call(gain_sum_kernel, "gain_pack", [out, out], (gb0, *g12, g3), smems=0)


def gain_pack_kernel(*refs):
    out_ref = refs[-1]
    total = refs[0][...] + refs[1][...] + refs[2][...] + refs[3][...]
    filler = jnp.zeros((LANES - total.shape[0], total.shape[1]), F32)
    out_ref[...] = jnp.concatenate([total, filler], axis=0).T.astype(BF16)


def gain_pack(parts):
    out = sds((parts[0].shape[1], LANES), BF16)
    return kernel_call(gain_pack_kernel, "gain_pack", out, tuple(parts), smems=0)


def tokens_back_kernel(ids_ref, x_ref, keep_ref, got_ref, dh0_ref, dh1_ref, gain_ref, out_ref):
    side = ids_ref[1]
    rows = got_ref.shape[0]

    def body(at):
        far = pl.ds(pl.multiple_of(side * rows + at.start, STEP), STEP)
        e = keep_ref[at, :].astype(F32) + got_ref[at, :].astype(F32)
        n0, r0 = norm_stats(x_ref[far, :].astype(F32))
        dh = jnp.where(side == 0, dh0_ref[at, :], dh1_ref[at, :])
        join_cores(ids_ref, dh + norm_back(n0, r0, e * gain_ref[0:1, :]), out_ref, at)

    row_steps(rows, body)


def tokens_back(ids, x, keep, got, dhs, gain):
    return kernel_call(
        tokens_back_kernel, "tokens_back", sds(got.shape, F32), (ids, x, keep, got, *dhs, gain),
    )


def split_kernel(up_ref, down_ref, up_out, down_out):
    half = up_out.shape[0]
    up_out[...] = up_ref[:half, :]
    down_out[...] = down_ref[half:, :]


def split(up, down):
    out = sds((up.shape[0] // 2, up.shape[1]), BF16)
    return kernel_call(split_kernel, "split", [out, out], (up, down), smems=0)


def stage_kernel(*refs):
    ins, out_ref, sem = refs[:-2], refs[-2], refs[-1]
    copies, start = [], 0
    for ref in ins:
        parts = [ref.at[i] for i in range(ref.shape[0])] if len(ref.shape) == 3 else [ref]
        for part in parts:
            cols = part.shape[1]
            dst = out_ref.at[:, pl.ds(start, cols)]
            copies.append(pltpu.make_async_copy(part, dst, sem.at[len(copies)]))
            start += cols
    for copy in copies:
        copy.start()
    for copy in copies:
        copy.wait()


def stage(*arrays):
    rows = arrays[0].shape[-2]
    cols = sum(a.size // rows for a in arrays)
    return pl.pallas_call(
        stage_kernel,
        in_specs=[pl.BlockSpec(memory_space=pltpu.HBM)] * len(arrays),
        out_specs=whole(),
        out_shape=sds((rows, cols), BF16),
        scratch_shapes=[pltpu.SemaphoreType.DMA((4 * len(arrays),))],
        compiler_params=pltpu.CompilerParams(vmem_limit_bytes=VMEM_LIMIT),
        cost_estimate=cost_of("stage"),
        name="stage",
    )(*arrays)


def assemble_kernel(places, *refs):
    ins, out, sem = refs[: len(places)], refs[-2], refs[-1]
    copies = []
    for i, (src, at) in enumerate(zip(ins, places)):
        copies.append(pltpu.make_async_copy(src, out.at[pl.ds(at, src.shape[0])], sem.at[i]))
    for copy in copies:
        copy.start()
    for copy in copies:
        copy.wait()


def assemble(places, pieces):
    rows = sum(piece.shape[0] for piece in pieces)
    return pl.pallas_call(
        functools.partial(assemble_kernel, places),
        in_specs=[anywhere()] * len(pieces),
        out_specs=whole(),
        out_shape=sds((rows, pieces[0].shape[1]), BF16),
        scratch_shapes=[pltpu.SemaphoreType.DMA((len(pieces),))],
        compiler_params=pltpu.CompilerParams(vmem_limit_bytes=VMEM_LIMIT),
        cost_estimate=cost_of("assemble"),
        name="assemble",
    )(*pieces)


def term_rows(groups, block, index, to):
    total = None
    for refs in groups:
        if len(refs) == 2:
            ref, first = (refs[0], 0) if index == 0 else (refs[1], (index - 1) * block)
        else:
            ref, first = refs[0], index * block
        part = ref[first : first + block, to].astype(F32)
        total = part if total is None else total + part
    return total


def unflatten(refs, layout):
    groups, n = [], 0
    for terms in layout:
        group = []
        for count in terms:
            group.append(refs[n : n + count])
            n += count
        groups.append(group)
    return groups, refs[n:]


def ring_sum_kernel(layout, block, index, way, *refs):
    groups, refs = unflatten(refs, layout)
    out_ref, came = refs[-1], refs[:-1]
    half = block // 2
    start = 0
    for group in groups:
        cols = group[0][0].shape[1]
        for c in range(0, cols, UNITS):
            n = min(UNITS, cols - c)
            own, to = slice(c, c + n), slice(start + c, start + c + n)
            if index == 0:
                rows = slice(way * half, (way + 1) * half)
                total = sum(term[0][rows, own].astype(F32) for term in group)
                out_ref[:, to] = total.astype(BF16)
                continue
            total = term_rows(group, block, index + way, own)
            part = came[0][:, to].astype(F32)
            if part.shape[0] == block:
                out_ref[:, to] = (total + part).astype(BF16)
            else:
                hit = slice(0, half) if way == 0 else slice(half, block)
                rest = slice(half, block) if way == 0 else slice(0, half)
                out_ref[hit, to] = (total[hit] + part).astype(BF16)
                out_ref[rest, to] = total[rest].astype(BF16)
        start += cols


def ring_sum(index, way, block, groups, came=()):
    layout = [[len(term) for term in group] for group in groups]
    flat = [a for group in groups for term in group for a in term]
    cols = sum(group[0][0].shape[1] for group in groups)
    return kernel_call(
        functools.partial(ring_sum_kernel, layout, block, index, way), "ring_sum",
        sds((block // 2 if index == 0 else block, cols), BF16), (*flat, *came), smems=0,
    )


def ring_end_kernel(layout, splits, index, *refs):
    groups, refs = unflatten(refs, layout)
    (up, down), outs = refs[:2], refs[2:]
    block = up.shape[0]
    start, o = 0, 0
    for group, sizes in zip(groups, splits):
        here = 0
        for count, cols in sizes:
            for i in range(max(count, 1)):
                to, own = slice(start, start + cols), slice(here, here + cols)
                total = term_rows(group, block, index, own)
                total = total + up[:, to].astype(F32) + down[:, to].astype(F32)
                if count == 0:
                    turned = total.T
                    outs[o][...] = turned[0:4, :]
                    outs[o + 1][...] = turned[4:8, :]
                elif count > 1:
                    outs[o][i] = total
                else:
                    outs[o][...] = total
                start, here = start + cols, here + cols
            o += 2 if count == 0 else 1


def ring_end(size, groups, came, splits):
    layout = [[len(term) for term in group] for group in groups]
    flat = [a for group in groups for term in group for a in term]
    block = came[0].shape[0]
    shapes = []
    for sizes in splits:
        for count, cols in sizes:
            if count == 0:
                shapes += [(4, block)] * 2
            else:
                shapes.append((count, block, cols) if count > 1 else (block, cols))
    return kernel_call(
        functools.partial(ring_end_kernel, layout, splits, size - 1), "ring_end",
        [sds(shape, F32) for shape in shapes], (*flat, *came), smems=0,
    )


class Ring:
    def __init__(self, n_dp, ids):
        self.size = n_dp // 2
        self.ids = ids
        self.up = self.shift(1)
        self.down = self.shift(-1)
        self.cores = [(i, i ^ 1) for i in range(n_dp)]

    def shift(self, by):
        return [
            (2 * chip_of(p, self.size) + c, 2 * chip_of((p + by) % self.size, self.size) + c)
            for p in range(self.size)
            for c in range(2)
        ]


def swap_cores(ring, value):
    return lax.ppermute(value, "dp", ring.cores)


class Gather:
    def __init__(self, ring, piece):
        self.ring = ring
        self.rows = piece.shape[0]
        self.pieces, self.places = [piece], [ring_order(ring.size).index(0) * self.rows]
        self.step_now = 0
        self.up = self.down = piece

    def step(self, *deps):
        self.step_now += 1
        ring, step = self.ring, self.step_now
        up, down = self.up, self.down
        if deps:
            up, down = after(up, *deps), after(down, *deps)
        shift = 0
        if step == ring.size // 2:
            shift = up.shape[0] // 2
            up, down = split(up, down)
            self.sent = up, down
        self.up = lax.ppermute(up, "dp", ring.up)
        self.down = lax.ppermute(down, "dp", ring.down)
        self.pieces += [self.up, self.down]
        order = ring_order(ring.size)
        self.places += [
            order.index(step if shift else -step) * self.rows,
            order.index(step) * self.rows + shift,
        ]
        return self.up, self.down

    def end(self, *deps):
        pieces = self.pieces
        if deps:
            pieces = [after(pieces[0], *deps), *pieces[1:]]
        return assemble(self.places, pieces)


class Reduce:
    def __init__(self, ring, block, groups):
        self.ring, self.block, self.groups = ring, block, groups
        self.index = 0
        self.came = ()

    def step(self, *deps):
        groups = self.groups
        if deps:
            first = groups[0][0]
            groups = [[(after(first[0], *deps), *first[1:]), *groups[0][1:]], *groups[1:]]
        if self.index == 0:
            groups = [[(term[0],) for term in group] for group in groups]
        sent, came = [], []
        for way, perm in enumerate((self.ring.up, self.ring.down)):
            sent.append(ring_sum(self.index, way, self.block, groups, self.came[way : way + 1]))
            came.append(lax.ppermute(sent[way], "dp", perm))
        self.sent, self.came = tuple(sent), tuple(came)
        self.index += 2 if self.index else 1
        return self.came

    def end(self, splits, *deps):
        came = self.came
        if deps:
            came = after(came[0], *deps), came[1]
        return ring_end(self.ring.size, self.groups, came, splits)


def per_device(n_dp, tokens, seq_lengths, ln_gain, ln_bias, w_qkv, w_out, w_up, w_down, cotangent):
    ids = jnp.stack([lax.axis_index("dp"), lax.axis_index("mp")]).astype(jnp.int32)
    ring = Ring(n_dp, ids)
    count, width = tokens.shape
    rows = count // 2
    w_rows, units = w_up.shape
    cols = w_out.shape[0]

    def swap_sides(value):
        return lax.ppermute(value, "mp", [(0, 1), (1, 0)])

    done = {}

    def dep(name):
        found = []
        for other in ORDER.get(name, ()):
            value = done[other]
            found += list(value) if isinstance(value, (tuple, list)) else [value]
        return found

    def tie(value, name):
        others = dep(name)
        return after(value, *others) if others else value

    def both(own, name):
        return [own, swap_cores(ring, tie(own, name))]

    g1 = Gather(ring, stage(after(w_qkv, ids), w_out.T))
    done["s11"] = g1.step()
    cot_got = done["cot_got"] = swap_sides(tie(cotangent, "cot_swap"))
    stage2, stage3 = stage(w_up), stage(w_down.T)
    done["stages"] = stage2, stage3
    done["s12"] = g1.step(*dep("s12"))
    x, a1, gain, bias = prepare(ids, tokens, ln_gain, ln_bias)
    done["a1"] = a1
    done["s13"] = g1.step(*dep("s13"))
    done["s14"] = g1.step(*dep("s14"))
    done["s14_sent"] = g1.sent
    g2 = Gather(ring, tie(stage2, "s21"))
    done["s21"] = g2.step()
    g3 = Gather(ring, tie(stage3, "s31"))
    done["s31"] = g3.step()
    own = done["own1"] = g1.end(*dep("own1"))
    w1 = both(own, "w1")
    cos, sin = rotary_pair(tie(seq_lengths, "rotary"), count)
    cot = done["cot"] = cotangent_rows(tie(ids, "cot"), cotangent, cot_got)
    done["s22"] = g2.step(*dep("s22"))
    qkv = done["qkv"] = qkv_project(tie(a1, "qkv"), w1, cos, sin)
    probs, outs, ys, a3s, mids, zs, backs, mid_backs = [], [], [], [], [], [], [], []
    for c in range(2):
        p, o, part = attend(c * rows, rows, tie(seq_lengths, f"attend{c}"), qkv, w1)
        probs.append(p)
        outs.append(o)
        done[f"part{c}"] = part
        if c == 0:
            ys.append((part, swap_sides(part)))
            done["y0"] = ys[0][1]
    done["s32"] = g3.step(*dep("s32"))
    done["s23"] = g2.step(*dep("s23"))
    ys.append((part, swap_sides(tie(part, "y1"))))
    done["y1"] = ys[1][1]
    done["s33"] = g3.step(*dep("s33"))
    done["s24"] = g2.step(*dep("s24"))
    own = done["own2"] = g2.end(*dep("own2"))
    w2 = both(own, "w2")
    a3s.append(mid_norm(0, tie(x, "norm0"), *ys[0], gain, bias))
    done["norm0"] = a3s[0]
    done["s34"] = g3.step(*dep("s34"))
    own = done["own3"] = g3.end(*dep("own3"))
    w3 = both(own, "w3")
    mids.append(up_project(tie(a3s[0], "up0"), w2))
    done["up0"] = mids[0][0]
    part = down_project(tie(mids[0][0], "down0"), w3)
    done["down0"] = part
    zs.append((part, swap_sides(part)))
    a3s.append(mid_norm(1, tie(x, "norm1"), *ys[1], gain, bias))
    done["norm1"] = a3s[1]
    mids.append(up_project(tie(a3s[1], "up1"), w2))
    done["up1"] = mids[1][0]
    part = down_project(tie(mids[1][0], "down1"), w3)
    done["down1"] = part
    zs.append((part, swap_sides(part)))
    for c in range(2):
        z = zs[c][0], tie(zs[c][1], f"back{c}")
        dz, du, part = mlp_back(c, *z, cot, gain, mids[c][1], w3, w2)
        backs.append((dz, du, (part, swap_sides(part))))
        done[f"back{c}"], done[f"da{c}"] = dz, backs[c][2][1]
    dzs, dus = [b[0] for b in backs], [b[1] for b in backs]
    gs = [m[0] for m in mids]

    def mid(c):
        w = mid_back(c, tie(x, f"mid{c}"), *ys[c], *backs[c][2], cot, gain, bias, w1)
        done[f"mid{c}"] = w[0]
        mid_backs.append(w)

    def grad(which, products, name):
        others = dep(name)
        if others:
            (lefts, rights), rest = products[0], products[1:]
            products = [([after(lefts[0], *others), *lefts[1:]], rights), *rest]
        term = weight_grad(which, ring.size, products)
        done[name] = term[0]
        return term

    def swap_term(term, name):
        far = swap_cores(ring, term[0])
        done[name + "_far"] = far
        return far, swap_cores(ring, after(term[1], far, *dep(name + "_near")))

    def ring_step(reduce, name):
        done[name] = reduce.step(*dep(name))
        done[name + "_sent"] = reduce.sent

    down_other = grad(1, [(dzs, gs)], "down_other")
    up_other = grad(1, [(a3s, dus)], "up_other")
    down_mine = grad(0, [(dzs, gs)], "down_mine")
    down_got = swap_term(down_other, "down")
    up_mine = grad(0, [(a3s, dus)], "up_mine")
    up_got = swap_term(up_other, "up")
    mlp_ring = Reduce(ring, w_rows, [[down_mine, down_got], [up_mine, up_got]])
    ring_step(mlp_ring, "m1")
    mid(0)
    output, gb3 = last_norm(tie(ids, "last"), x, cot, gain, bias, ys, zs)
    done["last"] = output
    ring_step(mlp_ring, "m2")
    mid(1)
    grads = [m[2] for m in mid_backs]
    g_qkv = done["g_qkv"] = attend_back(tie(qkv, "g_qkv"), probs, outs, grads, cos, sin)
    attn_products = [([a1], [g_qkv]), ([m[1] for m in mid_backs], outs)]
    attn_other = grad(1, attn_products, "attn_other")
    attn_got = swap_term(attn_other, "attn")
    ring_step(mlp_ring, "m3")
    part_keep, part_give, gb0 = in_back(ids, tie(g_qkv, "in_back"), x, w1)
    done["in_back"] = part_keep
    gain_mine, gain_other = gain_sum(gb0, [m[3] for m in mid_backs], gb3)
    done["gain_sum"] = gain_mine
    gain_terms = [
        gain_mine,
        swap_cores(ring, gain_other),
        swap_sides(gain_mine),
        lax.ppermute(gain_other, ("dp", "mp"), [(i, i ^ 3) for i in range(2 * n_dp)]),
    ]
    attn_mine = grad(0, attn_products, "attn_mine")
    gains = gain_pack([tie(gain_terms[0], "gains"), *gain_terms[1:]])
    done["gains"] = gains
    part_got = done["part_got"] = swap_sides(tie(part_give, "part_give"))
    attn_ring = Reduce(ring, w_rows, [[attn_mine, attn_got], [(gains,)]])
    ring_step(attn_ring, "q1")
    ring_step(mlp_ring, "m4")
    ring_step(attn_ring, "q2")
    grad_tokens = done["tokens"] = tokens_back(
        tie(ids, "tokens"), x, part_keep, part_got, [m[0] for m in mid_backs], gain
    )
    ring_step(attn_ring, "q3")
    grad_down, grad_up = mlp_ring.end([[(1, units)], [(1, units)]], *dep("m_end"))
    done["m_end"] = grad_down
    ring_step(attn_ring, "q4")
    grad_qkv, grad_out, grad_gain, grad_bias = attn_ring.end([[(3, cols), (1, cols)], [(0, LANES)]])
    return output, grad_tokens, grad_qkv, grad_out.T, grad_up, grad_down.T, grad_gain, grad_bias


def layer_norm(values, norm_gain, norm_bias):
    average = jnp.mean(values, axis=-1, keepdims=True)
    centred = values - average
    variance = jnp.mean(centred * centred, axis=-1, keepdims=True)
    return centred * lax.rsqrt(variance + NORM_EPS) * norm_gain + norm_bias


def norm_pull(values, norm_gain, norm_bias, grad_result):
    result, puller = jax.vjp(layer_norm, values, norm_gain, norm_bias)
    return puller(grad_result)


def seq_layout(lengths, block_size):
    block_count = lengths.shape[0]
    block_ids = jnp.arange(block_count, dtype=jnp.int32)
    starts = lengths > 0
    earlier = starts[None, :] & (block_ids[None, :] <= block_ids[:, None])
    owners = jnp.max(jnp.where(earlier, block_ids[None, :], 0), axis=1)
    owner_len = jnp.sum(
        jnp.where(block_ids[None, :] == owners[:, None], lengths[None, :], 0), axis=1
    )
    places = jnp.arange(block_count * block_size, dtype=jnp.int32)
    tok_owner = jnp.repeat(owners, block_size)
    position = places - tok_owner * block_size
    is_valid = position < jnp.repeat(owner_len, block_size)
    allowed = (
        (tok_owner[:, None] == tok_owner[None, :])
        & (places[None, :] <= places[:, None])
        & is_valid[None, :]
    )
    return (position, allowed)


def rotary_tables(position, width):
    frequency = ROPE_BASE ** (-jnp.arange(width // 2, dtype=jnp.float32) * 2.0 / width)
    angles = position.astype(jnp.float32)[:, None] * frequency[None, :]
    return (jnp.cos(angles), jnp.sin(angles))


def rotate(values, cos_table, sin_table):
    half_width = values.shape[-1] // 2
    front_half = values[..., :half_width]
    back_half = values[..., half_width:]
    cos_part = cos_table[:, None, :]
    sin_part = sin_table[:, None, :]
    return jnp.concatenate(
        [
            front_half * cos_part - back_half * sin_part,
            back_half * cos_part + front_half * sin_part,
        ],
        axis=-1,
    )


def attention_scores(queries, keys_rot, allowed, scale):
    raw_scores = (
        jnp.einsum("hqd,hkd->hqk", queries, keys_rot, preferred_element_type=jnp.float32) * scale
    )
    return jnp.where(allowed[None, :, :], raw_scores, MASK_FILL)


def plain_device(tokens, seq_lengths, ln_gain, ln_bias, w_qkv, w_out, w_up, w_down, cotangent):
    full_qkv, full_out, full_up, full_down = (
        lax.all_gather(w_qkv, "dp", axis=1, tiled=True),
        lax.all_gather(w_out, "dp", axis=1, tiled=True),
        lax.all_gather(w_up, "dp", axis=0, tiled=True),
        lax.all_gather(w_down, "dp", axis=1, tiled=True),
    )
    tok_count = tokens.shape[0]
    shard_rows = cotangent.shape[0]
    row_start = lax.axis_index("mp") * shard_rows
    heads_here = full_out.shape[0] // HD
    scale = HD ** (-0.5)
    position, allowed = seq_layout(seq_lengths, BLOCK)
    cos_table, sin_table = rotary_tables(position, HD)

    def to_heads(values):
        return jnp.transpose(values.reshape(tok_count, heads_here, HD), (1, 0, 2))

    def from_heads(values):
        return jnp.transpose(values, (1, 0, 2)).reshape(tok_count, heads_here * HD)

    def rotated(values):
        return rotate(values.reshape(tok_count, heads_here, HD), cos_table, sin_table)

    inputs = tokens.astype(jnp.float32)
    normed_in = layer_norm(inputs, ln_gain[0], ln_bias[0]).astype(jnp.bfloat16)
    projected = jnp.einsum("td,cde->cte", normed_in, full_qkv, preferred_element_type=jnp.float32)
    queries = jnp.transpose(rotated(projected[0]), (1, 0, 2)).astype(jnp.bfloat16)
    keys_rot = jnp.transpose(rotated(projected[1]), (1, 0, 2)).astype(jnp.bfloat16)
    values_h = to_heads(projected[2]).astype(jnp.bfloat16)
    scores = attention_scores(queries, keys_rot, allowed, scale)
    top_score = jnp.max(scores, axis=-1, keepdims=True)
    expo = jnp.exp(scores - top_score)
    row_total = jnp.sum(expo, axis=-1, keepdims=True)
    probs = expo / row_total
    log_total = top_score + jnp.log(row_total)
    attended = jnp.einsum(
        "hqk,hkd->hqd", probs.astype(jnp.bfloat16), values_h, preferred_element_type=jnp.float32
    )
    mixed_heads = from_heads(attended).astype(jnp.bfloat16)
    attn_part = jnp.dot(mixed_heads, full_out, preferred_element_type=jnp.float32)
    attn_sum = lax.psum_scatter(
        attn_part.astype(jnp.bfloat16), "mp", scatter_dimension=0, tiled=True
    ).astype(jnp.float32)
    resid_in = lax.dynamic_slice_in_dim(inputs, row_start, shard_rows, 0)
    hidden_state = resid_in + layer_norm(attn_sum, ln_gain[1], ln_bias[1])
    normed_mid = layer_norm(hidden_state, ln_gain[2], ln_bias[2]).astype(jnp.bfloat16)
    mlp_input = lax.all_gather(normed_mid, "mp", axis=0, tiled=True)
    pre_act = jnp.dot(mlp_input, full_up, preferred_element_type=jnp.float32)
    act_low = jax.nn.gelu(pre_act, approximate=True).astype(jnp.bfloat16)
    mlp_part = jnp.dot(act_low, full_down, preferred_element_type=jnp.float32)
    mlp_sum = lax.psum_scatter(
        mlp_part.astype(jnp.bfloat16), "mp", scatter_dimension=0, tiled=True
    ).astype(jnp.float32)
    output = (hidden_state + layer_norm(mlp_sum, ln_gain[3], ln_bias[3])).astype(jnp.bfloat16)
    grad_result = cotangent.astype(jnp.float32)
    grad_mlp_sum, grad_gain3, grad_bias3 = norm_pull(mlp_sum, ln_gain[3], ln_bias[3], grad_result)
    grad_mlp_rows = lax.all_gather(grad_mlp_sum.astype(jnp.bfloat16), "mp", axis=0, tiled=True)
    grad_down = jnp.einsum("tf,te->fe", act_low, grad_mlp_rows, preferred_element_type=jnp.float32)
    grad_act = jnp.einsum("te,fe->tf", grad_mlp_rows, full_down, preferred_element_type=jnp.float32)
    gelu_puller = jax.vjp(lambda values: jax.nn.gelu(values, approximate=True), pre_act)[1]
    grad_pre = gelu_puller(grad_act)[0].astype(jnp.bfloat16)
    grad_up = jnp.einsum("td,tf->df", mlp_input, grad_pre, preferred_element_type=jnp.float32)
    grad_mid_part = jnp.einsum("tf,df->td", grad_pre, full_up, preferred_element_type=jnp.float32)
    grad_mid = lax.psum_scatter(
        grad_mid_part.astype(jnp.bfloat16), "mp", scatter_dimension=0, tiled=True
    ).astype(jnp.float32)
    grad_hidden_norm, grad_gain2, grad_bias2 = norm_pull(
        hidden_state, ln_gain[2], ln_bias[2], grad_mid
    )
    grad_hidden = grad_result + grad_hidden_norm
    grad_attn_sum, grad_gain1, grad_bias1 = norm_pull(attn_sum, ln_gain[1], ln_bias[1], grad_hidden)
    grad_attn_rows = lax.all_gather(grad_attn_sum.astype(jnp.bfloat16), "mp", axis=0, tiled=True)
    grad_outproj = jnp.einsum(
        "tc,te->ce", mixed_heads, grad_attn_rows, preferred_element_type=jnp.float32
    )
    grad_mixed = jnp.einsum(
        "te,ce->tc", grad_attn_rows, full_out, preferred_element_type=jnp.float32
    ).astype(jnp.bfloat16)
    grad_heads = to_heads(grad_mixed)
    again_scores = attention_scores(queries, keys_rot, allowed, scale)
    again_probs = jnp.exp(again_scores - log_total)
    grad_probs = jnp.einsum(
        "hqd,hkd->hqk", grad_heads, values_h, preferred_element_type=jnp.float32
    )
    grad_values = jnp.einsum(
        "hqk,hqd->hkd",
        again_probs.astype(jnp.bfloat16),
        grad_heads,
        preferred_element_type=jnp.float32,
    )
    row_dot = jnp.sum(again_probs * grad_probs, axis=-1, keepdims=True)
    grad_scores = (again_probs * (grad_probs - row_dot) * scale).astype(jnp.bfloat16)
    grad_q_rot = jnp.einsum(
        "hqk,hkd->hqd", grad_scores, keys_rot, preferred_element_type=jnp.float32
    )
    grad_k_rot = jnp.einsum(
        "hqk,hqd->hkd", grad_scores, queries, preferred_element_type=jnp.float32
    )
    zero_heads = jnp.zeros((tok_count, heads_here, HD), jnp.float32)
    unrotate = jax.vjp(lambda values: rotate(values, cos_table, sin_table), zero_heads)[1]
    grad_query = unrotate(jnp.transpose(grad_q_rot, (1, 0, 2)))[0].reshape(
        tok_count, heads_here * HD
    )
    grad_key = unrotate(jnp.transpose(grad_k_rot, (1, 0, 2)))[0].reshape(tok_count, heads_here * HD)
    grad_value = from_heads(grad_values)
    grad_proj = jnp.stack(
        [
            grad_query.astype(jnp.bfloat16),
            grad_key.astype(jnp.bfloat16),
            grad_value.astype(jnp.bfloat16),
        ]
    )
    grad_qkv = jnp.einsum("td,cte->cde", normed_in, grad_proj, preferred_element_type=jnp.float32)
    grad_in_part = jnp.einsum(
        "cte,cde->td", grad_proj, full_qkv, preferred_element_type=jnp.float32
    )
    grad_in = lax.psum_scatter(
        grad_in_part.astype(jnp.bfloat16), "mp", scatter_dimension=0, tiled=True
    ).astype(jnp.float32)
    grad_norm_in, grad_gain0, grad_bias0 = norm_pull(resid_in, ln_gain[0], ln_bias[0], grad_in)
    grad_tokens = grad_hidden + grad_norm_in
    gain_grads = jnp.stack([grad_gain0, grad_gain1, grad_gain2, grad_gain3])
    bias_grads = jnp.stack([grad_bias0, grad_bias1, grad_bias2, grad_bias3])
    gain_grads, bias_grads = (
        lax.psum(gain_grads.astype(jnp.bfloat16), "mp").astype(jnp.float32),
        lax.psum(bias_grads.astype(jnp.bfloat16), "mp").astype(jnp.float32),
    )
    grad_qkv, grad_outproj, grad_up, grad_down, gain_grads, bias_grads = (
        lax.psum_scatter(
            grad_qkv.astype(jnp.bfloat16), "dp", scatter_dimension=1, tiled=True
        ).astype(jnp.float32),
        lax.psum_scatter(
            grad_outproj.astype(jnp.bfloat16), "dp", scatter_dimension=1, tiled=True
        ).astype(jnp.float32),
        lax.psum_scatter(
            grad_up.astype(jnp.bfloat16), "dp", scatter_dimension=0, tiled=True
        ).astype(jnp.float32),
        lax.psum_scatter(
            grad_down.astype(jnp.bfloat16), "dp", scatter_dimension=1, tiled=True
        ).astype(jnp.float32),
        lax.psum_scatter(
            gain_grads.astype(jnp.bfloat16), "dp", scatter_dimension=1, tiled=True
        ).astype(jnp.float32),
        lax.psum_scatter(
            bias_grads.astype(jnp.bfloat16), "dp", scatter_dimension=1, tiled=True
        ).astype(jnp.float32),
    )
    return (output, grad_tokens, grad_qkv, grad_outproj, grad_up, grad_down, gain_grads, bias_grads)


def solution(mesh):
    placed = (
        P("dp", None),
        P("dp"),
        P(),
        P(),
        P(None, "dp", "mp"),
        P("mp", "dp"),
        P("dp", "mp"),
        P("mp", "dp"),
        P(("dp", "mp"), None),
    )
    n_dp, n_mp = mesh.shape["dp"], mesh.shape["mp"]

    def layer(tokens, *rest):
        if n_mp == 2 and tokens.shape[1] == n_dp * LANES // 2:
            return per_device(n_dp, tokens, *rest)
        return plain_device(tokens, *rest)

    return jax.shard_map(
        layer,
        mesh=mesh,
        in_specs=placed,
        out_specs=(
            P(("dp", "mp"), None),
            P(("dp", "mp"), None),
            P(None, "dp", "mp"),
            P("mp", "dp"),
            P("dp", "mp"),
            P("mp", "dp"),
            P(None, "dp"),
            P(None, "dp"),
        ),
        check_vma=False,
    )
```
